32 devices in a mesh: dp: 16 (over z, y, x), tensor: 2 (over core).
Axes of the slice: x: 2, y: 2, z: 4, core: 2. Of those that a mesh axis runs over, the one named last changes fastest.
Arguments:
- stream: bfloat16 [10240, 1024], P(('dp', 'tensor')), may hold values from -24 to 24
- counts: int32 [32], P('dp'), may hold values from 16 to 256
- cotangent: bfloat16 [10240, 1024], P(('dp', 'tensor')), may hold values from -6 to 6
- w_qkv: bfloat16 [3, 1024, 1024], P(None, 'dp', 'tensor'), may hold values from -0.1875 to 0.1875
- b_qv: float32 [2, 1024], replicated, may hold values from -1.5 to 1.5
- w_out: bfloat16 [1024, 1024], P('tensor', 'dp'), may hold values from -0.75 to 0.75
- b_out: float32 [1024], replicated, may hold values from -1.8 to 1.8
- w_fc1: bfloat16 [1024, 4096], P('dp', 'tensor'), may hold values from -0.35 to 0.35
- b_fc1: float32 [4096], replicated, may hold values from -3 to 3
- w_fc2: bfloat16 [4096, 1024], P('tensor', 'dp'), may hold values from -0.09375 to 0.09375
- b_fc2: float32 [1024], replicated, may hold values from -1.8 to 1.8
- gain_one: float32 [1024], replicated, may hold values from 0.25 to 1.75
- shift_one: float32 [1024], replicated, may hold values from -1.8 to 1.8
- gain_two: float32 [1024], replicated, may hold values from 0.25 to 1.75
- shift_two: float32 [1024], replicated, may hold values from -1.8 to 1.8
Outputs:
- activations: bfloat16 [10240, 1024], P(('dp', 'tensor'))
- grad_input: float32 [10240, 1024], P(('dp', 'tensor'))
- grad_w_qkv: float32 [3, 1024, 1024], P(None, 'dp', 'tensor')
- grad_b_qv: float32 [2, 1024], P(None, ('dp', 'tensor'))
- grad_w_out: float32 [1024, 1024], P('tensor', 'dp')
- grad_b_out: float32 [1024], P(('dp', 'tensor'))
- grad_w_fc1: float32 [1024, 4096], P('dp', 'tensor')
- grad_b_fc1: float32 [4096], P(('dp', 'tensor'))
- grad_w_fc2: float32 [4096, 1024], P('tensor', 'dp')
- grad_b_fc2: float32 [1024], P(('dp', 'tensor'))
- grad_gain_one: float32 [1024], P(('dp', 'tensor'))
- grad_shift_one: float32 [1024], P(('dp', 'tensor'))
- grad_gain_two: float32 [1024], P(('dp', 'tensor'))
- grad_shift_two: float32 [1024], P(('dp', 'tensor'))
- rms_stats: float32 [5], replicated
The draws below stay inside these ranges and needn't reach their ends.
All inputs are finite; a program needn't handle non-finite values.
Results may differ from the reference program's by a relative error of at most 0.02.
Values may be sent and summed in bfloat16 or wider, within the bound.
A program may use at most 128 MiB of HBM per device.

```python
import math
import jax
import jax.numpy as jnp
from jax import lax

D = 1024
H = 16
HD = 64
FF = 4096
BUFFER = 64
PATCHES = 256
SLOTS = 320
IMAGES = 32
TOKENS = 10240


def draw_stream(key, part):
    image_pos = jnp.arange(IMAGES, dtype=jnp.float32) / max(IMAGES - 1, 1)
    noise = jnp.clip(jax.random.normal(key, (IMAGES, SLOTS, D), jnp.float32), -4.0, 4.0)
    values = noise * (1.0 + 2.0 * image_pos)[:, None, None]
    return values.reshape(TOKENS, D).astype(jnp.bfloat16)


def draw_w_fc1(key, part):
    key = jax.random.fold_in(key, 11)
    unit_key = jax.random.fold_in(key, 3)
    entries = jnp.clip(jax.random.normal(key, (D, FF), jnp.float32), -4.0, 4.0)
    offsets = jnp.clip(jax.random.normal(unit_key, (1, FF), jnp.float32), -3.0, 3.0)
    values = (entries + 0.4 * offsets) * D ** (-0.5)
    return values.astype(jnp.bfloat16)


def touch_ends(values, stream_key, smallest, largest):
    longest = values.shape.index(max(values.shape))
    spots = []
    for shift in (0, 1):
        where = [jax.random.randint(jax.random.fold_in(stream_key, axis), (), 0, length) for axis, length in enumerate(values.shape)]
        where[longest] = (where[longest] + shift) % values.shape[longest]
        spots.append(tuple(where))
    return values.at[spots[0]].set(smallest).at[spots[1]].set(largest)


def level_of(key, extent, shards, low, high):
    level = 1.0
    for dim, parts in shards:
        heights = jax.random.uniform(jax.random.fold_in(jax.random.fold_in(key, 6), dim), (parts,), jnp.float32, low / len(shards), high / len(shards))
        level = level * jnp.repeat(jnp.exp(heights), extent[dim] // parts).reshape((-1,) + (1,) * (len(extent) - 1 - dim))
    return level


def bell_draw(own_key, dims, width, bound, cuts=(), kind=jnp.bfloat16):
    factor_of = level_of(own_key, dims, cuts, -0.22, 0.18) if cuts else 1.0
    values = jax.random.normal(own_key, dims, jnp.float32) * width * factor_of
    return jnp.minimum(jnp.maximum(values, -bound), bound).astype(kind)


def setup_inputs(seed: int = 0) -> dict:
    arg_keys = jax.random.split(jax.random.key(seed), 16)
    stream = draw_stream(jax.random.fold_in(arg_keys[15], 71), 0)
    counts = touch_ends(jax.random.randint(arg_keys[1], (IMAGES,), PATCHES // 16, PATCHES + 1), jax.random.fold_in(arg_keys[1], 1), PATCHES // 16, PATCHES).astype(jnp.int32)
    cotangent = bell_draw(arg_keys[2], (TOKENS, D), 1.0, 6.0, ((0, 32),))
    w_qkv = bell_draw(arg_keys[3], (3, D, D), D ** -0.5, 0.1875, ((1, 16), (2, 2)))
    b_qv = bell_draw(arg_keys[4], (2, D), 0.25, 1.5, (), jnp.float32)
    w_out = bell_draw(arg_keys[5], (D, D), HD ** -0.5, 0.75, ((0, 2), (1, 16)))
    b_out = bell_draw(arg_keys[6], (D,), 0.3, 1.8, (), jnp.float32)
    w_fc1 = draw_w_fc1(jax.random.fold_in(arg_keys[15], 71), 0)
    b_fc1 = bell_draw(arg_keys[8], (FF,), 0.5, 3.0, (), jnp.float32)
    w_fc2 = bell_draw(arg_keys[9], (FF, D), FF ** -0.5, 0.09375, ((0, 2), (1, 16)))
    b_fc2 = bell_draw(arg_keys[10], (D,), 0.3, 1.8, (), jnp.float32)
    gain_one = jnp.clip(1.0 + 0.15 * jax.random.normal(arg_keys[11], (D,), jnp.float32), 0.25, 1.75)
    shift_one = bell_draw(arg_keys[12], (D,), 0.3, 1.8, (), jnp.float32)
    gain_two = jnp.clip(1.0 + 0.15 * jax.random.normal(arg_keys[13], (D,), jnp.float32), 0.25, 1.75)
    shift_two = bell_draw(arg_keys[14], (D,), 0.3, 1.8, (), jnp.float32)
    return dict(stream=stream, counts=counts, cotangent=cotangent, w_qkv=w_qkv, b_qv=b_qv, w_out=w_out, b_out=b_out, w_fc1=w_fc1, b_fc1=b_fc1, w_fc2=w_fc2, b_fc2=b_fc2, gain_one=gain_one, shift_one=shift_one, gain_two=gain_two, shift_two=shift_two)


@jax.custom_vjp
def low(v):
    return lax.optimization_barrier(v.astype(jnp.bfloat16)).astype(jnp.float32)

@jax.custom_vjp
def low_back(v):
    return v

def low_keep(v):
    return (low(v), None)

def low_pass(kept, grad):
    return (grad,)

def back_keep(v):
    return (v, None)

def back_low(kept, grad):
    return (low(grad),)
low.defvjp(low_keep, low_pass)
low_back.defvjp(back_keep, back_low)
eps_norm = 1e-06
highest_precision = lax.Precision.HIGHEST

def layer_norm(values, gain, shift):
    centre = lax.optimization_barrier(jnp.mean(values, axis=-1, keepdims=True))
    offset = values - centre
    spread = lax.optimization_barrier(jnp.mean(offset * offset, axis=-1, keepdims=True))
    return offset * lax.rsqrt(spread + eps_norm) * gain + shift

def forward(stream_rows, validity, w_qkv, b_qv, w_out, b_out, w_fc1, b_fc1, w_fc2, b_fc2, gain_one, shift_one, gain_two, shift_two):
    image_count = validity.shape[0]
    row_count = stream_rows.shape[0]
    scale = HD ** (-0.5)
    normed_one = low(layer_norm(stream_rows, gain_one, shift_one))
    queries = low(low_back(jnp.dot(normed_one, w_qkv[0], precision=highest_precision) + b_qv[0]))
    key_rows = low(low_back(jnp.dot(normed_one, w_qkv[1], precision=highest_precision)))
    values = low(low_back(jnp.dot(normed_one, w_qkv[2], precision=highest_precision) + b_qv[1]))
    shape_heads = (image_count, SLOTS, H, HD)
    scores = jnp.einsum('bqhd,bkhd->bhqk', queries.reshape(shape_heads), key_rows.reshape(shape_heads), precision=highest_precision)
    scores = low_back(scores * scale)
    scores = jnp.where(validity[:, None, None, :] > 0, scores, -1e+30)
    highest = lax.optimization_barrier(jnp.max(scores, axis=-1, keepdims=True))
    expo_terms = jnp.exp(scores - highest)
    probs = low(expo_terms / lax.optimization_barrier(jnp.sum(expo_terms, axis=-1, keepdims=True)))
    mixture = jnp.einsum('bhqk,bkhd->bqhd', probs, values.reshape(shape_heads), precision=highest_precision)
    attn_heads = low(low_back(mixture.reshape(row_count, H * HD)))
    branch = low_back(jnp.dot(attn_heads, w_out, precision=highest_precision) + b_out)
    middle = stream_rows + branch
    normed_two = low(layer_norm(middle, gain_two, shift_two))
    hidden_pre = low_back(jnp.dot(normed_two, w_fc1, precision=highest_precision) + b_fc1)
    hidden_act = low(jax.nn.gelu(hidden_pre, approximate=False))
    feed = low_back(jnp.dot(hidden_act, w_fc2, precision=highest_precision) + b_fc2)
    result = middle + feed
    row_valid = validity.reshape(row_count, 1)
    squares = jnp.stack([jnp.sum(row_valid * member * member) for member in (stream_rows, middle, result, branch, feed)])
    return (result * row_valid, squares)

def reference(stream, counts, cotangent, w_qkv, b_qv, w_out, b_out, w_fc1, b_fc1, w_fc2, b_fc2, gain_one, shift_one, gain_two, shift_two):
    group = math.gcd(IMAGES, 8)
    steps_count = IMAGES // group
    params = tuple((member.astype(jnp.float32) for member in (w_qkv, b_qv, w_out, b_out, w_fc1, b_fc1, w_fc2, b_fc2, gain_one, shift_one, gain_two, shift_two)))
    slot_index = jnp.arange(SLOTS, dtype=jnp.int32)
    validity = (slot_index[None, :] < (BUFFER + counts)[:, None]).astype(jnp.float32)
    stream_blocks = stream.astype(jnp.float32).reshape(steps_count, group * SLOTS, D)
    cot_blocks = cotangent.astype(jnp.float32).reshape(steps_count, group * SLOTS, D)
    valid_blocks = validity.reshape(steps_count, group, SLOTS)

    def advance(carried, inputs):
        stream_rows, cot_rows, valid_rows = inputs

        def block_forward(rows_in, *weights):
            return forward(rows_in, valid_rows, *weights)
        output, pullback, squares = jax.vjp(block_forward, stream_rows, *params, has_aux=True)
        gradients = pullback(cot_rows)
        carried_next = (carried[0] + squares,) + tuple((running + gradient for running, gradient in zip(carried[1:], gradients[1:])))
        return (carried_next, (output, gradients[0]))
    start_state = (jnp.zeros((5,), jnp.float32),) + tuple((jnp.zeros(member.shape, jnp.float32) for member in params))
    carried, (outputs, input_grads) = lax.scan(advance, start_state, (stream_blocks, cot_blocks, valid_blocks))
    valid_count = jnp.sum(validity)
    rms_stats = jnp.sqrt(carried[0] / (valid_count * D))
    totals = carried[1:]
    return (outputs.reshape(TOKENS, D).astype(jnp.bfloat16), input_grads.reshape(TOKENS, D), totals[0], totals[1], totals[2], totals[3], totals[4], totals[5], totals[6], totals[7], totals[8], totals[9], totals[10], totals[11], rms_stats)
```

```python
import jax
import jax.numpy as jnp
from jax import lax
from jax.experimental import pallas as pl
from jax.experimental.pallas import tpu as pltpu
from jax.sharding import PartitionSpec as P

MESH = pl.DeviceIdType.MESH


class Place:
    def __init__(self):
        dp = lax.axis_index("dp")
        self.t = lax.axis_index("tensor")
        self.z, self.y, self.x = dp // 4, (dp // 2) % 2, dp % 2
        self.side = self.z // 2
        self.w = self.z + self.side * (3 - 2 * self.z)
        self.step = 1 - 2 * self.side
        self.dp = dp

    def order(self, k):
        o = (self.w, 1 - self.w, 2, 3)[k]
        return 3 * self.side + self.step * o

    def chip(self, z, y, x):
        return z * 4 + y * 2 + x

    def inward(self):
        return (self.chip(self.z + self.step, self.y, self.x), self.t)

    def outward(self):
        return (self.chip(self.z - self.step, self.y, self.x), self.t)

    def across_x(self):
        return (self.chip(self.z, self.y, 1 - self.x), self.t)

    def across_y(self):
        return (self.chip(self.z, 1 - self.y, self.x), self.t)

    def twin(self):
        return (self.dp, 1 - self.t)


def enter(at):
    barrier = pltpu.get_barrier_semaphore()
    for other in (at.across_x(), at.across_y(), at.inward(), at.twin()):
        pl.semaphore_signal(barrier, inc=1, device_id=other, device_id_type=MESH)

    @pl.when(at.w == 1)
    def _():
        pl.semaphore_signal(barrier, inc=1, device_id=at.outward(), device_id_type=MESH)

    pl.semaphore_wait(barrier, 4 + at.w)


class Gather:
    def __init__(self, at, full, shard, pieces, send, recv):
        self.at, self.full, self.shard, self.pieces, self.send, self.recv = at, full, shard, pieces, send, recv

    def rows(self, p, z, y, x, part=None):
        c0, c1 = self.pieces[p]
        start, size = self.at.chip(z, y, x) * self.shard, self.shard
        if part is not None:
            size = self.shard // 2
            start = start + part * size
        return self.full.at[pl.ds(pl.multiple_of(start, size), size), pl.ds(c0, c1 - c0)]

    def copy(self, p, ref, s, r, other):
        return pltpu.make_async_remote_copy(
            src_ref=ref,
            dst_ref=ref,
            send_sem=self.send.at[p, s[0], s[1]],
            recv_sem=self.recv.at[p, r[0], r[1]],
            device_id=other,
            device_id_type=MESH,
        )

    def z_in(self, p, z):
        return self.copy(p, self.rows(p, z, self.at.y, self.at.x), (0, z), (0, z), self.at.inward())

    def z_out(self, p, z):
        return self.copy(p, self.rows(p, z, self.at.y, self.at.x), (5, z), (0, z), self.at.outward())

    def x_full(self, p, z):
        return self.copy(p, self.rows(p, z, self.at.y, self.at.x), (1, z), (1, z), self.at.across_x())

    def y_full(self, p, z):
        return self.copy(p, self.rows(p, z, self.at.y, self.at.x), (2, z), (2, z), self.at.across_y())

    def x_half(self, p, z):
        return self.copy(p, self.rows(p, z, 1 - self.at.y, self.at.x, 1), (3, z), (3, z), self.at.across_x())

    def y_half(self, p, z):
        return self.copy(p, self.rows(p, z, self.at.y, 1 - self.at.x, 0), (4, z), (4, z), self.at.across_y())

    def arrived(self, p, kind, z):
        at = self.at
        ref = (
            lambda: self.rows(p, z, at.y, at.x),
            lambda: self.rows(p, z, at.y, 1 - at.x),
            lambda: self.rows(p, z, 1 - at.y, at.x),
            lambda: self.rows(p, z, 1 - at.y, 1 - at.x, 1),
            lambda: self.rows(p, z, 1 - at.y, 1 - at.x, 0),
        )[kind]()
        self.copy(p, ref, (kind, z), (kind, z), at.across_x()).wait_recv()

    def line(self, p, k):
        at = self.at
        z = at.order(k)
        if k > 0:
            self.arrived(p, 0, z)
        if k == 0:
            self.z_in(p, z).start()
        if k == 1:

            @pl.when(at.w == 1)
            def _():
                self.z_in(p, z).start()

        else:

            @pl.when(at.w == 1)
            def _():
                self.z_out(p, z).start()

        self.x_full(p, z).start()
        self.y_full(p, z).start()

    def plane(self, p, k):
        z = self.at.order(k)
        self.arrived(p, 1, z)
        self.y_half(p, z).start()
        self.arrived(p, 2, z)
        self.x_half(p, z).start()

    def finish(self, p):
        for k in range(4):
            z = self.at.order(k)
            self.arrived(p, 3, z)
            self.arrived(p, 4, z)

    def drain(self, p):
        at = self.at
        for k in range(4):
            z = at.order(k)
            if k == 0:
                self.z_in(p, z).wait_send()
            if k == 1:

                @pl.when(at.w == 1)
                def _(z=z):
                    self.z_in(p, z).wait_send()

            else:

                @pl.when(at.w == 1)
                def _(z=z):
                    self.z_out(p, z).wait_send()

            self.x_full(p, z).wait_send()
            self.y_full(p, z).wait_send()
            self.x_half(p, z).wait_send()
            self.y_half(p, z).wait_send()


class Scatter:
    def __init__(self, at, full, shard, pieces, xh, yh, xf, yf, zl, send, recv):
        self.at, self.full, self.shard, self.pieces = at, full, shard, pieces
        self.xh, self.yh, self.xf, self.yf, self.zl = xh, yh, xf, yf, zl
        self.send, self.recv = send, recv

    def cols(self, p):
        c0, c1 = self.pieces[p]
        return pl.ds(c0, c1 - c0)

    def rows(self, p, z, y, x, part=None):
        start, size = self.at.chip(z, y, x) * self.shard, self.shard
        if part is not None:
            size = self.shard // 2
            start = start + part * size
        ref, c0, c1 = self.full(p)
        return ref.at[pl.ds(pl.multiple_of(start, size), size), pl.ds(c0, c1 - c0)]

    def copy(self, p, src, dst, s, r, other):
        return pltpu.make_async_remote_copy(
            src_ref=src,
            dst_ref=dst,
            send_sem=self.send.at[p, s[0], s[1]],
            recv_sem=self.recv.at[p, r[0], r[1]],
            device_id=other,
            device_id_type=MESH,
        )

    def x_half(self, p, z):
        at = self.at
        return self.copy(
            p, self.rows(p, z, 1 - at.y, 1 - at.x, 0), self.xh.at[z, :, self.cols(p)], (1, z), (1, z), at.across_x()
        )

    def y_half(self, p, z):
        at = self.at
        return self.copy(
            p, self.rows(p, z, 1 - at.y, 1 - at.x, 1), self.yh.at[z, :, self.cols(p)], (2, z), (2, z), at.across_y()
        )

    def x_full(self, p, z):
        at = self.at
        return self.copy(
            p, self.rows(p, z, at.y, 1 - at.x), self.xf.at[z, :, self.cols(p)], (3, z), (3, z), at.across_x()
        )

    def y_full(self, p, z):
        at = self.at
        return self.copy(
            p, self.rows(p, z, 1 - at.y, at.x), self.yf.at[z, :, self.cols(p)], (4, z), (4, z), at.across_y()
        )

    def z_in(self, p, z, slot):
        at = self.at
        return self.copy(
            p, self.rows(p, z, at.y, at.x), self.zl.at[slot, :, self.cols(p)], (0, z), (0, slot), at.inward()
        )

    def z_out(self, p, z, slot):
        at = self.at
        return self.copy(
            p, self.rows(p, z, at.y, at.x), self.zl.at[slot, :, self.cols(p)], (0, z), (0, slot), at.outward()
        )

    def begin(self, p):
        for k in (3, 2, 1, 0):
            z = self.at.order(k)
            self.x_half(p, z).start()
            self.y_half(p, z).start()

    def plane(self, p, k):
        at = self.at
        z = at.order(k)
        self.x_half(p, z).wait_recv()
        ref = self.rows(p, z, 1 - at.y, at.x, 0)
        ref[...] = ref[...] + self.xh[z, :, self.cols(p)]
        self.y_full(p, z).start()
        self.y_half(p, z).wait_recv()
        ref = self.rows(p, z, at.y, 1 - at.x, 1)
        ref[...] = ref[...] + self.yh[z, :, self.cols(p)]
        self.x_full(p, z).start()

    def wait_line(self, p, z, slot):
        self.z_in(p, z, slot).wait_recv()

    def line(self, p, k, out=None):
        at = self.at
        z = at.order(k)
        self.x_full(p, z).wait_recv()
        self.y_full(p, z).wait_recv()
        ref = self.rows(p, z, at.y, at.x)
        total = (
            ref[...].astype(jnp.float32)
            + self.xf[z, :, self.cols(p)].astype(jnp.float32)
            + self.yf[z, :, self.cols(p)].astype(jnp.float32)
        )
        if k > 0:

            @pl.when(at.w == 0)
            def _():
                ref[...] = total.astype(jnp.bfloat16)
                self.z_in(p, z, z).start()

            @pl.when(at.w == 1)
            def _():
                self.wait_line(p, z, z)
                ref[...] = (total + self.zl[z, :, self.cols(p)].astype(jnp.float32)).astype(jnp.bfloat16)
                if k == 3:
                    self.z_in(p, z, z).start()
                elif k == 2:
                    self.z_in(p, z, 4).start()
                else:
                    self.z_out(p, z, 4).start()

        else:
            self.wait_line(p, z, 4)
            total = total + self.zl[4, :, self.cols(p)].astype(jnp.float32)

            @pl.when(at.w == 0)
            def _():
                out[...] = total

            @pl.when(at.w == 1)
            def _():
                self.wait_line(p, z, z)
                out[...] = total + self.zl[z, :, self.cols(p)].astype(jnp.float32)

    def drain(self, p):
        at = self.at
        for k in range(4):
            z = at.order(k)
            for c in (self.x_half(p, z), self.y_half(p, z), self.x_full(p, z), self.y_full(p, z)):
                c.wait_send()
            if k > 0:
                self.z_in(p, z, z).wait_send()

WIDTHS = (1536, 512, 1024, 1024, 1024, 1024)


def pieces_of():
    out, c = [], 0
    for n in WIDTHS:
        out.append((c, c + n))
        c += n
    return out


def gather_kernel(own_ref, full_ref, held, sem, send, recv):
    at = Place()
    shard = own_ref.shape[0]
    enter(at)
    pieces = pieces_of()
    g = Gather(at, held, shard, pieces, send, recv)
    cp = pltpu.make_async_copy(own_ref, held.at[pl.ds(pl.multiple_of(at.dp * shard, shard), shard), :], sem)
    cp.start()
    cp.wait()
    n = len(pieces)
    g.line(0, 0)
    for p in range(n):
        for k in range(1, 4):
            g.line(p, k)
            g.plane(p, k - 1)
            if k == 2 and p + 1 < n:
                g.line(p + 1, 0)
        g.plane(p, 3)
    for p in range(n):
        g.finish(p)
        g.drain(p)
    cp = pltpu.make_async_copy(held, full_ref, sem)
    cp.start()
    cp.wait()


def scatter_kernel(g_ref, out_ref, held, xh, yh, xf, yf, zl, sem, send, recv):
    at = Place()
    shard = out_ref.shape[0]
    enter(at)
    pieces = pieces_of()
    cp = pltpu.make_async_copy(g_ref, held, sem)
    cp.start()
    cp.wait()
    s = Scatter(at, lambda p: (held,) + pieces[p], shard, pieces, xh, yh, xf, yf, zl, send, recv)
    n = len(pieces)
    s.begin(0)
    for p in range(n):
        if p + 1 < n:
            s.begin(p + 1)
        for k in (3, 2, 1, 0):
            s.plane(p, k)
        if p > 0:
            for k in (3, 2, 1, 0):
                s.line(p - 1, k, out_ref.at[:, s.cols(p - 1)])
    for k in (3, 2, 1, 0):
        s.line(n - 1, k, out_ref.at[:, s.cols(n - 1)])
    for p in range(n):
        s.drain(p)


def gather_all(own):
    shard, cols = own.shape
    n = len(WIDTHS)
    return pl.pallas_call(
        gather_kernel,
        out_shape=jax.ShapeDtypeStruct((16 * shard, cols), jnp.bfloat16),
        in_specs=[pl.BlockSpec(memory_space=pl.ANY)],
        out_specs=pl.BlockSpec(memory_space=pl.ANY),
        scratch_shapes=[
            pltpu.VMEM((16 * shard, cols), jnp.bfloat16),
            pltpu.SemaphoreType.DMA,
            pltpu.SemaphoreType.DMA((n, 6, 4)),
            pltpu.SemaphoreType.DMA((n, 5, 4)),
        ],
        compiler_params=pltpu.CompilerParams(collective_id=1, has_side_effects=True, vmem_limit_bytes=48 << 20),
    )(own)


def scatter_all(grads):
    rows, cols = grads.shape
    shard = rows // 16
    n = len(WIDTHS)
    bf = jnp.bfloat16
    return pl.pallas_call(
        scatter_kernel,
        out_shape=jax.ShapeDtypeStruct((shard, cols), jnp.float32),
        in_specs=[pl.BlockSpec(memory_space=pl.ANY)],
        out_specs=pl.BlockSpec(memory_space=pltpu.VMEM),
        scratch_shapes=[
            pltpu.VMEM((rows, cols), bf),
            pltpu.VMEM((4, shard // 2, cols), bf),
            pltpu.VMEM((4, shard // 2, cols), bf),
            pltpu.VMEM((4, shard, cols), bf),
            pltpu.VMEM((4, shard, cols), bf),
            pltpu.VMEM((5, shard, cols), bf),
            pltpu.SemaphoreType.DMA,
            pltpu.SemaphoreType.DMA((n, 5, 4)),
            pltpu.SemaphoreType.DMA((n, 5, 5)),
        ],
        compiler_params=pltpu.CompilerParams(collective_id=2, has_side_effects=True, vmem_limit_bytes=48 << 20),
    )(grads)


HD = 64
BUFFER = 64
SLOTS = 320


eps_norm = 1e-06


def layer_norm(values, gain, shift):
    centre = jnp.mean(values, axis=-1, keepdims=True)
    offset = values - centre
    spread = jnp.mean(offset * offset, axis=-1, keepdims=True)
    return offset * lax.rsqrt(spread + eps_norm) * gain + shift


def gelu_exact(values):
    return jax.nn.gelu(values, approximate=False)


def masked_scores(queries, key_rows, validity):
    scores = jnp.einsum(
        "bqhd,bkhd->bhqk", queries, key_rows, preferred_element_type=jnp.float32
    ) * HD ** (-0.5)
    return jnp.where(validity[:, None, None, :] > 0, scores, -1e30)


def attend_block(members):
    queries, key_rows, values, validity = members
    scores = masked_scores(queries, key_rows, validity)
    highest = jnp.max(scores, axis=-1, keepdims=True)
    expo_terms = jnp.exp(scores - highest)
    totals = jnp.sum(expo_terms, axis=-1, keepdims=True)
    weights = (expo_terms / totals).astype(jnp.bfloat16)
    mixture = jnp.einsum("bhqk,bkhd->bqhd", weights, values, preferred_element_type=jnp.float32)
    return (mixture.astype(jnp.bfloat16), (highest + jnp.log(totals))[..., 0])


def attend_back(members):
    queries, key_rows, values, validity, log_total, d_mixture = members
    scores = masked_scores(queries, key_rows, validity)
    probs = jnp.exp(scores - log_total[..., None])
    d_values = jnp.einsum(
        "bhqk,bqhd->bkhd", probs.astype(jnp.bfloat16), d_mixture, preferred_element_type=jnp.float32
    )
    d_probs = jnp.einsum("bqhd,bkhd->bhqk", d_mixture, values, preferred_element_type=jnp.float32)
    d_scores = (probs * (d_probs - jnp.sum(probs * d_probs, axis=-1, keepdims=True))).astype(
        jnp.bfloat16
    )
    d_queries = jnp.einsum(
        "bhqk,bkhd->bqhd", d_scores, key_rows, preferred_element_type=jnp.float32
    ) * HD ** (-0.5)
    d_keys = jnp.einsum(
        "bhqk,bqhd->bkhd", d_scores, queries, preferred_element_type=jnp.float32
    ) * HD ** (-0.5)
    return (
        d_queries.astype(jnp.bfloat16),
        d_keys.astype(jnp.bfloat16),
        d_values.astype(jnp.bfloat16),
    )


def local(
    stream,
    counts,
    cotangent,
    w_qkv,
    b_qv,
    w_out,
    b_out,
    w_fc1,
    b_fc1,
    w_fc2,
    b_fc2,
    gain_one,
    shift_one,
    gain_two,
    shift_two,
):
    tensor_pos = lax.axis_index("tensor")
    own_rows = stream.shape[0]
    width = stream.shape[1]
    own_images = own_rows // SLOTS
    slot_index = jnp.arange(SLOTS, dtype=jnp.int32)
    validity_all = (slot_index[None, :] < (BUFFER + counts)[:, None]).astype(jnp.float32)
    own_validity = lax.dynamic_slice_in_dim(validity_all, tensor_pos * own_images, own_images, 0)
    own_valid = own_validity.reshape(own_rows, 1)
    fast = lax.axis_size("dp") == 16 and lax.axis_size("tensor") == 2
    if fast:
        own = jnp.concatenate([w_qkv[0], w_qkv[1], w_qkv[2], w_out.T, w_fc1, w_fc2.T], axis=1)
        full = gather_all(own)
        qkv_full = jnp.stack([full[:, 0:512], full[:, 512:1024], full[:, 1024:1536]])
        out_full = full[:, 1536:2048].T
        up_full = full[None, :, 2048:4096]
        down_full = full[:, 4096:6144].T
    else:
        qkv_full, out_full, up_full, down_full = (
            lax.all_gather(w_qkv, "dp", axis=1, tiled=True),
            lax.all_gather(w_out, "dp", axis=1, tiled=True),
            lax.all_gather(w_fc1[None], "dp", axis=1, tiled=True),
            lax.all_gather(w_fc2, "dp", axis=1, tiled=True),
        )
    head_width = w_qkv.shape[2]
    unit_width = w_fc1.shape[1]
    bias_query = lax.dynamic_slice_in_dim(b_qv[0], tensor_pos * head_width, head_width, 0)
    bias_value = lax.dynamic_slice_in_dim(b_qv[1], tensor_pos * head_width, head_width, 0)
    bias_up = lax.dynamic_slice_in_dim(b_fc1, tensor_pos * unit_width, unit_width, 0)
    up_full = up_full[0]
    group_images = validity_all.shape[0]
    group_rows = group_images * SLOTS
    local_heads = head_width // HD
    pairing = 2
    block_count = group_images // pairing
    blocked_valid = validity_all.reshape(block_count, pairing, SLOTS)
    stream_f = stream.astype(jnp.float32)
    normed_one = layer_norm(stream_f, gain_one, shift_one).astype(jnp.bfloat16)
    first_rows = lax.all_gather(normed_one, "tensor", axis=0, tiled=True)
    projected = jnp.einsum("rd,cde->rce", first_rows, qkv_full, preferred_element_type=jnp.float32)
    shape_heads = (block_count, pairing, SLOTS, local_heads, HD)
    queries = (projected[:, 0] + bias_query).astype(jnp.bfloat16).reshape(shape_heads)
    key_rows = projected[:, 1].astype(jnp.bfloat16).reshape(shape_heads)
    values = (projected[:, 2] + bias_value).astype(jnp.bfloat16).reshape(shape_heads)
    mixture, log_total = lax.map(attend_block, (queries, key_rows, values, blocked_valid))
    attn_heads = mixture.reshape(group_rows, head_width)
    taken = attn_heads
    attn_total = lax.psum_scatter(
        jnp.dot(taken, out_full, preferred_element_type=jnp.float32).astype(jnp.bfloat16),
        "tensor",
        scatter_dimension=0,
        tiled=True,
    ).astype(jnp.float32)
    branch = attn_total + b_out
    middle = stream_f + branch
    normed_two = layer_norm(middle, gain_two, shift_two).astype(jnp.bfloat16)
    second_rows = lax.all_gather(normed_two, "tensor", axis=0, tiled=True)
    hidden_pre = jnp.dot(second_rows, up_full, preferred_element_type=jnp.float32) + bias_up
    hidden_act = gelu_exact(hidden_pre).astype(jnp.bfloat16)
    taken = hidden_act
    mlp_total = lax.psum_scatter(
        jnp.dot(taken, down_full, preferred_element_type=jnp.float32).astype(jnp.bfloat16),
        "tensor",
        scatter_dimension=0,
        tiled=True,
    ).astype(jnp.float32)
    feed = mlp_total + b_fc2
    result = middle + feed
    activations = (result * own_valid).astype(jnp.bfloat16)
    squares = jnp.stack(
        [
            jnp.sum(own_valid * member * member)
            for member in (stream_f, middle, result, branch, feed)
        ]
    )
    square_sums, valid_count = lax.psum((squares, jnp.sum(own_valid)), ("dp", "tensor"))
    rms_stats = jnp.sqrt(square_sums / (valid_count * width))
    d_result = cotangent.astype(jnp.float32) * own_valid
    d_feed_low = d_result.astype(jnp.bfloat16)
    d_feed_rows = lax.all_gather(d_feed_low, "tensor", axis=0, tiled=True)
    d_act = jnp.einsum("rd,ud->ru", d_feed_rows, down_full, preferred_element_type=jnp.float32)
    unused_act, gelu_pullback = jax.vjp(gelu_exact, hidden_pre)
    d_pre = gelu_pullback(d_act)[0].astype(jnp.bfloat16)
    grad_down = jnp.einsum("ru,rd->ud", hidden_act, d_feed_rows, preferred_element_type=jnp.float32)
    grad_up = jnp.einsum("rd,ru->du", second_rows, d_pre, preferred_element_type=jnp.float32)
    grad_bias_up = jnp.sum(d_pre, axis=0, dtype=jnp.float32)
    grad_bias_down = jnp.sum(d_feed_low, axis=0, dtype=jnp.float32)
    taken = d_pre
    d_normed_two = lax.psum_scatter(
        jnp.einsum("ru,du->rd", taken, up_full, preferred_element_type=jnp.float32).astype(
            jnp.bfloat16
        ),
        "tensor",
        scatter_dimension=0,
        tiled=True,
    ).astype(jnp.float32)
    unused_two, norm_two_pullback = jax.vjp(layer_norm, middle, gain_two, shift_two)
    d_middle_norm, grad_gain_two, grad_shift_two = norm_two_pullback(d_normed_two)
    d_middle = d_result + d_middle_norm
    d_branch_low = d_middle.astype(jnp.bfloat16)
    grad_bias_out = jnp.sum(d_branch_low, axis=0, dtype=jnp.float32)
    d_branch_rows = lax.all_gather(d_branch_low, "tensor", axis=0, tiled=True)
    d_attn = jnp.einsum(
        "rd,hd->rh", d_branch_rows, out_full, preferred_element_type=jnp.float32
    ).astype(jnp.bfloat16)
    grad_out = jnp.einsum(
        "rh,rd->hd", attn_heads, d_branch_rows, preferred_element_type=jnp.float32
    )
    d_queries, d_keys, d_values = lax.map(
        attend_back,
        (queries, key_rows, values, blocked_valid, log_total, d_attn.reshape(shape_heads)),
    )
    d_projected = jnp.stack(
        [
            d_queries.reshape(group_rows, head_width),
            d_keys.reshape(group_rows, head_width),
            d_values.reshape(group_rows, head_width),
        ],
        axis=1,
    )
    grad_qkv = jnp.einsum(
        "rd,rce->cde", first_rows, d_projected, preferred_element_type=jnp.float32
    )
    bias_terms = jnp.sum(d_projected, axis=0, dtype=jnp.float32)
    taken = d_projected
    d_normed_one = lax.psum_scatter(
        jnp.einsum("rce,cde->rd", taken, qkv_full, preferred_element_type=jnp.float32).astype(
            jnp.bfloat16
        ),
        "tensor",
        scatter_dimension=0,
        tiled=True,
    ).astype(jnp.float32)
    unused_one, norm_one_pullback = jax.vjp(layer_norm, stream_f, gain_one, shift_one)
    d_stream_norm, grad_gain_one, grad_shift_one = norm_one_pullback(d_normed_one)
    grad_input = d_middle + d_stream_norm
    grad_up = grad_up[None]
    bias_qv_full = lax.dynamic_update_slice(
        jnp.zeros((2, width), jnp.float32),
        jnp.stack([bias_terms[0], bias_terms[2]]),
        (jnp.int32(0), tensor_pos * head_width),
    )
    bias_up_full = lax.dynamic_update_slice(
        jnp.zeros((b_fc1.shape[0],), jnp.float32), grad_bias_up, (tensor_pos * unit_width,)
    )
    if fast:
        low = lambda v: v.astype(jnp.bfloat16)
        grads = jnp.concatenate(
            [low(grad_qkv[0]), low(grad_qkv[1]), low(grad_qkv[2]), low(grad_out).T, low(grad_up[0]), low(grad_down).T],
            axis=1,
        )
        part = scatter_all(grads)
        qkv_part = jnp.stack([part[:, 0:512], part[:, 512:1024], part[:, 1024:1536]])
        out_part = part[:, 1536:2048].T
        up_part = part[None, :, 2048:4096]
        down_part = part[:, 4096:6144].T
    else:
        qkv_part, out_part, up_part, down_part = (
            lax.psum_scatter(
                grad_qkv.astype(jnp.bfloat16), "dp", scatter_dimension=1, tiled=True
            ).astype(jnp.float32),
            lax.psum_scatter(
                grad_out.astype(jnp.bfloat16), "dp", scatter_dimension=1, tiled=True
            ).astype(jnp.float32),
            lax.psum_scatter(
                grad_up.astype(jnp.bfloat16), "dp", scatter_dimension=1, tiled=True
            ).astype(jnp.float32),
            lax.psum_scatter(
                grad_down.astype(jnp.bfloat16), "dp", scatter_dimension=1, tiled=True
            ).astype(jnp.float32),
        )
    small_parts = (
        lax.psum_scatter(bias_qv_full, ("dp", "tensor"), scatter_dimension=1, tiled=True),
        lax.psum_scatter(grad_bias_out, ("dp", "tensor"), scatter_dimension=0, tiled=True),
        lax.psum_scatter(bias_up_full, ("dp", "tensor"), scatter_dimension=0, tiled=True),
        lax.psum_scatter(grad_bias_down, ("dp", "tensor"), scatter_dimension=0, tiled=True),
        lax.psum_scatter(grad_gain_one, ("dp", "tensor"), scatter_dimension=0, tiled=True),
        lax.psum_scatter(grad_shift_one, ("dp", "tensor"), scatter_dimension=0, tiled=True),
        lax.psum_scatter(grad_gain_two, ("dp", "tensor"), scatter_dimension=0, tiled=True),
        lax.psum_scatter(grad_shift_two, ("dp", "tensor"), scatter_dimension=0, tiled=True),
    )
    return (
        activations,
        grad_input,
        qkv_part,
        small_parts[0],
        out_part,
        small_parts[1],
        up_part[0],
        small_parts[2],
        down_part,
        small_parts[3],
        small_parts[4],
        small_parts[5],
        small_parts[6],
        small_parts[7],
        rms_stats,
    )


def solution(mesh):
    return jax.shard_map(
        local,
        mesh=mesh,
        in_specs=(
            P(("dp", "tensor"), None),
            P("dp"),
            P(("dp", "tensor"), None),
            P(None, "dp", "tensor"),
            P(),
            P("tensor", "dp"),
            P(),
            P("dp", "tensor"),
            P(),
            P("tensor", "dp"),
            P(),
            P(),
            P(),
            P(),
            P(),
        ),
        out_specs=(
            P(("dp", "tensor"), None),
            P(("dp", "tensor"), None),
            P(None, "dp", "tensor"),
            P(None, ("dp", "tensor")),
            P("tensor", "dp"),
            P(("dp", "tensor")),
            P("dp", "tensor"),
            P(("dp", "tensor")),
            P("tensor", "dp"),
            P(("dp", "tensor")),
            P(("dp", "tensor")),
            P(("dp", "tensor")),
            P(("dp", "tensor")),
            P(("dp", "tensor")),
            P(),
        ),
        check_vma=False,
    )
```

```python
import jax
import jax.numpy as jnp
from jax import lax
from jax.experimental import pallas as pl
from jax.experimental.pallas import tpu as pltpu
from jax.sharding import PartitionSpec as P

HD = 64
BUFFER = 64
SLOTS = 320


eps_norm = 1e-06


MESH = pl.DeviceIdType.MESH


class Place:
    def __init__(self):
        dp = lax.axis_index("dp")
        self.t = lax.axis_index("tensor")
        self.z, self.y, self.x = dp // 4, (dp // 2) % 2, dp % 2
        self.side = self.z // 2
        self.w = self.z + self.side * (3 - 2 * self.z)
        self.step = 1 - 2 * self.side
        self.dp = dp

    def order(self, k):
        o = (self.w, 1 - self.w, 2, 3)[k]
        return 3 * self.side + self.step * o

    def chip(self, z, y, x):
        return z * 4 + y * 2 + x

    def inward(self):
        return (self.chip(self.z + self.step, self.y, self.x), self.t)

    def outward(self):
        return (self.chip(self.z - self.step, self.y, self.x), self.t)

    def across_x(self):
        return (self.chip(self.z, self.y, 1 - self.x), self.t)

    def across_y(self):
        return (self.chip(self.z, 1 - self.y, self.x), self.t)

    def near(self):
        return (self.chip(self.z + 1 - 2 * (self.z % 2), self.y, self.x), self.t)

    def far(self):
        return (self.chip((self.z + 2) % 4, self.y, self.x), self.t)

    def twin(self):
        return (self.dp, 1 - self.t)


def enter(at):
    barrier = pltpu.get_barrier_semaphore()
    for other in (at.across_x(), at.across_y(), at.inward(), at.twin(), at.far()):
        pl.semaphore_signal(barrier, inc=1, device_id=other, device_id_type=MESH)

    @pl.when(at.w == 1)
    def _():
        pl.semaphore_signal(barrier, inc=1, device_id=at.outward(), device_id_type=MESH)

    pl.semaphore_wait(barrier, 5 + at.w)


class Gather:
    def __init__(self, at, full, shard, pieces, send, recv):
        self.at, self.full, self.shard, self.pieces, self.send, self.recv = at, full, shard, pieces, send, recv

    def rows(self, p, z, y, x, part=None):
        c0, c1 = self.pieces[p]
        start, size = self.at.chip(z, y, x) * self.shard, self.shard
        if part is not None:
            size = self.shard // 2
            start = start + part * size
        return self.full.at[pl.ds(pl.multiple_of(start, size), size), pl.ds(c0, c1 - c0)]

    def copy(self, p, ref, s, r, other):
        return pltpu.make_async_remote_copy(
            src_ref=ref,
            dst_ref=ref,
            send_sem=self.send.at[p, s[0], s[1]],
            recv_sem=self.recv.at[p, r[0], r[1]],
            device_id=other,
            device_id_type=MESH,
        )

    def z_in(self, p, z):
        return self.copy(p, self.rows(p, z, self.at.y, self.at.x), (0, z), (0, z), self.at.inward())

    def z_out(self, p, z):
        return self.copy(p, self.rows(p, z, self.at.y, self.at.x), (5, z), (0, z), self.at.outward())

    def x_full(self, p, z):
        return self.copy(p, self.rows(p, z, self.at.y, self.at.x), (1, z), (1, z), self.at.across_x())

    def y_full(self, p, z):
        return self.copy(p, self.rows(p, z, self.at.y, self.at.x), (2, z), (2, z), self.at.across_y())

    def x_half(self, p, z):
        return self.copy(p, self.rows(p, z, 1 - self.at.y, self.at.x, 1), (3, z), (3, z), self.at.across_x())

    def y_half(self, p, z):
        return self.copy(p, self.rows(p, z, self.at.y, 1 - self.at.x, 0), (4, z), (4, z), self.at.across_y())

    def arrived(self, p, kind, z):
        at = self.at
        ref = (
            lambda: self.rows(p, z, at.y, at.x),
            lambda: self.rows(p, z, at.y, 1 - at.x),
            lambda: self.rows(p, z, 1 - at.y, at.x),
            lambda: self.rows(p, z, 1 - at.y, 1 - at.x, 1),
            lambda: self.rows(p, z, 1 - at.y, 1 - at.x, 0),
        )[kind]()
        self.copy(p, ref, (kind, z), (kind, z), at.across_x()).wait_recv()

    def line(self, p, k):
        at = self.at
        z = at.order(k)
        if k > 0:
            self.arrived(p, 0, z)
        if k == 0:
            self.z_in(p, z).start()
        if k == 1:

            @pl.when(at.w == 1)
            def _():
                self.z_in(p, z).start()

        else:

            @pl.when(at.w == 1)
            def _():
                self.z_out(p, z).start()

        self.x_full(p, z).start()
        self.y_full(p, z).start()

    def plane(self, p, k):
        z = self.at.order(k)
        self.arrived(p, 1, z)
        self.y_half(p, z).start()
        self.arrived(p, 2, z)
        self.x_half(p, z).start()

    def finish(self, p):
        for k in range(4):
            z = self.at.order(k)
            self.arrived(p, 3, z)
            self.arrived(p, 4, z)

    def drain(self, p):
        at = self.at
        for k in range(4):
            z = at.order(k)
            if k == 0:
                self.z_in(p, z).wait_send()
            if k == 1:

                @pl.when(at.w == 1)
                def _(z=z):
                    self.z_in(p, z).wait_send()

            else:

                @pl.when(at.w == 1)
                def _(z=z):
                    self.z_out(p, z).wait_send()

            self.x_full(p, z).wait_send()
            self.y_full(p, z).wait_send()
            self.x_half(p, z).wait_send()
            self.y_half(p, z).wait_send()


class Scatter:
    def __init__(self, at, full, shard, pieces, xh, yh, xf, yf, zl, send, recv):
        self.at, self.full, self.shard, self.pieces = at, full, shard, pieces
        self.xh, self.yh, self.xf, self.yf, self.zl = xh, yh, xf, yf, zl
        self.send, self.recv = send, recv

    def cols(self, p):
        c0, c1 = self.pieces[p]
        return pl.ds(c0, c1 - c0)

    def rows(self, p, z, y, x, part=None):
        start, size = self.at.chip(z, y, x) * self.shard, self.shard
        if part is not None:
            size = self.shard // 2
            start = start + part * size
        ref, c0, c1 = self.full(p)
        return ref.at[pl.ds(pl.multiple_of(start, size), size), pl.ds(c0, c1 - c0)]

    def copy(self, p, src, dst, s, r, other):
        return pltpu.make_async_remote_copy(
            src_ref=src,
            dst_ref=dst,
            send_sem=self.send.at[p, s[0], s[1]],
            recv_sem=self.recv.at[p, r[0], r[1]],
            device_id=other,
            device_id_type=MESH,
        )

    def x_half(self, p, z):
        at = self.at
        return self.copy(
            p, self.rows(p, z, 1 - at.y, 1 - at.x, 0), self.xh.at[z, :, self.cols(p)], (1, z), (1, z), at.across_x()
        )

    def y_half(self, p, z):
        at = self.at
        return self.copy(
            p, self.rows(p, z, 1 - at.y, 1 - at.x, 1), self.yh.at[z, :, self.cols(p)], (2, z), (2, z), at.across_y()
        )

    def x_full(self, p, z):
        at = self.at
        return self.copy(
            p, self.rows(p, z, at.y, 1 - at.x), self.xf.at[z, :, self.cols(p)], (3, z), (3, z), at.across_x()
        )

    def y_full(self, p, z):
        at = self.at
        return self.copy(
            p, self.rows(p, z, 1 - at.y, at.x), self.yf.at[z, :, self.cols(p)], (4, z), (4, z), at.across_y()
        )

    def z_in(self, p, z, slot):
        at = self.at
        return self.copy(
            p, self.rows(p, z, at.y, at.x), self.zl.at[slot, :, self.cols(p)], (0, z), (0, slot), at.inward()
        )

    def z_out(self, p, z, slot):
        at = self.at
        return self.copy(
            p, self.rows(p, z, at.y, at.x), self.zl.at[slot, :, self.cols(p)], (0, z), (0, slot), at.outward()
        )

    def begin(self, p):
        for k in (3, 2, 1, 0):
            z = self.at.order(k)
            self.x_half(p, z).start()
            self.y_half(p, z).start()

    def plane(self, p, k):
        at = self.at
        z = at.order(k)
        self.x_half(p, z).wait_recv()
        ref = self.rows(p, z, 1 - at.y, at.x, 0)
        ref[...] = ref[...] + self.xh[z, :, self.cols(p)]
        self.y_full(p, z).start()
        self.y_half(p, z).wait_recv()
        ref = self.rows(p, z, at.y, 1 - at.x, 1)
        ref[...] = ref[...] + self.yh[z, :, self.cols(p)]
        self.x_full(p, z).start()

    def wait_line(self, p, z, slot):
        self.z_in(p, z, slot).wait_recv()

    def line(self, p, k, out=None):
        at = self.at
        z = at.order(k)
        self.x_full(p, z).wait_recv()
        self.y_full(p, z).wait_recv()
        ref = self.rows(p, z, at.y, at.x)
        total = (
            ref[...].astype(jnp.float32)
            + self.xf[z, :, self.cols(p)].astype(jnp.float32)
            + self.yf[z, :, self.cols(p)].astype(jnp.float32)
        )
        if k > 0:

            @pl.when(at.w == 0)
            def _():
                ref[...] = total.astype(jnp.bfloat16)
                self.z_in(p, z, z).start()

            @pl.when(at.w == 1)
            def _():
                self.wait_line(p, z, z)
                ref[...] = (total + self.zl[z, :, self.cols(p)].astype(jnp.float32)).astype(jnp.bfloat16)
                if k == 3:
                    self.z_in(p, z, z).start()
                elif k == 2:
                    self.z_in(p, z, 4).start()
                else:
                    self.z_out(p, z, 4).start()

        else:
            self.wait_line(p, z, 4)
            total = total + self.zl[4, :, self.cols(p)].astype(jnp.float32)

            @pl.when(at.w == 0)
            def _():
                out(total)

            @pl.when(at.w == 1)
            def _():
                self.wait_line(p, z, z)
                out(total + self.zl[z, :, self.cols(p)].astype(jnp.float32))

    def drain(self, p):
        at = self.at
        for k in range(4):
            z = at.order(k)
            for c in (self.x_half(p, z), self.y_half(p, z), self.x_full(p, z), self.y_full(p, z)):
                c.wait_send()
            if k > 0:
                self.z_in(p, z, z).wait_send()


WIDTHS = (1536, 512, 1024, 1024, 1024, 1024)
QKV, OUT, UP, DOWN = 0, 1536, 2048, 4096
BF, F32 = jnp.bfloat16, jnp.float32
SUMS = ("bq", "bv", "bout", "bdown", "g1", "s1", "g2", "s2", "x", "mid", "res", "branch", "feed")
BLOCK = 32


def pieces_of():
    out, c = [], 0
    for n in WIDTHS:
        out.append((c, c + n))
        c += n
    return out


def nn(a, b):
    return lax.dot_general(a, b, (((1,), (0,)), ((), ())), preferred_element_type=F32)


def nt(a, b):
    return lax.dot_general(a, b, (((1,), (1,)), ((), ())), preferred_element_type=F32)


def at_rows(start, size):
    return pl.ds(pl.multiple_of(start, size), size)


def fold(v):
    return jnp.sum(v.reshape(v.shape[0] // 8, 8, v.shape[1]), axis=0)


def normed(v):
    centre = jnp.mean(v, axis=1, keepdims=True)
    offset = v - centre
    r = lax.rsqrt(jnp.mean(offset * offset, axis=1, keepdims=True) + eps_norm)
    return offset * r, r


def norm_back(dy, n, r, gain):
    dn = dy * gain
    first = jnp.mean(dn, axis=1, keepdims=True)
    second = jnp.mean(dn * n, axis=1, keepdims=True)
    return r * (dn - first - n * second)


def block_kernel(
    counts, x_ref, cot_ref, wqkv, wout, wup, wdown, bqv, bout, bup, bdown, g1, s1, g2, s2,
    act_out, gin_out, o_qkv, o_out, o_up, o_down, o_sums,
    W, G2, xh, yh, xf, yf, zl, rows1, dfeed, qkv, probs, heads, mid, rows2, act, gp, datt, dproj,
    tall, own_a, own_b, send_a, send_b, got, acc, acc_up, sums, sums_got,
    sem_in, ag_send, ag_recv, rs_send, rs_recv, pair_send, pair_recv, sums_send, sums_recv,
):
    at = Place()
    t = at.t
    shard = wup.shape[0]
    pieces = pieces_of()
    n_pieces = len(pieces)
    own = x_ref.shape[0]
    group = 2 * own
    width = x_ref.shape[1]
    mine = at_rows(t * own, own)
    dbr = dfeed
    theirs = at_rows((1 - t) * own, own)

    here = at_rows(at.dp * shard, shard)
    loads = [
        pltpu.make_async_copy(src, W.at[here, pl.ds(c0, n)], sem_in.at[i])
        for i, (src, c0, n) in enumerate(
            [(wqkv.at[j], QKV + 512 * j, 512) for j in range(3)]
            + [(wout, OUT, 512), (wup, UP, 2048), (wdown, DOWN, 2048)]
        )
    ]
    for c in loads:
        c.start()
    enter(at)
    g = Gather(at, W, shard, pieces, ag_send, ag_recv)
    for c in loads:
        c.wait()
    g.line(0, 0)

    steps = []
    for p in range(n_pieces):
        for k in range(4):
            def step(p=p, k=k):
                if k < 3:
                    g.line(p, k + 1)
                g.plane(p, k)
                if k == 1 and p + 1 < n_pieces:
                    g.line(p + 1, 0)
            steps.append(step)
    done = [0]

    def gather(n):
        while n > 0 and done[0] < len(steps):
            steps[done[0]]()
            done[0] += 1
            n -= 1

    def need(p):
        gather(4 * p + 5 - done[0])
        g.finish(p)

    home = {0: (W, UP, UP + 1536), 1: (W, UP + 1536, DOWN), 2: (W, DOWN, DOWN + 1024), 3: (W, DOWN + 1024, DOWN + 2048),
            4: (G2, 0, 1024), 5: (G2, 1024, 2048)}
    sc = Scatter(at, lambda p: home[p], shard, pieces, xh, yh, xf, yf, zl, rs_send, rs_recv)

    def write(p):
        def store(total):
            if p == 0:
                for j in range(3):
                    o_qkv[j] = total[:, 512 * j : 512 * (j + 1)]
            elif p == 1:
                o_out[...] = total
            elif p < 4:
                o_up[:, (p - 2) * 1024 : (p - 1) * 1024] = total
            else:
                o_down[:, (p - 4) * 1024 : (p - 3) * 1024] = total
        return store

    queue = []

    def reduce_begin(p):
        sc.begin(p)
        for k in (3, 2, 1, 0):
            queue.append(lambda p=p, k=k: sc.plane(p, k))
        for k in (3, 2, 1, 0):
            queue.append(lambda p=p, k=k: sc.line(p, k, write(p)))

    def scatter(n):
        while n > 0 and queue:
            queue.pop(0)()
            n -= 1

    def pair(i, src, dst):
        return pltpu.make_async_remote_copy(
            src_ref=src, dst_ref=dst, send_sem=pair_send.at[i], recv_sem=pair_recv.at[i],
            device_id=at.twin(), device_id_type=MESH,
        )

    def share(i, ref):
        c = pair(i, ref.at[mine, :], ref.at[mine, :])
        c.start()
        return c

    def take(i, ref):
        pair(i, ref.at[theirs, :], ref.at[theirs, :]).wait_recv()

    for ref in (acc, acc_up):
        ref[...] = jnp.zeros_like(ref)
    total_of = {name: acc.at[i] for i, name in enumerate(SUMS)}

    def add(name, v):
        ref = total_of[name]
        ref[...] += fold(v)

    def valid_of(image, start, size):
        slot = lax.broadcasted_iota(jnp.int32, (size, 1), 0) + start
        return slot < counts[image] + BUFFER

    def each_block(body):
        def go(b, _):
            body(b * BLOCK, pl.ds(pl.multiple_of(b * BLOCK, BLOCK), BLOCK))
            return 0
        lax.fori_loop(0, own // BLOCK, go, 0)

    def tiles(first, last, body, size=256):
        def go(i, _):
            body(pl.multiple_of(i * size, size))
            return 0
        lax.fori_loop(first // size, last // size, go, 0)

    def flip(src):
        def body(c):
            tall[pl.ds(c, 128), :] = src[:, pl.ds(c, 128)].T
        tiles(0, src.shape[1], body, 128)

    def first_norm(b, r):
        xv = x_ref[r, :].astype(F32)
        keep = valid_of(t, b, BLOCK).astype(F32)
        n, _ = normed(xv)
        mine_b = pl.ds(pl.multiple_of(t * own + b, BLOCK), BLOCK)
        rows1[mine_b, :] = (n * g1[...] + s1[...]).astype(BF)
        add("x", keep * xv * xv)
        low = (cot_ref[r, :].astype(F32) * keep).astype(BF)
        dfeed[mine_b, :] = low
        add("bdown", low.astype(F32))

    each_block(first_norm)
    shares = [share(0, rows1), share(1, dfeed)]
    gather(1)
    take(1, dfeed)
    flip(dfeed)
    gather(1)
    take(0, rows1)
    need(0)

    def project(c):
        v = nn(rows1[...], W[:, pl.ds(c, 256)])
        part = c // 512
        inside = pl.ds(pl.multiple_of(c % 512 + t * 512, 256), 256)
        bias = jnp.where(part == 0, bqv[0:1, inside], jnp.where(part == 2, bqv[1:2, inside], 0.0))
        scale = jnp.where(part == 0, HD**-0.5, 1.0)
        qkv[:, pl.ds(c, 256)] = ((v + bias) * scale).astype(BF)

    tiles(0, 1536, project)
    gather(2)

    first_lanes = lax.broadcasted_iota(jnp.int32, (own, 128), 1) < HD

    def attend(it):
        image, j = it // 4, it % 4
        r = pl.ds(pl.multiple_of(image * own, own), own)
        c = j * 128
        q2 = qkv[r, pl.ds(pl.multiple_of(c, 128), 128)]
        k2 = qkv[r, pl.ds(pl.multiple_of(c + 512, 128), 128)]
        v_t = qkv[r, pl.ds(pl.multiple_of(c + 1024, 128), 128)].T
        hide = jnp.where(valid_of(image, 0, own), 0.0, -1e30)
        outs = []
        for a in range(2):
            qm = jnp.where(first_lanes if a == 0 else ~first_lanes, q2, jnp.zeros_like(q2))
            s = nt(k2, qm) + hide
            e = jnp.exp(s - jnp.max(s, axis=0, keepdims=True))
            low = (e * (1.0 / jnp.sum(e, axis=0, keepdims=True))).astype(BF)
            probs[it * 2 + a] = low
            outs.append(nn(v_t[a * HD : (a + 1) * HD], low))
        heads[r, pl.ds(pl.multiple_of(c, 128), 128)] = jnp.concatenate(outs, axis=0).T.astype(BF)

    def attend_some(first, last, body):
        def go(i, _):
            body(i)
            return 0
        lax.fori_loop(first, last, go, 0)

    for i in range(4):
        attend_some(2 * i, 2 * i + 2, attend)
        gather(1)
    need(1)

    def reduced(i, src, cols, k, keep, send):
        def other(c):
            send[:, pl.ds(c, 256)] = nt(src[theirs, :], W[pl.ds(c, 256), cols]).astype(BF)
        tiles(0, width, other)
        copy = pair(i, send, got.at[k])
        copy.start()
        def self(c):
            keep[:, pl.ds(c, 256)] = nt(src[mine, :], W[pl.ds(c, 256), cols])
        tiles(0, width, self)
        return copy

    branch_copy = reduced(2, heads, pl.ds(OUT, 512), 0, own_a, send_a)
    gather(1)
    branch_copy.wait()

    def second_norm(b, r):
        keep = valid_of(t, b, BLOCK).astype(F32)
        branch = own_a[r, :] + got[0, r, :].astype(F32) + bout[...]
        m = x_ref[r, :].astype(F32) + branch
        mid[r, :] = m
        add("branch", keep * branch * branch)
        add("mid", keep * m * m)
        n, _ = normed(m)
        rows2[pl.ds(pl.multiple_of(t * own + b, BLOCK), BLOCK), :] = (n * g2[...] + s2[...]).astype(BF)

    each_block(second_norm)
    shares.append(share(3, rows2))
    gather(1)
    take(3, rows2)

    def hidden(c):
        u = nn(rows2[...], W[:, pl.ds(UP + c, 256)]) + bup[:, pl.ds(pl.multiple_of(t * 2048 + c, 256), 256)]
        below = 0.5 * (1.0 + lax.erf(u * (0.5**0.5)))
        dense = jnp.exp(-0.5 * u * u) * 0.3989422804014327
        act[:, pl.ds(c, 256)] = (u * below).astype(BF)
        gp[:, pl.ds(c, 256)] = (below + u * dense).astype(BF)

    def grad_down(c):
        G2[:, pl.ds(c, 256)] = nn(tall[...], act[:, pl.ds(c, 256)]).astype(BF)

    need(2)
    tiles(0, 1024, hidden)
    gather(1)
    tiles(0, 1024, grad_down)
    need(3)
    tiles(1024, 2048, hidden)
    gather(1)
    tiles(1024, 2048, grad_down)
    flip(rows2)
    reduce_begin(4)

    def back_act(c):
        d = nn(dfeed[...], W[:, pl.ds(DOWN + c, 256)])
        low = (d * gp[:, pl.ds(c, 256)].astype(F32)).astype(BF)
        gp[:, pl.ds(c, 256)] = low
        acc_up[t, :, pl.ds(c, 256)] += fold(low.astype(F32))

    need(4)
    tiles(0, 1024, back_act)
    gather(9)
    reduce_begin(5)
    need(5)
    tiles(1024, 2048, back_act)
    two_copy = reduced(4, gp, pl.ds(UP, 2048), 1, own_a, send_a)
    feed_copy = reduced(5, act, pl.ds(DOWN, 2048), 2, own_b, send_b)
    for p in range(n_pieces):
        g.drain(p)
    scatter(2)

    def grad_up(c):
        W[:, pl.ds(DOWN + c, 256)] = nn(tall[...], gp[:, pl.ds(c, 256)]).astype(BF)

    two_copy.wait()
    shares[1].wait_send()

    def second_back(b, r):
        dy = own_a[r, :] + got[1, r, :].astype(F32)
        n, scale = normed(mid[r, :])
        keep = valid_of(t, b, BLOCK).astype(F32)
        add("g2", dy * n)
        add("s2", dy)
        d = cot_ref[r, :].astype(F32) * keep + norm_back(dy, n, scale, g2[...])
        gin_out[r, :] = d
        low = d.astype(BF)
        dbr[pl.ds(pl.multiple_of(t * own + b, BLOCK), BLOCK), :] = low
        add("bout", low.astype(F32))

    each_block(second_back)
    shares.append(share(6, dbr))
    tiles(0, 1024, grad_up)
    reduce_begin(2)
    scatter(2)
    tiles(1024, 2048, grad_up)
    reduce_begin(3)
    scatter(2)
    take(6, dbr)

    def back_heads(c):
        datt[:, pl.ds(c, 256)] = nn(dbr[...], W[:, pl.ds(OUT + c, 256)]).astype(BF)

    tiles(0, 512, back_heads)
    flip(dbr)

    def grad_out(c):
        W[:, pl.ds(UP + 1536 + c, 256)] = nn(tall[...], heads[:, pl.ds(c, 256)]).astype(BF)

    tiles(0, 512, grad_out)
    reduce_begin(1)
    scatter(4)

    def attend_back(it):
        image, j = it // 4, it % 4
        r = pl.ds(pl.multiple_of(image * own, own), own)
        c = j * 128
        q2 = qkv[r, pl.ds(pl.multiple_of(c, 128), 128)]
        k_t = qkv[r, pl.ds(pl.multiple_of(c + 512, 128), 128)].T
        v2 = qkv[r, pl.ds(pl.multiple_of(c + 1024, 128), 128)]
        da = datt[r, pl.ds(pl.multiple_of(c, 128), 128)]
        dq, dk, dv = [], [], []
        for a in range(2):
            dam = jnp.where(first_lanes if a == 0 else ~first_lanes, da, jnp.zeros_like(da))
            low = probs[it * 2 + a]
            p = low.astype(F32)
            dp = nt(v2, dam)
            ds = (p * (dp - jnp.sum(p * dp, axis=0, keepdims=True))).astype(BF)
            dq.append(nn(k_t[a * HD : (a + 1) * HD], ds))
            dk.append(nn(ds, q2))
            dv.append(nn(low, da))
        for base, v in (
            (0, jnp.concatenate(dq, axis=0).T * HD**-0.5),
            (512, jnp.where(first_lanes, dk[0], dk[1])),
            (1024, jnp.where(first_lanes, dv[0], dv[1])),
        ):
            v = v.astype(BF)
            dproj[r, pl.ds(pl.multiple_of(base + c, 128), 128)] = v
            if base != 512:
                lanes = pl.ds(pl.multiple_of(t * 512 + c, 128), 128)
                ref = total_of["bq" if base == 0 else "bv"]
                ref[:, lanes] += fold(v.astype(F32))

    for i in range(4):
        attend_some(2 * i, 2 * i + 2, attend_back)
        scatter(4)

    one_copy = reduced(7, dproj, pl.ds(QKV, 1536), 3, own_a, send_a)
    flip(rows1)

    def grad_qkv(c):
        W[:, pl.ds(UP + c, 256)] = nn(tall[...], dproj[:, pl.ds(c, 256)]).astype(BF)

    tiles(0, 1536, grad_qkv)
    reduce_begin(0)
    one_copy.wait()

    def first_back(b, r):
        dy = own_a[r, :] + got[3, r, :].astype(F32)
        n, scale = normed(x_ref[r, :].astype(F32))
        add("g1", dy * n)
        add("s1", dy)
        gin_out[r, :] += norm_back(dy, n, scale, g1[...])

    each_block(first_back)
    scatter(4)
    feed_copy.wait()

    def finish_feed(b, r):
        keep = valid_of(t, b, BLOCK).astype(F32)
        feed = own_b[r, :] + got[2, r, :].astype(F32) + bdown[...]
        res = mid[r, :] + feed
        add("feed", keep * feed * feed)
        add("res", keep * res * res)
        act_out[r, :] = (keep * res).astype(BF)

    each_block(finish_feed)

    for i in range(8):
        sums[i : i + 1, :] = jnp.sum(acc[i], axis=0, keepdims=True)
    for i in range(4):
        sums[8 + i : 9 + i, :] = jnp.sum(acc_up[i // 2, :, (i % 2) * 1024 : (i % 2 + 1) * 1024], axis=0, keepdims=True)
    lane = lax.broadcasted_iota(jnp.int32, (1, width), 1)
    row = jnp.where(lane == 5, (counts[t] + BUFFER).astype(F32), 0.0)
    for i, name in enumerate(("x", "mid", "res", "branch", "feed")):
        row = jnp.where(lane == i, jnp.sum(jnp.sum(total_of[name][...], axis=0, keepdims=True), axis=1, keepdims=True), row)
    sums[12:13, :] = row
    sums[13:16, :] = jnp.zeros((3, width), F32)
    for i, other in enumerate((at.twin(), at.across_x(), at.across_y(), at.near(), at.far())):
        c = pltpu.make_async_remote_copy(
            src_ref=sums, dst_ref=sums_got.at[i], send_sem=sums_send.at[i], recv_sem=sums_recv.at[i],
            device_id=other, device_id_type=MESH,
        )
        c.start()
        scatter(2)
        c.wait()
        sums[...] += sums_got[i]
    o_sums[...] = sums[...]
    scatter(1000)
    for p in range(n_pieces):
        sc.drain(p)
    for i in (0, 2, 3):
        shares[i].wait_send()


def block(counts, stream, cotangent, w_qkv, w_out_t, w_up, w_down_t, b_qv, b_out, b_up, b_down, g1, s1, g2, s2):
    own, width = stream.shape
    shard = w_up.shape[0]
    n = len(WIDTHS)
    cols = sum(WIDTHS)
    rows = 16 * shard
    group = 2 * own
    vmem = pl.BlockSpec(memory_space=pltpu.VMEM)
    hbm = pl.BlockSpec(memory_space=pl.ANY)
    dma = pltpu.SemaphoreType.DMA
    row = lambda v: v.reshape(1, -1)
    return pl.pallas_call(
        block_kernel,
        out_shape=(
            jax.ShapeDtypeStruct((own, width), BF),
            jax.ShapeDtypeStruct((own, width), F32),
            jax.ShapeDtypeStruct((3, shard, 512), F32),
            jax.ShapeDtypeStruct((shard, 512), F32),
            jax.ShapeDtypeStruct((shard, 2048), F32),
            jax.ShapeDtypeStruct((shard, 2048), F32),
            jax.ShapeDtypeStruct((16, width), F32),
        ),
        in_specs=[pl.BlockSpec(memory_space=pltpu.SMEM), vmem, vmem, hbm, hbm, hbm, hbm] + [vmem] * 8,
        out_specs=(vmem,) * 7,
        scratch_shapes=[
            pltpu.VMEM((rows, cols), BF),
            pltpu.VMEM((rows, 2048), BF),
            pltpu.VMEM((4, shard // 2, cols), BF),
            pltpu.VMEM((4, shard // 2, cols), BF),
            pltpu.VMEM((4, shard, cols), BF),
            pltpu.VMEM((4, shard, cols), BF),
            pltpu.VMEM((5, shard, cols), BF),
            pltpu.VMEM((group, width), BF),
            pltpu.VMEM((group, width), BF),
            pltpu.VMEM((group, 1536), BF),
            pltpu.VMEM((16, own, own), BF),
            pltpu.VMEM((group, 512), BF),
            pltpu.VMEM((own, width), F32),
            pltpu.VMEM((group, width), BF),
            pltpu.VMEM((group, 2048), BF),
            pltpu.VMEM((group, 2048), BF),
            pltpu.VMEM((group, 512), BF),
            pltpu.VMEM((group, 1536), BF),
            pltpu.VMEM((width, group), BF),
            pltpu.VMEM((own, width), F32),
            pltpu.VMEM((own, width), F32),
            pltpu.VMEM((own, width), BF),
            pltpu.VMEM((own, width), BF),
            pltpu.VMEM((4, own, width), BF),
            pltpu.VMEM((len(SUMS), 8, width), F32),
            pltpu.VMEM((2, 8, 2048), F32),
            pltpu.VMEM((16, width), F32),
            pltpu.VMEM((5, 16, width), F32),
            dma((6,)),
            dma((n, 6, 4)),
            dma((n, 5, 4)),
            dma((n, 5, 4)),
            dma((n, 5, 5)),
            dma((8,)),
            dma((8,)),
            dma((5,)),
            dma((5,)),
        ],
        compiler_params=pltpu.CompilerParams(
            collective_id=1, has_side_effects=True, vmem_limit_bytes=63 << 20
        ),
    )(
        counts, stream, cotangent, w_qkv, w_out_t, w_up, w_down_t,
        b_qv, row(b_out), row(b_up), row(b_down), row(g1), row(s1), row(g2), row(s2),
    )


def local_fast(
    stream, counts, cotangent, w_qkv, b_qv, w_out, b_out, w_fc1, b_fc1, w_fc2, b_fc2,
    gain_one, shift_one, gain_two, shift_two,
):
    acts, grad_in, p_qkv, p_out, p_up, p_down, sums = block(
        counts, stream, cotangent, w_qkv, w_out.T, w_fc1, w_fc2.T, b_qv, b_out, b_fc1, b_fc2,
        gain_one, shift_one, gain_two, shift_two,
    )
    place = lax.axis_index("dp") * 2 + lax.axis_index("tensor")
    vectors = lax.dynamic_slice(sums[:8], (0, place * 32), (8, 32))
    up = lax.dynamic_slice(sums[8:12].reshape(-1), (place * 128,), (128,))
    rms = jnp.sqrt(sums[12, :5] / (sums[12, 5] * stream.shape[1]))
    return (
        acts, grad_in, p_qkv, vectors[0:2], p_out.T, vectors[2], p_up, up, p_down.T, vectors[3],
        vectors[4], vectors[5], vectors[6], vectors[7], rms,
    )


def layer_norm(values, gain, shift):
    centre = jnp.mean(values, axis=-1, keepdims=True)
    offset = values - centre
    spread = jnp.mean(offset * offset, axis=-1, keepdims=True)
    return offset * lax.rsqrt(spread + eps_norm) * gain + shift


def gelu_exact(values):
    return jax.nn.gelu(values, approximate=False)


def masked_scores(queries, key_rows, validity):
    scores = jnp.einsum(
        "bqhd,bkhd->bhqk", queries, key_rows, preferred_element_type=jnp.float32
    ) * HD ** (-0.5)
    return jnp.where(validity[:, None, None, :] > 0, scores, -1e30)


def attend_block(members):
    queries, key_rows, values, validity = members
    scores = masked_scores(queries, key_rows, validity)
    highest = jnp.max(scores, axis=-1, keepdims=True)
    expo_terms = jnp.exp(scores - highest)
    totals = jnp.sum(expo_terms, axis=-1, keepdims=True)
    weights = (expo_terms / totals).astype(jnp.bfloat16)
    mixture = jnp.einsum("bhqk,bkhd->bqhd", weights, values, preferred_element_type=jnp.float32)
    return (mixture.astype(jnp.bfloat16), (highest + jnp.log(totals))[..., 0])


def attend_back(members):
    queries, key_rows, values, validity, log_total, d_mixture = members
    scores = masked_scores(queries, key_rows, validity)
    probs = jnp.exp(scores - log_total[..., None])
    d_values = jnp.einsum(
        "bhqk,bqhd->bkhd", probs.astype(jnp.bfloat16), d_mixture, preferred_element_type=jnp.float32
    )
    d_probs = jnp.einsum("bqhd,bkhd->bhqk", d_mixture, values, preferred_element_type=jnp.float32)
    d_scores = (probs * (d_probs - jnp.sum(probs * d_probs, axis=-1, keepdims=True))).astype(
        jnp.bfloat16
    )
    d_queries = jnp.einsum(
        "bhqk,bkhd->bqhd", d_scores, key_rows, preferred_element_type=jnp.float32
    ) * HD ** (-0.5)
    d_keys = jnp.einsum(
        "bhqk,bqhd->bkhd", d_scores, queries, preferred_element_type=jnp.float32
    ) * HD ** (-0.5)
    return (
        d_queries.astype(jnp.bfloat16),
        d_keys.astype(jnp.bfloat16),
        d_values.astype(jnp.bfloat16),
    )


def local(
    stream,
    counts,
    cotangent,
    w_qkv,
    b_qv,
    w_out,
    b_out,
    w_fc1,
    b_fc1,
    w_fc2,
    b_fc2,
    gain_one,
    shift_one,
    gain_two,
    shift_two,
):
    tensor_pos = lax.axis_index("tensor")
    own_rows = stream.shape[0]
    width = stream.shape[1]
    own_images = own_rows // SLOTS
    slot_index = jnp.arange(SLOTS, dtype=jnp.int32)
    validity_all = (slot_index[None, :] < (BUFFER + counts)[:, None]).astype(jnp.float32)
    own_validity = lax.dynamic_slice_in_dim(validity_all, tensor_pos * own_images, own_images, 0)
    own_valid = own_validity.reshape(own_rows, 1)
    qkv_full, out_full, up_full, down_full = (
        lax.all_gather(w_qkv, "dp", axis=1, tiled=True),
        lax.all_gather(w_out, "dp", axis=1, tiled=True),
        lax.all_gather(w_fc1[None], "dp", axis=1, tiled=True),
        lax.all_gather(w_fc2, "dp", axis=1, tiled=True),
    )
    head_width = w_qkv.shape[2]
    unit_width = w_fc1.shape[1]
    bias_query = lax.dynamic_slice_in_dim(b_qv[0], tensor_pos * head_width, head_width, 0)
    bias_value = lax.dynamic_slice_in_dim(b_qv[1], tensor_pos * head_width, head_width, 0)
    bias_up = lax.dynamic_slice_in_dim(b_fc1, tensor_pos * unit_width, unit_width, 0)
    up_full = up_full[0]
    group_images = validity_all.shape[0]
    group_rows = group_images * SLOTS
    local_heads = head_width // HD
    pairing = 2
    block_count = group_images // pairing
    blocked_valid = validity_all.reshape(block_count, pairing, SLOTS)
    stream_f = stream.astype(jnp.float32)
    normed_one = layer_norm(stream_f, gain_one, shift_one).astype(jnp.bfloat16)
    first_rows = lax.all_gather(normed_one, "tensor", axis=0, tiled=True)
    projected = jnp.einsum("rd,cde->rce", first_rows, qkv_full, preferred_element_type=jnp.float32)
    shape_heads = (block_count, pairing, SLOTS, local_heads, HD)
    queries = (projected[:, 0] + bias_query).astype(jnp.bfloat16).reshape(shape_heads)
    key_rows = projected[:, 1].astype(jnp.bfloat16).reshape(shape_heads)
    values = (projected[:, 2] + bias_value).astype(jnp.bfloat16).reshape(shape_heads)
    mixture, log_total = lax.map(attend_block, (queries, key_rows, values, blocked_valid))
    attn_heads = mixture.reshape(group_rows, head_width)
    taken = attn_heads
    attn_total = lax.psum_scatter(
        jnp.dot(taken, out_full, preferred_element_type=jnp.float32).astype(jnp.bfloat16),
        "tensor",
        scatter_dimension=0,
        tiled=True,
    ).astype(jnp.float32)
    branch = attn_total + b_out
    middle = stream_f + branch
    normed_two = layer_norm(middle, gain_two, shift_two).astype(jnp.bfloat16)
    second_rows = lax.all_gather(normed_two, "tensor", axis=0, tiled=True)
    hidden_pre = jnp.dot(second_rows, up_full, preferred_element_type=jnp.float32) + bias_up
    hidden_act = gelu_exact(hidden_pre).astype(jnp.bfloat16)
    taken = hidden_act
    mlp_total = lax.psum_scatter(
        jnp.dot(taken, down_full, preferred_element_type=jnp.float32).astype(jnp.bfloat16),
        "tensor",
        scatter_dimension=0,
        tiled=True,
    ).astype(jnp.float32)
    feed = mlp_total + b_fc2
    result = middle + feed
    activations = (result * own_valid).astype(jnp.bfloat16)
    squares = jnp.stack(
        [
            jnp.sum(own_valid * member * member)
            for member in (stream_f, middle, result, branch, feed)
        ]
    )
    square_sums, valid_count = lax.psum((squares, jnp.sum(own_valid)), ("dp", "tensor"))
    rms_stats = jnp.sqrt(square_sums / (valid_count * width))
    d_result = cotangent.astype(jnp.float32) * own_valid
    d_feed_low = d_result.astype(jnp.bfloat16)
    d_feed_rows = lax.all_gather(d_feed_low, "tensor", axis=0, tiled=True)
    d_act = jnp.einsum("rd,ud->ru", d_feed_rows, down_full, preferred_element_type=jnp.float32)
    unused_act, gelu_pullback = jax.vjp(gelu_exact, hidden_pre)
    d_pre = gelu_pullback(d_act)[0].astype(jnp.bfloat16)
    grad_down = jnp.einsum("ru,rd->ud", hidden_act, d_feed_rows, preferred_element_type=jnp.float32)
    grad_up = jnp.einsum("rd,ru->du", second_rows, d_pre, preferred_element_type=jnp.float32)
    grad_bias_up = jnp.sum(d_pre, axis=0, dtype=jnp.float32)
    grad_bias_down = jnp.sum(d_feed_low, axis=0, dtype=jnp.float32)
    taken = d_pre
    d_normed_two = lax.psum_scatter(
        jnp.einsum("ru,du->rd", taken, up_full, preferred_element_type=jnp.float32).astype(
            jnp.bfloat16
        ),
        "tensor",
        scatter_dimension=0,
        tiled=True,
    ).astype(jnp.float32)
    unused_two, norm_two_pullback = jax.vjp(layer_norm, middle, gain_two, shift_two)
    d_middle_norm, grad_gain_two, grad_shift_two = norm_two_pullback(d_normed_two)
    d_middle = d_result + d_middle_norm
    d_branch_low = d_middle.astype(jnp.bfloat16)
    grad_bias_out = jnp.sum(d_branch_low, axis=0, dtype=jnp.float32)
    d_branch_rows = lax.all_gather(d_branch_low, "tensor", axis=0, tiled=True)
    d_attn = jnp.einsum(
        "rd,hd->rh", d_branch_rows, out_full, preferred_element_type=jnp.float32
    ).astype(jnp.bfloat16)
    grad_out = jnp.einsum(
        "rh,rd->hd", attn_heads, d_branch_rows, preferred_element_type=jnp.float32
    )
    d_queries, d_keys, d_values = lax.map(
        attend_back,
        (queries, key_rows, values, blocked_valid, log_total, d_attn.reshape(shape_heads)),
    )
    d_projected = jnp.stack(
        [
            d_queries.reshape(group_rows, head_width),
            d_keys.reshape(group_rows, head_width),
            d_values.reshape(group_rows, head_width),
        ],
        axis=1,
    )
    grad_qkv = jnp.einsum(
        "rd,rce->cde", first_rows, d_projected, preferred_element_type=jnp.float32
    )
    bias_terms = jnp.sum(d_projected, axis=0, dtype=jnp.float32)
    taken = d_projected
    d_normed_one = lax.psum_scatter(
        jnp.einsum("rce,cde->rd", taken, qkv_full, preferred_element_type=jnp.float32).astype(
            jnp.bfloat16
        ),
        "tensor",
        scatter_dimension=0,
        tiled=True,
    ).astype(jnp.float32)
    unused_one, norm_one_pullback = jax.vjp(layer_norm, stream_f, gain_one, shift_one)
    d_stream_norm, grad_gain_one, grad_shift_one = norm_one_pullback(d_normed_one)
    grad_input = d_middle + d_stream_norm
    grad_up = grad_up[None]
    bias_qv_full = lax.dynamic_update_slice(
        jnp.zeros((2, width), jnp.float32),
        jnp.stack([bias_terms[0], bias_terms[2]]),
        (jnp.int32(0), tensor_pos * head_width),
    )
    bias_up_full = lax.dynamic_update_slice(
        jnp.zeros((b_fc1.shape[0],), jnp.float32), grad_bias_up, (tensor_pos * unit_width,)
    )
    qkv_part, out_part, up_part, down_part = (
        lax.psum_scatter(
            grad_qkv.astype(jnp.bfloat16), "dp", scatter_dimension=1, tiled=True
        ).astype(jnp.float32),
        lax.psum_scatter(
            grad_out.astype(jnp.bfloat16), "dp", scatter_dimension=1, tiled=True
        ).astype(jnp.float32),
        lax.psum_scatter(
            grad_up.astype(jnp.bfloat16), "dp", scatter_dimension=1, tiled=True
        ).astype(jnp.float32),
        lax.psum_scatter(
            grad_down.astype(jnp.bfloat16), "dp", scatter_dimension=1, tiled=True
        ).astype(jnp.float32),
    )
    small_parts = (
        lax.psum_scatter(bias_qv_full, ("dp", "tensor"), scatter_dimension=1, tiled=True),
        lax.psum_scatter(grad_bias_out, ("dp", "tensor"), scatter_dimension=0, tiled=True),
        lax.psum_scatter(bias_up_full, ("dp", "tensor"), scatter_dimension=0, tiled=True),
        lax.psum_scatter(grad_bias_down, ("dp", "tensor"), scatter_dimension=0, tiled=True),
        lax.psum_scatter(grad_gain_one, ("dp", "tensor"), scatter_dimension=0, tiled=True),
        lax.psum_scatter(grad_shift_one, ("dp", "tensor"), scatter_dimension=0, tiled=True),
        lax.psum_scatter(grad_gain_two, ("dp", "tensor"), scatter_dimension=0, tiled=True),
        lax.psum_scatter(grad_shift_two, ("dp", "tensor"), scatter_dimension=0, tiled=True),
    )
    return (
        activations,
        grad_input,
        qkv_part,
        small_parts[0],
        out_part,
        small_parts[1],
        up_part[0],
        small_parts[2],
        down_part,
        small_parts[3],
        small_parts[4],
        small_parts[5],
        small_parts[6],
        small_parts[7],
        rms_stats,
    )


def solution(mesh):
    fast = mesh.shape["dp"] == 16 and mesh.shape["tensor"] == 2
    return jax.shard_map(
        local_fast if fast else local,
        mesh=mesh,
        in_specs=(
            P(("dp", "tensor"), None),
            P("dp"),
            P(("dp", "tensor"), None),
            P(None, "dp", "tensor"),
            P(),
            P("tensor", "dp"),
            P(),
            P("dp", "tensor"),
            P(),
            P("tensor", "dp"),
            P(),
            P(),
            P(),
            P(),
            P(),
        ),
        out_specs=(
            P(("dp", "tensor"), None),
            P(("dp", "tensor"), None),
            P(None, "dp", "tensor"),
            P(None, ("dp", "tensor")),
            P("tensor", "dp"),
            P(("dp", "tensor")),
            P("dp", "tensor"),
            P(("dp", "tensor")),
            P("tensor", "dp"),
            P(("dp", "tensor")),
            P(("dp", "tensor")),
            P(("dp", "tensor")),
            P(("dp", "tensor")),
            P(("dp", "tensor")),
            P(),
        ),
        check_vma=False,
    )
```

```python
import jax
import jax.numpy as jnp
from jax import lax
from jax.experimental import pallas as pl
from jax.experimental.pallas import tpu as pltpu
from jax.sharding import PartitionSpec as P

HD = 64
BUFFER = 64
SLOTS = 320


eps_norm = 1e-06


MESH = pl.DeviceIdType.MESH


class Place:
    def __init__(self):
        dp = lax.axis_index("dp")
        self.t = lax.axis_index("tensor")
        self.z, self.y, self.x = dp // 4, (dp // 2) % 2, dp % 2
        self.side = self.z // 2
        self.w = self.z + self.side * (3 - 2 * self.z)
        self.step = 1 - 2 * self.side
        self.dp = dp

    def order(self, k):
        o = (self.w, 1 - self.w, 2, 3)[k]
        return 3 * self.side + self.step * o

    def chip(self, z, y, x):
        return z * 4 + y * 2 + x

    def inward(self):
        return (self.chip(self.z + self.step, self.y, self.x), self.t)

    def outward(self):
        return (self.chip(self.z - self.step, self.y, self.x), self.t)

    def across_x(self):
        return (self.chip(self.z, self.y, 1 - self.x), self.t)

    def across_y(self):
        return (self.chip(self.z, 1 - self.y, self.x), self.t)

    def near(self):
        return (self.chip(self.z + 1 - 2 * (self.z % 2), self.y, self.x), self.t)

    def far(self):
        return (self.chip((self.z + 2) % 4, self.y, self.x), self.t)

    def twin(self):
        return (self.dp, 1 - self.t)


def enter(at):
    barrier = pltpu.get_barrier_semaphore()
    for other in (at.across_x(), at.across_y(), at.inward(), at.twin(), at.far()):
        pl.semaphore_signal(barrier, inc=1, device_id=other, device_id_type=MESH)

    @pl.when(at.w == 1)
    def _():
        pl.semaphore_signal(barrier, inc=1, device_id=at.outward(), device_id_type=MESH)

    pl.semaphore_wait(barrier, 5 + at.w)


class Gather:
    def __init__(self, at, full, shard, pieces, send, recv):
        self.at, self.full, self.shard, self.pieces, self.send, self.recv = at, full, shard, pieces, send, recv

    def rows(self, p, z, y, x, part=None):
        c0, c1 = self.pieces[p]
        start, size = self.at.chip(z, y, x) * self.shard, self.shard
        if part is not None:
            size = self.shard // 2
            start = start + part * size
        return self.full.at[pl.ds(pl.multiple_of(start, size), size), pl.ds(c0, c1 - c0)]

    def copy(self, p, ref, s, r, other):
        return pltpu.make_async_remote_copy(
            src_ref=ref,
            dst_ref=ref,
            send_sem=self.send.at[p, s[0], s[1]],
            recv_sem=self.recv.at[p, r[0], r[1]],
            device_id=other,
            device_id_type=MESH,
        )

    def z_in(self, p, z):
        return self.copy(p, self.rows(p, z, self.at.y, self.at.x), (0, z), (0, z), self.at.inward())

    def z_out(self, p, z):
        return self.copy(p, self.rows(p, z, self.at.y, self.at.x), (5, z), (0, z), self.at.outward())

    def x_full(self, p, z):
        return self.copy(p, self.rows(p, z, self.at.y, self.at.x), (1, z), (1, z), self.at.across_x())

    def y_full(self, p, z):
        return self.copy(p, self.rows(p, z, self.at.y, self.at.x), (2, z), (2, z), self.at.across_y())

    def x_half(self, p, z):
        return self.copy(p, self.rows(p, z, 1 - self.at.y, self.at.x, 1), (3, z), (3, z), self.at.across_x())

    def y_half(self, p, z):
        return self.copy(p, self.rows(p, z, self.at.y, 1 - self.at.x, 0), (4, z), (4, z), self.at.across_y())

    def arrived(self, p, kind, z):
        at = self.at
        ref = (
            lambda: self.rows(p, z, at.y, at.x),
            lambda: self.rows(p, z, at.y, 1 - at.x),
            lambda: self.rows(p, z, 1 - at.y, at.x),
            lambda: self.rows(p, z, 1 - at.y, 1 - at.x, 1),
            lambda: self.rows(p, z, 1 - at.y, 1 - at.x, 0),
        )[kind]()
        self.copy(p, ref, (kind, z), (kind, z), at.across_x()).wait_recv()

    def line(self, p, k):
        at = self.at
        z = at.order(k)
        if k > 0:
            self.arrived(p, 0, z)
        if k == 0:
            self.z_in(p, z).start()
        if k == 1:

            @pl.when(at.w == 1)
            def _():
                self.z_in(p, z).start()

        else:

            @pl.when(at.w == 1)
            def _():
                self.z_out(p, z).start()

        self.x_full(p, z).start()
        self.y_full(p, z).start()

    def plane(self, p, k):
        z = self.at.order(k)
        self.arrived(p, 1, z)
        self.y_half(p, z).start()
        self.arrived(p, 2, z)
        self.x_half(p, z).start()

    def finish(self, p):
        for k in range(4):
            z = self.at.order(k)
            self.arrived(p, 3, z)
            self.arrived(p, 4, z)

    def drain(self, p):
        at = self.at
        for k in range(4):
            z = at.order(k)
            if k == 0:
                self.z_in(p, z).wait_send()
            if k == 1:

                @pl.when(at.w == 1)
                def _(z=z):
                    self.z_in(p, z).wait_send()

            else:

                @pl.when(at.w == 1)
                def _(z=z):
                    self.z_out(p, z).wait_send()

            self.x_full(p, z).wait_send()
            self.y_full(p, z).wait_send()
            self.x_half(p, z).wait_send()
            self.y_half(p, z).wait_send()


class Scatter:
    def __init__(self, at, full, shard, pieces, xh, yh, xf, yf, zl, send, recv):
        self.at, self.full, self.shard, self.pieces = at, full, shard, pieces
        self.xh, self.yh, self.xf, self.yf, self.zl = xh, yh, xf, yf, zl
        self.send, self.recv = send, recv

    def cols(self, p):
        c0, c1 = self.pieces[p]
        return pl.ds(c0, c1 - c0)

    def rows(self, p, z, y, x, part=None):
        start, size = self.at.chip(z, y, x) * self.shard, self.shard
        if part is not None:
            size = self.shard // 2
            start = start + part * size
        ref, c0, c1 = self.full(p)
        return ref.at[pl.ds(pl.multiple_of(start, size), size), pl.ds(c0, c1 - c0)]

    def copy(self, p, src, dst, s, r, other):
        return pltpu.make_async_remote_copy(
            src_ref=src,
            dst_ref=dst,
            send_sem=self.send.at[p, s[0], s[1]],
            recv_sem=self.recv.at[p, r[0], r[1]],
            device_id=other,
            device_id_type=MESH,
        )

    def x_half(self, p, z):
        at = self.at
        return self.copy(
            p, self.rows(p, z, 1 - at.y, 1 - at.x, 0), self.xh.at[z, :, self.cols(p)], (1, z), (1, z), at.across_x()
        )

    def y_half(self, p, z):
        at = self.at
        return self.copy(
            p, self.rows(p, z, 1 - at.y, 1 - at.x, 1), self.yh.at[z, :, self.cols(p)], (2, z), (2, z), at.across_y()
        )

    def x_full(self, p, z):
        at = self.at
        return self.copy(
            p, self.rows(p, z, at.y, 1 - at.x), self.xf.at[z, :, self.cols(p)], (3, z), (3, z), at.across_x()
        )

    def y_full(self, p, z):
        at = self.at
        return self.copy(
            p, self.rows(p, z, 1 - at.y, at.x), self.yf.at[z, :, self.cols(p)], (4, z), (4, z), at.across_y()
        )

    def z_in(self, p, z, slot):
        at = self.at
        return self.copy(
            p, self.rows(p, z, at.y, at.x), self.zl.at[slot, :, self.cols(p)], (0, z), (0, slot), at.inward()
        )

    def z_out(self, p, z, slot):
        at = self.at
        return self.copy(
            p, self.rows(p, z, at.y, at.x), self.zl.at[slot, :, self.cols(p)], (0, z), (0, slot), at.outward()
        )

    def begin(self, p):
        for k in (3, 2, 1, 0):
            z = self.at.order(k)
            self.x_half(p, z).start()
            self.y_half(p, z).start()

    def plane(self, p, k):
        at = self.at
        z = at.order(k)
        self.x_half(p, z).wait_recv()
        ref = self.rows(p, z, 1 - at.y, at.x, 0)
        ref[...] = ref[...] + self.xh[z, :, self.cols(p)]
        self.y_full(p, z).start()
        self.y_half(p, z).wait_recv()
        ref = self.rows(p, z, at.y, 1 - at.x, 1)
        ref[...] = ref[...] + self.yh[z, :, self.cols(p)]
        self.x_full(p, z).start()

    def wait_line(self, p, z, slot):
        self.z_in(p, z, slot).wait_recv()

    def line(self, p, k, out=None):
        at = self.at
        z = at.order(k)
        self.x_full(p, z).wait_recv()
        self.y_full(p, z).wait_recv()
        ref = self.rows(p, z, at.y, at.x)
        total = (
            ref[...].astype(jnp.float32)
            + self.xf[z, :, self.cols(p)].astype(jnp.float32)
            + self.yf[z, :, self.cols(p)].astype(jnp.float32)
        )
        if k > 0:

            @pl.when(at.w == 0)
            def _():
                ref[...] = total.astype(jnp.bfloat16)
                self.z_in(p, z, z).start()

            @pl.when(at.w == 1)
            def _():
                self.wait_line(p, z, z)
                ref[...] = (total + self.zl[z, :, self.cols(p)].astype(jnp.float32)).astype(jnp.bfloat16)
                if k == 3:
                    self.z_in(p, z, z).start()
                elif k == 2:
                    self.z_in(p, z, 4).start()
                else:
                    self.z_out(p, z, 4).start()

        else:
            self.wait_line(p, z, 4)
            total = total + self.zl[4, :, self.cols(p)].astype(jnp.float32)

            @pl.when(at.w == 0)
            def _():
                out(total)

            @pl.when(at.w == 1)
            def _():
                self.wait_line(p, z, z)
                out(total + self.zl[z, :, self.cols(p)].astype(jnp.float32))

    def drain(self, p):
        at = self.at
        for k in range(4):
            z = at.order(k)
            for c in (self.x_half(p, z), self.y_half(p, z), self.x_full(p, z), self.y_full(p, z)):
                c.wait_send()
            if k > 0:
                self.z_in(p, z, z).wait_send()


class PairGather:
    def __init__(self, at, full, shard, columns, sources, send, recv):
        self.at, self.full, self.shard, self.columns, self.sources = at, full, shard, columns, sources
        self.send, self.recv = send, recv

    def far_x(self, h):
        return self.at.x if h == 0 else 1 - self.at.x

    def rows(self, m, z, y, x):
        c0, n = self.columns[m]
        start = self.at.chip(z, y, x) * self.shard
        return self.full.at[pl.ds(pl.multiple_of(start, self.shard), self.shard), pl.ds(c0, n)]

    def copy(self, m, h, src, dst, s, r, z, other):
        i = 2 * m + h
        return pltpu.make_async_remote_copy(
            src_ref=src,
            dst_ref=dst,
            send_sem=self.send.at[i, s, z],
            recv_sem=self.recv.at[i, r, z],
            device_id=other,
            device_id_type=MESH,
        )

    def x_copy(self, m):
        at = self.at
        c0, n = self.columns[m]
        src = self.sources[m].at[:, pl.ds(pl.multiple_of((1 - at.x) * n, n), n)]
        return self.copy(m, 1, src, self.rows(m, at.z, at.y, at.x), 3, 2, at.z, at.across_x())

    def z_in(self, m, h, z):
        ref = self.rows(m, z, self.at.y, self.far_x(h))
        return self.copy(m, h, ref, ref, 0, 0, z, self.at.inward())

    def z_out(self, m, h, z):
        ref = self.rows(m, z, self.at.y, self.far_x(h))
        return self.copy(m, h, ref, ref, 1, 0, z, self.at.outward())

    def y_copy(self, m, h, z):
        ref = self.rows(m, z, self.at.y, self.far_x(h))
        return self.copy(m, h, ref, ref, 2, 1, z, self.at.across_y())

    def line(self, m, h, k):
        at = self.at
        z = at.order(k)
        if k > 0:
            ref = self.rows(m, z, at.y, self.far_x(h))
            self.copy(m, h, ref, ref, 0, 0, z, at.inward()).wait_recv()
        elif h == 1:
            ref = self.rows(m, z, at.y, self.far_x(h))
            self.copy(m, h, ref, ref, 0, 2, z, at.across_x()).wait_recv()
        if k == 0:
            self.z_in(m, h, z).start()
        if k == 1:

            @pl.when(at.w == 1)
            def _():
                self.z_in(m, h, z).start()

        else:

            @pl.when(at.w == 1)
            def _():
                self.z_out(m, h, z).start()

    def cross(self, m, h, k):
        self.y_copy(m, h, self.at.order(k)).start()

    def finish(self, m):
        at = self.at
        for h in range(2):
            for k in range(4):
                z = at.order(k)
                ref = self.rows(m, z, 1 - at.y, self.far_x(h))
                self.copy(m, h, ref, ref, 2, 1, z, at.across_y()).wait_recv()

    def drain(self, m):
        at = self.at
        self.x_copy(m).wait_send()
        for h in range(2):
            for k in range(4):
                z = at.order(k)
                if k == 0:
                    self.z_in(m, h, z).wait_send()
                if k == 1:

                    @pl.when(at.w == 1)
                    def _(z=z):
                        self.z_in(m, h, z).wait_send()

                else:

                    @pl.when(at.w == 1)
                    def _(z=z):
                        self.z_out(m, h, z).wait_send()

                self.y_copy(m, h, z).wait_send()


class PairScatter:
    def __init__(self, at, full, shard, yf, zl, xs, xr, send, recv):
        self.at, self.full, self.shard = at, full, shard
        self.yf, self.zl, self.xs, self.xr, self.send, self.recv = yf, zl, xs, xr, send, recv

    def unit(self, m, z, y):
        ref, c0, n = self.full(m)
        size = 2 * self.shard
        return ref.at[pl.ds(pl.multiple_of((z * 2 + y) * size, size), size), pl.ds(c0, n)]

    def copy(self, m, src, dst, s, r, other):
        return pltpu.make_async_remote_copy(
            src_ref=src,
            dst_ref=dst,
            send_sem=self.send.at[m, s[0], s[1]],
            recv_sem=self.recv.at[m, r[0], r[1]],
            device_id=other,
            device_id_type=MESH,
        )

    def y_copy(self, m, z):
        at = self.at
        return self.copy(m, self.unit(m, z, 1 - at.y), self.yf.at[m, z], (1, z), (1, z), at.across_y())

    def z_copy(self, m, z, slot, other):
        return self.copy(m, self.unit(m, z, self.at.y), self.zl.at[m, slot], (0, z), (0, slot), other)

    def x_copy(self, m):
        return self.copy(m, self.xs.at[m], self.xr.at[m], (2, 0), (2, 0), self.at.across_x())

    def begin(self, m):
        for k in (3, 2, 1, 0):
            self.y_copy(m, self.at.order(k)).start()

    def line(self, m, k, out):
        at = self.at
        z = at.order(k)
        self.y_copy(m, z).wait_recv()
        ref = self.unit(m, z, at.y)
        if k > 0:

            @pl.when(at.w == 0)
            def _():
                ref[...] = ref[...] + self.yf[m, z]
                self.z_copy(m, z, z, at.inward()).start()

            @pl.when(at.w == 1)
            def _():
                self.z_copy(m, z, z, at.inward()).wait_recv()
                ref[...] = (
                    ref[...].astype(jnp.float32)
                    + self.yf[m, z].astype(jnp.float32)
                    + self.zl[m, z].astype(jnp.float32)
                ).astype(jnp.bfloat16)
                if k == 3:
                    self.z_copy(m, z, z, at.inward()).start()
                elif k == 2:
                    self.z_copy(m, z, 4, at.inward()).start()
                else:
                    self.z_copy(m, z, 4, at.outward()).start()

        else:
            self.z_copy(m, z, 4, at.inward()).wait_recv()

            def total(x, second):
                full, c0, n = self.full(m)
                size = self.shard
                own = full[pl.ds(pl.multiple_of(at.chip(z, at.y, x) * size, size), size), pl.ds(c0, n)]
                part = pl.ds(pl.multiple_of(x * size, size), size)
                v = (
                    own.astype(jnp.float32)
                    + self.yf[m, z, part, :].astype(jnp.float32)
                    + self.zl[m, 4, part, :].astype(jnp.float32)
                )
                if second:
                    v = v + self.zl[m, z, part, :].astype(jnp.float32)
                return v

            def put(second):
                self.xs[m] = total(1 - at.x, second).astype(jnp.bfloat16)
                self.x_copy(m).start()
                out(at.x, total(at.x, second))

            @pl.when(at.w == 0)
            def _():
                put(False)

            @pl.when(at.w == 1)
            def _():
                self.z_copy(m, z, z, at.inward()).wait_recv()
                put(True)

    def last(self, m, out):
        self.x_copy(m).wait_recv()
        out(1 - self.at.x, self.xr[m].astype(jnp.float32))

    def drain(self, m):
        at = self.at
        for k in range(4):
            z = at.order(k)
            self.y_copy(m, z).wait_send()
            if k > 0:
                self.z_copy(m, z, z, at.inward()).wait_send()
        self.x_copy(m).wait_send()


QKV, OUT, UP, DOWN, COLS = 0, 1536, 2048, 3072, 4096
GATHERED = ((0, 1536), (1536, 2048))
SCATTERED = ((512, 1536), (0, 512), (1536, 2048))
BF, F32 = jnp.bfloat16, jnp.float32
SUMS = ("bq", "bv", "bout", "bdown", "g1", "s1", "g2", "s2", "x", "mid", "res", "branch", "feed")
BLOCK = 32


def nn(a, b):
    return lax.dot_general(a, b, (((1,), (0,)), ((), ())), preferred_element_type=F32)


def nt(a, b):
    return lax.dot_general(a, b, (((1,), (1,)), ((), ())), preferred_element_type=F32)


def at_rows(start, size):
    return pl.ds(pl.multiple_of(start, size), size)


def fold(v):
    return jnp.sum(v.reshape(v.shape[0] // 8, 8, v.shape[1]), axis=0)


def normed(v):
    centre = jnp.mean(v, axis=1, keepdims=True)
    offset = v - centre
    r = lax.rsqrt(jnp.mean(offset * offset, axis=1, keepdims=True) + eps_norm)
    return offset * r, r


def norm_back(dy, n, r, gain):
    dn = dy * gain
    first = jnp.mean(dn, axis=1, keepdims=True)
    second = jnp.mean(dn * n, axis=1, keepdims=True)
    return r * (dn - first - n * second)


def block_kernel(
    counts, x_ref, cot_ref, wqkv, wout, wup, wdown, bqv, bout, bup, bdown, g1, s1, g2, s2,
    act_out, gin_out, o_qkv, o_out, o_up, o_down, o_sums,
    W, G2, G3, xh, yh, xf, yf, zl, yf2, zl2, xs2, xr2,
    rows1, dfeed, qkv, probs, heads, mid, rows2, act, gp, datt,
    tall, own_a, own_b, own_c, send_t, send_x, got, got_t, acc, acc_up, sums, sums_got,
    sem_in, ag_send, ag_recv, pg_send, pg_recv, rs_send, rs_recv, ps_send, ps_recv,
    pair_send, pair_recv, sums_send, sums_recv,
):
    at = Place()
    t, x = at.t, at.x
    shard = wup.shape[0]
    own = x_ref.shape[0]
    width = x_ref.shape[1]
    dbr = dfeed.at[0 : 2 * own, :]
    dproj = qkv

    def spot(far_x, far_t):
        return at_rows((far_x * 2 + far_t) * own, own)

    mine, theirs = at_rows(t * own, own), at_rows((1 - t) * own, own)

    here = at_rows(at.dp * shard, shard)
    quarter = pl.ds(pl.multiple_of(x * 1024, 1024), 1024)
    loads = [
        pltpu.make_async_copy(src, W.at[here, pl.ds(c0, n)], sem_in.at[i])
        for i, (src, c0, n) in enumerate(
            [(wqkv.at[j], QKV + 512 * j, 512) for j in range(3)]
            + [(wout, OUT, 512), (wup.at[:, quarter], UP, 1024), (wdown.at[:, quarter], DOWN, 1024)]
        )
    ]
    for c in loads:
        c.start()
    enter(at)
    g = Gather(at, W, shard, GATHERED, ag_send, ag_recv)
    pg = PairGather(at, W, shard, ((UP, 1024), (DOWN, 1024)), (wup, wdown), pg_send, pg_recv)
    for c in loads:
        c.wait()
    g.line(0, 0)

    steps = []
    ends = {}

    def plan(f, *a):
        steps.append(lambda: f(*a))

    def attention_step(p, k):
        if k < 3:
            plan(g.line, p, k + 1)
        plan(g.plane, p, k)

    attention_step(0, 0)
    plan(pg.x_copy(0).start)
    plan(pg.line, 0, 0, 0)
    attention_step(0, 1)
    plan(g.line, 1, 0)
    attention_step(0, 2)
    plan(pg.line, 0, 0, 1)
    attention_step(0, 3)
    plan(pg.line, 0, 1, 0)
    plan(pg.x_copy(1).start)
    ends["qkv"] = len(steps)
    for k in range(4):
        attention_step(1, k)
        if k < 2:
            plan(pg.line, 0, 0, k + 2)
        else:
            plan(pg.line, 0, 1, k - 1)
    ends["out"] = len(steps)
    for k in range(4):
        plan(pg.cross, 0, 0, k)
    plan(pg.line, 0, 1, 3)
    plan(pg.line, 1, 0, 0)
    plan(pg.line, 1, 1, 0)
    for k in range(4):
        plan(pg.cross, 0, 1, k)
    for h in range(2):
        for k in range(1, 4):
            plan(pg.line, 1, h, k)
        for k in range(4):
            plan(pg.cross, 1, h, k)
        if h == 0:
            ends["up"] = len(steps)
    ends["down"] = len(steps)
    done = [0]

    def gather(n):
        while n > 0 and done[0] < len(steps):
            steps[done[0]]()
            done[0] += 1
            n -= 1

    def need(name):
        gather(ends[name] - done[0])
        if name == "qkv":
            g.finish(0)
        elif name == "out":
            g.finish(1)
        else:
            pg.finish(0 if name == "up" else 1)

    home = {0: (W, DOWN, DOWN + 1024), 1: (G3, 0, 512), 2: (G3, 512, 1024)}
    sc = Scatter(at, lambda p: home[p], shard, SCATTERED, xh, yh, xf, yf, zl, rs_send, rs_recv)
    home_pair = {0: (W, UP, 1024), 1: (G2, 0, 1024)}
    ps = PairScatter(at, lambda m: home_pair[m], shard, yf2, zl2, xs2, xr2, ps_send, ps_recv)

    def write(p):
        def store(total):
            if p == 0:
                o_qkv[1] = total[:, :512]
                o_qkv[2] = total[:, 512:]
            elif p == 1:
                o_qkv[0] = total
            else:
                o_out[...] = total
        return store

    def write_pair(m):
        ref = o_up if m == 0 else o_down

        def store(far_x, total):
            ref[:, pl.ds(pl.multiple_of(far_x * 1024, 1024), 1024)] = total
        return store

    queue = []

    def reduce_begin(p):
        sc.begin(p)
        for k in (3, 2, 1, 0):
            queue.append(lambda p=p, k=k: sc.plane(p, k))
        for k in (3, 2, 1, 0):
            queue.append(lambda p=p, k=k: sc.line(p, k, write(p)))

    def reduce_pair(m):
        ps.begin(m)
        for k in (3, 2, 1, 0):
            queue.append(lambda m=m, k=k: ps.line(m, k, write_pair(m)))

    def scatter(n):
        while n > 0 and queue:
            queue.pop(0)()
            n -= 1

    def send(i, src, dst, other):
        return pltpu.make_async_remote_copy(
            src_ref=src, dst_ref=dst, send_sem=pair_send.at[i], recv_sem=pair_recv.at[i],
            device_id=other, device_id_type=MESH,
        )

    def share(i, ref, r, other):
        c = send(i, ref.at[r, :], ref.at[r, :], other)
        c.start()
        return c

    def take(i, ref, r):
        send(i, ref.at[r, :], ref.at[r, :], at.twin()).wait_recv()

    for ref in (acc, acc_up):
        ref[...] = jnp.zeros_like(ref)
    total_of = {name: acc.at[i] for i, name in enumerate(SUMS)}

    def add(name, v):
        ref = total_of[name]
        ref[...] += fold(v)

    def valid_of(image, start, size):
        slot = lax.broadcasted_iota(jnp.int32, (size, 1), 0) + start
        return slot < counts[image] + BUFFER

    def each_block(body):
        def go(b, _):
            body(b * BLOCK, pl.ds(pl.multiple_of(b * BLOCK, BLOCK), BLOCK))
            return 0
        lax.fori_loop(0, own // BLOCK, go, 0)

    def tiles(first, last, body, size=256):
        def go(i, _):
            body(pl.multiple_of(i * size, size))
            return 0
        lax.fori_loop(first // size, last // size, go, 0)

    def flip(src):
        def body(c):
            tall[pl.ds(c, 128), 0 : src.shape[0]] = src[:, pl.ds(c, 128)].T
        tiles(0, src.shape[1], body, 128)

    def first_norm(b, r):
        xv = x_ref[r, :].astype(F32)
        keep = valid_of(t, b, BLOCK).astype(F32)
        n, _ = normed(xv)
        mine_b = pl.ds(pl.multiple_of(t * own + b, BLOCK), BLOCK)
        rows1[mine_b, :] = (n * g1[...] + s1[...]).astype(BF)
        add("x", keep * xv * xv)
        low = (cot_ref[r, :].astype(F32) * keep).astype(BF)
        dfeed[pl.ds(pl.multiple_of((x * 2 + t) * own + b, BLOCK), BLOCK), :] = low
        add("bdown", low.astype(F32))

    each_block(first_norm)
    shares = [share(0, rows1, mine, at.twin()), share(1, dfeed, spot(x, t), at.twin())]
    gather(3)
    take(0, rows1, theirs)
    need("qkv")
    shares.append(share(2, dfeed, spot(x, t), at.across_x()))

    def project(c):
        v = nn(rows1[...], W[:, pl.ds(c, 256)])
        part = c // 512
        inside = pl.ds(pl.multiple_of(c % 512 + t * 512, 256), 256)
        bias = jnp.where(part == 0, bqv[0:1, inside], jnp.where(part == 2, bqv[1:2, inside], 0.0))
        scale = jnp.where(part == 0, HD**-0.5, 1.0)
        qkv[:, pl.ds(c, 256)] = ((v + bias) * scale).astype(BF)

    tiles(0, 1536, project)
    gather(2)

    first_lanes = lax.broadcasted_iota(jnp.int32, (own, 128), 1) < HD

    def attend(it):
        image, j = it // 4, it % 4
        r = pl.ds(pl.multiple_of(image * own, own), own)
        c = j * 128
        q2 = qkv[r, pl.ds(pl.multiple_of(c, 128), 128)]
        k2 = qkv[r, pl.ds(pl.multiple_of(c + 512, 128), 128)]
        v_t = qkv[r, pl.ds(pl.multiple_of(c + 1024, 128), 128)].T
        hide = jnp.where(valid_of(image, 0, own), 0.0, -1e30)
        outs = []
        for a in range(2):
            qm = jnp.where(first_lanes if a == 0 else ~first_lanes, q2, jnp.zeros_like(q2))
            s = nt(k2, qm) + hide
            e = jnp.exp(s - jnp.max(s, axis=0, keepdims=True))
            low = (e * (1.0 / jnp.sum(e, axis=0, keepdims=True))).astype(BF)
            probs[it * 2 + a] = low
            outs.append(nn(v_t[a * HD : (a + 1) * HD], low))
        heads[r, pl.ds(pl.multiple_of(c, 128), 128)] = jnp.concatenate(outs, axis=0).T.astype(BF)

    def attend_some(first, last, body):
        def go(i, _):
            body(i)
            return 0
        lax.fori_loop(first, last, go, 0)

    for i in range(4):
        attend_some(2 * i, 2 * i + 2, attend)
        gather(3)
    need("out")

    def reduced(i, src, cols, keep):
        def other(c):
            send_t[0, :, pl.ds(c, 256)] = nt(src[theirs, :], W[pl.ds(c, 256), cols]).astype(BF)
        tiles(0, width, other)
        copy = send(i, send_t.at[0], got.at[0 if i == 3 else 1], at.twin())
        copy.start()
        def self(c):
            keep[:, pl.ds(c, 256)] = nt(src[mine, :], W[pl.ds(c, 256), cols])
        tiles(0, width, self)
        return copy

    branch_copy = reduced(3, heads, pl.ds(OUT, 512), own_a)
    gather(2)
    branch_copy.wait()

    def second_norm(b, r):
        keep = valid_of(t, b, BLOCK).astype(F32)
        branch = own_a[r, :] + got[0, r, :].astype(F32) + bout[...]
        m = x_ref[r, :].astype(F32) + branch
        mid[r, :] = m
        add("branch", keep * branch * branch)
        add("mid", keep * m * m)
        n, _ = normed(m)
        rows2[pl.ds(pl.multiple_of((x * 2 + t) * own + b, BLOCK), BLOCK), :] = (n * g2[...] + s2[...]).astype(BF)

    each_block(second_norm)
    shares.append(share(4, rows2, spot(x, t), at.across_x()))
    shares.append(share(5, rows2, spot(x, t), at.twin()))
    gather(1)

    take(2, dfeed, spot(1 - x, t))
    shares.append(share(6, dfeed, spot(1 - x, t), at.twin()))
    take(1, dfeed, spot(x, 1 - t))
    take(6, dfeed, spot(1 - x, 1 - t))
    flip(dfeed)
    take(5, rows2, spot(x, 1 - t))

    chip_rows = lambda far_x: at_rows(far_x * 2 * own, 2 * own)

    def hidden(far_x):
        r = chip_rows(far_x)

        def body(c):
            lanes = pl.ds(pl.multiple_of(t * 2048 + x * 1024 + c, 256), 256)
            u = nn(rows2[r, :], W[:, pl.ds(UP + c, 256)]) + bup[:, lanes]
            below = 0.5 * (1.0 + lax.erf(u * (0.5**0.5)))
            dense = jnp.exp(-0.5 * u * u) * 0.3989422804014327
            act[r, pl.ds(c, 256)] = (u * below).astype(BF)
            gp[r, pl.ds(c, 256)] = (below + u * dense).astype(BF)
        tiles(0, 1024, body)

    def grad_down(c):
        G2[:, pl.ds(c, 256)] = nn(tall[...], act[:, pl.ds(c, 256)]).astype(BF)

    need("up")
    hidden(x)
    gather(2)
    take(4, rows2, spot(1 - x, t))
    shares.append(share(7, rows2, spot(1 - x, t), at.twin()))
    take(7, rows2, spot(1 - x, 1 - t))
    hidden(1 - x)
    gather(2)
    tiles(0, 1024, grad_down)
    flip(rows2)
    gather(100)
    reduce_pair(1)

    def back_act(far_x):
        r = chip_rows(far_x)

        def body(c):
            d = nn(dfeed[r, :], W[:, pl.ds(DOWN + c, 256)])
            low = (d * gp[r, pl.ds(c, 256)].astype(F32)).astype(BF)
            gp[r, pl.ds(c, 256)] = low
            acc_up[t * 2 + x, :, pl.ds(c, 256)] += fold(low.astype(F32))
        tiles(0, 1024, body)

    def product(src, r, cols, put):
        def body(c):
            put(pl.ds(c, 256), nt(src[r, :], W[pl.ds(c, 256), cols]))
        tiles(0, width, body)

    class Sum4:
        def __init__(self, i, n, src, cols, keep):
            self.i, self.n, self.src, self.cols, self.keep = i, n, src, cols, keep

        def away(self, far_x, slot):
            def put(c, v):
                send_t[slot, :, c] = v.astype(BF)
            product(self.src, spot(far_x, 1 - t), self.cols, put)
            copy = send(self.i + slot, send_t.at[slot], got_t.at[self.n, slot], at.twin())
            copy.start()
            return copy

        def far(self):
            first = self.away(1 - x, 0)

            def put(c, v):
                own_b[:, c] = v
            product(self.src, spot(1 - x, t), self.cols, put)
            first.wait()

            def body(b, r):
                send_x[self.n, r, :] = (own_b[r, :] + got_t[self.n, 0, r, :].astype(F32)).astype(BF)
            each_block(body)
            self.cross = send(self.i + 2, send_x.at[self.n], got.at[2 + self.n], at.across_x())
            self.cross.start()

        def near(self):
            second = self.away(x, 1)

            def put(c, v):
                self.keep[:, c] = v
            product(self.src, spot(x, t), self.cols, put)
            second.wait()

        def value(self, r):
            return self.keep[r, :] + got_t[self.n, 1, r, :].astype(F32) + got[2 + self.n, r, :].astype(F32)

    need("down")
    back_act(1 - x)
    two = Sum4(8, 0, gp, pl.ds(UP, 1024), own_a)
    two.far()
    scatter(1)
    back_act(x)
    two.near()
    for p in range(2):
        g.drain(p)
        pg.drain(p)
    scatter(1)

    def grad_up(c):
        W[:, pl.ds(UP + c, 256)] = nn(tall[...], gp[:, pl.ds(c, 256)]).astype(BF)

    tiles(0, 1024, grad_up)
    reduce_pair(0)
    scatter(1)
    four = Sum4(11, 1, act, pl.ds(DOWN, 1024), own_c)
    four.far()
    scatter(1)
    four.near()
    two.cross.wait()
    for i in (1, 2, 5):
        shares[i].wait_send()

    def second_back(b, r):
        dy = two.value(r)
        n, scale = normed(mid[r, :])
        keep = valid_of(t, b, BLOCK).astype(F32)
        add("g2", dy * n)
        add("s2", dy)
        d = cot_ref[r, :].astype(F32) * keep + norm_back(dy, n, scale, g2[...])
        gin_out[r, :] = d
        low = d.astype(BF)
        dbr[pl.ds(pl.multiple_of(t * own + b, BLOCK), BLOCK), :] = low
        add("bout", low.astype(F32))

    each_block(second_back)
    shares.append(share(14, dbr, mine, at.twin()))
    scatter(1)
    take(14, dbr, theirs)

    def back_heads(c):
        datt[:, pl.ds(c, 256)] = nn(dbr[...], W[:, pl.ds(OUT + c, 256)]).astype(BF)

    tiles(0, 512, back_heads)
    flip(dbr)
    short = pl.ds(0, 2 * own)

    def grad_out(c):
        G3[:, pl.ds(512 + c, 256)] = nn(tall[:, short], heads[:, pl.ds(c, 256)]).astype(BF)

    tiles(0, 512, grad_out)
    reduce_begin(2)
    scatter(2)

    def attend_back(it):
        image, j = it // 4, it % 4
        r = pl.ds(pl.multiple_of(image * own, own), own)
        c = j * 128
        q2 = qkv[r, pl.ds(pl.multiple_of(c, 128), 128)]
        k_t = qkv[r, pl.ds(pl.multiple_of(c + 512, 128), 128)].T
        v2 = qkv[r, pl.ds(pl.multiple_of(c + 1024, 128), 128)]
        da = datt[r, pl.ds(pl.multiple_of(c, 128), 128)]
        dq, dk, dv = [], [], []
        for a in range(2):
            dam = jnp.where(first_lanes if a == 0 else ~first_lanes, da, jnp.zeros_like(da))
            low = probs[it * 2 + a]
            p = low.astype(F32)
            dp = nt(v2, dam)
            ds = (p * (dp - jnp.sum(p * dp, axis=0, keepdims=True))).astype(BF)
            dq.append(nn(k_t[a * HD : (a + 1) * HD], ds))
            dk.append(nn(ds, q2))
            dv.append(nn(low, da))
        for base, v in (
            (0, jnp.concatenate(dq, axis=0).T * HD**-0.5),
            (512, jnp.where(first_lanes, dk[0], dk[1])),
            (1024, jnp.where(first_lanes, dv[0], dv[1])),
        ):
            v = v.astype(BF)
            dproj[r, pl.ds(pl.multiple_of(base + c, 128), 128)] = v
            if base != 512:
                lanes = pl.ds(pl.multiple_of(t * 512 + c, 128), 128)
                ref = total_of["bq" if base == 0 else "bv"]
                ref[:, lanes] += fold(v.astype(F32))

    for i in range(4):
        attend_some(2 * i, 2 * i + 2, attend_back)
        scatter(3)

    one_copy = reduced(15, dproj, pl.ds(QKV, 1536), own_a)
    flip(rows1)

    def grad_kv(c):
        W[:, pl.ds(DOWN + c, 256)] = nn(tall[:, short], dproj[:, pl.ds(512 + c, 256)]).astype(BF)

    def grad_q(c):
        G3[:, pl.ds(c, 256)] = nn(tall[:, short], dproj[:, pl.ds(c, 256)]).astype(BF)

    tiles(0, 1024, grad_kv)
    reduce_begin(0)
    tiles(0, 512, grad_q)
    reduce_begin(1)
    one_copy.wait()

    def first_back(b, r):
        dy = own_a[r, :] + got[1, r, :].astype(F32)
        n, scale = normed(x_ref[r, :].astype(F32))
        add("g1", dy * n)
        add("s1", dy)
        gin_out[r, :] += norm_back(dy, n, scale, g1[...])

    each_block(first_back)
    scatter(4)
    four.cross.wait()

    def finish_feed(b, r):
        keep = valid_of(t, b, BLOCK).astype(F32)
        feed = four.value(r) + bdown[...]
        res = mid[r, :] + feed
        add("feed", keep * feed * feed)
        add("res", keep * res * res)
        act_out[r, :] = (keep * res).astype(BF)

    each_block(finish_feed)

    for i in range(8):
        sums[i : i + 1, :] = jnp.sum(acc[i], axis=0, keepdims=True)
    for i in range(4):
        sums[8 + i : 9 + i, :] = jnp.sum(acc_up[i], axis=0, keepdims=True)
    lane = lax.broadcasted_iota(jnp.int32, (1, width), 1)
    row = jnp.where(lane == 5, (counts[t] + BUFFER).astype(F32), 0.0)
    for i, name in enumerate(("x", "mid", "res", "branch", "feed")):
        row = jnp.where(lane == i, jnp.sum(jnp.sum(total_of[name][...], axis=0, keepdims=True), axis=1, keepdims=True), row)
    sums[12:13, :] = row
    sums[13:16, :] = jnp.zeros((3, width), F32)
    for i, other in enumerate((at.twin(), at.across_x(), at.across_y(), at.near(), at.far())):
        c = pltpu.make_async_remote_copy(
            src_ref=sums, dst_ref=sums_got.at[i], send_sem=sums_send.at[i], recv_sem=sums_recv.at[i],
            device_id=other, device_id_type=MESH,
        )
        c.start()
        scatter(2)
        c.wait()
        sums[...] += sums_got[i]
    o_sums[...] = sums[...]
    scatter(1000)
    for m in (1, 0):
        ps.last(m, write_pair(m))
        ps.drain(m)
    for p in range(3):
        sc.drain(p)
    for i in (0, 3, 4, 6, 7):
        shares[i].wait_send()


def block(counts, stream, cotangent, w_qkv, w_out_t, w_up, w_down_t, b_qv, b_out, b_up, b_down, g1, s1, g2, s2):
    own, width = stream.shape
    shard = w_up.shape[0]
    rows = 16 * shard
    group = 2 * own
    vmem = pl.BlockSpec(memory_space=pltpu.VMEM)
    hbm = pl.BlockSpec(memory_space=pl.ANY)
    dma = pltpu.SemaphoreType.DMA
    row = lambda v: v.reshape(1, -1)
    return pl.pallas_call(
        block_kernel,
        out_shape=(
            jax.ShapeDtypeStruct((own, width), BF),
            jax.ShapeDtypeStruct((own, width), F32),
            jax.ShapeDtypeStruct((3, shard, 512), F32),
            jax.ShapeDtypeStruct((shard, 512), F32),
            jax.ShapeDtypeStruct((shard, 2048), F32),
            jax.ShapeDtypeStruct((shard, 2048), F32),
            jax.ShapeDtypeStruct((16, width), F32),
        ),
        in_specs=[pl.BlockSpec(memory_space=pltpu.SMEM), vmem, vmem, hbm, hbm, hbm, hbm] + [vmem] * 8,
        out_specs=(vmem,) * 7,
        scratch_shapes=[
            pltpu.VMEM((rows, COLS), BF),
            pltpu.VMEM((rows, 1024), BF),
            pltpu.VMEM((rows, 1024), BF),
            pltpu.VMEM((4, shard // 2, 2048), BF),
            pltpu.VMEM((4, shard // 2, 2048), BF),
            pltpu.VMEM((4, shard, 2048), BF),
            pltpu.VMEM((4, shard, 2048), BF),
            pltpu.VMEM((5, shard, 2048), BF),
            pltpu.VMEM((2, 4, 2 * shard, 1024), BF),
            pltpu.VMEM((2, 5, 2 * shard, 1024), BF),
            pltpu.VMEM((2, shard, 1024), BF),
            pltpu.VMEM((2, shard, 1024), BF),
            pltpu.VMEM((group, width), BF),
            pltpu.VMEM((2 * group, width), BF),
            pltpu.VMEM((group, 1536), BF),
            pltpu.VMEM((16, own, own), BF),
            pltpu.VMEM((group, 512), BF),
            pltpu.VMEM((own, width), F32),
            pltpu.VMEM((2 * group, width), BF),
            pltpu.VMEM((2 * group, 1024), BF),
            pltpu.VMEM((2 * group, 1024), BF),
            pltpu.VMEM((group, 512), BF),
            pltpu.VMEM((width, 2 * group), BF),
            pltpu.VMEM((own, width), F32),
            pltpu.VMEM((own, width), F32),
            pltpu.VMEM((own, width), F32),
            pltpu.VMEM((2, own, width), BF),
            pltpu.VMEM((2, own, width), BF),
            pltpu.VMEM((4, own, width), BF),
            pltpu.VMEM((2, 2, own, width), BF),
            pltpu.VMEM((len(SUMS), 8, width), F32),
            pltpu.VMEM((4, 8, 1024), F32),
            pltpu.VMEM((16, width), F32),
            pltpu.VMEM((5, 16, width), F32),
            dma((6,)),
            dma((2, 6, 4)),
            dma((2, 5, 4)),
            dma((4, 4, 4)),
            dma((4, 3, 4)),
            dma((3, 5, 4)),
            dma((3, 5, 5)),
            dma((2, 3, 4)),
            dma((2, 3, 5)),
            dma((16,)),
            dma((16,)),
            dma((5,)),
            dma((5,)),
        ],
        compiler_params=pltpu.CompilerParams(
            collective_id=1, has_side_effects=True, vmem_limit_bytes=63 << 20
        ),
    )(
        counts, stream, cotangent, w_qkv, w_out_t, w_up, w_down_t,
        b_qv, row(b_out), row(b_up), row(b_down), row(g1), row(s1), row(g2), row(s2),
    )


def local_fast(
    stream, counts, cotangent, w_qkv, b_qv, w_out, b_out, w_fc1, b_fc1, w_fc2, b_fc2,
    gain_one, shift_one, gain_two, shift_two,
):
    acts, grad_in, p_qkv, p_out, p_up, p_down, sums = block(
        counts, stream, cotangent, w_qkv, w_out.T, w_fc1, w_fc2.T, b_qv, b_out, b_fc1, b_fc2,
        gain_one, shift_one, gain_two, shift_two,
    )
    place = lax.axis_index("dp") * 2 + lax.axis_index("tensor")
    vectors = lax.dynamic_slice(sums[:8], (0, place * 32), (8, 32))
    up = lax.dynamic_slice(sums[8:12].reshape(-1), (place * 128,), (128,))
    rms = jnp.sqrt(sums[12, :5] / (sums[12, 5] * stream.shape[1]))
    return (
        acts, grad_in, p_qkv, vectors[0:2], p_out.T, vectors[2], p_up, up, p_down.T, vectors[3],
        vectors[4], vectors[5], vectors[6], vectors[7], rms,
    )


def layer_norm(values, gain, shift):
    centre = jnp.mean(values, axis=-1, keepdims=True)
    offset = values - centre
    spread = jnp.mean(offset * offset, axis=-1, keepdims=True)
    return offset * lax.rsqrt(spread + eps_norm) * gain + shift


def gelu_exact(values):
    return jax.nn.gelu(values, approximate=False)


def masked_scores(queries, key_rows, validity):
    scores = jnp.einsum(
        "bqhd,bkhd->bhqk", queries, key_rows, preferred_element_type=jnp.float32
    ) * HD ** (-0.5)
    return jnp.where(validity[:, None, None, :] > 0, scores, -1e30)


def attend_block(members):
    queries, key_rows, values, validity = members
    scores = masked_scores(queries, key_rows, validity)
    highest = jnp.max(scores, axis=-1, keepdims=True)
    expo_terms = jnp.exp(scores - highest)
    totals = jnp.sum(expo_terms, axis=-1, keepdims=True)
    weights = (expo_terms / totals).astype(jnp.bfloat16)
    mixture = jnp.einsum("bhqk,bkhd->bqhd", weights, values, preferred_element_type=jnp.float32)
    return (mixture.astype(jnp.bfloat16), (highest + jnp.log(totals))[..., 0])


def attend_back(members):
    queries, key_rows, values, validity, log_total, d_mixture = members
    scores = masked_scores(queries, key_rows, validity)
    probs = jnp.exp(scores - log_total[..., None])
    d_values = jnp.einsum(
        "bhqk,bqhd->bkhd", probs.astype(jnp.bfloat16), d_mixture, preferred_element_type=jnp.float32
    )
    d_probs = jnp.einsum("bqhd,bkhd->bhqk", d_mixture, values, preferred_element_type=jnp.float32)
    d_scores = (probs * (d_probs - jnp.sum(probs * d_probs, axis=-1, keepdims=True))).astype(
        jnp.bfloat16
    )
    d_queries = jnp.einsum(
        "bhqk,bkhd->bqhd", d_scores, key_rows, preferred_element_type=jnp.float32
    ) * HD ** (-0.5)
    d_keys = jnp.einsum(
        "bhqk,bqhd->bkhd", d_scores, queries, preferred_element_type=jnp.float32
    ) * HD ** (-0.5)
    return (
        d_queries.astype(jnp.bfloat16),
        d_keys.astype(jnp.bfloat16),
        d_values.astype(jnp.bfloat16),
    )


def local(
    stream,
    counts,
    cotangent,
    w_qkv,
    b_qv,
    w_out,
    b_out,
    w_fc1,
    b_fc1,
    w_fc2,
    b_fc2,
    gain_one,
    shift_one,
    gain_two,
    shift_two,
):
    tensor_pos = lax.axis_index("tensor")
    own_rows = stream.shape[0]
    width = stream.shape[1]
    own_images = own_rows // SLOTS
    slot_index = jnp.arange(SLOTS, dtype=jnp.int32)
    validity_all = (slot_index[None, :] < (BUFFER + counts)[:, None]).astype(jnp.float32)
    own_validity = lax.dynamic_slice_in_dim(validity_all, tensor_pos * own_images, own_images, 0)
    own_valid = own_validity.reshape(own_rows, 1)
    qkv_full, out_full, up_full, down_full = (
        lax.all_gather(w_qkv, "dp", axis=1, tiled=True),
        lax.all_gather(w_out, "dp", axis=1, tiled=True),
        lax.all_gather(w_fc1[None], "dp", axis=1, tiled=True),
        lax.all_gather(w_fc2, "dp", axis=1, tiled=True),
    )
    head_width = w_qkv.shape[2]
    unit_width = w_fc1.shape[1]
    bias_query = lax.dynamic_slice_in_dim(b_qv[0], tensor_pos * head_width, head_width, 0)
    bias_value = lax.dynamic_slice_in_dim(b_qv[1], tensor_pos * head_width, head_width, 0)
    bias_up = lax.dynamic_slice_in_dim(b_fc1, tensor_pos * unit_width, unit_width, 0)
    up_full = up_full[0]
    group_images = validity_all.shape[0]
    group_rows = group_images * SLOTS
    local_heads = head_width // HD
    pairing = 2
    block_count = group_images // pairing
    blocked_valid = validity_all.reshape(block_count, pairing, SLOTS)
    stream_f = stream.astype(jnp.float32)
    normed_one = layer_norm(stream_f, gain_one, shift_one).astype(jnp.bfloat16)
    first_rows = lax.all_gather(normed_one, "tensor", axis=0, tiled=True)
    projected = jnp.einsum("rd,cde->rce", first_rows, qkv_full, preferred_element_type=jnp.float32)
    shape_heads = (block_count, pairing, SLOTS, local_heads, HD)
    queries = (projected[:, 0] + bias_query).astype(jnp.bfloat16).reshape(shape_heads)
    key_rows = projected[:, 1].astype(jnp.bfloat16).reshape(shape_heads)
    values = (projected[:, 2] + bias_value).astype(jnp.bfloat16).reshape(shape_heads)
    mixture, log_total = lax.map(attend_block, (queries, key_rows, values, blocked_valid))
    attn_heads = mixture.reshape(group_rows, head_width)
    taken = attn_heads
    attn_total = lax.psum_scatter(
        jnp.dot(taken, out_full, preferred_element_type=jnp.float32).astype(jnp.bfloat16),
        "tensor",
        scatter_dimension=0,
        tiled=True,
    ).astype(jnp.float32)
    branch = attn_total + b_out
    middle = stream_f + branch
    normed_two = layer_norm(middle, gain_two, shift_two).astype(jnp.bfloat16)
    second_rows = lax.all_gather(normed_two, "tensor", axis=0, tiled=True)
    hidden_pre = jnp.dot(second_rows, up_full, preferred_element_type=jnp.float32) + bias_up
    hidden_act = gelu_exact(hidden_pre).astype(jnp.bfloat16)
    taken = hidden_act
    mlp_total = lax.psum_scatter(
        jnp.dot(taken, down_full, preferred_element_type=jnp.float32).astype(jnp.bfloat16),
        "tensor",
        scatter_dimension=0,
        tiled=True,
    ).astype(jnp.float32)
    feed = mlp_total + b_fc2
    result = middle + feed
    activations = (result * own_valid).astype(jnp.bfloat16)
    squares = jnp.stack(
        [
            jnp.sum(own_valid * member * member)
            for member in (stream_f, middle, result, branch, feed)
        ]
    )
    square_sums, valid_count = lax.psum((squares, jnp.sum(own_valid)), ("dp", "tensor"))
    rms_stats = jnp.sqrt(square_sums / (valid_count * width))
    d_result = cotangent.astype(jnp.float32) * own_valid
    d_feed_low = d_result.astype(jnp.bfloat16)
    d_feed_rows = lax.all_gather(d_feed_low, "tensor", axis=0, tiled=True)
    d_act = jnp.einsum("rd,ud->ru", d_feed_rows, down_full, preferred_element_type=jnp.float32)
    unused_act, gelu_pullback = jax.vjp(gelu_exact, hidden_pre)
    d_pre = gelu_pullback(d_act)[0].astype(jnp.bfloat16)
    grad_down = jnp.einsum("ru,rd->ud", hidden_act, d_feed_rows, preferred_element_type=jnp.float32)
    grad_up = jnp.einsum("rd,ru->du", second_rows, d_pre, preferred_element_type=jnp.float32)
    grad_bias_up = jnp.sum(d_pre, axis=0, dtype=jnp.float32)
    grad_bias_down = jnp.sum(d_feed_low, axis=0, dtype=jnp.float32)
    taken = d_pre
    d_normed_two = lax.psum_scatter(
        jnp.einsum("ru,du->rd", taken, up_full, preferred_element_type=jnp.float32).astype(
            jnp.bfloat16
        ),
        "tensor",
        scatter_dimension=0,
        tiled=True,
    ).astype(jnp.float32)
    unused_two, norm_two_pullback = jax.vjp(layer_norm, middle, gain_two, shift_two)
    d_middle_norm, grad_gain_two, grad_shift_two = norm_two_pullback(d_normed_two)
    d_middle = d_result + d_middle_norm
    d_branch_low = d_middle.astype(jnp.bfloat16)
    grad_bias_out = jnp.sum(d_branch_low, axis=0, dtype=jnp.float32)
    d_branch_rows = lax.all_gather(d_branch_low, "tensor", axis=0, tiled=True)
    d_attn = jnp.einsum(
        "rd,hd->rh", d_branch_rows, out_full, preferred_element_type=jnp.float32
    ).astype(jnp.bfloat16)
    grad_out = jnp.einsum(
        "rh,rd->hd", attn_heads, d_branch_rows, preferred_element_type=jnp.float32
    )
    d_queries, d_keys, d_values = lax.map(
        attend_back,
        (queries, key_rows, values, blocked_valid, log_total, d_attn.reshape(shape_heads)),
    )
    d_projected = jnp.stack(
        [
            d_queries.reshape(group_rows, head_width),
            d_keys.reshape(group_rows, head_width),
            d_values.reshape(group_rows, head_width),
        ],
        axis=1,
    )
    grad_qkv = jnp.einsum(
        "rd,rce->cde", first_rows, d_projected, preferred_element_type=jnp.float32
    )
    bias_terms = jnp.sum(d_projected, axis=0, dtype=jnp.float32)
    taken = d_projected
    d_normed_one = lax.psum_scatter(
        jnp.einsum("rce,cde->rd", taken, qkv_full, preferred_element_type=jnp.float32).astype(
            jnp.bfloat16
        ),
        "tensor",
        scatter_dimension=0,
        tiled=True,
    ).astype(jnp.float32)
    unused_one, norm_one_pullback = jax.vjp(layer_norm, stream_f, gain_one, shift_one)
    d_stream_norm, grad_gain_one, grad_shift_one = norm_one_pullback(d_normed_one)
    grad_input = d_middle + d_stream_norm
    grad_up = grad_up[None]
    bias_qv_full = lax.dynamic_update_slice(
        jnp.zeros((2, width), jnp.float32),
        jnp.stack([bias_terms[0], bias_terms[2]]),
        (jnp.int32(0), tensor_pos * head_width),
    )
    bias_up_full = lax.dynamic_update_slice(
        jnp.zeros((b_fc1.shape[0],), jnp.float32), grad_bias_up, (tensor_pos * unit_width,)
    )
    qkv_part, out_part, up_part, down_part = (
        lax.psum_scatter(
            grad_qkv.astype(jnp.bfloat16), "dp", scatter_dimension=1, tiled=True
        ).astype(jnp.float32),
        lax.psum_scatter(
            grad_out.astype(jnp.bfloat16), "dp", scatter_dimension=1, tiled=True
        ).astype(jnp.float32),
        lax.psum_scatter(
            grad_up.astype(jnp.bfloat16), "dp", scatter_dimension=1, tiled=True
        ).astype(jnp.float32),
        lax.psum_scatter(
            grad_down.astype(jnp.bfloat16), "dp", scatter_dimension=1, tiled=True
        ).astype(jnp.float32),
    )
    small_parts = (
        lax.psum_scatter(bias_qv_full, ("dp", "tensor"), scatter_dimension=1, tiled=True),
        lax.psum_scatter(grad_bias_out, ("dp", "tensor"), scatter_dimension=0, tiled=True),
        lax.psum_scatter(bias_up_full, ("dp", "tensor"), scatter_dimension=0, tiled=True),
        lax.psum_scatter(grad_bias_down, ("dp", "tensor"), scatter_dimension=0, tiled=True),
        lax.psum_scatter(grad_gain_one, ("dp", "tensor"), scatter_dimension=0, tiled=True),
        lax.psum_scatter(grad_shift_one, ("dp", "tensor"), scatter_dimension=0, tiled=True),
        lax.psum_scatter(grad_gain_two, ("dp", "tensor"), scatter_dimension=0, tiled=True),
        lax.psum_scatter(grad_shift_two, ("dp", "tensor"), scatter_dimension=0, tiled=True),
    )
    return (
        activations,
        grad_input,
        qkv_part,
        small_parts[0],
        out_part,
        small_parts[1],
        up_part[0],
        small_parts[2],
        down_part,
        small_parts[3],
        small_parts[4],
        small_parts[5],
        small_parts[6],
        small_parts[7],
        rms_stats,
    )


def solution(mesh):
    fast = mesh.shape["dp"] == 16 and mesh.shape["tensor"] == 2
    return jax.shard_map(
        local_fast if fast else local,
        mesh=mesh,
        in_specs=(
            P(("dp", "tensor"), None),
            P("dp"),
            P(("dp", "tensor"), None),
            P(None, "dp", "tensor"),
            P(),
            P("tensor", "dp"),
            P(),
            P("dp", "tensor"),
            P(),
            P("tensor", "dp"),
            P(),
            P(),
            P(),
            P(),
            P(),
        ),
        out_specs=(
            P(("dp", "tensor"), None),
            P(("dp", "tensor"), None),
            P(None, "dp", "tensor"),
            P(None, ("dp", "tensor")),
            P("tensor", "dp"),
            P(("dp", "tensor")),
            P("dp", "tensor"),
            P(("dp", "tensor")),
            P("tensor", "dp"),
            P(("dp", "tensor")),
            P(("dp", "tensor")),
            P(("dp", "tensor")),
            P(("dp", "tensor")),
            P(("dp", "tensor")),
            P(),
        ),
        check_vma=False,
    )
```

```python
import jax
import jax.numpy as jnp
from jax import lax
from jax.experimental import pallas as pl
from jax.experimental.pallas import tpu as pltpu
from jax.sharding import PartitionSpec as P

HD = 64
BUFFER = 64
SLOTS = 320


eps_norm = 1e-06


MESH = pl.DeviceIdType.MESH


class Place:
    def __init__(self):
        dp = lax.axis_index("dp")
        self.t = lax.axis_index("tensor")
        self.z, self.y, self.x = dp // 4, (dp // 2) % 2, dp % 2
        self.side = self.z // 2
        self.w = self.z + self.side * (3 - 2 * self.z)
        self.step = 1 - 2 * self.side
        self.dp = dp

    def order(self, k):
        o = (self.w, 1 - self.w, 2, 3)[k]
        return 3 * self.side + self.step * o

    def chip(self, z, y, x):
        return z * 4 + y * 2 + x

    def inward(self):
        return (self.chip(self.z + self.step, self.y, self.x), self.t)

    def outward(self):
        return (self.chip(self.z - self.step, self.y, self.x), self.t)

    def across_x(self):
        return (self.chip(self.z, self.y, 1 - self.x), self.t)

    def across_y(self):
        return (self.chip(self.z, 1 - self.y, self.x), self.t)

    def near(self):
        return (self.chip(self.z + 1 - 2 * (self.z % 2), self.y, self.x), self.t)

    def far(self):
        return (self.chip((self.z + 2) % 4, self.y, self.x), self.t)

    def twin(self):
        return (self.dp, 1 - self.t)


def enter(at):
    barrier = pltpu.get_barrier_semaphore()
    for other in (at.across_x(), at.across_y(), at.inward(), at.twin(), at.far()):
        pl.semaphore_signal(barrier, inc=1, device_id=other, device_id_type=MESH)

    @pl.when(at.w == 1)
    def _():
        pl.semaphore_signal(barrier, inc=1, device_id=at.outward(), device_id_type=MESH)

    pl.semaphore_wait(barrier, 5 + at.w)


class Gather:
    def __init__(self, at, full, shard, pieces, send, recv):
        self.at, self.full, self.shard, self.pieces, self.send, self.recv = at, full, shard, pieces, send, recv

    def rows(self, p, z, y, x, part=None):
        c0, c1 = self.pieces[p]
        start, size = self.at.chip(z, y, x) * self.shard, self.shard
        if part is not None:
            size = self.shard // 2
            start = start + part * size
        return self.full.at[pl.ds(pl.multiple_of(start, size), size), pl.ds(c0, c1 - c0)]

    def copy(self, p, ref, s, r, other):
        return pltpu.make_async_remote_copy(
            src_ref=ref,
            dst_ref=ref,
            send_sem=self.send.at[p, s[0], s[1]],
            recv_sem=self.recv.at[p, r[0], r[1]],
            device_id=other,
            device_id_type=MESH,
        )

    def z_in(self, p, z):
        return self.copy(p, self.rows(p, z, self.at.y, self.at.x), (0, z), (0, z), self.at.inward())

    def z_out(self, p, z):
        return self.copy(p, self.rows(p, z, self.at.y, self.at.x), (5, z), (0, z), self.at.outward())

    def x_full(self, p, z):
        return self.copy(p, self.rows(p, z, self.at.y, self.at.x), (1, z), (1, z), self.at.across_x())

    def y_full(self, p, z):
        return self.copy(p, self.rows(p, z, self.at.y, self.at.x), (2, z), (2, z), self.at.across_y())

    def x_half(self, p, z):
        return self.copy(p, self.rows(p, z, 1 - self.at.y, self.at.x, 1), (3, z), (3, z), self.at.across_x())

    def y_half(self, p, z):
        return self.copy(p, self.rows(p, z, self.at.y, 1 - self.at.x, 0), (4, z), (4, z), self.at.across_y())

    def arrived(self, p, kind, z):
        at = self.at
        ref = (
            lambda: self.rows(p, z, at.y, at.x),
            lambda: self.rows(p, z, at.y, 1 - at.x),
            lambda: self.rows(p, z, 1 - at.y, at.x),
            lambda: self.rows(p, z, 1 - at.y, 1 - at.x, 1),
            lambda: self.rows(p, z, 1 - at.y, 1 - at.x, 0),
        )[kind]()
        self.copy(p, ref, (kind, z), (kind, z), at.across_x()).wait_recv()

    def line(self, p, k):
        at = self.at
        z = at.order(k)
        if k > 0:
            self.arrived(p, 0, z)
        if k == 0:
            self.z_in(p, z).start()
        if k == 1:

            @pl.when(at.w == 1)
            def _():
                self.z_in(p, z).start()

        else:

            @pl.when(at.w == 1)
            def _():
                self.z_out(p, z).start()

        self.x_full(p, z).start()
        self.y_full(p, z).start()

    def plane(self, p, k):
        z = self.at.order(k)
        self.arrived(p, 1, z)
        self.y_half(p, z).start()
        self.arrived(p, 2, z)
        self.x_half(p, z).start()

    def finish(self, p):
        for k in range(4):
            z = self.at.order(k)
            self.arrived(p, 3, z)
            self.arrived(p, 4, z)

    def drain(self, p):
        at = self.at
        for k in range(4):
            z = at.order(k)
            if k == 0:
                self.z_in(p, z).wait_send()
            if k == 1:

                @pl.when(at.w == 1)
                def _(z=z):
                    self.z_in(p, z).wait_send()

            else:

                @pl.when(at.w == 1)
                def _(z=z):
                    self.z_out(p, z).wait_send()

            self.x_full(p, z).wait_send()
            self.y_full(p, z).wait_send()
            self.x_half(p, z).wait_send()
            self.y_half(p, z).wait_send()


class Scatter:
    def __init__(self, at, full, shard, pieces, xh, yh, xf, yf, zl, send, recv):
        self.at, self.full, self.shard, self.pieces = at, full, shard, pieces
        self.xh, self.yh, self.xf, self.yf, self.zl = xh, yh, xf, yf, zl
        self.send, self.recv = send, recv

    def cols(self, p):
        c0, c1 = self.pieces[p]
        return pl.ds(c0, c1 - c0)

    def rows(self, p, z, y, x, part=None):
        start, size = self.at.chip(z, y, x) * self.shard, self.shard
        if part is not None:
            size = self.shard // 2
            start = start + part * size
        ref, c0, c1 = self.full(p)
        return ref.at[pl.ds(pl.multiple_of(start, size), size), pl.ds(c0, c1 - c0)]

    def copy(self, p, src, dst, s, r, other):
        return pltpu.make_async_remote_copy(
            src_ref=src,
            dst_ref=dst,
            send_sem=self.send.at[p, s[0], s[1]],
            recv_sem=self.recv.at[p, r[0], r[1]],
            device_id=other,
            device_id_type=MESH,
        )

    def x_half(self, p, z):
        at = self.at
        return self.copy(
            p, self.rows(p, z, 1 - at.y, 1 - at.x, 0), self.xh.at[z, :, self.cols(p)], (1, z), (1, z), at.across_x()
        )

    def y_half(self, p, z):
        at = self.at
        return self.copy(
            p, self.rows(p, z, 1 - at.y, 1 - at.x, 1), self.yh.at[z, :, self.cols(p)], (2, z), (2, z), at.across_y()
        )

    def x_full(self, p, z):
        at = self.at
        return self.copy(
            p, self.rows(p, z, at.y, 1 - at.x), self.xf.at[z, :, self.cols(p)], (3, z), (3, z), at.across_x()
        )

    def y_full(self, p, z):
        at = self.at
        return self.copy(
            p, self.rows(p, z, 1 - at.y, at.x), self.yf.at[z, :, self.cols(p)], (4, z), (4, z), at.across_y()
        )

    def z_in(self, p, z, slot):
        at = self.at
        return self.copy(
            p, self.rows(p, z, at.y, at.x), self.zl.at[slot, :, self.cols(p)], (0, z), (0, slot), at.inward()
        )

    def z_out(self, p, z, slot):
        at = self.at
        return self.copy(
            p, self.rows(p, z, at.y, at.x), self.zl.at[slot, :, self.cols(p)], (0, z), (0, slot), at.outward()
        )

    def begin(self, p, k):
        z = self.at.order(k)
        self.x_half(p, z).start()
        self.y_half(p, z).start()

    def plane(self, p, k):
        at = self.at
        z = at.order(k)
        self.x_half(p, z).wait_recv()
        ref = self.rows(p, z, 1 - at.y, at.x, 0)
        ref[...] = ref[...] + self.xh[z, :, self.cols(p)]
        self.y_full(p, z).start()
        self.y_half(p, z).wait_recv()
        ref = self.rows(p, z, at.y, 1 - at.x, 1)
        ref[...] = ref[...] + self.yh[z, :, self.cols(p)]
        self.x_full(p, z).start()

    def wait_line(self, p, z, slot):
        self.z_in(p, z, slot).wait_recv()

    def line(self, p, k, out=None):
        at = self.at
        z = at.order(k)
        self.x_full(p, z).wait_recv()
        self.y_full(p, z).wait_recv()
        ref = self.rows(p, z, at.y, at.x)
        total = (
            ref[...].astype(jnp.float32)
            + self.xf[z, :, self.cols(p)].astype(jnp.float32)
            + self.yf[z, :, self.cols(p)].astype(jnp.float32)
        )
        if k > 0:

            @pl.when(at.w == 0)
            def _():
                ref[...] = total.astype(jnp.bfloat16)
                self.z_in(p, z, z).start()

            @pl.when(at.w == 1)
            def _():
                self.wait_line(p, z, z)
                ref[...] = (total + self.zl[z, :, self.cols(p)].astype(jnp.float32)).astype(jnp.bfloat16)
                if k == 3:
                    self.z_in(p, z, z).start()
                elif k == 2:
                    self.z_in(p, z, 4).start()
                else:
                    self.z_out(p, z, 4).start()

        else:
            self.wait_line(p, z, 4)
            total = total + self.zl[4, :, self.cols(p)].astype(jnp.float32)

            @pl.when(at.w == 0)
            def _():
                out(total)

            @pl.when(at.w == 1)
            def _():
                self.wait_line(p, z, z)
                out(total + self.zl[z, :, self.cols(p)].astype(jnp.float32))

    def drain(self, p):
        at = self.at
        for k in range(4):
            z = at.order(k)
            for c in (self.x_half(p, z), self.y_half(p, z), self.x_full(p, z), self.y_full(p, z)):
                c.wait_send()
            if k > 0:
                self.z_in(p, z, z).wait_send()


class PairGather:
    def __init__(self, at, full, shard, columns, sources, send, recv):
        self.at, self.full, self.shard, self.columns, self.sources = at, full, shard, columns, sources
        self.send, self.recv = send, recv

    def far_x(self, h):
        return self.at.x if h == 0 else 1 - self.at.x

    def rows(self, m, z, y, x):
        c0, n = self.columns[m]
        start = self.at.chip(z, y, x) * self.shard
        return self.full.at[pl.ds(pl.multiple_of(start, self.shard), self.shard), pl.ds(c0, n)]

    def copy(self, m, h, src, dst, s, r, z, other):
        i = 2 * m + h
        return pltpu.make_async_remote_copy(
            src_ref=src,
            dst_ref=dst,
            send_sem=self.send.at[i, s, z],
            recv_sem=self.recv.at[i, r, z],
            device_id=other,
            device_id_type=MESH,
        )

    def x_copy(self, m):
        at = self.at
        c0, n = self.columns[m]
        src = self.sources[m].at[:, pl.ds(pl.multiple_of((1 - at.x) * n, n), n)]
        return self.copy(m, 1, src, self.rows(m, at.z, at.y, at.x), 3, 2, at.z, at.across_x())

    def z_in(self, m, h, z):
        ref = self.rows(m, z, self.at.y, self.far_x(h))
        return self.copy(m, h, ref, ref, 0, 0, z, self.at.inward())

    def z_out(self, m, h, z):
        ref = self.rows(m, z, self.at.y, self.far_x(h))
        return self.copy(m, h, ref, ref, 1, 0, z, self.at.outward())

    def y_copy(self, m, h, z):
        ref = self.rows(m, z, self.at.y, self.far_x(h))
        return self.copy(m, h, ref, ref, 2, 1, z, self.at.across_y())

    def line(self, m, h, k):
        at = self.at
        z = at.order(k)
        if k > 0:
            ref = self.rows(m, z, at.y, self.far_x(h))
            self.copy(m, h, ref, ref, 0, 0, z, at.inward()).wait_recv()
        elif h == 1:
            ref = self.rows(m, z, at.y, self.far_x(h))
            self.copy(m, h, ref, ref, 0, 2, z, at.across_x()).wait_recv()
        if k == 0:
            self.z_in(m, h, z).start()
        if k == 1:

            @pl.when(at.w == 1)
            def _():
                self.z_in(m, h, z).start()

        else:

            @pl.when(at.w == 1)
            def _():
                self.z_out(m, h, z).start()

    def cross(self, m, h, k):
        self.y_copy(m, h, self.at.order(k)).start()

    def finish(self, m):
        at = self.at
        for h in range(2):
            for k in range(4):
                z = at.order(k)
                ref = self.rows(m, z, 1 - at.y, self.far_x(h))
                self.copy(m, h, ref, ref, 2, 1, z, at.across_y()).wait_recv()

    def drain(self, m):
        at = self.at
        self.x_copy(m).wait_send()
        for h in range(2):
            for k in range(4):
                z = at.order(k)
                if k == 0:
                    self.z_in(m, h, z).wait_send()
                if k == 1:

                    @pl.when(at.w == 1)
                    def _(z=z):
                        self.z_in(m, h, z).wait_send()

                else:

                    @pl.when(at.w == 1)
                    def _(z=z):
                        self.z_out(m, h, z).wait_send()

                self.y_copy(m, h, z).wait_send()


class PairScatter:
    def __init__(self, at, full, shard, yf, zl, xs, xr, send, recv):
        self.at, self.full, self.shard = at, full, shard
        self.yf, self.zl, self.xs, self.xr, self.send, self.recv = yf, zl, xs, xr, send, recv

    def unit(self, m, z, y):
        ref, c0, n = self.full(m)
        size = 2 * self.shard
        return ref.at[pl.ds(pl.multiple_of((z * 2 + y) * size, size), size), pl.ds(c0, n)]

    def copy(self, m, src, dst, s, r, other):
        return pltpu.make_async_remote_copy(
            src_ref=src,
            dst_ref=dst,
            send_sem=self.send.at[m, s[0], s[1]],
            recv_sem=self.recv.at[m, r[0], r[1]],
            device_id=other,
            device_id_type=MESH,
        )

    def y_copy(self, m, z):
        at = self.at
        return self.copy(m, self.unit(m, z, 1 - at.y), self.yf.at[m, z], (1, z), (1, z), at.across_y())

    def z_copy(self, m, z, slot, other):
        return self.copy(m, self.unit(m, z, self.at.y), self.zl.at[m, slot], (0, z), (0, slot), other)

    def x_copy(self, m):
        return self.copy(m, self.xs.at[m], self.xr.at[m], (2, 0), (2, 0), self.at.across_x())

    def begin(self, m, k):
        self.y_copy(m, self.at.order(k)).start()

    def line(self, m, k, out):
        at = self.at
        z = at.order(k)
        self.y_copy(m, z).wait_recv()
        ref = self.unit(m, z, at.y)
        if k > 0:

            @pl.when(at.w == 0)
            def _():
                ref[...] = ref[...] + self.yf[m, z]
                self.z_copy(m, z, z, at.inward()).start()

            @pl.when(at.w == 1)
            def _():
                self.z_copy(m, z, z, at.inward()).wait_recv()
                ref[...] = (
                    ref[...].astype(jnp.float32)
                    + self.yf[m, z].astype(jnp.float32)
                    + self.zl[m, z].astype(jnp.float32)
                ).astype(jnp.bfloat16)
                if k == 3:
                    self.z_copy(m, z, z, at.inward()).start()
                elif k == 2:
                    self.z_copy(m, z, 4, at.inward()).start()
                else:
                    self.z_copy(m, z, 4, at.outward()).start()

        else:
            self.z_copy(m, z, 4, at.inward()).wait_recv()

            def total(x, second):
                full, c0, n = self.full(m)
                size = self.shard
                own = full[pl.ds(pl.multiple_of(at.chip(z, at.y, x) * size, size), size), pl.ds(c0, n)]
                part = pl.ds(pl.multiple_of(x * size, size), size)
                v = (
                    own.astype(jnp.float32)
                    + self.yf[m, z, part, :].astype(jnp.float32)
                    + self.zl[m, 4, part, :].astype(jnp.float32)
                )
                if second:
                    v = v + self.zl[m, z, part, :].astype(jnp.float32)
                return v

            def put(second):
                self.xs[m] = total(1 - at.x, second).astype(jnp.bfloat16)
                self.x_copy(m).start()
                out(at.x, total(at.x, second))

            @pl.when(at.w == 0)
            def _():
                put(False)

            @pl.when(at.w == 1)
            def _():
                self.z_copy(m, z, z, at.inward()).wait_recv()
                put(True)

    def last(self, m, out):
        self.x_copy(m).wait_recv()
        out(1 - self.at.x, self.xr[m].astype(jnp.float32))

    def drain(self, m):
        at = self.at
        for k in range(4):
            z = at.order(k)
            self.y_copy(m, z).wait_send()
            if k > 0:
                self.z_copy(m, z, z, at.inward()).wait_send()
        self.x_copy(m).wait_send()


QKV, OUT, UP, DOWN, COLS = 0, 1536, 2048, 3072, 4096
GATHERED = ((0, 512), (512, 1024), (1024, 1536), (1536, 2048))
SCATTERED = ((0, 512), (512, 1024), (1024, 1536), (1536, 2048))
GATHER_PLAN = (
    ((0, 2, 0), (0, 1, 0), (0, 0, 0), (0, 3, 0), (0, 0, 1), (1, 0, 0), (0, 1, 1), (0, 1, 2), (1, 1, 0), (3, 0, 0, 0), (0, 2, 1), (0, 2, 2), (1, 1, 1), (0, 0, 2), (0, 1, 3), (3, 0, 0, 1), (0, 3, 1), (0, 2, 3), (1, 1, 2), (1, 0, 1), (3, 0, 0, 2), (0, 0, 3), (1, 2, 0), (3, 1, 0, 0), (1, 2, 1), (1, 2, 2),),
    ((1, 0, 2), (1, 1, 3), (3, 0, 0, 3), (1, 0, 3), (1, 2, 3), (0, 3, 2), (0, 3, 3), (1, 3, 0), (2, 0), (2, 1), (4, 1, 0, 0), (3, 1, 0, 1),),
    (),
    ((4, 0, 0, 0),),
    (),
    (),
    (),
    ((1, 3, 1), (1, 3, 2), (1, 3, 3), (4, 0, 0, 1), (5,),),
    ((3, 0, 1, 0),),
    (),
    (),
    (),
    ((3, 1, 0, 2), (3, 1, 1, 0), (4, 0, 1, 0),),
    (),
    ((4, 1, 1, 0), (3, 0, 1, 1), (4, 0, 0, 2), (4, 0, 1, 1),),
    (),
    (),
    (),
    ((4, 0, 0, 3),),
    ((3, 0, 1, 2),),
    (),
    (),
    ((4, 0, 1, 2), (3, 0, 1, 3), (4, 0, 1, 3), (3, 1, 1, 1), (3, 1, 1, 2), (4, 1, 1, 1), (4, 1, 1, 2), (4, 1, 0, 1), (3, 1, 1, 3),),
    (),
    ((3, 1, 0, 3), (4, 1, 0, 2),),
    (),
    (),
    ((4, 1, 1, 3),),
    (),
    (),
    (),
    (),
    (),
    ((4, 1, 0, 3),),
)
SCATTER_PLAN = (
    (),
    (),
    (),
    ((3, 1, 3),),
    (),
    (),
    (),
    ((3, 1, 2), (3, 1, 1),),
    ((4, 1, 3),),
    (),
    (),
    ((3, 1, 0), (4, 1, 2),),
    (),
    ((4, 1, 1),),
    ((3, 0, 3),),
    (),
    (),
    ((3, 0, 2),),
    (),
    (),
    (),
    (),
    (),
    ((3, 0, 1), (0, 3, 3),),
    (),
    (),
    ((4, 1, 0),),
    ((0, 3, 2),),
    ((3, 0, 0), (0, 3, 1), (0, 3, 0),),
    (),
    ((1, 3, 3),),
    (),
    ((1, 3, 2),),
    (),
    (),
    (),
    (),
    ((0, 2, 3), (0, 1, 3), (4, 0, 3), (0, 2, 2), (1, 3, 1),),
    (),
    ((0, 0, 3), (0, 2, 1), (1, 1, 3),),
    ((0, 2, 0), (1, 0, 3), (1, 3, 0), (2, 3, 3), (0, 1, 2), (0, 0, 2), (1, 2, 3), (4, 0, 2), (0, 0, 1), (1, 2, 2), (4, 0, 1),),
    ((0, 1, 1),),
    ((1, 0, 2),),
    (),
    (),
    ((1, 0, 1), (2, 2, 3), (1, 1, 2), (1, 1, 1), (0, 0, 0), (2, 3, 2), (0, 1, 0),),
    ((2, 0, 3),),
    ((1, 2, 1), (2, 1, 3),),
    (),
    ((4, 0, 0), (2, 3, 1), (1, 1, 0), (2, 1, 2),),
    (),
    ((1, 2, 0), (2, 2, 2), (2, 1, 1), (2, 2, 1), (5, 1), (1, 0, 0),),
    (),
    ((5, 0), (2, 0, 2), (2, 0, 1), (2, 3, 0), (2, 2, 0), (2, 1, 0),),
    ((2, 0, 0),),
)
BF, F32 = jnp.bfloat16, jnp.float32
SUMS = ("bq", "bv", "bout", "bdown", "g1", "s1", "g2", "s2", "x", "mid", "res", "branch", "feed")
BLOCK = 32


def nn(a, b):
    return lax.dot_general(a, b, (((1,), (0,)), ((), ())), preferred_element_type=F32)


def nt(a, b):
    return lax.dot_general(a, b, (((1,), (1,)), ((), ())), preferred_element_type=F32)


def at_rows(start, size):
    return pl.ds(pl.multiple_of(start, size), size)


def fold(v):
    return jnp.sum(v.reshape(v.shape[0] // 8, 8, v.shape[1]), axis=0)


def normed(v):
    centre = jnp.mean(v, axis=1, keepdims=True)
    offset = v - centre
    r = lax.rsqrt(jnp.mean(offset * offset, axis=1, keepdims=True) + eps_norm)
    return offset * r, r


def norm_back(dy, n, r, gain):
    dn = dy * gain
    first = jnp.mean(dn, axis=1, keepdims=True)
    second = jnp.mean(dn * n, axis=1, keepdims=True)
    return r * (dn - first - n * second)


def block_kernel(
    counts, x_ref, cot_ref, wqkv, wout, wup, wdown, bqv, bout, bup, bdown, g1, s1, g2, s2,
    act_out, gin_out, o_qkv, o_out, o_up, o_down, o_sums,
    W, G2, G3, xh, yh, xf, yf, zl, yf2, zl2, xs2, xr2,
    rows1, dfeed, qkv, probs, heads, mid, rows2, act, gp, datt,
    tall, own_a, own_c, send_t, send_x, got, got_t, acc, acc_up, sums, sums_got,
    sem_in, ag_send, ag_recv, pg_send, pg_recv, rs_send, rs_recv, ps_send, ps_recv,
    pair_send, pair_recv, sums_send, sums_recv,
):
    at = Place()
    t, x = at.t, at.x
    shard = wup.shape[0]
    own = x_ref.shape[0]
    width = x_ref.shape[1]
    dbr = dfeed.at[0 : 2 * own, :]
    dproj = qkv

    def spot(far_x, far_t):
        return at_rows((far_x * 2 + far_t) * own, own)

    mine, theirs = at_rows(t * own, own), at_rows((1 - t) * own, own)

    here = at_rows(at.dp * shard, shard)
    quarter = pl.ds(pl.multiple_of(x * 1024, 1024), 1024)
    loads = [
        pltpu.make_async_copy(src, W.at[here, pl.ds(c0, n)], sem_in.at[i])
        for i, (src, c0, n) in enumerate(
            [(wqkv.at[j], QKV + 512 * j, 512) for j in range(3)]
            + [(wout, OUT, 512), (wup.at[:, quarter], UP, 1024), (wdown.at[:, quarter], DOWN, 1024)]
        )
    ]
    for c in loads:
        c.start()
    enter(at)
    g = Gather(at, W, shard, GATHERED, ag_send, ag_recv)
    pg = PairGather(at, W, shard, ((UP, 1024), (DOWN, 1024)), (wup, wdown), pg_send, pg_recv)
    for c in loads:
        c.wait()

    def gather_step(kind, *a):
        if kind == 0:
            g.line(*a)
        elif kind == 1:
            g.plane(*a)
        elif kind == 2:
            pg.x_copy(*a).start()
        elif kind == 3:
            pg.line(*a)
        elif kind == 4:
            pg.cross(*a)
        else:
            shares.append(share(2, dfeed, spot(x, t), at.across_x()))

    plan = list(GATHER_PLAN)

    def gather(last):
        while plan and len(GATHER_PLAN) - len(plan) <= last:
            for step in plan.pop(0):
                gather_step(*step)

    home = {0: (G3, 0, 512), 1: (W, DOWN, DOWN + 512), 2: (W, DOWN + 512, COLS), 3: (G3, 512, 1024)}
    sc = Scatter(at, lambda p: home[p], shard, SCATTERED, xh, yh, xf, yf, zl, rs_send, rs_recv)
    home_pair = {0: (W, UP, 1024), 1: (G2, 0, 1024)}
    ps = PairScatter(at, lambda m: home_pair[m], shard, yf2, zl2, xs2, xr2, ps_send, ps_recv)

    def write(p):
        def store(total):
            if p < 3:
                o_qkv[p] = total
            else:
                o_out[...] = total
        return store

    def write_pair(m):
        ref = o_up if m == 0 else o_down

        def store(far_x, total):
            ref[:, pl.ds(pl.multiple_of(far_x * 1024, 1024), 1024)] = total
        return store

    def scatter_step(kind, p, k=None):
        if kind == 0:
            sc.begin(p, k)
        elif kind == 1:
            sc.plane(p, k)
        elif kind == 2:
            sc.line(p, k, write(p))
        elif kind == 3:
            ps.begin(p, k)
        elif kind == 4:
            ps.line(p, k, write_pair(p))
        else:
            ps.last(p, write_pair(p))

    back_plan = list(SCATTER_PLAN)

    def scatter(last):
        while back_plan and len(SCATTER_PLAN) - len(back_plan) <= last:
            for step in back_plan.pop(0):
                scatter_step(*step)

    def send(i, src, dst, other):
        return pltpu.make_async_remote_copy(
            src_ref=src, dst_ref=dst, send_sem=pair_send.at[i], recv_sem=pair_recv.at[i],
            device_id=other, device_id_type=MESH,
        )

    def share(i, ref, r, other):
        c = send(i, ref.at[r, :], ref.at[r, :], other)
        c.start()
        return c

    def take(i, ref, r):
        send(i, ref.at[r, :], ref.at[r, :], at.twin()).wait_recv()

    for ref in (acc, acc_up):
        ref[...] = jnp.zeros_like(ref)
    total_of = {name: acc.at[i] for i, name in enumerate(SUMS)}

    def add(name, v):
        ref = total_of[name]
        ref[...] += fold(v)

    def valid_of(image, start, size):
        slot = lax.broadcasted_iota(jnp.int32, (size, 1), 0) + start
        return slot < counts[image] + BUFFER

    def each_block(body):
        def go(b, _):
            body(b * BLOCK, pl.ds(pl.multiple_of(b * BLOCK, BLOCK), BLOCK))
            return 0
        lax.fori_loop(0, own // BLOCK, go, 0)

    def tiles(first, last, body, size=256):
        def go(i, _):
            body(pl.multiple_of(i * size, size))
            return 0
        lax.fori_loop(first // size, last // size, go, 0)

    def flip(src):
        def body(c):
            tall[pl.ds(c, 128), 0 : src.shape[0]] = src[:, pl.ds(c, 128)].T
        tiles(0, src.shape[1], body, 128)

    def first_norm(b, r):
        xv = x_ref[r, :].astype(F32)
        keep = valid_of(t, b, BLOCK).astype(F32)
        n, _ = normed(xv)
        mine_b = pl.ds(pl.multiple_of(t * own + b, BLOCK), BLOCK)
        rows1[mine_b, :] = (n * g1[...] + s1[...]).astype(BF)
        add("x", keep * xv * xv)
        low = (cot_ref[r, :].astype(F32) * keep).astype(BF)
        dfeed[pl.ds(pl.multiple_of((x * 2 + t) * own + b, BLOCK), BLOCK), :] = low
        add("bdown", low.astype(F32))

    gather(0)
    each_block(first_norm)
    shares = [share(0, rows1, mine, at.twin()), share(1, dfeed, spot(x, t), at.twin())]
    for p in range(3):
        gather(1 + p)
        g.finish(p)
    take(0, rows1, theirs)
    gather(5)

    def project(c):
        v = nn(rows1[...], W[:, pl.ds(c, 256)])
        part = c // 512
        inside = pl.ds(pl.multiple_of(c % 512 + t * 512, 256), 256)
        bias = jnp.where(part == 0, bqv[0:1, inside], jnp.where(part == 2, bqv[1:2, inside], 0.0))
        scale = jnp.where(part == 0, HD**-0.5, 1.0)
        qkv[:, pl.ds(c, 256)] = ((v + bias) * scale).astype(BF)

    tiles(0, 1536, project)

    first_lanes = lax.broadcasted_iota(jnp.int32, (own, 128), 1) < HD

    def attend(it):
        image, j = it // 4, it % 4
        r = pl.ds(pl.multiple_of(image * own, own), own)
        c = j * 128
        q2 = qkv[r, pl.ds(pl.multiple_of(c, 128), 128)]
        k2 = qkv[r, pl.ds(pl.multiple_of(c + 512, 128), 128)]
        v_t = qkv[r, pl.ds(pl.multiple_of(c + 1024, 128), 128)].T
        hide = jnp.where(valid_of(image, 0, own), 0.0, -1e30)
        outs = []
        for a in range(2):
            qm = jnp.where(first_lanes if a == 0 else ~first_lanes, q2, jnp.zeros_like(q2))
            s = nt(k2, qm) + hide
            e = jnp.exp(s - jnp.max(s, axis=0, keepdims=True))
            low = (e * (1.0 / jnp.sum(e, axis=0, keepdims=True))).astype(BF)
            probs[it * 2 + a] = low
            outs.append(nn(v_t[a * HD : (a + 1) * HD], low))
        heads[r, pl.ds(pl.multiple_of(c, 128), 128)] = jnp.concatenate(outs, axis=0).T.astype(BF)

    def attend_some(first, last, body):
        def go(i, _):
            body(i)
            return 0
        lax.fori_loop(first, last, go, 0)

    first = 0
    for i in range(1, 9):
        if i == 8 or GATHER_PLAN[6 + i]:
            gather(6 + first)
            attend_some(first, i, attend)
            first = i
    gather(14)
    g.finish(3)
    gather(17)

    def reduced(i, src, cols, keep):
        def other(c):
            send_t[0, :, pl.ds(c, 256)] = nt(src[theirs, :], W[pl.ds(c, 256), cols]).astype(BF)
        tiles(0, width, other)
        copy = send(i, send_t.at[0], got.at[0 if i == 3 else 1], at.twin())
        copy.start()
        def self(c):
            keep[:, pl.ds(c, 256)] = nt(src[mine, :], W[pl.ds(c, 256), cols])
        tiles(0, width, self)
        return copy

    branch_copy = reduced(3, heads, pl.ds(OUT, 512), own_a)
    gather(18)
    branch_copy.wait()

    def second_norm(b, r):
        keep = valid_of(t, b, BLOCK).astype(F32)
        branch = own_a[r, :] + got[0, r, :].astype(F32) + bout[...]
        m = x_ref[r, :].astype(F32) + branch
        mid[r, :] = m
        add("branch", keep * branch * branch)
        add("mid", keep * m * m)
        n, _ = normed(m)
        rows2[pl.ds(pl.multiple_of((x * 2 + t) * own + b, BLOCK), BLOCK), :] = (n * g2[...] + s2[...]).astype(BF)

    gather(19)
    each_block(second_norm)
    shares.append(share(4, rows2, spot(x, t), at.across_x()))
    shares.append(share(5, rows2, spot(x, t), at.twin()))
    gather(22)

    take(2, dfeed, spot(1 - x, t))
    shares.append(share(6, dfeed, spot(1 - x, t), at.twin()))
    take(1, dfeed, spot(x, 1 - t))
    take(6, dfeed, spot(1 - x, 1 - t))
    gather(23)
    flip(dfeed)
    take(5, rows2, spot(x, 1 - t))

    chip_rows = lambda far_x: at_rows(far_x * 2 * own, 2 * own)

    def hidden(far_x):
        r = chip_rows(far_x)

        def body(c):
            lanes = pl.ds(pl.multiple_of(t * 2048 + x * 1024 + c, 256), 256)
            u = nn(rows2[r, :], W[:, pl.ds(UP + c, 256)]) + bup[:, lanes]
            below = 0.5 * (1.0 + lax.erf(u * (0.5**0.5)))
            dense = jnp.exp(-0.5 * u * u) * 0.3989422804014327
            act[r, pl.ds(c, 256)] = (u * below).astype(BF)
            gp[r, pl.ds(c, 256)] = (below + u * dense).astype(BF)
        tiles(0, 1024, body)

    def grad_down(c):
        G2[:, pl.ds(c, 256)] = nn(tall[...], act[:, pl.ds(c, 256)]).astype(BF)

    gather(24)
    pg.finish(0)
    gather(26)
    hidden(x)
    gather(28)
    take(4, rows2, spot(1 - x, t))
    shares.append(share(7, rows2, spot(1 - x, t), at.twin()))
    take(7, rows2, spot(1 - x, 1 - t))
    gather(31)
    hidden(1 - x)
    gather(33)
    tiles(0, 1024, grad_down)
    gather(100)
    scatter(1)
    flip(rows2)

    def back_act(far_x):
        r = chip_rows(far_x)

        def body(c):
            d = nn(dfeed[r, :], W[:, pl.ds(DOWN + c, 256)])
            low = (d * gp[r, pl.ds(c, 256)].astype(F32)).astype(BF)
            gp[r, pl.ds(c, 256)] = low
            acc_up[t * 2 + x, :, pl.ds(c, 256)] += fold(low.astype(F32))
        tiles(0, 1024, body)

    def product(src, r, cols, put):
        def body(c):
            put(pl.ds(c, 256), nt(src[r, :], W[pl.ds(c, 256), cols]))
        tiles(0, width, body)

    class Sum4:
        def __init__(self, i, n, src, cols, keep, parts):
            self.i, self.n, self.src, self.cols, self.keep, self.parts = i, n, src, cols, keep, parts

        def away(self, far_x, slot):
            def put(c, v):
                send_t[slot, :, c] = v.astype(BF)
            product(self.src, spot(far_x, 1 - t), self.cols, put)
            copy = send(self.i + slot, send_t.at[slot], got_t.at[self.n, slot], at.twin())
            copy.start()
            return copy

        def far(self):
            first = self.away(1 - x, 0)

            def put(c, v):
                send_x[self.n, :, c] = v.astype(BF)
            product(self.src, spot(1 - x, t), self.cols, put)
            scatter(self.parts[0])
            first.wait()

            def body(b, r):
                send_x[self.n, r, :] = send_x[self.n, r, :] + got_t[self.n, 0, r, :]
            each_block(body)
            self.cross = send(self.i + 2, send_x.at[self.n], got.at[2 + self.n], at.across_x())
            scatter(self.parts[1])
            self.cross.start()

        def near(self):
            second = self.away(x, 1)

            def put(c, v):
                self.keep[:, c] = v
            product(self.src, spot(x, t), self.cols, put)
            second.wait()

        def value(self, r):
            return self.keep[r, :] + got_t[self.n, 1, r, :].astype(F32) + got[2 + self.n, r, :].astype(F32)

    pg.finish(1)
    scatter(2)
    back_act(1 - x)
    scatter(3)
    two = Sum4(8, 0, gp, pl.ds(UP, 1024), own_a, (4, 5))
    two.far()
    scatter(6)
    back_act(x)
    scatter(7)
    two.near()
    for p in range(4):
        g.drain(p)
    for m in range(2):
        pg.drain(m)
    scatter(8)

    def grad_up(c):
        W[:, pl.ds(UP + c, 256)] = nn(tall[...], gp[:, pl.ds(c, 256)]).astype(BF)

    tiles(0, 512, grad_up)
    scatter(9)
    tiles(512, 1024, grad_up)
    scatter(11)
    four = Sum4(11, 1, act, pl.ds(DOWN, 1024), own_c, (11, 12))
    four.far()
    scatter(13)
    four.near()
    scatter(14)
    two.cross.wait()
    for i in (1, 2, 5):
        shares[i].wait_send()

    def second_back(b, r):
        dy = two.value(r)
        n, scale = normed(mid[r, :])
        keep = valid_of(t, b, BLOCK).astype(F32)
        add("g2", dy * n)
        add("s2", dy)
        d = cot_ref[r, :].astype(F32) * keep + norm_back(dy, n, scale, g2[...])
        gin_out[r, :] = d
        low = d.astype(BF)
        dbr[pl.ds(pl.multiple_of(t * own + b, BLOCK), BLOCK), :] = low
        add("bout", low.astype(F32))

    scatter(16)
    each_block(second_back)
    shares.append(share(14, dbr, mine, at.twin()))
    scatter(17)
    take(14, dbr, theirs)
    scatter(18)

    def back_heads(c):
        datt[:, pl.ds(c, 256)] = nn(dbr[...], W[:, pl.ds(OUT + c, 256)]).astype(BF)

    tiles(0, 512, back_heads)
    scatter(19)
    flip(dbr)
    scatter(20)
    short = pl.ds(0, 2 * own)

    def grad_out(c):
        G3[:, pl.ds(512 + c, 256)] = nn(tall[:, short], heads[:, pl.ds(c, 256)]).astype(BF)

    tiles(0, 512, grad_out)

    def attend_back(it):
        image, j = it // 4, it % 4
        r = pl.ds(pl.multiple_of(image * own, own), own)
        c = j * 128
        q2 = qkv[r, pl.ds(pl.multiple_of(c, 128), 128)]
        k_t = qkv[r, pl.ds(pl.multiple_of(c + 512, 128), 128)].T
        v2 = qkv[r, pl.ds(pl.multiple_of(c + 1024, 128), 128)]
        da = datt[r, pl.ds(pl.multiple_of(c, 128), 128)]
        dq, dk, dv = [], [], []
        for a in range(2):
            dam = jnp.where(first_lanes if a == 0 else ~first_lanes, da, jnp.zeros_like(da))
            low = probs[it * 2 + a]
            p = low.astype(F32)
            dp = nt(v2, dam)
            ds = (p * (dp - jnp.sum(p * dp, axis=0, keepdims=True))).astype(BF)
            dq.append(nn(k_t[a * HD : (a + 1) * HD], ds))
            dk.append(nn(ds, q2))
            dv.append(nn(low, da))
        for base, v in (
            (0, jnp.concatenate(dq, axis=0).T * HD**-0.5),
            (512, jnp.where(first_lanes, dk[0], dk[1])),
            (1024, jnp.where(first_lanes, dv[0], dv[1])),
        ):
            v = v.astype(BF)
            dproj[r, pl.ds(pl.multiple_of(base + c, 128), 128)] = v
            if base != 512:
                lanes = pl.ds(pl.multiple_of(t * 512 + c, 128), 128)
                ref = total_of["bq" if base == 0 else "bv"]
                ref[:, lanes] += fold(v.astype(F32))

    first = 0
    for i in range(1, 9):
        if i == 8 or SCATTER_PLAN[22 + i]:
            scatter(22 + first)
            attend_some(first, i, attend_back)
            first = i

    scatter(30)
    one_copy = reduced(15, dproj, pl.ds(QKV, 1536), own_a)
    scatter(32)
    flip(rows1)

    def grad_kv(c):
        W[:, pl.ds(DOWN + c, 256)] = nn(tall[:, short], dproj[:, pl.ds(512 + c, 256)]).astype(BF)

    def grad_q(c):
        G3[:, pl.ds(c, 256)] = nn(tall[:, short], dproj[:, pl.ds(c, 256)]).astype(BF)

    scatter(33)
    tiles(0, 512, grad_kv)
    scatter(35)
    tiles(512, 1024, grad_kv)
    scatter(37)
    tiles(0, 512, grad_q)
    scatter(39)
    one_copy.wait()

    def first_back(b, r):
        dy = own_a[r, :] + got[1, r, :].astype(F32)
        n, scale = normed(x_ref[r, :].astype(F32))
        add("g1", dy * n)
        add("s1", dy)
        gin_out[r, :] += norm_back(dy, n, scale, g1[...])

    scatter(40)
    each_block(first_back)
    scatter(41)
    four.cross.wait()

    def finish_feed(b, r):
        keep = valid_of(t, b, BLOCK).astype(F32)
        feed = four.value(r) + bdown[...]
        res = mid[r, :] + feed
        add("feed", keep * feed * feed)
        add("res", keep * res * res)
        act_out[r, :] = (keep * res).astype(BF)

    scatter(42)
    each_block(finish_feed)
    scatter(43)

    for i in range(8):
        sums[i : i + 1, :] = jnp.sum(acc[i], axis=0, keepdims=True)
    for i in range(4):
        sums[8 + i : 9 + i, :] = jnp.sum(acc_up[i], axis=0, keepdims=True)
    lane = lax.broadcasted_iota(jnp.int32, (1, width), 1)
    row = jnp.where(lane == 5, (counts[t] + BUFFER).astype(F32), 0.0)
    for i, name in enumerate(("x", "mid", "res", "branch", "feed")):
        row = jnp.where(lane == i, jnp.sum(jnp.sum(total_of[name][...], axis=0, keepdims=True), axis=1, keepdims=True), row)
    sums[12:13, :] = row
    sums[13:16, :] = jnp.zeros((3, width), F32)
    for i, other in enumerate((at.twin(), at.across_x(), at.across_y(), at.near(), at.far())):
        c = pltpu.make_async_remote_copy(
            src_ref=sums, dst_ref=sums_got.at[i], send_sem=sums_send.at[i], recv_sem=sums_recv.at[i],
            device_id=other, device_id_type=MESH,
        )
        c.start()
        scatter(45 + 2 * i)
        c.wait()
        sums[...] += sums_got[i]
    o_sums[...] = sums[...]
    scatter(1000)
    for m in (1, 0):
        ps.drain(m)
    for p in range(4):
        sc.drain(p)
    for i in (0, 3, 4, 6, 7):
        shares[i].wait_send()


def block(counts, stream, cotangent, w_qkv, w_out_t, w_up, w_down_t, b_qv, b_out, b_up, b_down, g1, s1, g2, s2):
    own, width = stream.shape
    shard = w_up.shape[0]
    rows = 16 * shard
    group = 2 * own
    vmem = pl.BlockSpec(memory_space=pltpu.VMEM)
    hbm = pl.BlockSpec(memory_space=pl.ANY)
    dma = pltpu.SemaphoreType.DMA
    row = lambda v: v.reshape(1, -1)
    return pl.pallas_call(
        block_kernel,
        out_shape=(
            jax.ShapeDtypeStruct((own, width), BF),
            jax.ShapeDtypeStruct((own, width), F32),
            jax.ShapeDtypeStruct((3, shard, 512), F32),
            jax.ShapeDtypeStruct((shard, 512), F32),
            jax.ShapeDtypeStruct((shard, 2048), F32),
            jax.ShapeDtypeStruct((shard, 2048), F32),
            jax.ShapeDtypeStruct((16, width), F32),
        ),
        in_specs=[pl.BlockSpec(memory_space=pltpu.SMEM), vmem, vmem, hbm, hbm, hbm, hbm] + [vmem] * 8,
        out_specs=(vmem,) * 7,
        scratch_shapes=[
            pltpu.VMEM((rows, COLS), BF),
            pltpu.VMEM((rows, 1024), BF),
            pltpu.VMEM((rows, 1024), BF),
            pltpu.VMEM((4, shard // 2, 2048), BF),
            pltpu.VMEM((4, shard // 2, 2048), BF),
            pltpu.VMEM((4, shard, 2048), BF),
            pltpu.VMEM((4, shard, 2048), BF),
            pltpu.VMEM((5, shard, 2048), BF),
            pltpu.VMEM((2, 4, 2 * shard, 1024), BF),
            pltpu.VMEM((2, 5, 2 * shard, 1024), BF),
            pltpu.VMEM((2, shard, 1024), BF),
            pltpu.VMEM((2, shard, 1024), BF),
            pltpu.VMEM((group, width), BF),
            pltpu.VMEM((2 * group, width), BF),
            pltpu.VMEM((group, 1536), BF),
            pltpu.VMEM((16, own, own), BF),
            pltpu.VMEM((group, 512), BF),
            pltpu.VMEM((own, width), F32),
            pltpu.VMEM((2 * group, width), BF),
            pltpu.VMEM((2 * group, 1024), BF),
            pltpu.VMEM((2 * group, 1024), BF),
            pltpu.VMEM((group, 512), BF),
            pltpu.VMEM((width, 2 * group), BF),
            pltpu.VMEM((own, width), F32),
            pltpu.VMEM((own, width), F32),
            pltpu.VMEM((2, own, width), BF),
            pltpu.VMEM((2, own, width), BF),
            pltpu.VMEM((4, own, width), BF),
            pltpu.VMEM((2, 2, own, width), BF),
            pltpu.VMEM((len(SUMS), 8, width), F32),
            pltpu.VMEM((4, 8, 1024), F32),
            pltpu.VMEM((16, width), F32),
            pltpu.VMEM((5, 16, width), F32),
            dma((6,)),
            dma((4, 6, 4)),
            dma((4, 5, 4)),
            dma((4, 4, 4)),
            dma((4, 3, 4)),
            dma((4, 5, 4)),
            dma((4, 5, 5)),
            dma((2, 3, 4)),
            dma((2, 3, 5)),
            dma((16,)),
            dma((16,)),
            dma((5,)),
            dma((5,)),
        ],
        compiler_params=pltpu.CompilerParams(
            collective_id=1, has_side_effects=True, vmem_limit_bytes=63 << 20
        ),
    )(
        counts, stream, cotangent, w_qkv, w_out_t, w_up, w_down_t,
        b_qv, row(b_out), row(b_up), row(b_down), row(g1), row(s1), row(g2), row(s2),
    )


def local_fast(
    stream, counts, cotangent, w_qkv, b_qv, w_out, b_out, w_fc1, b_fc1, w_fc2, b_fc2,
    gain_one, shift_one, gain_two, shift_two,
):
    acts, grad_in, p_qkv, p_out, p_up, p_down, sums = block(
        counts, stream, cotangent, w_qkv, w_out.T, w_fc1, w_fc2.T, b_qv, b_out, b_fc1, b_fc2,
        gain_one, shift_one, gain_two, shift_two,
    )
    place = lax.axis_index("dp") * 2 + lax.axis_index("tensor")
    vectors = lax.dynamic_slice(sums[:8], (0, place * 32), (8, 32))
    up = lax.dynamic_slice(sums[8:12].reshape(-1), (place * 128,), (128,))
    rms = jnp.sqrt(sums[12, :5] / (sums[12, 5] * stream.shape[1]))
    return (
        acts, grad_in, p_qkv, vectors[0:2], p_out.T, vectors[2], p_up, up, p_down.T, vectors[3],
        vectors[4], vectors[5], vectors[6], vectors[7], rms,
    )


def layer_norm(values, gain, shift):
    centre = jnp.mean(values, axis=-1, keepdims=True)
    offset = values - centre
    spread = jnp.mean(offset * offset, axis=-1, keepdims=True)
    return offset * lax.rsqrt(spread + eps_norm) * gain + shift


def gelu_exact(values):
    return jax.nn.gelu(values, approximate=False)


def masked_scores(queries, key_rows, validity):
    scores = jnp.einsum(
        "bqhd,bkhd->bhqk", queries, key_rows, preferred_element_type=jnp.float32
    ) * HD ** (-0.5)
    return jnp.where(validity[:, None, None, :] > 0, scores, -1e30)


def attend_block(members):
    queries, key_rows, values, validity = members
    scores = masked_scores(queries, key_rows, validity)
    highest = jnp.max(scores, axis=-1, keepdims=True)
    expo_terms = jnp.exp(scores - highest)
    totals = jnp.sum(expo_terms, axis=-1, keepdims=True)
    weights = (expo_terms / totals).astype(jnp.bfloat16)
    mixture = jnp.einsum("bhqk,bkhd->bqhd", weights, values, preferred_element_type=jnp.float32)
    return (mixture.astype(jnp.bfloat16), (highest + jnp.log(totals))[..., 0])


def attend_back(members):
    queries, key_rows, values, validity, log_total, d_mixture = members
    scores = masked_scores(queries, key_rows, validity)
    probs = jnp.exp(scores - log_total[..., None])
    d_values = jnp.einsum(
        "bhqk,bqhd->bkhd", probs.astype(jnp.bfloat16), d_mixture, preferred_element_type=jnp.float32
    )
    d_probs = jnp.einsum("bqhd,bkhd->bhqk", d_mixture, values, preferred_element_type=jnp.float32)
    d_scores = (probs * (d_probs - jnp.sum(probs * d_probs, axis=-1, keepdims=True))).astype(
        jnp.bfloat16
    )
    d_queries = jnp.einsum(
        "bhqk,bkhd->bqhd", d_scores, key_rows, preferred_element_type=jnp.float32
    ) * HD ** (-0.5)
    d_keys = jnp.einsum(
        "bhqk,bqhd->bkhd", d_scores, queries, preferred_element_type=jnp.float32
    ) * HD ** (-0.5)
    return (
        d_queries.astype(jnp.bfloat16),
        d_keys.astype(jnp.bfloat16),
        d_values.astype(jnp.bfloat16),
    )


def local(
    stream,
    counts,
    cotangent,
    w_qkv,
    b_qv,
    w_out,
    b_out,
    w_fc1,
    b_fc1,
    w_fc2,
    b_fc2,
    gain_one,
    shift_one,
    gain_two,
    shift_two,
):
    tensor_pos = lax.axis_index("tensor")
    own_rows = stream.shape[0]
    width = stream.shape[1]
    own_images = own_rows // SLOTS
    slot_index = jnp.arange(SLOTS, dtype=jnp.int32)
    validity_all = (slot_index[None, :] < (BUFFER + counts)[:, None]).astype(jnp.float32)
    own_validity = lax.dynamic_slice_in_dim(validity_all, tensor_pos * own_images, own_images, 0)
    own_valid = own_validity.reshape(own_rows, 1)
    qkv_full, out_full, up_full, down_full = (
        lax.all_gather(w_qkv, "dp", axis=1, tiled=True),
        lax.all_gather(w_out, "dp", axis=1, tiled=True),
        lax.all_gather(w_fc1[None], "dp", axis=1, tiled=True),
        lax.all_gather(w_fc2, "dp", axis=1, tiled=True),
    )
    head_width = w_qkv.shape[2]
    unit_width = w_fc1.shape[1]
    bias_query = lax.dynamic_slice_in_dim(b_qv[0], tensor_pos * head_width, head_width, 0)
    bias_value = lax.dynamic_slice_in_dim(b_qv[1], tensor_pos * head_width, head_width, 0)
    bias_up = lax.dynamic_slice_in_dim(b_fc1, tensor_pos * unit_width, unit_width, 0)
    up_full = up_full[0]
    group_images = validity_all.shape[0]
    group_rows = group_images * SLOTS
    local_heads = head_width // HD
    pairing = 2
    block_count = group_images // pairing
    blocked_valid = validity_all.reshape(block_count, pairing, SLOTS)
    stream_f = stream.astype(jnp.float32)
    normed_one = layer_norm(stream_f, gain_one, shift_one).astype(jnp.bfloat16)
    first_rows = lax.all_gather(normed_one, "tensor", axis=0, tiled=True)
    projected = jnp.einsum("rd,cde->rce", first_rows, qkv_full, preferred_element_type=jnp.float32)
    shape_heads = (block_count, pairing, SLOTS, local_heads, HD)
    queries = (projected[:, 0] + bias_query).astype(jnp.bfloat16).reshape(shape_heads)
    key_rows = projected[:, 1].astype(jnp.bfloat16).reshape(shape_heads)
    values = (projected[:, 2] + bias_value).astype(jnp.bfloat16).reshape(shape_heads)
    mixture, log_total = lax.map(attend_block, (queries, key_rows, values, blocked_valid))
    attn_heads = mixture.reshape(group_rows, head_width)
    taken = attn_heads
    attn_total = lax.psum_scatter(
        jnp.dot(taken, out_full, preferred_element_type=jnp.float32).astype(jnp.bfloat16),
        "tensor",
        scatter_dimension=0,
        tiled=True,
    ).astype(jnp.float32)
    branch = attn_total + b_out
    middle = stream_f + branch
    normed_two = layer_norm(middle, gain_two, shift_two).astype(jnp.bfloat16)
    second_rows = lax.all_gather(normed_two, "tensor", axis=0, tiled=True)
    hidden_pre = jnp.dot(second_rows, up_full, preferred_element_type=jnp.float32) + bias_up
    hidden_act = gelu_exact(hidden_pre).astype(jnp.bfloat16)
    taken = hidden_act
    mlp_total = lax.psum_scatter(
        jnp.dot(taken, down_full, preferred_element_type=jnp.float32).astype(jnp.bfloat16),
        "tensor",
        scatter_dimension=0,
        tiled=True,
    ).astype(jnp.float32)
    feed = mlp_total + b_fc2
    result = middle + feed
    activations = (result * own_valid).astype(jnp.bfloat16)
    squares = jnp.stack(
        [
            jnp.sum(own_valid * member * member)
            for member in (stream_f, middle, result, branch, feed)
        ]
    )
    square_sums, valid_count = lax.psum((squares, jnp.sum(own_valid)), ("dp", "tensor"))
    rms_stats = jnp.sqrt(square_sums / (valid_count * width))
    d_result = cotangent.astype(jnp.float32) * own_valid
    d_feed_low = d_result.astype(jnp.bfloat16)
    d_feed_rows = lax.all_gather(d_feed_low, "tensor", axis=0, tiled=True)
    d_act = jnp.einsum("rd,ud->ru", d_feed_rows, down_full, preferred_element_type=jnp.float32)
    unused_act, gelu_pullback = jax.vjp(gelu_exact, hidden_pre)
    d_pre = gelu_pullback(d_act)[0].astype(jnp.bfloat16)
    grad_down = jnp.einsum("ru,rd->ud", hidden_act, d_feed_rows, preferred_element_type=jnp.float32)
    grad_up = jnp.einsum("rd,ru->du", second_rows, d_pre, preferred_element_type=jnp.float32)
    grad_bias_up = jnp.sum(d_pre, axis=0, dtype=jnp.float32)
    grad_bias_down = jnp.sum(d_feed_low, axis=0, dtype=jnp.float32)
    taken = d_pre
    d_normed_two = lax.psum_scatter(
        jnp.einsum("ru,du->rd", taken, up_full, preferred_element_type=jnp.float32).astype(
            jnp.bfloat16
        ),
        "tensor",
        scatter_dimension=0,
        tiled=True,
    ).astype(jnp.float32)
    unused_two, norm_two_pullback = jax.vjp(layer_norm, middle, gain_two, shift_two)
    d_middle_norm, grad_gain_two, grad_shift_two = norm_two_pullback(d_normed_two)
    d_middle = d_result + d_middle_norm
    d_branch_low = d_middle.astype(jnp.bfloat16)
    grad_bias_out = jnp.sum(d_branch_low, axis=0, dtype=jnp.float32)
    d_branch_rows = lax.all_gather(d_branch_low, "tensor", axis=0, tiled=True)
    d_attn = jnp.einsum(
        "rd,hd->rh", d_branch_rows, out_full, preferred_element_type=jnp.float32
    ).astype(jnp.bfloat16)
    grad_out = jnp.einsum(
        "rh,rd->hd", attn_heads, d_branch_rows, preferred_element_type=jnp.float32
    )
    d_queries, d_keys, d_values = lax.map(
        attend_back,
        (queries, key_rows, values, blocked_valid, log_total, d_attn.reshape(shape_heads)),
    )
    d_projected = jnp.stack(
        [
            d_queries.reshape(group_rows, head_width),
            d_keys.reshape(group_rows, head_width),
            d_values.reshape(group_rows, head_width),
        ],
        axis=1,
    )
    grad_qkv = jnp.einsum(
        "rd,rce->cde", first_rows, d_projected, preferred_element_type=jnp.float32
    )
    bias_terms = jnp.sum(d_projected, axis=0, dtype=jnp.float32)
    taken = d_projected
    d_normed_one = lax.psum_scatter(
        jnp.einsum("rce,cde->rd", taken, qkv_full, preferred_element_type=jnp.float32).astype(
            jnp.bfloat16
        ),
        "tensor",
        scatter_dimension=0,
        tiled=True,
    ).astype(jnp.float32)
    unused_one, norm_one_pullback = jax.vjp(layer_norm, stream_f, gain_one, shift_one)
    d_stream_norm, grad_gain_one, grad_shift_one = norm_one_pullback(d_normed_one)
    grad_input = d_middle + d_stream_norm
    grad_up = grad_up[None]
    bias_qv_full = lax.dynamic_update_slice(
        jnp.zeros((2, width), jnp.float32),
        jnp.stack([bias_terms[0], bias_terms[2]]),
        (jnp.int32(0), tensor_pos * head_width),
    )
    bias_up_full = lax.dynamic_update_slice(
        jnp.zeros((b_fc1.shape[0],), jnp.float32), grad_bias_up, (tensor_pos * unit_width,)
    )
    qkv_part, out_part, up_part, down_part = (
        lax.psum_scatter(
            grad_qkv.astype(jnp.bfloat16), "dp", scatter_dimension=1, tiled=True
        ).astype(jnp.float32),
        lax.psum_scatter(
            grad_out.astype(jnp.bfloat16), "dp", scatter_dimension=1, tiled=True
        ).astype(jnp.float32),
        lax.psum_scatter(
            grad_up.astype(jnp.bfloat16), "dp", scatter_dimension=1, tiled=True
        ).astype(jnp.float32),
        lax.psum_scatter(
            grad_down.astype(jnp.bfloat16), "dp", scatter_dimension=1, tiled=True
        ).astype(jnp.float32),
    )
    small_parts = (
        lax.psum_scatter(bias_qv_full, ("dp", "tensor"), scatter_dimension=1, tiled=True),
        lax.psum_scatter(grad_bias_out, ("dp", "tensor"), scatter_dimension=0, tiled=True),
        lax.psum_scatter(bias_up_full, ("dp", "tensor"), scatter_dimension=0, tiled=True),
        lax.psum_scatter(grad_bias_down, ("dp", "tensor"), scatter_dimension=0, tiled=True),
        lax.psum_scatter(grad_gain_one, ("dp", "tensor"), scatter_dimension=0, tiled=True),
        lax.psum_scatter(grad_shift_one, ("dp", "tensor"), scatter_dimension=0, tiled=True),
        lax.psum_scatter(grad_gain_two, ("dp", "tensor"), scatter_dimension=0, tiled=True),
        lax.psum_scatter(grad_shift_two, ("dp", "tensor"), scatter_dimension=0, tiled=True),
    )
    return (
        activations,
        grad_input,
        qkv_part,
        small_parts[0],
        out_part,
        small_parts[1],
        up_part[0],
        small_parts[2],
        down_part,
        small_parts[3],
        small_parts[4],
        small_parts[5],
        small_parts[6],
        small_parts[7],
        rms_stats,
    )


def solution(mesh):
    fast = mesh.shape["dp"] == 16 and mesh.shape["tensor"] == 2
    return jax.shard_map(
        local_fast if fast else local,
        mesh=mesh,
        in_specs=(
            P(("dp", "tensor"), None),
            P("dp"),
            P(("dp", "tensor"), None),
            P(None, "dp", "tensor"),
            P(),
            P("tensor", "dp"),
            P(),
            P("dp", "tensor"),
            P(),
            P("tensor", "dp"),
            P(),
            P(),
            P(),
            P(),
            P(),
        ),
        out_specs=(
            P(("dp", "tensor"), None),
            P(("dp", "tensor"), None),
            P(None, "dp", "tensor"),
            P(None, ("dp", "tensor")),
            P("tensor", "dp"),
            P(("dp", "tensor")),
            P("dp", "tensor"),
            P(("dp", "tensor")),
            P("tensor", "dp"),
            P(("dp", "tensor")),
            P(("dp", "tensor")),
            P(("dp", "tensor")),
            P(("dp", "tensor")),
            P(("dp", "tensor")),
            P(),
        ),
        check_vma=False,
    )
```

```python
import jax
import jax.numpy as jnp
from jax import lax
from jax.experimental import pallas as pl
from jax.experimental.pallas import tpu as pltpu
from jax.sharding import PartitionSpec as P

HD = 64
BUFFER = 64
SLOTS = 320


eps_norm = 1e-06


MESH = pl.DeviceIdType.MESH


class Place:
    def __init__(self):
        dp = lax.axis_index("dp")
        self.t = lax.axis_index("tensor")
        self.z, self.y, self.x = dp // 4, (dp // 2) % 2, dp % 2
        self.side = self.z // 2
        self.w = self.z + self.side * (3 - 2 * self.z)
        self.step = 1 - 2 * self.side
        self.dp = dp

    def order(self, k):
        o = (self.w, 1 - self.w, 2, 3)[k]
        return 3 * self.side + self.step * o

    def chip(self, z, y, x):
        return z * 4 + y * 2 + x

    def inward(self):
        return (self.chip(self.z + self.step, self.y, self.x), self.t)

    def outward(self):
        return (self.chip(self.z - self.step, self.y, self.x), self.t)

    def across_x(self):
        return (self.chip(self.z, self.y, 1 - self.x), self.t)

    def across_y(self):
        return (self.chip(self.z, 1 - self.y, self.x), self.t)

    def near(self):
        return (self.chip(self.z + 1 - 2 * (self.z % 2), self.y, self.x), self.t)

    def far(self):
        return (self.chip((self.z + 2) % 4, self.y, self.x), self.t)

    def twin(self):
        return (self.dp, 1 - self.t)


def enter(at):
    barrier = pltpu.get_barrier_semaphore()
    for other in (at.across_x(), at.across_y(), at.inward(), at.twin(), at.far()):
        pl.semaphore_signal(barrier, inc=1, device_id=other, device_id_type=MESH)

    @pl.when(at.w == 1)
    def _():
        pl.semaphore_signal(barrier, inc=1, device_id=at.outward(), device_id_type=MESH)

    pl.semaphore_wait(barrier, 5 + at.w)


class Gather:
    def __init__(self, at, full, shard, pieces, send, recv):
        self.at, self.full, self.shard, self.pieces, self.send, self.recv = at, full, shard, pieces, send, recv

    def rows(self, p, z, y, x, part=None):
        c0, c1 = self.pieces[p]
        start, size = self.at.chip(z, y, x) * self.shard, self.shard
        if part is not None:
            size = self.shard // 2
            start = start + part * size
        return self.full.at[pl.ds(pl.multiple_of(start, size), size), pl.ds(c0, c1 - c0)]

    def copy(self, p, ref, s, r, other):
        return pltpu.make_async_remote_copy(
            src_ref=ref,
            dst_ref=ref,
            send_sem=self.send.at[p, s[0], s[1]],
            recv_sem=self.recv.at[p, r[0], r[1]],
            device_id=other,
            device_id_type=MESH,
        )

    def z_in(self, p, z):
        return self.copy(p, self.rows(p, z, self.at.y, self.at.x), (0, z), (0, z), self.at.inward())

    def z_out(self, p, z):
        return self.copy(p, self.rows(p, z, self.at.y, self.at.x), (5, z), (0, z), self.at.outward())

    def x_full(self, p, z):
        return self.copy(p, self.rows(p, z, self.at.y, self.at.x), (1, z), (1, z), self.at.across_x())

    def y_full(self, p, z):
        return self.copy(p, self.rows(p, z, self.at.y, self.at.x), (2, z), (2, z), self.at.across_y())

    def x_half(self, p, z):
        return self.copy(p, self.rows(p, z, 1 - self.at.y, self.at.x, 1), (3, z), (3, z), self.at.across_x())

    def y_half(self, p, z):
        return self.copy(p, self.rows(p, z, self.at.y, 1 - self.at.x, 0), (4, z), (4, z), self.at.across_y())

    def arrived(self, p, kind, z):
        at = self.at
        ref = (
            lambda: self.rows(p, z, at.y, at.x),
            lambda: self.rows(p, z, at.y, 1 - at.x),
            lambda: self.rows(p, z, 1 - at.y, at.x),
            lambda: self.rows(p, z, 1 - at.y, 1 - at.x, 1),
            lambda: self.rows(p, z, 1 - at.y, 1 - at.x, 0),
        )[kind]()
        self.copy(p, ref, (kind, z), (kind, z), at.across_x()).wait_recv()

    def line(self, p, k, w):
        at = self.at

        @pl.when(at.w == w)
        def _():
            z = at.order(k)
            if k > 0:
                self.arrived(p, 0, z)
            if k == 0 or (k == 1 and w == 1):
                self.z_in(p, z).start()
            if w == 1 and k != 1:
                self.z_out(p, z).start()
            self.x_full(p, z).start()
            self.y_full(p, z).start()

    def plane(self, p, k):
        z = self.at.order(k)
        self.arrived(p, 1, z)
        self.y_half(p, z).start()
        self.arrived(p, 2, z)
        self.x_half(p, z).start()

    def finish(self, p):
        for k in range(4):
            z = self.at.order(k)
            self.arrived(p, 3, z)
            self.arrived(p, 4, z)

    def drain(self, p):
        at = self.at
        for k in range(4):
            z = at.order(k)
            if k == 0:
                self.z_in(p, z).wait_send()
            if k == 1:

                @pl.when(at.w == 1)
                def _(z=z):
                    self.z_in(p, z).wait_send()

            else:

                @pl.when(at.w == 1)
                def _(z=z):
                    self.z_out(p, z).wait_send()

            self.x_full(p, z).wait_send()
            self.y_full(p, z).wait_send()
            self.x_half(p, z).wait_send()
            self.y_half(p, z).wait_send()


class Scatter:
    def __init__(self, at, full, shard, pieces, xh, yh, xf, yf, zl, send, recv):
        self.at, self.full, self.shard, self.pieces = at, full, shard, pieces
        self.xh, self.yh, self.xf, self.yf, self.zl = xh, yh, xf, yf, zl
        self.send, self.recv = send, recv

    def cols(self, p):
        c0, c1 = self.pieces[p]
        return pl.ds(c0, c1 - c0)

    def rows(self, p, z, y, x, part=None):
        start, size = self.at.chip(z, y, x) * self.shard, self.shard
        if part is not None:
            size = self.shard // 2
            start = start + part * size
        ref, c0, c1 = self.full(p)
        return ref.at[pl.ds(pl.multiple_of(start, size), size), pl.ds(c0, c1 - c0)]

    def copy(self, p, src, dst, s, r, other):
        return pltpu.make_async_remote_copy(
            src_ref=src,
            dst_ref=dst,
            send_sem=self.send.at[p, s[0], s[1]],
            recv_sem=self.recv.at[p, r[0], r[1]],
            device_id=other,
            device_id_type=MESH,
        )

    def x_half(self, p, z):
        at = self.at
        return self.copy(
            p, self.rows(p, z, 1 - at.y, 1 - at.x, 0), self.xh.at[z, :, self.cols(p)], (1, z), (1, z), at.across_x()
        )

    def y_half(self, p, z):
        at = self.at
        return self.copy(
            p, self.rows(p, z, 1 - at.y, 1 - at.x, 1), self.yh.at[z, :, self.cols(p)], (2, z), (2, z), at.across_y()
        )

    def x_full(self, p, z):
        at = self.at
        return self.copy(
            p, self.rows(p, z, at.y, 1 - at.x), self.xf.at[z, :, self.cols(p)], (3, z), (3, z), at.across_x()
        )

    def y_full(self, p, z):
        at = self.at
        return self.copy(
            p, self.rows(p, z, 1 - at.y, at.x), self.yf.at[z, :, self.cols(p)], (4, z), (4, z), at.across_y()
        )

    def z_in(self, p, z, slot):
        at = self.at
        return self.copy(
            p, self.rows(p, z, at.y, at.x), self.zl.at[slot, :, self.cols(p)], (0, z), (0, slot), at.inward()
        )

    def z_out(self, p, z, slot):
        at = self.at
        return self.copy(
            p, self.rows(p, z, at.y, at.x), self.zl.at[slot, :, self.cols(p)], (0, z), (0, slot), at.outward()
        )

    def begin(self, p, k):
        z = self.at.order(k)
        self.x_half(p, z).start()
        self.y_half(p, z).start()

    def plane(self, p, k):
        at = self.at
        z = at.order(k)
        self.x_half(p, z).wait_recv()
        ref = self.rows(p, z, 1 - at.y, at.x, 0)
        ref[...] = ref[...] + self.xh[z, :, self.cols(p)]
        self.y_full(p, z).start()
        self.y_half(p, z).wait_recv()
        ref = self.rows(p, z, at.y, 1 - at.x, 1)
        ref[...] = ref[...] + self.yh[z, :, self.cols(p)]
        self.x_full(p, z).start()

    def wait_line(self, p, z, slot):
        self.z_in(p, z, slot).wait_recv()

    def line(self, p, k, w, out):
        at = self.at

        @pl.when(at.w == w)
        def _():
            z = at.order(k)
            self.x_full(p, z).wait_recv()
            self.y_full(p, z).wait_recv()
            ref = self.rows(p, z, at.y, at.x)
            parts = [self.xf.at[z, :, self.cols(p)], self.yf.at[z, :, self.cols(p)]]
            if w == 1:
                self.wait_line(p, z, z)
                parts.append(self.zl.at[z, :, self.cols(p)])
            if k == 0:
                self.wait_line(p, z, 4)
                parts.append(self.zl.at[4, :, self.cols(p)])
            total = ref[...].astype(jnp.float32)
            for part in parts:
                total = total + part[...].astype(jnp.float32)
            if k == 0:
                out(total)
            else:
                ref[...] = total.astype(jnp.bfloat16)
                if w == 0 or k == 3:
                    self.z_in(p, z, z).start()
                elif k == 2:
                    self.z_in(p, z, 4).start()
                else:
                    self.z_out(p, z, 4).start()

    def drain(self, p):
        at = self.at
        for k in range(4):
            z = at.order(k)
            for c in (self.x_half(p, z), self.y_half(p, z), self.x_full(p, z), self.y_full(p, z)):
                c.wait_send()
            if k > 0:
                self.z_in(p, z, z).wait_send()


class PairGather:
    def __init__(self, at, full, shard, columns, sources, send, recv):
        self.at, self.full, self.shard, self.columns, self.sources = at, full, shard, columns, sources
        self.send, self.recv = send, recv

    def far_x(self, h):
        return self.at.x if h == 0 else 1 - self.at.x

    def rows(self, m, z, y, x):
        c0, n = self.columns[m]
        start = self.at.chip(z, y, x) * self.shard
        return self.full.at[pl.ds(pl.multiple_of(start, self.shard), self.shard), pl.ds(c0, n)]

    def copy(self, m, h, src, dst, s, r, z, other):
        i = 2 * m + h
        return pltpu.make_async_remote_copy(
            src_ref=src,
            dst_ref=dst,
            send_sem=self.send.at[i, s, z],
            recv_sem=self.recv.at[i, r, z],
            device_id=other,
            device_id_type=MESH,
        )

    def x_copy(self, m):
        at = self.at
        c0, n = self.columns[m]
        src = self.sources[m].at[:, pl.ds(pl.multiple_of((1 - at.x) * n, n), n)]
        return self.copy(m, 1, src, self.rows(m, at.z, at.y, at.x), 3, 2, at.z, at.across_x())

    def z_in(self, m, h, z):
        ref = self.rows(m, z, self.at.y, self.far_x(h))
        return self.copy(m, h, ref, ref, 0, 0, z, self.at.inward())

    def z_out(self, m, h, z):
        ref = self.rows(m, z, self.at.y, self.far_x(h))
        return self.copy(m, h, ref, ref, 1, 0, z, self.at.outward())

    def y_copy(self, m, h, z):
        ref = self.rows(m, z, self.at.y, self.far_x(h))
        return self.copy(m, h, ref, ref, 2, 1, z, self.at.across_y())

    def line(self, m, h, k, w):
        at = self.at

        @pl.when(at.w == w)
        def _():
            z = at.order(k)
            ref = self.rows(m, z, at.y, self.far_x(h))
            if k > 0:
                self.copy(m, h, ref, ref, 0, 0, z, at.inward()).wait_recv()
            elif h == 1:
                self.copy(m, h, ref, ref, 0, 2, z, at.across_x()).wait_recv()
            if k == 0 or (k == 1 and w == 1):
                self.z_in(m, h, z).start()
            if w == 1 and k != 1:
                self.z_out(m, h, z).start()

    def cross(self, m, h, k, w):
        @pl.when(self.at.w == w)
        def _():
            self.y_copy(m, h, self.at.order(k)).start()

    def finish(self, m):
        at = self.at
        for h in range(2):
            for k in range(4):
                z = at.order(k)
                ref = self.rows(m, z, 1 - at.y, self.far_x(h))
                self.copy(m, h, ref, ref, 2, 1, z, at.across_y()).wait_recv()

    def drain(self, m):
        at = self.at
        self.x_copy(m).wait_send()
        for h in range(2):
            for k in range(4):
                z = at.order(k)
                if k == 0:
                    self.z_in(m, h, z).wait_send()
                if k == 1:

                    @pl.when(at.w == 1)
                    def _(z=z):
                        self.z_in(m, h, z).wait_send()

                else:

                    @pl.when(at.w == 1)
                    def _(z=z):
                        self.z_out(m, h, z).wait_send()

                self.y_copy(m, h, z).wait_send()


class PairScatter:
    def __init__(self, at, full, shard, first, units, xs, xr, send, recv):
        self.at, self.full, self.shard, self.first = at, full, shard, first
        self.units, self.xs, self.xr, self.send, self.recv = units, xs, xr, send, recv
        self.base = {1: 0, 0: 11 if 1 in first else 9}

    def unit(self, m, z, y):
        ref, c0, n = self.full(m)
        size = 2 * self.shard
        return ref.at[pl.ds(pl.multiple_of((z * 2 + y) * size, size), size), pl.ds(c0, n)]

    def copy(self, m, src, dst, s, r, other):
        return pltpu.make_async_remote_copy(
            src_ref=src,
            dst_ref=dst,
            send_sem=self.send.at[m, s[0], s[1]],
            recv_sem=self.recv.at[m, r[0], r[1]],
            device_id=other,
            device_id_type=MESH,
        )

    def from_y(self, m, z):
        return self.units.at[self.base[m] + (10 if m in self.first else z)]

    def from_z(self, m, col, slot):
        return self.units.at[self.base[m] + (5 * col if m in self.first else 4) + slot]

    def column(self, col):
        return self.at.y if col == 0 else 1 - self.at.y

    def y_copy(self, m, z):
        return self.copy(m, self.unit(m, z, 1 - self.at.y), self.from_y(m, z), (1, z), (1, z), self.at.across_y())

    def z_copy(self, m, col, z, slot, other):
        return self.copy(
            m, self.unit(m, z, self.column(col)), self.from_z(m, col, slot), (3 + col, z), (3 + col, slot), other
        )

    def x_copy(self, m):
        return self.copy(m, self.xs.at[m], self.xr.at[m], (2, 0), (2, 0), self.at.across_x())

    def begin(self, m, k):
        self.y_copy(m, self.at.order(k)).start()

    def pass_on(self, m, col, k, w):
        at = self.at
        z = at.order(k)
        if w == 0:
            self.z_copy(m, col, z, z, at.inward()).start()
        elif k == 1:
            self.z_copy(m, col, z, 4, at.outward()).start()
        else:
            self.z_copy(m, col, z, z if k == 3 else 4, at.inward()).start()

    def add_line(self, m, col, k, w, extra):
        at = self.at
        z = at.order(k)
        ref = self.unit(m, z, self.column(col))
        parts = list(extra)
        if k == 0:
            self.z_copy(m, col, z, 4, at.inward()).wait_recv()
            parts.append(self.from_z(m, col, 4))
        if w == 1:
            self.z_copy(m, col, z, z, at.inward()).wait_recv()
            parts.append(self.from_z(m, col, z))
        if parts:
            v = ref[...].astype(jnp.float32)
            for part in parts:
                v = v + part[...].astype(jnp.float32)
            ref[...] = v.astype(jnp.bfloat16)

    def finish(self, m, out, second):
        at = self.at
        size = self.shard
        full, c0, n = self.full(m)

        def total(x):
            rows = pl.ds(pl.multiple_of(at.chip(at.z, at.y, x) * size, size), size)
            v = full[rows, pl.ds(c0, n)].astype(jnp.float32)
            if second:
                v = v + self.from_y(m, at.z)[pl.ds(pl.multiple_of(x * size, size), size), :].astype(jnp.float32)
            return v

        self.xs[m] = total(1 - at.x).astype(jnp.bfloat16)
        self.x_copy(m).start()
        out(at.x, total(at.x))

    def line(self, m, k, w, out):
        at = self.at

        @pl.when(at.w == w)
        def _():
            z = at.order(k)
            self.y_copy(m, z).wait_recv()
            self.add_line(m, 0, k, w, [self.from_y(m, z)])
            if k > 0:
                self.pass_on(m, 0, k, w)
            else:
                self.finish(m, out, False)

    def line_first(self, m, col, k, w):
        @pl.when(self.at.w == w)
        def _():
            self.add_line(m, col, k, w, [])
            if k > 0:
                self.pass_on(m, col, k, w)
            elif col == 1:
                self.y_copy(m, self.at.z).start()

    def meet(self, m, out):
        self.y_copy(m, self.at.z).wait_recv()
        self.finish(m, out, True)

    def last(self, m, out):
        self.x_copy(m).wait_recv()
        out(1 - self.at.x, self.xr[m].astype(jnp.float32))

    def drain(self, m):
        at = self.at
        for k in range(4):
            z = at.order(k)
            if m not in self.first or k == 0:
                self.y_copy(m, z).wait_send()
            if k > 0:
                for col in range(2 if m in self.first else 1):
                    self.z_copy(m, col, z, z, at.inward()).wait_send()
        self.x_copy(m).wait_send()


QKV, OUT, UP, DOWN, COLS = 0, 1536, 2048, 3072, 4096
PIECES = ((0, 384), (384, 768), (768, 1152), (1152, 1536), (1536, 2048))
LINE_FIRST = ()
PLAN = (
    ((2, 0), (0, 2, 0, 0), (0, 0, 0, 0), (0, 1, 0, 0), (3, 0, 0, 0, 0), (0, 3, 0, 0), (4, 0, 0, 0, 0), (0, 2, 0, 1), (0, 3, 0, 1), (0, 1, 0, 1), (0, 1, 1, 0), (0, 0, 0, 1), (0, 2, 1, 1), (0, 1, 1, 1), (0, 1, 2, 1), (0, 0, 1, 0), (0, 0, 1, 1), (0, 0, 2, 1), (0, 1, 3, 1), (3, 0, 1, 0, 0), (0, 3, 1, 1), (0, 3, 2, 1), (1, 0, 0), (0, 2, 1, 0), (0, 0, 3, 1), (3, 0, 0, 0, 1), (3, 1, 0, 0, 0), (1, 3, 0), (0, 2, 2, 1), (0, 3, 1, 0), (0, 1, 2, 0),),
    ((0, 3, 3, 1), (0, 3, 2, 0), (0, 4, 0, 0), (3, 0, 1, 0, 1), (0, 0, 2, 0), (2, 1), (3, 0, 0, 1, 1), (1, 1, 0), (0, 2, 3, 1), (0, 1, 3, 0), (4, 0, 1, 0, 0), (3, 0, 1, 1, 0), (1, 1, 1), (1, 0, 1), (0, 0, 3, 0), (1, 2, 0), (3, 0, 0, 1, 0), (0, 2, 2, 0), (4, 0, 0, 0, 1), (0, 2, 3, 0), (3, 0, 0, 2, 1), (1, 0, 2), (1, 0, 3), (1, 1, 2), (0, 4, 0, 1), (3, 1, 1, 0, 0), (0, 3, 3, 0), (1, 1, 3), (0, 4, 1, 1), (0, 4, 2, 1), (0, 4, 3, 1), (3, 1, 1, 0, 1), (3, 0, 1, 1, 1), (3, 1, 0, 0, 1), (1, 2, 1), (1, 3, 1), (3, 0, 0, 3, 1), (3, 0, 0, 2, 0), (1, 2, 2), (3, 0, 1, 2, 1), (3, 1, 1, 1, 1),),
    (),
    ((1, 2, 3), (0, 4, 1, 0), (0, 4, 2, 0), (0, 4, 3, 0), (1, 3, 2), (1, 3, 3),),
    (),
    (),
    (),
    ((1, 4, 0), (3, 1, 0, 1, 0), (1, 4, 1), (4, 1, 0, 0, 1), (4, 1, 1, 0, 1),),
    ((3, 1, 1, 1, 0), (3, 1, 0, 1, 1), (1, 4, 2), (1, 4, 3), (4, 0, 1, 1, 0), (3, 1, 1, 2, 1),),
    ((5,), (4, 0, 0, 1, 0), (3, 0, 0, 3, 0),),
    ((3, 0, 1, 3, 1), (3, 1, 0, 2, 1), (4, 1, 1, 0, 0), (3, 0, 1, 2, 0), (4, 0, 1, 2, 0),),
    (),
    (),
    (),
    (),
    ((4, 0, 0, 2, 0), (4, 0, 1, 0, 1), (4, 0, 1, 1, 1),),
    ((3, 1, 0, 3, 1),),
    (),
    ((4, 0, 0, 3, 0), (3, 1, 1, 3, 1), (4, 0, 1, 2, 1), (4, 0, 1, 3, 1),),
    (),
    (),
    (),
    (),
    ((4, 0, 0, 1, 1), (4, 0, 0, 2, 1),),
    ((4, 1, 0, 0, 0), (4, 0, 0, 3, 1), (4, 1, 0, 1, 1), (3, 0, 1, 3, 0), (4, 0, 1, 3, 0), (3, 1, 0, 2, 0), (4, 1, 1, 1, 0), (3, 1, 1, 2, 0), (3, 1, 1, 3, 0), (4, 1, 1, 1, 1), (4, 1, 1, 2, 1),),
    ((4, 1, 0, 2, 1), (4, 1, 0, 1, 0), (4, 1, 1, 2, 0), (4, 1, 0, 3, 1), (4, 1, 0, 2, 0), (3, 1, 0, 3, 0), (4, 1, 1, 3, 0), (4, 1, 1, 3, 1),),
    ((4, 1, 0, 3, 0),),
    (),
    (),
    (),
    (),
    (),
    (),
    (),
    (),
    (),
    (),
    (),
    (),
    ((13, 1, 3),),
    (),
    (),
    ((13, 1, 2),),
    (),
    (),
    ((13, 1, 1),),
    (),
    (),
    ((13, 0, 3),),
    (),
    (),
    (),
    (),
    (),
    ((13, 0, 2), (13, 1, 0),),
    (),
    (),
    (),
    (),
    (),
    (),
    ((14, 1, 3, 0), (10, 4, 3), (10, 4, 2),),
    (),
    ((13, 0, 1),),
    ((14, 1, 2, 0),),
    (),
    ((14, 0, 3, 0),),
    ((10, 4, 1),),
    ((14, 0, 2, 0),),
    ((11, 4, 3),),
    ((10, 0, 3), (14, 1, 3, 1), (10, 0, 2), (10, 1, 3), (10, 0, 1),),
    ((11, 4, 2), (10, 1, 2), (10, 1, 1),),
    ((11, 0, 3), (11, 0, 2), (11, 0, 1),),
    ((14, 1, 1, 0), (10, 4, 0), (10, 0, 0), (14, 1, 2, 1), (13, 0, 0), (10, 1, 0), (14, 1, 1, 1),),
    ((11, 4, 1),),
    (),
    ((14, 0, 3, 1), (11, 1, 3), (11, 1, 2), (14, 0, 1, 0), (10, 2, 3),),
    (),
    (),
    ((11, 4, 0), (14, 0, 2, 1), (14, 1, 0, 0), (11, 1, 1),),
    ((10, 3, 3), (12, 4, 3, 0),),
    ((10, 2, 2), (14, 1, 0, 1),),
    (),
    ((11, 0, 0), (12, 4, 2, 0),),
    (),
    ((10, 3, 2), (11, 3, 3), (12, 0, 3, 0), (10, 3, 1), (14, 0, 1, 1), (12, 1, 3, 0), (12, 4, 3, 1), (11, 2, 3), (10, 3, 0), (12, 1, 2, 0),),
    (),
    ((14, 0, 0, 1), (11, 3, 2), (12, 0, 2, 0), (12, 3, 3, 0), (12, 4, 2, 1), (12, 4, 1, 1), (12, 0, 3, 1), (10, 2, 1), (11, 3, 1), (12, 4, 1, 0), (10, 2, 0),),
    ((12, 1, 3, 1),),
    ((12, 1, 2, 1), (12, 0, 2, 1), (12, 0, 1, 1), (11, 2, 2), (12, 3, 3, 1), (12, 2, 3, 0), (11, 2, 1), (12, 3, 2, 0), (14, 0, 0, 0), (12, 0, 1, 0),),
    (),
    ((12, 2, 2, 0), (12, 2, 1, 0), (11, 3, 0), (12, 1, 1, 1), (11, 1, 0), (12, 2, 3, 1), (12, 3, 1, 0), (12, 3, 2, 1), (12, 3, 1, 1), (12, 1, 1, 0),),
    (),
    ((11, 2, 0), (12, 0, 0, 0), (12, 2, 2, 1), (12, 2, 1, 1), (15, 1), (15, 0), (12, 4, 0, 1), (12, 3, 0, 0), (12, 0, 0, 1), (12, 4, 0, 0), (12, 1, 0, 0), (12, 3, 0, 1),),
    (),
    ((12, 2, 0, 1), (12, 1, 0, 1), (12, 2, 0, 0),),
)
BF, F32 = jnp.bfloat16, jnp.float32
SUMS = ("bq", "bv", "bout", "bdown", "g1", "s1", "g2", "s2", "x", "mid", "res", "branch", "feed")
BLOCK = 32


def nn(a, b):
    return lax.dot_general(a, b, (((1,), (0,)), ((), ())), preferred_element_type=F32)


def nt(a, b):
    return lax.dot_general(a, b, (((1,), (1,)), ((), ())), preferred_element_type=F32)


def at_rows(start, size):
    return pl.ds(pl.multiple_of(start, size), size)


def fold(v):
    return jnp.sum(v.reshape(v.shape[0] // 8, 8, v.shape[1]), axis=0)


def normed(v):
    centre = jnp.mean(v, axis=1, keepdims=True)
    offset = v - centre
    r = lax.rsqrt(jnp.mean(offset * offset, axis=1, keepdims=True) + eps_norm)
    return offset * r, r


def norm_back(dy, n, r, gain):
    dn = dy * gain
    first = jnp.mean(dn, axis=1, keepdims=True)
    second = jnp.mean(dn * n, axis=1, keepdims=True)
    return r * (dn - first - n * second)


def block_kernel(
    counts, x_ref, cot_ref, wqkv, wout, wup, wdown, bqv, bout, bup, bdown, g1, s1, g2, s2,
    act_out, gin_out, o_qkv, o_out, o_up, o_down, o_sums,
    W, G2, G3, xh, yh, xf, yf, zl, units, xs2, xr2,
    rows1, dfeed, qkv, probs, heads, mid, rows2, act, gp, datt,
    tall, own_a, own_c, send_t, send_x, got, got_t, acc, acc_up, sums, sums_got,
    sem_in, ag_send, ag_recv, pg_send, pg_recv, rs_send, rs_recv, ps_send, ps_recv,
    pair_send, pair_recv, sums_send, sums_recv,
):
    at = Place()
    t, x = at.t, at.x
    shard = wup.shape[0]
    own = x_ref.shape[0]
    width = x_ref.shape[1]
    dbr = dfeed.at[0 : 2 * own, :]
    dproj = qkv

    def spot(far_x, far_t):
        return at_rows((far_x * 2 + far_t) * own, own)

    mine, theirs = at_rows(t * own, own), at_rows((1 - t) * own, own)

    here = at_rows(at.dp * shard, shard)
    quarter = pl.ds(pl.multiple_of(x * 1024, 1024), 1024)
    loads = [
        pltpu.make_async_copy(src, W.at[here, pl.ds(c0, n)], sem_in.at[i])
        for i, (src, c0, n) in enumerate(
            [(wqkv.at[j, :, pl.ds(128 * h, 128)], QKV + 384 * h + 128 * j, 128) for h in range(4) for j in range(3)]
            + [(wout, OUT, 512), (wup.at[:, quarter], UP, 1024), (wdown.at[:, quarter], DOWN, 1024)]
        )
    ]
    for c in loads:
        c.start()
    enter(at)
    g = Gather(at, W, shard, PIECES, ag_send, ag_recv)
    pg = PairGather(at, W, shard, ((UP, 1024), (DOWN, 1024)), (wup, wdown), pg_send, pg_recv)
    for c in loads:
        c.wait()

    home = {0: (W, DOWN, DOWN + 384), 1: (W, DOWN + 384, DOWN + 768), 2: (G3, 512, 896), 3: (W, OUT, OUT + 384), 4: (G3, 0, 512)}
    sc = Scatter(at, lambda p: home[p], shard, PIECES, xh, yh, xf, yf, zl, rs_send, rs_recv)
    home_pair = {0: (W, UP, 1024), 1: (G2, 0, 1024)}
    ps = PairScatter(at, lambda m: home_pair[m], shard, LINE_FIRST, units, xs2, xr2, ps_send, ps_recv)

    def write(p):
        def store(total):
            if p < 4:
                for j in range(3):
                    o_qkv[j, :, 128 * p : 128 * (p + 1)] = total[:, 128 * j : 128 * (j + 1)]
            else:
                o_out[...] = total
        return store

    def write_pair(m):
        ref = o_up if m == 0 else o_down

        def store(far_x, total):
            ref[:, pl.ds(pl.multiple_of(far_x * 1024, 1024), 1024)] = total
        return store

    def share_feed():
        shares.append(share(2, dfeed, spot(x, t), at.across_x()))

    actions = {
        0: g.line, 1: g.plane, 2: lambda m: pg.x_copy(m).start(), 3: pg.line, 4: pg.cross, 5: share_feed,
        10: sc.begin, 11: sc.plane, 12: lambda p, k, w: sc.line(p, k, w, write(p)),
        13: ps.begin, 14: lambda m, k, w: ps.line(m, k, w, write_pair(m)), 15: lambda m: ps.last(m, write_pair(m)),
        16: ps.line_first, 17: lambda m: ps.meet(m, write_pair(m)),
    }
    done = [0]

    def run(part):
        while done[0] <= min(part, len(PLAN) - 1):
            for kind, *a in PLAN[done[0]]:
                actions[kind](*a)
            done[0] += 1

    def quiet(part):
        return part >= len(PLAN) or not PLAN[part]

    def send(i, src, dst, other):
        return pltpu.make_async_remote_copy(
            src_ref=src, dst_ref=dst, send_sem=pair_send.at[i], recv_sem=pair_recv.at[i],
            device_id=other, device_id_type=MESH,
        )

    def share(i, ref, r, other):
        c = send(i, ref.at[r, :], ref.at[r, :], other)
        c.start()
        return c

    def take(i, ref, r):
        send(i, ref.at[r, :], ref.at[r, :], at.twin()).wait_recv()

    for ref in (acc, acc_up):
        ref[...] = jnp.zeros_like(ref)
    total_of = {name: acc.at[i] for i, name in enumerate(SUMS)}

    def add(name, v):
        ref = total_of[name]
        ref[...] += fold(v)

    def valid_of(image, start, size):
        slot = lax.broadcasted_iota(jnp.int32, (size, 1), 0) + start
        return slot < counts[image] + BUFFER

    def each_block(body):
        def go(b, _):
            body(b * BLOCK, pl.ds(pl.multiple_of(b * BLOCK, BLOCK), BLOCK))
            return 0
        lax.fori_loop(0, own // BLOCK, go, 0)

    def tiles(first, last, body, size=256):
        def go(i, _):
            body(pl.multiple_of(i * size, size))
            return 0
        lax.fori_loop(first // size, last // size, go, 0)

    def flip(src, first=0):
        def body(c):
            tall[pl.ds(c, 128), first : first + src.shape[0]] = src[:, pl.ds(c, 128)].T
        tiles(0, src.shape[1], body, 128)

    def first_norm(b, r):
        xv = x_ref[r, :].astype(F32)
        keep = valid_of(t, b, BLOCK).astype(F32)
        n, _ = normed(xv)
        mine_b = pl.ds(pl.multiple_of(t * own + b, BLOCK), BLOCK)
        rows1[mine_b, :] = (n * g1[...] + s1[...]).astype(BF)
        add("x", keep * xv * xv)
        low = (cot_ref[r, :].astype(F32) * keep).astype(BF)
        dfeed[pl.ds(pl.multiple_of((x * 2 + t) * own + b, BLOCK), BLOCK), :] = low
        add("bdown", low.astype(F32))

    run(0)
    each_block(first_norm)
    shares = [share(0, rows1, mine, at.twin()), share(1, dfeed, spot(x, t), at.twin())]

    def project(j):
        heads_of = pl.ds(pl.multiple_of(t * 512 + 128 * j, 128), 128)
        cols = pl.ds(QKV + 384 * j, 384)
        bias = jnp.concatenate([bqv[0:1, heads_of], jnp.zeros((1, 128), F32), bqv[1:2, heads_of]], axis=1)
        scale = jnp.where(lax.broadcasted_iota(jnp.int32, (1, 384), 1) < 128, HD**-0.5, 1.0)

        def body(i, _):
            r = at_rows(i * own, own)
            qkv[r, pl.ds(384 * j, 384)] = ((nn(rows1[r, :], W[:, cols]) + bias) * scale).astype(BF)
            return 0
        lax.fori_loop(0, 2, body, 0)

    first_lanes = lax.broadcasted_iota(jnp.int32, (own, 128), 1) < HD

    def attend(image, j):
        r = pl.ds(pl.multiple_of(image * own, own), own)
        c = 384 * j
        q2 = qkv[r, c : c + 128]
        k2 = qkv[r, c + 128 : c + 256]
        v_t = qkv[r, c + 256 : c + 384].T
        hide = jnp.where(valid_of(image, 0, own), 0.0, -1e30)
        outs = []
        for a in range(2):
            qm = jnp.where(first_lanes if a == 0 else ~first_lanes, q2, jnp.zeros_like(q2))
            s = nt(k2, qm) + hide
            e = jnp.exp(s - jnp.max(s, axis=0, keepdims=True))
            low = (e * (1.0 / jnp.sum(e, axis=0, keepdims=True))).astype(BF)
            probs[(j * 2 + image) * 2 + a] = low
            outs.append(nn(v_t[a * HD : (a + 1) * HD], low))
        heads[r, 128 * j : 128 * (j + 1)] = jnp.concatenate(outs, axis=0).T.astype(BF)

    def images(part, body, j):
        run(part)
        if quiet(part + 1):
            def go(i, _):
                body(i, j)
                return 0
            lax.fori_loop(0, 2, go, 0)
        else:
            body(0, j)
            run(part + 1)
            body(1, j)

    for j in range(4):
        run(1 + 4 * j)
        g.finish(j)
        if j == 0:
            take(0, rows1, theirs)
        run(2 + 4 * j)
        project(j)
        images(3 + 4 * j, attend, j)
    run(17)
    g.finish(4)
    run(18)

    def others(i, src, cols, k):
        def body(c):
            send_t[0, :, pl.ds(c, 256)] = nt(src[theirs, :], W[pl.ds(c, 256), cols]).astype(BF)
        tiles(0, width, body)
        copy = send(i, send_t.at[0], got.at[k], at.twin())
        copy.start()
        return copy

    def owns(src, cols, keep):
        def body(c):
            keep[:, pl.ds(c, 256)] = nt(src[mine, :], W[pl.ds(c, 256), cols])
        tiles(0, width, body)

    branch_copy = others(3, heads, pl.ds(OUT, 512), 0)
    run(19)
    owns(heads, pl.ds(OUT, 512), own_a)
    run(20)
    branch_copy.wait()

    def second_norm(b, r):
        keep = valid_of(t, b, BLOCK).astype(F32)
        branch = own_a[r, :] + got[0, r, :].astype(F32) + bout[...]
        m = x_ref[r, :].astype(F32) + branch
        mid[r, :] = m
        add("branch", keep * branch * branch)
        add("mid", keep * m * m)
        n, _ = normed(m)
        rows2[pl.ds(pl.multiple_of((x * 2 + t) * own + b, BLOCK), BLOCK), :] = (n * g2[...] + s2[...]).astype(BF)

    run(21)
    each_block(second_norm)
    run(22)
    shares.append(share(4, rows2, spot(x, t), at.across_x()))
    shares.append(share(5, rows2, spot(x, t), at.twin()))
    run(23)

    take(2, dfeed, spot(1 - x, t))
    shares.append(share(6, dfeed, spot(1 - x, t), at.twin()))
    take(1, dfeed, spot(x, 1 - t))
    take(6, dfeed, spot(1 - x, 1 - t))
    run(24)
    flip(dfeed)
    take(5, rows2, spot(x, 1 - t))

    chip_rows = lambda far_x: at_rows(far_x * 2 * own, 2 * own)

    def halves(part, body):
        run(part)
        if quiet(part + 1):
            tiles(0, 1024, body)
        else:
            tiles(0, 512, body)
            run(part + 1)
            tiles(512, 1024, body)

    def hidden(far_x, part):
        r = chip_rows(far_x)

        def body(c):
            lanes = pl.ds(pl.multiple_of(t * 2048 + x * 1024 + c, 256), 256)
            u = nn(rows2[r, :], W[:, pl.ds(UP + c, 256)]) + bup[:, lanes]
            below = 0.5 * (1.0 + lax.erf(u * (0.5**0.5)))
            dense = jnp.exp(-0.5 * u * u) * 0.3989422804014327
            act[r, pl.ds(c, 256)] = (u * below).astype(BF)
            gp[r, pl.ds(c, 256)] = (below + u * dense).astype(BF)
        halves(part, body)

    def grad_down(c):
        G2[:, pl.ds(c, 256)] = nn(tall[...], act[:, pl.ds(c, 256)]).astype(BF)

    run(25)
    pg.finish(0)
    hidden(x, 26)
    run(28)
    take(4, rows2, spot(1 - x, t))
    shares.append(share(7, rows2, spot(1 - x, t), at.twin()))
    run(29)
    take(7, rows2, spot(1 - x, 1 - t))
    hidden(1 - x, 30)
    halves(33, grad_down)
    run(36)
    flip(rows2)
    run(37)

    def back_act(far_x):
        r = chip_rows(far_x)

        def body(c):
            d = nn(dfeed[r, :], W[:, pl.ds(DOWN + c, 256)])
            low = (d * gp[r, pl.ds(c, 256)].astype(F32)).astype(BF)
            gp[r, pl.ds(c, 256)] = low
            acc_up[t * 2 + x, :, pl.ds(c, 256)] += fold(low.astype(F32))
        tiles(0, 1024, body)

    def product(src, r, cols, put):
        def body(c):
            put(pl.ds(c, 256), nt(src[r, :], W[pl.ds(c, 256), cols]))
        tiles(0, width, body)

    class Sum4:
        def __init__(self, i, n, src, cols, keep, parts):
            self.i, self.n, self.src, self.cols, self.keep, self.parts = i, n, src, cols, keep, parts

        def away(self, far_x, slot):
            def put(c, v):
                send_t[slot, :, c] = v.astype(BF)
            product(self.src, spot(far_x, 1 - t), self.cols, put)
            copy = send(self.i + slot, send_t.at[slot], got_t.at[self.n, slot], at.twin())
            copy.start()
            return copy

        def far(self):
            first = self.away(1 - x, 0)

            def put(c, v):
                send_x[self.n, :, c] = v.astype(BF)
            product(self.src, spot(1 - x, t), self.cols, put)
            run(self.parts[0])
            first.wait()

            def body(b, r):
                send_x[self.n, r, :] = send_x[self.n, r, :] + got_t[self.n, 0, r, :]
            each_block(body)
            self.cross = send(self.i + 2, send_x.at[self.n], got.at[2 + self.n], at.across_x())
            run(self.parts[1])
            self.cross.start()

        def near(self):
            second = self.away(x, 1)

            def put(c, v):
                self.keep[:, c] = v
            product(self.src, spot(x, t), self.cols, put)
            second.wait()

        def value(self, r):
            return self.keep[r, :] + got_t[self.n, 1, r, :].astype(F32) + got[2 + self.n, r, :].astype(F32)

    pg.finish(1)
    run(39)
    back_act(1 - x)
    run(40)
    two = Sum4(8, 0, gp, pl.ds(UP, 1024), own_a, (41, 42))
    two.far()
    run(43)
    back_act(x)
    run(44)
    two.near()
    for p in range(5):
        g.drain(p)
    for m in range(2):
        pg.drain(m)

    def grad_up(c):
        W[:, pl.ds(UP + c, 256)] = nn(tall[...], gp[:, pl.ds(c, 256)]).astype(BF)

    halves(45, grad_up)
    run(48)
    four = Sum4(11, 1, act, pl.ds(DOWN, 1024), own_c, (49, 50))
    four.far()
    run(51)
    four.near()
    run(52)
    two.cross.wait()
    for i in (1, 2, 5):
        shares[i].wait_send()

    def second_back(b, r):
        dy = two.value(r)
        n, scale = normed(mid[r, :])
        keep = valid_of(t, b, BLOCK).astype(F32)
        add("g2", dy * n)
        add("s2", dy)
        d = cot_ref[r, :].astype(F32) * keep + norm_back(dy, n, scale, g2[...])
        gin_out[r, :] = d
        low = d.astype(BF)
        dbr[pl.ds(pl.multiple_of(t * own + b, BLOCK), BLOCK), :] = low
        add("bout", low.astype(F32))

    run(54)
    each_block(second_back)
    shares.append(share(14, dbr, mine, at.twin()))
    run(55)
    take(14, dbr, theirs)
    run(56)

    def back_heads(c):
        datt[:, pl.ds(c, 256)] = nn(dbr[...], W[:, pl.ds(OUT + c, 256)]).astype(BF)

    tiles(0, 512, back_heads)
    run(57)
    flip(dbr)
    run(58)
    flip(rows1, 2 * own)
    run(59)
    short, rest = pl.ds(0, 2 * own), pl.ds(2 * own, 2 * own)

    def grad_out(c):
        G3[:, pl.ds(c, 256)] = nn(tall[:, short], heads[:, pl.ds(c, 256)]).astype(BF)

    tiles(0, 512, grad_out)
    run(60)

    def grad_heads(p):
        ref, c0, c1 = home[p]

        def body(i, _):
            r = at_rows(i * 256, 256)
            ref[r, c0:c1] = nn(tall[r, rest], dproj[:, 384 * p : 384 * (p + 1)]).astype(BF)
            return 0
        lax.fori_loop(0, width // 256, body, 0)

    def attend_back(image, j):
        r = pl.ds(pl.multiple_of(image * own, own), own)
        c = 384 * j
        q2 = qkv[r, c : c + 128]
        k_t = qkv[r, c + 128 : c + 256].T
        v2 = qkv[r, c + 256 : c + 384]
        da = datt[r, 128 * j : 128 * (j + 1)]
        dq, dk, dv = [], [], []
        for a in range(2):
            dam = jnp.where(first_lanes if a == 0 else ~first_lanes, da, jnp.zeros_like(da))
            low = probs[(j * 2 + image) * 2 + a]
            p = low.astype(F32)
            dp = nt(v2, dam)
            ds = (p * (dp - jnp.sum(p * dp, axis=0, keepdims=True))).astype(BF)
            dq.append(nn(k_t[a * HD : (a + 1) * HD], ds))
            dk.append(nn(ds, q2))
            dv.append(nn(low, da))
        for base, v in (
            (0, jnp.concatenate(dq, axis=0).T * HD**-0.5),
            (128, jnp.where(first_lanes, dk[0], dk[1])),
            (256, jnp.where(first_lanes, dv[0], dv[1])),
        ):
            v = v.astype(BF)
            dproj[r, c + base : c + base + 128] = v
            if base != 128:
                lanes = pl.ds(pl.multiple_of(t * 512 + 128 * j, 128), 128)
                ref = total_of["bq" if base == 0 else "bv"]
                ref[:, lanes] += fold(v.astype(F32))

    def finish_feed(b, r):
        keep = valid_of(t, b, BLOCK).astype(F32)
        feed = four.value(r) + bdown[...]
        res = mid[r, :] + feed
        add("feed", keep * feed * feed)
        add("res", keep * res * res)
        act_out[r, :] = (keep * res).astype(BF)

    for j in range(3):
        images(61 + 4 * j, attend_back, j)
        run(63 + 4 * j)
        grad_heads(j)
    run(73)
    four.cross.wait()
    run(74)
    each_block(finish_feed)
    images(75, attend_back, 3)
    run(77)
    one_copy = others(15, dproj, pl.ds(QKV, 1536), 1)
    run(78)
    grad_heads(3)
    run(80)
    owns(dproj, pl.ds(QKV, 1536), own_a)
    run(81)
    one_copy.wait()
    run(82)

    def first_back(b, r):
        dy = own_a[r, :] + got[1, r, :].astype(F32)
        n, scale = normed(x_ref[r, :].astype(F32))
        add("g1", dy * n)
        add("s1", dy)
        gin_out[r, :] += norm_back(dy, n, scale, g1[...])

    each_block(first_back)
    run(83)

    for i in range(8):
        sums[i : i + 1, :] = jnp.sum(acc[i], axis=0, keepdims=True)
    for i in range(4):
        sums[8 + i : 9 + i, :] = jnp.sum(acc_up[i], axis=0, keepdims=True)
    lane = lax.broadcasted_iota(jnp.int32, (1, width), 1)
    row = jnp.where(lane == 5, (counts[t] + BUFFER).astype(F32), 0.0)
    for i, name in enumerate(("x", "mid", "res", "branch", "feed")):
        row = jnp.where(lane == i, jnp.sum(jnp.sum(total_of[name][...], axis=0, keepdims=True), axis=1, keepdims=True), row)
    sums[12:13, :] = row
    sums[13:16, :] = jnp.zeros((3, width), F32)
    for i, other in enumerate((at.twin(), at.across_x(), at.across_y(), at.near(), at.far())):
        c = pltpu.make_async_remote_copy(
            src_ref=sums, dst_ref=sums_got.at[i], send_sem=sums_send.at[i], recv_sem=sums_recv.at[i],
            device_id=other, device_id_type=MESH,
        )
        run(84 + 2 * i)
        c.start()
        run(85 + 2 * i)
        c.wait()
        sums[...] += sums_got[i]
    o_sums[...] = sums[...]
    run(1000)
    for m in (1, 0):
        ps.drain(m)
    for p in range(5):
        sc.drain(p)
    for i in (0, 3, 4, 6, 7):
        shares[i].wait_send()


def block(counts, stream, cotangent, w_qkv, w_out_t, w_up, w_down_t, b_qv, b_out, b_up, b_down, g1, s1, g2, s2):
    own, width = stream.shape
    shard = w_up.shape[0]
    rows = 16 * shard
    group = 2 * own
    vmem = pl.BlockSpec(memory_space=pltpu.VMEM)
    hbm = pl.BlockSpec(memory_space=pl.ANY)
    dma = pltpu.SemaphoreType.DMA
    row = lambda v: v.reshape(1, -1)
    return pl.pallas_call(
        block_kernel,
        out_shape=(
            jax.ShapeDtypeStruct((own, width), BF),
            jax.ShapeDtypeStruct((own, width), F32),
            jax.ShapeDtypeStruct((3, shard, 512), F32),
            jax.ShapeDtypeStruct((shard, 512), F32),
            jax.ShapeDtypeStruct((shard, 2048), F32),
            jax.ShapeDtypeStruct((shard, 2048), F32),
            jax.ShapeDtypeStruct((16, width), F32),
        ),
        in_specs=[pl.BlockSpec(memory_space=pltpu.SMEM), vmem, vmem, hbm, hbm, hbm, hbm] + [vmem] * 8,
        out_specs=(vmem,) * 7,
        scratch_shapes=[
            pltpu.VMEM((rows, COLS), BF),
            pltpu.VMEM((rows, 1024), BF),
            pltpu.VMEM((rows, 1024), BF),
            pltpu.VMEM((4, shard // 2, 2048), BF),
            pltpu.VMEM((4, shard // 2, 2048), BF),
            pltpu.VMEM((4, shard, 2048), BF),
            pltpu.VMEM((4, shard, 2048), BF),
            pltpu.VMEM((5, shard, 2048), BF),
            pltpu.VMEM((18 + 2 * len(LINE_FIRST), 2 * shard, 1024), BF),
            pltpu.VMEM((2, shard, 1024), BF),
            pltpu.VMEM((2, shard, 1024), BF),
            pltpu.VMEM((group, width), BF),
            pltpu.VMEM((2 * group, width), BF),
            pltpu.VMEM((group, 1536), BF),
            pltpu.VMEM((16, own, own), BF),
            pltpu.VMEM((group, 512), BF),
            pltpu.VMEM((own, width), F32),
            pltpu.VMEM((2 * group, width), BF),
            pltpu.VMEM((2 * group, 1024), BF),
            pltpu.VMEM((2 * group, 1024), BF),
            pltpu.VMEM((group, 512), BF),
            pltpu.VMEM((width, 2 * group), BF),
            pltpu.VMEM((own, width), F32),
            pltpu.VMEM((own, width), F32),
            pltpu.VMEM((2, own, width), BF),
            pltpu.VMEM((2, own, width), BF),
            pltpu.VMEM((4, own, width), BF),
            pltpu.VMEM((2, 2, own, width), BF),
            pltpu.VMEM((len(SUMS), 8, width), F32),
            pltpu.VMEM((4, 8, 1024), F32),
            pltpu.VMEM((16, width), F32),
            pltpu.VMEM((5, 16, width), F32),
            dma((15,)),
            dma((5, 6, 4)),
            dma((5, 5, 4)),
            dma((4, 4, 4)),
            dma((4, 3, 4)),
            dma((5, 5, 4)),
            dma((5, 5, 5)),
            dma((2, 6, 4)),
            dma((2, 6, 5)),
            dma((16,)),
            dma((16,)),
            dma((5,)),
            dma((5,)),
        ],
        compiler_params=pltpu.CompilerParams(
            collective_id=1, has_side_effects=True, vmem_limit_bytes=63 << 20
        ),
    )(
        counts, stream, cotangent, w_qkv, w_out_t, w_up, w_down_t,
        b_qv, row(b_out), row(b_up), row(b_down), row(g1), row(s1), row(g2), row(s2),
    )


def close_kernel(*refs):
    big, sums, out, small, held, sem = refs[:6], refs[6], refs[7:13], refs[13:22], refs[22:28], refs[28]
    loads = [pltpu.make_async_copy(a, h, sem.at[0, i]) for i, (a, h) in enumerate(zip(big, held))]
    copies = [pltpu.make_async_copy(h, b, sem.at[1, i]) for i, (h, b) in enumerate(zip(held, out))]
    for c in loads:
        c.start()
    place = lax.axis_index("dp") * 2 + lax.axis_index("tensor")
    width = sums.shape[1]
    turned = pltpu.roll(sums[0:8, :], width - place * 32, 1)
    small[0][...] = turned[0:2, :32]
    for i in range(1, 7):
        small[i][...] = turned[i + 1 : i + 2, :32]
    up = pl.ds(pl.multiple_of((place % 8) * 128, 128), 128)
    which = lax.broadcasted_iota(jnp.int32, (8, 128), 0) == place // 8
    small[7][...] = jnp.sum(jnp.where(which, sums[8:16, up], 0.0), axis=0, keepdims=True)
    row = sums[12:13, :]
    small[8][...] = jnp.sqrt(row[:, 0:5] / (row[:, 5:6] * width))
    for load, c in zip(loads, copies):
        load.wait()
        c.start()
    for c in copies:
        c.wait()


def close(*arrays):
    vmem = pl.BlockSpec(memory_space=pltpu.VMEM)
    hbm = pl.BlockSpec(memory_space=pl.ANY)
    small = [(2, 32)] + [(1, 32)] * 6 + [(1, 128), (1, 5)]
    return pl.pallas_call(
        close_kernel,
        out_shape=tuple(jax.ShapeDtypeStruct(a.shape, a.dtype) for a in arrays[:6])
        + tuple(jax.ShapeDtypeStruct(n, F32) for n in small),
        in_specs=[hbm] * 6 + [vmem],
        out_specs=(hbm,) * 6 + (vmem,) * 9,
        scratch_shapes=[pltpu.VMEM(a.shape, a.dtype) for a in arrays[:6]] + [pltpu.SemaphoreType.DMA((2, 6))],
    )(*arrays)


def local_fast(
    stream, counts, cotangent, w_qkv, b_qv, w_out, b_out, w_fc1, b_fc1, w_fc2, b_fc2,
    gain_one, shift_one, gain_two, shift_two,
):
    acts, grad_in, p_qkv, p_out, p_up, p_down, bqv, *rest = close(
        *block(
            counts, stream, cotangent, w_qkv, w_out.T, w_fc1, w_fc2.T, b_qv, b_out, b_fc1, b_fc2,
            gain_one, shift_one, gain_two, shift_two,
        )
    )
    bout, bdown, gain1, shift1, gain2, shift2, bup, rms = (v.reshape(-1) for v in rest[:8])
    return (
        acts, grad_in, p_qkv, bqv, p_out.T, bout, p_up, bup, p_down.T, bdown,
        gain1, shift1, gain2, shift2, rms,
    )

def layer_norm(values, gain, shift):
    centre = jnp.mean(values, axis=-1, keepdims=True)
    offset = values - centre
    spread = jnp.mean(offset * offset, axis=-1, keepdims=True)
    return offset * lax.rsqrt(spread + eps_norm) * gain + shift


def gelu_exact(values):
    return jax.nn.gelu(values, approximate=False)


def masked_scores(queries, key_rows, validity):
    scores = jnp.einsum(
        "bqhd,bkhd->bhqk", queries, key_rows, preferred_element_type=jnp.float32
    ) * HD ** (-0.5)
    return jnp.where(validity[:, None, None, :] > 0, scores, -1e30)


def attend_block(members):
    queries, key_rows, values, validity = members
    scores = masked_scores(queries, key_rows, validity)
    highest = jnp.max(scores, axis=-1, keepdims=True)
    expo_terms = jnp.exp(scores - highest)
    totals = jnp.sum(expo_terms, axis=-1, keepdims=True)
    weights = (expo_terms / totals).astype(jnp.bfloat16)
    mixture = jnp.einsum("bhqk,bkhd->bqhd", weights, values, preferred_element_type=jnp.float32)
    return (mixture.astype(jnp.bfloat16), (highest + jnp.log(totals))[..., 0])


def attend_back(members):
    queries, key_rows, values, validity, log_total, d_mixture = members
    scores = masked_scores(queries, key_rows, validity)
    probs = jnp.exp(scores - log_total[..., None])
    d_values = jnp.einsum(
        "bhqk,bqhd->bkhd", probs.astype(jnp.bfloat16), d_mixture, preferred_element_type=jnp.float32
    )
    d_probs = jnp.einsum("bqhd,bkhd->bhqk", d_mixture, values, preferred_element_type=jnp.float32)
    d_scores = (probs * (d_probs - jnp.sum(probs * d_probs, axis=-1, keepdims=True))).astype(
        jnp.bfloat16
    )
    d_queries = jnp.einsum(
        "bhqk,bkhd->bqhd", d_scores, key_rows, preferred_element_type=jnp.float32
    ) * HD ** (-0.5)
    d_keys = jnp.einsum(
        "bhqk,bqhd->bkhd", d_scores, queries, preferred_element_type=jnp.float32
    ) * HD ** (-0.5)
    return (
        d_queries.astype(jnp.bfloat16),
        d_keys.astype(jnp.bfloat16),
        d_values.astype(jnp.bfloat16),
    )


def local(
    stream,
    counts,
    cotangent,
    w_qkv,
    b_qv,
    w_out,
    b_out,
    w_fc1,
    b_fc1,
    w_fc2,
    b_fc2,
    gain_one,
    shift_one,
    gain_two,
    shift_two,
):
    tensor_pos = lax.axis_index("tensor")
    own_rows = stream.shape[0]
    width = stream.shape[1]
    own_images = own_rows // SLOTS
    slot_index = jnp.arange(SLOTS, dtype=jnp.int32)
    validity_all = (slot_index[None, :] < (BUFFER + counts)[:, None]).astype(jnp.float32)
    own_validity = lax.dynamic_slice_in_dim(validity_all, tensor_pos * own_images, own_images, 0)
    own_valid = own_validity.reshape(own_rows, 1)
    qkv_full, out_full, up_full, down_full = (
        lax.all_gather(w_qkv, "dp", axis=1, tiled=True),
        lax.all_gather(w_out, "dp", axis=1, tiled=True),
        lax.all_gather(w_fc1[None], "dp", axis=1, tiled=True),
        lax.all_gather(w_fc2, "dp", axis=1, tiled=True),
    )
    head_width = w_qkv.shape[2]
    unit_width = w_fc1.shape[1]
    bias_query = lax.dynamic_slice_in_dim(b_qv[0], tensor_pos * head_width, head_width, 0)
    bias_value = lax.dynamic_slice_in_dim(b_qv[1], tensor_pos * head_width, head_width, 0)
    bias_up = lax.dynamic_slice_in_dim(b_fc1, tensor_pos * unit_width, unit_width, 0)
    up_full = up_full[0]
    group_images = validity_all.shape[0]
    group_rows = group_images * SLOTS
    local_heads = head_width // HD
    pairing = 2
    block_count = group_images // pairing
    blocked_valid = validity_all.reshape(block_count, pairing, SLOTS)
    stream_f = stream.astype(jnp.float32)
    normed_one = layer_norm(stream_f, gain_one, shift_one).astype(jnp.bfloat16)
    first_rows = lax.all_gather(normed_one, "tensor", axis=0, tiled=True)
    projected = jnp.einsum("rd,cde->rce", first_rows, qkv_full, preferred_element_type=jnp.float32)
    shape_heads = (block_count, pairing, SLOTS, local_heads, HD)
    queries = (projected[:, 0] + bias_query).astype(jnp.bfloat16).reshape(shape_heads)
    key_rows = projected[:, 1].astype(jnp.bfloat16).reshape(shape_heads)
    values = (projected[:, 2] + bias_value).astype(jnp.bfloat16).reshape(shape_heads)
    mixture, log_total = lax.map(attend_block, (queries, key_rows, values, blocked_valid))
    attn_heads = mixture.reshape(group_rows, head_width)
    taken = attn_heads
    attn_total = lax.psum_scatter(
        jnp.dot(taken, out_full, preferred_element_type=jnp.float32).astype(jnp.bfloat16),
        "tensor",
        scatter_dimension=0,
        tiled=True,
    ).astype(jnp.float32)
    branch = attn_total + b_out
    middle = stream_f + branch
    normed_two = layer_norm(middle, gain_two, shift_two).astype(jnp.bfloat16)
    second_rows = lax.all_gather(normed_two, "tensor", axis=0, tiled=True)
    hidden_pre = jnp.dot(second_rows, up_full, preferred_element_type=jnp.float32) + bias_up
    hidden_act = gelu_exact(hidden_pre).astype(jnp.bfloat16)
    taken = hidden_act
    mlp_total = lax.psum_scatter(
        jnp.dot(taken, down_full, preferred_element_type=jnp.float32).astype(jnp.bfloat16),
        "tensor",
        scatter_dimension=0,
        tiled=True,
    ).astype(jnp.float32)
    feed = mlp_total + b_fc2
    result = middle + feed
    activations = (result * own_valid).astype(jnp.bfloat16)
    squares = jnp.stack(
        [
            jnp.sum(own_valid * member * member)
            for member in (stream_f, middle, result, branch, feed)
        ]
    )
    square_sums, valid_count = lax.psum((squares, jnp.sum(own_valid)), ("dp", "tensor"))
    rms_stats = jnp.sqrt(square_sums / (valid_count * width))
    d_result = cotangent.astype(jnp.float32) * own_valid
    d_feed_low = d_result.astype(jnp.bfloat16)
    d_feed_rows = lax.all_gather(d_feed_low, "tensor", axis=0, tiled=True)
    d_act = jnp.einsum("rd,ud->ru", d_feed_rows, down_full, preferred_element_type=jnp.float32)
    unused_act, gelu_pullback = jax.vjp(gelu_exact, hidden_pre)
    d_pre = gelu_pullback(d_act)[0].astype(jnp.bfloat16)
    grad_down = jnp.einsum("ru,rd->ud", hidden_act, d_feed_rows, preferred_element_type=jnp.float32)
    grad_up = jnp.einsum("rd,ru->du", second_rows, d_pre, preferred_element_type=jnp.float32)
    grad_bias_up = jnp.sum(d_pre, axis=0, dtype=jnp.float32)
    grad_bias_down = jnp.sum(d_feed_low, axis=0, dtype=jnp.float32)
    taken = d_pre
    d_normed_two = lax.psum_scatter(
        jnp.einsum("ru,du->rd", taken, up_full, preferred_element_type=jnp.float32).astype(
            jnp.bfloat16
        ),
        "tensor",
        scatter_dimension=0,
        tiled=True,
    ).astype(jnp.float32)
    unused_two, norm_two_pullback = jax.vjp(layer_norm, middle, gain_two, shift_two)
    d_middle_norm, grad_gain_two, grad_shift_two = norm_two_pullback(d_normed_two)
    d_middle = d_result + d_middle_norm
    d_branch_low = d_middle.astype(jnp.bfloat16)
    grad_bias_out = jnp.sum(d_branch_low, axis=0, dtype=jnp.float32)
    d_branch_rows = lax.all_gather(d_branch_low, "tensor", axis=0, tiled=True)
    d_attn = jnp.einsum(
        "rd,hd->rh", d_branch_rows, out_full, preferred_element_type=jnp.float32
    ).astype(jnp.bfloat16)
    grad_out = jnp.einsum(
        "rh,rd->hd", attn_heads, d_branch_rows, preferred_element_type=jnp.float32
    )
    d_queries, d_keys, d_values = lax.map(
        attend_back,
        (queries, key_rows, values, blocked_valid, log_total, d_attn.reshape(shape_heads)),
    )
    d_projected = jnp.stack(
        [
            d_queries.reshape(group_rows, head_width),
            d_keys.reshape(group_rows, head_width),
            d_values.reshape(group_rows, head_width),
        ],
        axis=1,
    )
    grad_qkv = jnp.einsum(
        "rd,rce->cde", first_rows, d_projected, preferred_element_type=jnp.float32
    )
    bias_terms = jnp.sum(d_projected, axis=0, dtype=jnp.float32)
    taken = d_projected
    d_normed_one = lax.psum_scatter(
        jnp.einsum("rce,cde->rd", taken, qkv_full, preferred_element_type=jnp.float32).astype(
            jnp.bfloat16
        ),
        "tensor",
        scatter_dimension=0,
        tiled=True,
    ).astype(jnp.float32)
    unused_one, norm_one_pullback = jax.vjp(layer_norm, stream_f, gain_one, shift_one)
    d_stream_norm, grad_gain_one, grad_shift_one = norm_one_pullback(d_normed_one)
    grad_input = d_middle + d_stream_norm
    grad_up = grad_up[None]
    bias_qv_full = lax.dynamic_update_slice(
        jnp.zeros((2, width), jnp.float32),
        jnp.stack([bias_terms[0], bias_terms[2]]),
        (jnp.int32(0), tensor_pos * head_width),
    )
    bias_up_full = lax.dynamic_update_slice(
        jnp.zeros((b_fc1.shape[0],), jnp.float32), grad_bias_up, (tensor_pos * unit_width,)
    )
    qkv_part, out_part, up_part, down_part = (
        lax.psum_scatter(
            grad_qkv.astype(jnp.bfloat16), "dp", scatter_dimension=1, tiled=True
        ).astype(jnp.float32),
        lax.psum_scatter(
            grad_out.astype(jnp.bfloat16), "dp", scatter_dimension=1, tiled=True
        ).astype(jnp.float32),
        lax.psum_scatter(
            grad_up.astype(jnp.bfloat16), "dp", scatter_dimension=1, tiled=True
        ).astype(jnp.float32),
        lax.psum_scatter(
            grad_down.astype(jnp.bfloat16), "dp", scatter_dimension=1, tiled=True
        ).astype(jnp.float32),
    )
    small_parts = (
        lax.psum_scatter(bias_qv_full, ("dp", "tensor"), scatter_dimension=1, tiled=True),
        lax.psum_scatter(grad_bias_out, ("dp", "tensor"), scatter_dimension=0, tiled=True),
        lax.psum_scatter(bias_up_full, ("dp", "tensor"), scatter_dimension=0, tiled=True),
        lax.psum_scatter(grad_bias_down, ("dp", "tensor"), scatter_dimension=0, tiled=True),
        lax.psum_scatter(grad_gain_one, ("dp", "tensor"), scatter_dimension=0, tiled=True),
        lax.psum_scatter(grad_shift_one, ("dp", "tensor"), scatter_dimension=0, tiled=True),
        lax.psum_scatter(grad_gain_two, ("dp", "tensor"), scatter_dimension=0, tiled=True),
        lax.psum_scatter(grad_shift_two, ("dp", "tensor"), scatter_dimension=0, tiled=True),
    )
    return (
        activations,
        grad_input,
        qkv_part,
        small_parts[0],
        out_part,
        small_parts[1],
        up_part[0],
        small_parts[2],
        down_part,
        small_parts[3],
        small_parts[4],
        small_parts[5],
        small_parts[6],
        small_parts[7],
        rms_stats,
    )


def solution(mesh):
    fast = mesh.shape["dp"] == 16 and mesh.shape["tensor"] == 2
    return jax.shard_map(
        local_fast if fast else local,
        mesh=mesh,
        in_specs=(
            P(("dp", "tensor"), None),
            P("dp"),
            P(("dp", "tensor"), None),
            P(None, "dp", "tensor"),
            P(),
            P("tensor", "dp"),
            P(),
            P("dp", "tensor"),
            P(),
            P("tensor", "dp"),
            P(),
            P(),
            P(),
            P(),
            P(),
        ),
        out_specs=(
            P(("dp", "tensor"), None),
            P(("dp", "tensor"), None),
            P(None, "dp", "tensor"),
            P(None, ("dp", "tensor")),
            P("tensor", "dp"),
            P(("dp", "tensor")),
            P("dp", "tensor"),
            P(("dp", "tensor")),
            P("tensor", "dp"),
            P(("dp", "tensor")),
            P(("dp", "tensor")),
            P(("dp", "tensor")),
            P(("dp", "tensor")),
            P(("dp", "tensor")),
            P(),
        ),
        check_vma=False,
    )
```

```python
import jax
import jax.numpy as jnp
from jax import lax
from jax.experimental import pallas as pl
from jax.experimental.pallas import tpu as pltpu
from jax.sharding import PartitionSpec as P

HD = 64
BUFFER = 64
SLOTS = 320


eps_norm = 1e-06


MESH = pl.DeviceIdType.MESH


class Place:
    def __init__(self):
        dp = lax.axis_index("dp")
        self.t = lax.axis_index("tensor")
        self.z, self.y, self.x = dp // 4, (dp // 2) % 2, dp % 2
        self.side = self.z // 2
        self.w = self.z + self.side * (3 - 2 * self.z)
        self.step = 1 - 2 * self.side
        self.dp = dp

    def order(self, k):
        o = (self.w, 1 - self.w, 2, 3)[k]
        return 3 * self.side + self.step * o

    def chip(self, z, y, x):
        return z * 4 + y * 2 + x

    def inward(self):
        return (self.chip(self.z + self.step, self.y, self.x), self.t)

    def outward(self):
        return (self.chip(self.z - self.step, self.y, self.x), self.t)

    def across_x(self):
        return (self.chip(self.z, self.y, 1 - self.x), self.t)

    def across_y(self):
        return (self.chip(self.z, 1 - self.y, self.x), self.t)

    def near(self):
        return (self.chip(self.z + 1 - 2 * (self.z % 2), self.y, self.x), self.t)

    def far(self):
        return (self.chip((self.z + 2) % 4, self.y, self.x), self.t)

    def twin(self):
        return (self.dp, 1 - self.t)


def greet(at):
    barrier = pltpu.get_barrier_semaphore()
    for other in (at.across_x(), at.across_y(), at.inward(), at.twin(), at.far()):
        pl.semaphore_signal(barrier, inc=1, device_id=other, device_id_type=MESH)

    @pl.when(at.w == 1)
    def _():
        pl.semaphore_signal(barrier, inc=1, device_id=at.outward(), device_id_type=MESH)


def enter(at):
    pl.semaphore_wait(pltpu.get_barrier_semaphore(), 5 + at.w)


def settle(ref, sem, at, sent):
    copy = pltpu.make_async_remote_copy(
        src_ref=ref, dst_ref=ref, send_sem=sem, recv_sem=sem, device_id=at.twin(), device_id_type=MESH
    )
    if sent:
        copy.wait_send()
    else:
        copy.wait_recv()


class Gather:
    def __init__(self, at, full, shard, pieces, send, recv):
        self.at, self.full, self.shard, self.pieces, self.send, self.recv = at, full, shard, pieces, send, recv

    def rows(self, p, z, y, x, part=None):
        c0, c1 = self.pieces[p]
        start, size = self.at.chip(z, y, x) * self.shard, self.shard
        if part is not None:
            size = self.shard // 2
            start = start + part * size
        return self.full.at[pl.ds(pl.multiple_of(start, size), size), pl.ds(c0, c1 - c0)]

    def copy(self, p, ref, s, r, other):
        return pltpu.make_async_remote_copy(
            src_ref=ref,
            dst_ref=ref,
            send_sem=self.send.at[s],
            recv_sem=self.recv.at[p, r],
            device_id=other,
            device_id_type=MESH,
        )

    def z_in(self, p, z):
        return self.copy(p, self.rows(p, z, self.at.y, self.at.x), 1, z, self.at.inward())

    def z_out(self, p, z):
        return self.copy(p, self.rows(p, z, self.at.y, self.at.x), 1, z, self.at.outward())

    def x_full(self, p, z):
        return self.copy(p, self.rows(p, z, self.at.y, self.at.x), 0, 4 + z, self.at.across_x())

    def y_full(self, p, z):
        return self.copy(p, self.rows(p, z, self.at.y, self.at.x), 0, 8 + z, self.at.across_y())

    def x_half(self, p, z):
        return self.copy(p, self.rows(p, z, 1 - self.at.y, self.at.x, 1), 0, 12, self.at.across_x())

    def y_half(self, p, z):
        return self.copy(p, self.rows(p, z, self.at.y, 1 - self.at.x, 0), 0, 12, self.at.across_y())

    def arrived(self, p, kind, z):
        at = self.at
        ref = (
            lambda: self.rows(p, z, at.y, at.x),
            lambda: self.rows(p, z, at.y, 1 - at.x),
            lambda: self.rows(p, z, 1 - at.y, at.x),
        )[kind]()
        settle(ref, self.recv.at[p, 4 * kind + z], at, False)

    def line(self, p, k, w):
        at = self.at

        @pl.when(at.w == w)
        def _():
            z = at.order(k)
            if k > 0:
                self.arrived(p, 0, z)
            if k == 0 or (k == 1 and w == 1):
                self.z_in(p, z).start()
            if w == 1 and k != 1:
                self.z_out(p, z).start()
            self.x_full(p, z).start()
            self.y_full(p, z).start()

    def plane(self, p, k):
        z = self.at.order(k)
        self.arrived(p, 1, z)
        self.y_half(p, z).start()
        self.arrived(p, 2, z)
        self.x_half(p, z).start()

    def finish(self, p):
        c0, c1 = self.pieces[p]
        settle(self.full.at[0 : 4 * self.shard, c0:c1], self.recv.at[p, 12], self.at, False)

    def drain(self):
        n = sum(c1 - c0 for c0, c1 in self.pieces)
        settle(self.full.at[0 : 12 * self.shard, 0:n], self.send.at[0], self.at, True)
        for w, blocks in ((0, 1), (1, 5)):

            @pl.when(self.at.w == w)
            def _(blocks=blocks):
                settle(self.full.at[0 : blocks * self.shard, 0:n], self.send.at[1], self.at, True)


class Scatter:
    def __init__(self, at, full, shard, pieces, xh, yh, xf, yf, zl, send, recv):
        self.at, self.full, self.shard, self.pieces = at, full, shard, pieces
        self.xh, self.yh, self.xf, self.yf, self.zl = xh, yh, xf, yf, zl
        self.send, self.recv = send, recv

    def cols(self, p):
        c0, c1 = self.pieces[p]
        return pl.ds(c0, c1 - c0)

    def rows(self, p, z, y, x, part=None):
        start, size = self.at.chip(z, y, x) * self.shard, self.shard
        if part is not None:
            size = self.shard // 2
            start = start + part * size
        ref, c0, c1 = self.full(p)
        return ref.at[pl.ds(pl.multiple_of(start, size), size), pl.ds(c0, c1 - c0)]

    def copy(self, p, src, dst, r, other):
        return pltpu.make_async_remote_copy(
            src_ref=src,
            dst_ref=dst,
            send_sem=self.send.at[0],
            recv_sem=self.recv.at[p, r],
            device_id=other,
            device_id_type=MESH,
        )

    def x_half(self, p, z):
        at = self.at
        return self.copy(
            p, self.rows(p, z, 1 - at.y, 1 - at.x, 0), self.xh.at[z, :, self.cols(p)], z, at.across_x()
        )

    def y_half(self, p, z):
        at = self.at
        return self.copy(
            p, self.rows(p, z, 1 - at.y, 1 - at.x, 1), self.yh.at[z, :, self.cols(p)], z, at.across_y()
        )

    def x_full(self, p, z):
        at = self.at
        return self.copy(
            p, self.rows(p, z, at.y, 1 - at.x), self.xf.at[z, :, self.cols(p)], 4 + z, at.across_x()
        )

    def y_full(self, p, z):
        at = self.at
        return self.copy(
            p, self.rows(p, z, 1 - at.y, at.x), self.yf.at[z, :, self.cols(p)], 4 + z, at.across_y()
        )

    def z_in(self, p, z, slot):
        at = self.at
        return self.copy(
            p, self.rows(p, z, at.y, at.x), self.zl.at[slot, :, self.cols(p)], 8 + slot, at.inward()
        )

    def z_out(self, p, z, slot):
        at = self.at
        return self.copy(
            p, self.rows(p, z, at.y, at.x), self.zl.at[slot, :, self.cols(p)], 8 + slot, at.outward()
        )

    def begin(self, p, k):
        z = self.at.order(k)
        self.x_half(p, z).start()
        self.y_half(p, z).start()

    def plane(self, p, k):
        at = self.at
        z = at.order(k)
        settle(self.xf.at[z, :, self.cols(p)], self.recv.at[p, z], at, False)
        ref = self.rows(p, z, 1 - at.y, at.x, 0)
        ref[...] = ref[...] + self.xh[z, :, self.cols(p)]
        self.y_full(p, z).start()
        ref = self.rows(p, z, at.y, 1 - at.x, 1)
        ref[...] = ref[...] + self.yh[z, :, self.cols(p)]
        self.x_full(p, z).start()

    def wait_line(self, p, z, slot):
        self.z_in(p, z, slot).wait_recv()

    def line(self, p, k, w, out):
        at = self.at

        @pl.when(at.w == w)
        def _():
            z = at.order(k)
            full, c0, c1 = self.full(p)
            settle(full.at[0 : 2 * self.shard, c0:c1], self.recv.at[p, 4 + z], at, False)
            ref = self.rows(p, z, at.y, at.x)
            parts = [self.xf.at[z, :, self.cols(p)], self.yf.at[z, :, self.cols(p)]]
            if w == 1:
                self.wait_line(p, z, z)
                parts.append(self.zl.at[z, :, self.cols(p)])
            if k == 0:
                self.wait_line(p, z, 4)
                parts.append(self.zl.at[4, :, self.cols(p)])
            total = ref[...].astype(jnp.float32)
            for part in parts:
                total = total + part[...].astype(jnp.float32)
            if k == 0:
                out(total)
            else:
                ref[...] = total.astype(jnp.bfloat16)
                if w == 0 or k == 3:
                    self.z_in(p, z, z).start()
                elif k == 2:
                    self.z_in(p, z, 4).start()
                else:
                    self.z_out(p, z, 4).start()

    def drain(self, ref):
        settle(ref, self.send.at[0], self.at, True)


class PairGather:
    def __init__(self, at, full, shard, columns, sources, send, recv):
        self.at, self.full, self.shard, self.columns, self.sources = at, full, shard, columns, sources
        self.send, self.recv = send, recv

    def far_x(self, h):
        return self.at.x if h == 0 else 1 - self.at.x

    def rows(self, m, z, y, x):
        c0, n = self.columns[m]
        start = self.at.chip(z, y, x) * self.shard
        return self.full.at[pl.ds(pl.multiple_of(start, self.shard), self.shard), pl.ds(c0, n)]

    def copy(self, m, src, dst, s, r, other):
        return pltpu.make_async_remote_copy(
            src_ref=src,
            dst_ref=dst,
            send_sem=self.send.at[s],
            recv_sem=self.recv.at[m, r],
            device_id=other,
            device_id_type=MESH,
        )

    def x_copy(self, m):
        at = self.at
        c0, n = self.columns[m]
        src = self.sources[m].at[:, pl.ds(pl.multiple_of((1 - at.x) * n, n), n)]
        return self.copy(m, src, self.rows(m, at.z, at.y, at.x), 0, 8, at.across_x())

    def z_in(self, m, h, z):
        ref = self.rows(m, z, self.at.y, self.far_x(h))
        return self.copy(m, ref, ref, 1, 4 * h + z, self.at.inward())

    def z_out(self, m, h, z):
        ref = self.rows(m, z, self.at.y, self.far_x(h))
        return self.copy(m, ref, ref, 1, 4 * h + z, self.at.outward())

    def y_copy(self, m, h, z):
        ref = self.rows(m, z, self.at.y, self.far_x(h))
        return self.copy(m, ref, ref, 0, 9, self.at.across_y())

    def line(self, m, h, k, w):
        at = self.at

        @pl.when(at.w == w)
        def _():
            z = at.order(k)
            ref = self.rows(m, z, at.y, self.far_x(h))
            if k > 0:
                settle(ref, self.recv.at[m, 4 * h + z], at, False)
            elif h == 1:
                settle(ref, self.recv.at[m, 8], at, False)
            if k == 0 or (k == 1 and w == 1):
                self.z_in(m, h, z).start()
            if w == 1 and k != 1:
                self.z_out(m, h, z).start()

    def cross(self, m, h, k, w):
        @pl.when(self.at.w == w)
        def _():
            self.y_copy(m, h, self.at.order(k)).start()

    def finish(self, m):
        c0, n = self.columns[m]
        settle(self.full.at[0 : 8 * self.shard, pl.ds(c0, n)], self.recv.at[m, 9], self.at, False)

    def drain(self, ref):
        settle(ref.at[0 : 18 * self.shard, :], self.send.at[0], self.at, True)
        for w, blocks in ((0, 4), (1, 20)):

            @pl.when(self.at.w == w)
            def _(blocks=blocks):
                settle(ref.at[0 : blocks * self.shard, :], self.send.at[1], self.at, True)


class PairScatter:
    def __init__(self, at, full, shard, first, units, xs, xr, send, recv):
        self.at, self.full, self.shard, self.first = at, full, shard, first
        self.units, self.xs, self.xr, self.send, self.recv = units, xs, xr, send, recv
        self.base = {1: 0, 0: 11 if 1 in first else 9}

    def unit(self, m, z, y):
        ref, c0, n = self.full(m)
        size = 2 * self.shard
        return ref.at[pl.ds(pl.multiple_of((z * 2 + y) * size, size), size), pl.ds(c0, n)]

    def copy(self, m, src, dst, r, other):
        return pltpu.make_async_remote_copy(
            src_ref=src,
            dst_ref=dst,
            send_sem=self.send.at[0],
            recv_sem=self.recv.at[m, r],
            device_id=other,
            device_id_type=MESH,
        )

    def from_y(self, m, z):
        return self.units.at[self.base[m] + (10 if m in self.first else z)]

    def from_z(self, m, col, slot):
        return self.units.at[self.base[m] + (5 * col if m in self.first else 4) + slot]

    def column(self, col):
        return self.at.y if col == 0 else 1 - self.at.y

    def y_copy(self, m, z):
        return self.copy(m, self.unit(m, z, 1 - self.at.y), self.from_y(m, z), 10 if m in self.first else z, self.at.across_y())

    def z_copy(self, m, col, z, slot, other):
        return self.copy(
            m, self.unit(m, z, self.column(col)), self.from_z(m, col, slot), (5 * col if m in self.first else 4) + slot, other
        )

    def x_copy(self, m):
        return self.copy(m, self.xs.at[m], self.xr.at[m], 11, self.at.across_x())

    def begin(self, m, k):
        self.y_copy(m, self.at.order(k)).start()

    def pass_on(self, m, col, k, w):
        at = self.at
        z = at.order(k)
        if w == 0:
            self.z_copy(m, col, z, z, at.inward()).start()
        elif k == 1:
            self.z_copy(m, col, z, 4, at.outward()).start()
        else:
            self.z_copy(m, col, z, z if k == 3 else 4, at.inward()).start()

    def add_line(self, m, col, k, w, extra):
        at = self.at
        z = at.order(k)
        ref = self.unit(m, z, self.column(col))
        parts = list(extra)
        if k == 0:
            self.z_copy(m, col, z, 4, at.inward()).wait_recv()
            parts.append(self.from_z(m, col, 4))
        if w == 1:
            self.z_copy(m, col, z, z, at.inward()).wait_recv()
            parts.append(self.from_z(m, col, z))
        if parts:
            v = ref[...].astype(jnp.float32)
            for part in parts:
                v = v + part[...].astype(jnp.float32)
            ref[...] = v.astype(jnp.bfloat16)

    def finish(self, m, out, second):
        at = self.at
        size = self.shard
        full, c0, n = self.full(m)

        def total(x):
            rows = pl.ds(pl.multiple_of(at.chip(at.z, at.y, x) * size, size), size)
            v = full[rows, pl.ds(c0, n)].astype(jnp.float32)
            if second:
                v = v + self.from_y(m, at.z)[pl.ds(pl.multiple_of(x * size, size), size), :].astype(jnp.float32)
            return v

        self.xs[m] = total(1 - at.x).astype(jnp.bfloat16)
        self.x_copy(m).start()
        out(at.x, total(at.x))

    def line(self, m, k, w, out):
        at = self.at

        @pl.when(at.w == w)
        def _():
            z = at.order(k)
            self.y_copy(m, z).wait_recv()
            self.add_line(m, 0, k, w, [self.from_y(m, z)])
            if k > 0:
                self.pass_on(m, 0, k, w)
            else:
                self.finish(m, out, False)

    def line_first(self, m, col, k, w):
        @pl.when(self.at.w == w)
        def _():
            self.add_line(m, col, k, w, [])
            if k > 0:
                self.pass_on(m, col, k, w)
            elif col == 1:
                self.y_copy(m, self.at.z).start()

    def meet(self, m, out):
        self.y_copy(m, self.at.z).wait_recv()
        self.finish(m, out, True)

    def last(self, m, out):
        self.x_copy(m).wait_recv()
        out(1 - self.at.x, self.xr[m].astype(jnp.float32))

    def drain(self, ref):
        settle(ref, self.send.at[0], self.at, True)


QKV, OUT, UP, DOWN, COLS = 0, 1536, 2048, 3072, 4096
PIECES = ((0, 384), (384, 768), (768, 1152), (1152, 1536), (1536, 2048))
LINE_FIRST = ()
PLAN = (
    ((0, 3, 0, 1), (0, 0, 0, 1), (0, 2, 0, 1), (0, 3, 0, 0), (3, 1, 0, 0, 0), (0, 0, 0, 0), (0, 1, 0, 0), (0, 3, 1, 1), (3, 0, 0, 0, 1), (0, 3, 1, 0), (4, 1, 0, 0, 0), (0, 4, 0, 1), (0, 1, 0, 1), (0, 2, 0, 0), (0, 2, 1, 0), (3, 1, 0, 0, 1), (0, 0, 1, 1), (3, 0, 0, 0, 0), (4, 0, 0, 0, 1), (2, 0), (0, 0, 1, 0), (0, 0, 2, 1), (3, 0, 0, 1, 0), (4, 0, 0, 0, 0), (0, 1, 1, 1), (1, 2, 0), (0, 3, 2, 1), (0, 1, 2, 1), (3, 0, 1, 0, 0), (3, 0, 0, 1, 1), (1, 1, 0), (0, 4, 0, 0), (0, 4, 1, 0), (1, 0, 0), (0, 0, 2, 0), (0, 2, 1, 1), (0, 2, 2, 1), (0, 1, 1, 0), (0, 1, 2, 0), (0, 3, 2, 0), (0, 0, 3, 1), (0, 4, 1, 1), (2, 1), (3, 1, 0, 1, 1), (0, 0, 3, 0), (0, 2, 2, 0), (0, 1, 3, 1), (1, 0, 1), (3, 1, 0, 2, 1), (1, 3, 0), (1, 0, 2), (0, 3, 3, 1), (0, 1, 3, 0), (1, 0, 3), (0, 2, 3, 1), (3, 0, 0, 2, 1), (3, 1, 0, 3, 1), (1, 2, 1), (0, 2, 3, 0), (1, 3, 1),),
    ((1, 1, 1), (0, 4, 2, 1), (1, 1, 2),),
    ((1, 1, 3), (0, 4, 3, 1), (1, 2, 2), (3, 0, 1, 0, 1), (3, 1, 1, 0, 0), (3, 0, 0, 2, 0), (0, 3, 3, 0),),
    ((3, 1, 1, 0, 1), (1, 3, 2), (1, 2, 3), (3, 0, 1, 1, 1), (0, 4, 2, 0), (0, 4, 3, 0), (4, 0, 0, 1, 0), (4, 1, 0, 0, 1), (1, 3, 3),),
    (),
    ((4, 0, 1, 0, 1), (1, 4, 0), (1, 4, 1), (4, 0, 1, 0, 0), (1, 4, 2), (3, 0, 0, 3, 1),),
    ((4, 1, 1, 0, 1), (1, 4, 3),),
    ((3, 0, 1, 1, 0), (3, 1, 1, 1, 1), (5,), (4, 0, 1, 1, 1),),
    (),
    ((3, 0, 1, 2, 1), (4, 0, 0, 1, 1),),
    ((4, 0, 0, 2, 0),),
    (),
    ((3, 1, 0, 1, 0),),
    ((3, 0, 0, 3, 0), (3, 1, 1, 1, 0), (3, 0, 1, 3, 1),),
    (),
    (),
    ((3, 1, 1, 2, 1), (3, 0, 1, 2, 0), (4, 1, 0, 1, 0), (4, 0, 0, 2, 1), (4, 0, 1, 2, 1),),
    (),
    (),
    ((3, 1, 1, 3, 1), (4, 0, 0, 3, 1),),
    ((4, 0, 1, 3, 1), (4, 1, 0, 1, 1), (4, 1, 1, 1, 1), (4, 0, 1, 1, 0), (4, 0, 1, 2, 0), (3, 0, 1, 3, 0), (4, 0, 1, 3, 0), (3, 1, 0, 2, 0),),
    ((4, 1, 0, 2, 1),),
    ((4, 0, 0, 3, 0), (3, 1, 0, 3, 0), (3, 1, 1, 2, 0), (3, 1, 1, 3, 0),),
    (),
    (),
    ((4, 1, 0, 3, 1), (4, 1, 1, 0, 0), (4, 1, 1, 1, 0),),
    (),
    (),
    ((4, 1, 1, 2, 1), (4, 1, 0, 2, 0), (4, 1, 0, 3, 0), (4, 1, 1, 2, 0), (4, 1, 1, 3, 0), (4, 1, 1, 3, 1),),
    (),
    (),
    (),
    (),
    (),
    (),
    (),
    (),
    ((13, 1, 3), (13, 1, 2), (13, 1, 1), (13, 1, 0),),
    (),
    (),
    (),
    (),
    (),
    ((14, 1, 3, 0),),
    (),
    (),
    ((14, 1, 2, 0),),
    (),
    (),
    ((13, 0, 3),),
    ((14, 1, 3, 1),),
    ((13, 0, 2), (13, 0, 1),),
    (),
    (),
    (),
    (),
    (),
    (),
    (),
    (),
    (),
    (),
    (),
    ((14, 0, 3, 0),),
    (),
    (),
    ((10, 4, 3),),
    ((14, 1, 1, 0), (10, 0, 3),),
    (),
    ((14, 1, 2, 1), (14, 1, 1, 1), (14, 0, 2, 0), (10, 4, 2),),
    ((14, 0, 3, 1), (10, 4, 1), (10, 1, 3),),
    ((10, 4, 0),),
    ((11, 4, 3),),
    ((10, 2, 3), (10, 2, 2), (11, 4, 2), (10, 1, 2), (10, 1, 1), (14, 0, 1, 0),),
    ((10, 2, 1), (11, 1, 3), (12, 4, 3, 0), (10, 1, 0),),
    ((14, 1, 0, 0), (10, 0, 2), (11, 4, 1),),
    ((13, 0, 0), (11, 4, 0),),
    (),
    (),
    ((10, 2, 0), (11, 2, 3), (14, 1, 0, 1),),
    ((11, 0, 3),),
    ((14, 0, 2, 1), (11, 1, 2), (11, 2, 2),),
    ((10, 3, 3), (10, 3, 2), (10, 3, 1),),
    (),
    (),
    ((11, 1, 1), (12, 1, 3, 0), (10, 0, 1), (12, 4, 3, 1), (14, 0, 1, 1), (12, 4, 2, 0), (11, 0, 2), (12, 1, 2, 0), (11, 3, 3),),
    (),
    ((11, 2, 1), (12, 1, 3, 1), (12, 2, 3, 0), (11, 3, 2), (12, 2, 2, 0), (11, 3, 1), (12, 0, 3, 0), (12, 4, 2, 1), (12, 4, 1, 1),),
    (),
    ((10, 3, 0), (12, 1, 2, 1), (12, 3, 3, 0), (12, 2, 3, 1), (11, 2, 0), (12, 1, 1, 1), (12, 0, 2, 0), (10, 0, 0), (11, 1, 0), (12, 3, 2, 0),),
    (),
    ((12, 0, 3, 1), (11, 0, 1), (12, 4, 1, 0), (12, 3, 3, 1), (14, 0, 0, 0), (14, 0, 0, 1), (12, 2, 2, 1), (12, 2, 1, 0), (12, 2, 1, 1),),
    (),
    ((12, 3, 1, 0), (12, 1, 1, 0), (12, 3, 2, 1), (12, 3, 1, 1), (11, 3, 0), (11, 0, 0), (12, 0, 1, 0), (12, 0, 2, 1), (12, 0, 1, 1), (12, 1, 0, 0),),
    (),
    ((12, 4, 0, 1), (12, 2, 0, 0), (15, 0), (15, 1), (12, 1, 0, 1), (12, 4, 0, 0), (12, 3, 0, 0), (12, 2, 0, 1), (12, 3, 0, 1), (12, 0, 0, 1), (12, 0, 0, 0),),
)
BF, F32 = jnp.bfloat16, jnp.float32
SUMS = ("bq", "bv", "bout", "bdown", "g1", "s1", "g2", "s2", "x", "mid", "res", "branch", "feed")
BLOCK = 32


def nn(a, b):
    return lax.dot_general(a, b, (((1,), (0,)), ((), ())), preferred_element_type=F32)


def nt(a, b):
    return lax.dot_general(a, b, (((1,), (1,)), ((), ())), preferred_element_type=F32)


def tn(a, b):
    return lax.dot_general(a, b, (((0,), (0,)), ((), ())), preferred_element_type=F32)


def at_rows(start, size):
    return pl.ds(pl.multiple_of(start, size), size)


def fold(v):
    return jnp.sum(v.reshape(v.shape[0] // 8, 8, v.shape[1]), axis=0)


def normed(v):
    centre = jnp.mean(v, axis=1, keepdims=True)
    offset = v - centre
    r = lax.rsqrt(jnp.mean(offset * offset, axis=1, keepdims=True) + eps_norm)
    return offset * r, r


def norm_back(dy, n, r, gain):
    dn = dy * gain
    first = jnp.mean(dn, axis=1, keepdims=True)
    second = jnp.mean(dn * n, axis=1, keepdims=True)
    return r * (dn - first - n * second)


def block_kernel(
    counts, x_hbm, cot_hbm, wqkv, wout, wup, wdown, bqv, bout, bup, bdown, g1, s1, g2, s2,
    act_hbm, gin_hbm, qkv_hbm, out_hbm, up_hbm, down_hbm, o_sums,
    x_ref, cot_ref, act_out, gin_out, o_qkv, o_out, o_up, o_down,
    W, G2, G3, xh, yh, xf, yf, zl, units, xs2, xr2,
    rows1, dfeed, qkv, probs, heads, mid, rows2, act, gp, datt,
    own_a, own_c, send_t, send_x, got, got_t, acc, acc_up, sums, sums_got,
    sem_in, ag_send, ag_recv, pg_send, pg_recv, rs_send, rs_recv, ps_send, ps_recv,
    pair_send, pair_recv, sums_send, sums_recv,
):
    at = Place()
    greet(at)
    rows_in = [pltpu.make_async_copy(a, b, sem_in.at[1 + i]) for i, (a, b) in enumerate(((x_hbm, x_ref), (cot_hbm, cot_ref)))]
    for c in rows_in:
        c.start()
    t, x = at.t, at.x
    shard = wup.shape[0]
    own = x_ref.shape[0]
    width = x_ref.shape[1]
    dbr = dfeed.at[0 : 2 * own, :]
    dproj = qkv

    def spot(far_x, far_t):
        return at_rows((far_x * 2 + far_t) * own, own)

    mine, theirs = at_rows(t * own, own), at_rows((1 - t) * own, own)

    here = at_rows(at.dp * shard, shard)
    quarter = pl.ds(pl.multiple_of(x * 1024, 1024), 1024)
    loads = [
        pltpu.make_async_copy(src, W.at[here, pl.ds(c0, n)], sem_in.at[0])
        for src, c0, n in (
            [(wqkv.at[j, :, pl.ds(128 * h, 128)], QKV + 384 * h + 128 * j, 128) for h in range(4) for j in range(3)]
            + [(wout, OUT, 512), (wup.at[:, quarter], UP, 1024), (wdown.at[:, quarter], DOWN, 1024)]
        )
    ]
    for c in loads:
        c.start()
    enter(at)
    g = Gather(at, W, shard, PIECES, ag_send, ag_recv)
    pg = PairGather(at, W, shard, ((UP, 1024), (DOWN, 1024)), (wup, wdown), pg_send, pg_recv)
    pltpu.make_async_copy(W.at[here, :], W.at[here, :], sem_in.at[0]).wait()

    home = {0: (W, DOWN, DOWN + 384), 1: (W, DOWN + 384, DOWN + 768), 2: (G3, 512, 896), 3: (W, OUT, OUT + 384), 4: (G3, 0, 512)}
    sc = Scatter(at, lambda p: home[p], shard, PIECES, xh, yh, xf, yf, zl, rs_send, rs_recv)
    home_pair = {0: (W, UP, 1024), 1: (G2, 0, 1024)}
    ps = PairScatter(at, lambda m: home_pair[m], shard, LINE_FIRST, units, xs2, xr2, ps_send, ps_recv)

    def write(p):
        def store(total):
            if p < 4:
                for j in range(3):
                    o_qkv[j, :, 128 * p : 128 * (p + 1)] = total[:, 128 * j : 128 * (j + 1)]
            else:
                o_out[...] = total
        return store

    def write_pair(m):
        ref = o_up if m == 0 else o_down

        def store(far_x, total):
            ref[:, pl.ds(pl.multiple_of(far_x * 1024, 1024), 1024)] = total
        return store

    def share_feed():
        shares.append(share(2, dfeed, spot(x, t), at.across_x()))

    actions = {
        0: g.line, 1: g.plane, 2: lambda m: pg.x_copy(m).start(), 3: pg.line, 4: pg.cross, 5: share_feed,
        10: sc.begin, 11: sc.plane, 12: lambda p, k, w: sc.line(p, k, w, write(p)),
        13: ps.begin, 14: lambda m, k, w: ps.line(m, k, w, write_pair(m)), 15: lambda m: ps.last(m, write_pair(m)),
        16: ps.line_first, 17: lambda m: ps.meet(m, write_pair(m)),
    }
    done = [0]

    def run(part):
        while done[0] <= min(part, len(PLAN) - 1):
            for kind, *a in PLAN[done[0]]:
                actions[kind](*a)
            done[0] += 1

    def quiet(part):
        return part >= len(PLAN) or not PLAN[part]

    def send(i, src, dst, other):
        return pltpu.make_async_remote_copy(
            src_ref=src, dst_ref=dst, send_sem=pair_send.at[i], recv_sem=pair_recv.at[i],
            device_id=other, device_id_type=MESH,
        )

    def share(i, ref, r, other):
        c = send(i, ref.at[r, :], ref.at[r, :], other)
        c.start()
        return c

    def take(i, ref, r):
        send(i, ref.at[r, :], ref.at[r, :], at.twin()).wait_recv()

    for ref in (acc, acc_up):
        ref[...] = jnp.zeros_like(ref)
    total_of = {name: acc.at[i] for i, name in enumerate(SUMS)}

    def add(name, v):
        ref = total_of[name]
        ref[...] += fold(v)

    def valid_of(image, start, size):
        slot = lax.broadcasted_iota(jnp.int32, (size, 1), 0) + start
        return slot < counts[image] + BUFFER

    def each_block(body):
        def go(b, _):
            body(b * BLOCK, pl.ds(pl.multiple_of(b * BLOCK, BLOCK), BLOCK))
            return 0
        lax.fori_loop(0, own // BLOCK, go, 0)

    def tiles(first, last, body, size=256):
        def go(i, _):
            body(pl.multiple_of(i * size, size))
            return 0
        lax.fori_loop(first // size, last // size, go, 0)

    def first_norm(b, r):
        xv = x_ref[r, :].astype(F32)
        keep = valid_of(t, b, BLOCK).astype(F32)
        n, _ = normed(xv)
        mine_b = pl.ds(pl.multiple_of(t * own + b, BLOCK), BLOCK)
        rows1[mine_b, :] = (n * g1[...] + s1[...]).astype(BF)
        add("x", keep * xv * xv)
        low = (cot_ref[r, :].astype(F32) * keep).astype(BF)
        dfeed[pl.ds(pl.multiple_of((x * 2 + t) * own + b, BLOCK), BLOCK), :] = low
        add("bdown", low.astype(F32))

    for c in rows_in:
        c.wait()
    run(0)
    each_block(first_norm)
    shares = [share(0, rows1, mine, at.twin()), share(1, dfeed, spot(x, t), at.twin())]

    def project(j):
        heads_of = pl.ds(pl.multiple_of(t * 512 + 128 * j, 128), 128)
        cols = pl.ds(QKV + 384 * j, 384)
        bias = jnp.concatenate([bqv[0:1, heads_of], jnp.zeros((1, 128), F32), bqv[1:2, heads_of]], axis=1)
        scale = jnp.where(lax.broadcasted_iota(jnp.int32, (1, 384), 1) < 128, HD**-0.5, 1.0)

        qkv[:, pl.ds(384 * j, 384)] = ((nn(rows1[...], W[:, cols]) + bias) * scale).astype(BF)

    first_lanes = lax.broadcasted_iota(jnp.int32, (own, 128), 1) < HD

    def attend(image, j):
        r = pl.ds(pl.multiple_of(image * own, own), own)
        c = 384 * j
        q2 = qkv[r, c : c + 128]
        k2 = qkv[r, c + 128 : c + 256]
        v_t = qkv[r, c + 256 : c + 384].T
        hide = jnp.where(valid_of(image, 0, own), 0.0, -1e30)
        outs = []
        for a in range(2):
            qm = jnp.where(first_lanes if a == 0 else ~first_lanes, q2, jnp.zeros_like(q2))
            s = nt(k2, qm) + hide
            e = jnp.exp(s - jnp.max(s, axis=0, keepdims=True))
            low = (e * (1.0 / jnp.sum(e, axis=0, keepdims=True))).astype(BF)
            probs[(j * 2 + image) * 2 + a] = low
            outs.append(nn(v_t[a * HD : (a + 1) * HD], low))
        heads[r, 128 * j : 128 * (j + 1)] = jnp.concatenate(outs, axis=0).T.astype(BF)

    def images(part, body, j):
        run(part)
        if quiet(part + 1):
            def go(i, _):
                body(i, j)
                return 0
            lax.fori_loop(0, 2, go, 0)
        else:
            body(0, j)
            run(part + 1)
            body(1, j)

    for j in range(4):
        run(1 + 4 * j)
        g.finish(j)
        if j == 0:
            take(0, rows1, theirs)
        run(2 + 4 * j)
        project(j)
        images(3 + 4 * j, attend, j)
    run(17)
    g.finish(4)
    run(18)

    def others(i, src, cols, k):
        send_t[0] = nt(src[theirs, :], W[:, cols]).astype(BF)
        copy = send(i, send_t.at[0], got.at[k], at.twin())
        copy.start()
        return copy

    def owns(src, cols, keep):
        keep[...] = nt(src[mine, :], W[:, cols])

    branch_copy = others(3, heads, pl.ds(OUT, 512), 0)
    run(19)
    owns(heads, pl.ds(OUT, 512), own_a)
    run(20)
    branch_copy.wait()

    def second_norm(b, r):
        keep = valid_of(t, b, BLOCK).astype(F32)
        branch = own_a[r, :] + got[0, r, :].astype(F32) + bout[...]
        m = x_ref[r, :].astype(F32) + branch
        mid[r, :] = m
        add("branch", keep * branch * branch)
        add("mid", keep * m * m)
        n, _ = normed(m)
        rows2[pl.ds(pl.multiple_of((x * 2 + t) * own + b, BLOCK), BLOCK), :] = (n * g2[...] + s2[...]).astype(BF)

    run(21)
    each_block(second_norm)
    run(22)
    shares.append(share(4, rows2, spot(x, t), at.across_x()))
    shares.append(share(5, rows2, spot(x, t), at.twin()))
    run(23)

    take(2, dfeed, spot(1 - x, t))
    shares.append(share(6, dfeed, spot(1 - x, t), at.twin()))
    take(1, dfeed, spot(x, 1 - t))
    run(24)
    take(5, rows2, spot(x, 1 - t))

    chip_rows = lambda far_x: at_rows(far_x * 2 * own, 2 * own)

    def halves(part, body):
        run(part)
        if quiet(part + 1):
            tiles(0, 1024, body, 512)
        else:
            body(0)
            run(part + 1)
            body(512)

    def hidden(far_x, part):
        r = chip_rows(far_x)

        def body(c):
            lanes = pl.ds(pl.multiple_of(t * 2048 + x * 1024 + c, 512), 512)
            u = nn(rows2[r, :], W[:, pl.ds(UP + c, 512)]) + bup[:, lanes]
            below = 0.5 * (1.0 + lax.erf(u * (0.5**0.5)))
            dense = jnp.exp(-0.5 * u * u) * 0.3989422804014327
            act[r, pl.ds(c, 512)] = (u * below).astype(BF)
            gp[r, pl.ds(c, 512)] = (below + u * dense).astype(BF)
        halves(part, body)

    def grad_down(c):
        G2[:, pl.ds(c, 512)] = tn(dfeed[...], act[:, pl.ds(c, 512)]).astype(BF)

    run(25)
    pg.finish(0)
    hidden(x, 26)
    run(28)
    take(4, rows2, spot(1 - x, t))
    shares.append(share(7, rows2, spot(1 - x, t), at.twin()))
    run(29)
    take(7, rows2, spot(1 - x, 1 - t))
    hidden(1 - x, 30)
    take(6, dfeed, spot(1 - x, 1 - t))
    halves(33, grad_down)
    run(37)

    def back_act(far_x):
        r = chip_rows(far_x)

        def body(c):
            cols = pl.ds(c, 512)
            d = nn(dfeed[r, :], W[:, pl.ds(DOWN + c, 512)])
            low = (d * gp[r, cols].astype(F32)).astype(BF)
            gp[r, cols] = low
            acc_up[t * 2 + x, :, cols] += fold(low.astype(F32))
        tiles(0, 1024, body, 512)

    class Sum4:
        def __init__(self, i, n, src, cols, keep, parts):
            self.i, self.n, self.src, self.cols, self.keep, self.parts = i, n, src, cols, keep, parts

        def away(self, far_x, slot):
            send_t[slot] = nt(self.src[spot(far_x, 1 - t), :], W[:, self.cols]).astype(BF)
            copy = send(self.i + slot, send_t.at[slot], got_t.at[self.n, slot], at.twin())
            copy.start()
            return copy

        def far(self):
            first = self.away(1 - x, 0)

            send_x[self.n] = nt(self.src[spot(1 - x, t), :], W[:, self.cols]).astype(BF)
            run(self.parts[0])
            first.wait()

            def body(b, r):
                send_x[self.n, r, :] = send_x[self.n, r, :] + got_t[self.n, 0, r, :]
            each_block(body)
            self.cross = send(self.i + 2, send_x.at[self.n], got.at[2 + self.n], at.across_x())
            run(self.parts[1])
            self.cross.start()

        def near(self):
            self.second = self.away(x, 1)
            self.keep[...] = nt(self.src[spot(x, t), :], W[:, self.cols])

        def value(self, r):
            return self.keep[r, :] + got_t[self.n, 1, r, :].astype(F32) + got[2 + self.n, r, :].astype(F32)

    pg.finish(1)
    run(39)
    back_act(1 - x)
    run(40)
    two = Sum4(8, 0, gp, pl.ds(UP, 1024), own_a, (41, 42))
    two.far()
    run(43)
    back_act(x)
    run(44)
    two.near()
    g.drain()
    pg.drain(dfeed)

    def grad_up(c):
        W[:, pl.ds(UP + c, 512)] = tn(rows2[...], gp[:, pl.ds(c, 512)]).astype(BF)

    halves(45, grad_up)
    run(48)
    four = Sum4(11, 1, act, pl.ds(DOWN, 1024), own_c, (49, 50))
    four.far()
    run(51)
    two.second.wait()
    four.near()
    run(52)
    two.cross.wait()
    for i in (1, 2, 5):
        shares[i].wait_send()

    def second_back(b, r):
        dy = two.value(r)
        n, scale = normed(mid[r, :])
        keep = valid_of(t, b, BLOCK).astype(F32)
        add("g2", dy * n)
        add("s2", dy)
        d = cot_ref[r, :].astype(F32) * keep + norm_back(dy, n, scale, g2[...])
        gin_out[r, :] = d
        low = d.astype(BF)
        dbr[pl.ds(pl.multiple_of(t * own + b, BLOCK), BLOCK), :] = low
        add("bout", low.astype(F32))

    run(54)
    each_block(second_back)
    shares.append(share(14, dbr, mine, at.twin()))
    run(55)
    take(14, dbr, theirs)
    run(56)

    def back_heads(c):
        datt[:, pl.ds(c, 512)] = nn(dbr[...], W[:, pl.ds(OUT + c, 512)]).astype(BF)

    back_heads(0)
    run(59)

    def grad_out(c):
        G3[:, pl.ds(c, 512)] = tn(dbr[...], heads[:, pl.ds(c, 512)]).astype(BF)

    grad_out(0)
    run(60)

    def grad_heads(p):
        ref, c0, c1 = home[p]

        ref[:, c0:c1] = tn(rows1[...], dproj[:, 384 * p : 384 * (p + 1)]).astype(BF)

    def attend_back(image, j):
        r = pl.ds(pl.multiple_of(image * own, own), own)
        c = 384 * j
        q2 = qkv[r, c : c + 128]
        k_t = qkv[r, c + 128 : c + 256].T
        v2 = qkv[r, c + 256 : c + 384]
        da = datt[r, 128 * j : 128 * (j + 1)]
        dq, dk, dv = [], [], []
        for a in range(2):
            dam = jnp.where(first_lanes if a == 0 else ~first_lanes, da, jnp.zeros_like(da))
            low = probs[(j * 2 + image) * 2 + a]
            p = low.astype(F32)
            dp = nt(v2, dam)
            ds = (p * (dp - jnp.sum(p * dp, axis=0, keepdims=True))).astype(BF)
            dq.append(nn(k_t[a * HD : (a + 1) * HD], ds))
            dk.append(nn(ds, q2))
            dv.append(nn(low, da))
        for base, v in (
            (0, jnp.concatenate(dq, axis=0).T * HD**-0.5),
            (128, jnp.where(first_lanes, dk[0], dk[1])),
            (256, jnp.where(first_lanes, dv[0], dv[1])),
        ):
            v = v.astype(BF)
            dproj[r, c + base : c + base + 128] = v
            if base != 128:
                lanes = pl.ds(pl.multiple_of(t * 512 + 128 * j, 128), 128)
                ref = total_of["bq" if base == 0 else "bv"]
                ref[:, lanes] += fold(v.astype(F32))

    def finish_feed(b, r):
        keep = valid_of(t, b, BLOCK).astype(F32)
        feed = four.value(r) + bdown[...]
        res = mid[r, :] + feed
        add("feed", keep * feed * feed)
        add("res", keep * res * res)
        act_out[r, :] = (keep * res).astype(BF)

    for j in range(3):
        images(61 + 4 * j, attend_back, j)
        run(63 + 4 * j)
        grad_heads(j)
    run(73)
    four.second.wait()
    four.cross.wait()
    run(74)
    each_block(finish_feed)
    outs = [pltpu.make_async_copy(act_out, act_hbm, sem_in.at[3])]
    outs[0].start()
    images(75, attend_back, 3)
    run(77)
    one_copy = others(15, dproj, pl.ds(QKV, 1536), 1)
    run(78)
    grad_heads(3)
    run(80)
    owns(dproj, pl.ds(QKV, 1536), own_a)
    run(81)
    one_copy.wait()
    run(82)

    def first_back(b, r):
        dy = own_a[r, :] + got[1, r, :].astype(F32)
        n, scale = normed(x_ref[r, :].astype(F32))
        add("g1", dy * n)
        add("s1", dy)
        gin_out[r, :] += norm_back(dy, n, scale, g1[...])

    each_block(first_back)
    outs.append(pltpu.make_async_copy(gin_out, gin_hbm, sem_in.at[4]))
    outs[1].start()
    run(83)

    for i in range(8):
        sums[i : i + 1, :] = jnp.sum(acc[i], axis=0, keepdims=True)
    for i in range(4):
        sums[8 + i : 9 + i, :] = jnp.sum(acc_up[i], axis=0, keepdims=True)
    lane = lax.broadcasted_iota(jnp.int32, (1, width), 1)
    row = jnp.where(lane == 5, (counts[t] + BUFFER).astype(F32), 0.0)
    for i, name in enumerate(("x", "mid", "res", "branch", "feed")):
        row = jnp.where(lane == i, jnp.sum(jnp.sum(total_of[name][...], axis=0, keepdims=True), axis=1, keepdims=True), row)
    sums[12:13, :] = row
    sums[13:16, :] = jnp.zeros((3, width), F32)
    for i, other in enumerate((at.twin(), at.across_x(), at.across_y(), at.near(), at.far())):
        c = pltpu.make_async_remote_copy(
            src_ref=sums, dst_ref=sums_got.at[i], send_sem=sums_send.at[i], recv_sem=sums_recv.at[i],
            device_id=other, device_id_type=MESH,
        )
        run(84 + 2 * i)
        c.start()
        run(85 + 2 * i)
        c.wait()
        sums[...] += sums_got[i]
    o_sums[...] = sums[...]
    run(1000)
    for i, (a, b) in enumerate(((o_qkv, qkv_hbm), (o_out, out_hbm), (o_up, up_hbm), (o_down, down_hbm))):
        outs.append(pltpu.make_async_copy(a, b, sem_in.at[5 + i]))
        outs[-1].start()
    sent = W.at[0 : 15 * shard, 0:2048]
    sc.drain(sent)
    ps.drain(sent)
    for c in outs:
        c.wait()
    for i in (0, 3, 4, 6, 7):
        shares[i].wait_send()


def block(counts, stream, cotangent, w_qkv, w_out_t, w_up, w_down_t, b_qv, b_out, b_up, b_down, g1, s1, g2, s2):
    own, width = stream.shape
    shard = w_up.shape[0]
    rows = 16 * shard
    group = 2 * own
    vmem = pl.BlockSpec(memory_space=pltpu.VMEM)
    hbm = pl.BlockSpec(memory_space=pl.ANY)
    dma = pltpu.SemaphoreType.DMA
    row = lambda v: v.reshape(1, -1)
    return pl.pallas_call(
        block_kernel,
        out_shape=(
            jax.ShapeDtypeStruct((own, width), BF),
            jax.ShapeDtypeStruct((own, width), F32),
            jax.ShapeDtypeStruct((3, shard, 512), F32),
            jax.ShapeDtypeStruct((shard, 512), F32),
            jax.ShapeDtypeStruct((shard, 2048), F32),
            jax.ShapeDtypeStruct((shard, 2048), F32),
            jax.ShapeDtypeStruct((16, width), F32),
        ),
        in_specs=[pl.BlockSpec(memory_space=pltpu.SMEM)] + [hbm] * 6 + [vmem] * 8,
        out_specs=(hbm,) * 6 + (vmem,),
        scratch_shapes=[
            pltpu.VMEM((own, width), BF),
            pltpu.VMEM((own, width), BF),
            pltpu.VMEM((own, width), BF),
            pltpu.VMEM((own, width), F32),
            pltpu.VMEM((3, shard, 512), F32),
            pltpu.VMEM((shard, 512), F32),
            pltpu.VMEM((shard, 2048), F32),
            pltpu.VMEM((shard, 2048), F32),
            pltpu.VMEM((rows, COLS), BF),
            pltpu.VMEM((rows, 1024), BF),
            pltpu.VMEM((rows, 1024), BF),
            pltpu.VMEM((4, shard // 2, 2048), BF),
            pltpu.VMEM((4, shard // 2, 2048), BF),
            pltpu.VMEM((4, shard, 2048), BF),
            pltpu.VMEM((4, shard, 2048), BF),
            pltpu.VMEM((5, shard, 2048), BF),
            pltpu.VMEM((18 + 2 * len(LINE_FIRST), 2 * shard, 1024), BF),
            pltpu.VMEM((2, shard, 1024), BF),
            pltpu.VMEM((2, shard, 1024), BF),
            pltpu.VMEM((group, width), BF),
            pltpu.VMEM((2 * group, width), BF),
            pltpu.VMEM((group, 1536), BF),
            pltpu.VMEM((16, own, own), BF),
            pltpu.VMEM((group, 512), BF),
            pltpu.VMEM((own, width), F32),
            pltpu.VMEM((2 * group, width), BF),
            pltpu.VMEM((2 * group, 1024), BF),
            pltpu.VMEM((2 * group, 1024), BF),
            pltpu.VMEM((group, 512), BF),
            pltpu.VMEM((own, width), F32),
            pltpu.VMEM((own, width), F32),
            pltpu.VMEM((2, own, width), BF),
            pltpu.VMEM((2, own, width), BF),
            pltpu.VMEM((4, own, width), BF),
            pltpu.VMEM((2, 2, own, width), BF),
            pltpu.VMEM((len(SUMS), 8, width), F32),
            pltpu.VMEM((4, 8, 1024), F32),
            pltpu.VMEM((16, width), F32),
            pltpu.VMEM((5, 16, width), F32),
            dma((9,)),
            dma((2,)),
            dma((5, 13)),
            dma((2,)),
            dma((2, 10)),
            dma((1,)),
            dma((5, 13)),
            dma((1,)),
            dma((2, 12)),
            dma((16,)),
            dma((16,)),
            dma((5,)),
            dma((5,)),
        ],
        compiler_params=pltpu.CompilerParams(
            collective_id=1, has_side_effects=True, vmem_limit_bytes=63 << 20
        ),
    )(
        counts, stream, cotangent, w_qkv, w_out_t, w_up, w_down_t,
        b_qv, row(b_out), row(b_up), row(b_down), row(g1), row(s1), row(g2), row(s2),
    )


def close_kernel(*refs):
    big, sums, out, small, held, sem = refs[:6], refs[6], refs[7:13], refs[13:22], refs[22:28], refs[28]
    loads = [pltpu.make_async_copy(a, h, sem.at[0, i]) for i, (a, h) in enumerate(zip(big, held))]
    copies = [pltpu.make_async_copy(h, b, sem.at[1, i]) for i, (h, b) in enumerate(zip(held, out))]
    for c in loads:
        c.start()
    place = lax.axis_index("dp") * 2 + lax.axis_index("tensor")
    width = sums.shape[1]
    turned = pltpu.roll(sums[0:8, :], width - place * 32, 1)
    small[0][...] = turned[0:2, :32]
    for i in range(1, 7):
        small[i][...] = turned[i + 1 : i + 2, :32]
    up = pl.ds(pl.multiple_of((place % 8) * 128, 128), 128)
    which = lax.broadcasted_iota(jnp.int32, (8, 128), 0) == place // 8
    small[7][...] = jnp.sum(jnp.where(which, sums[8:16, up], 0.0), axis=0, keepdims=True)
    row = sums[12:13, :]
    small[8][...] = jnp.sqrt(row[:, 0:5] / (row[:, 5:6] * width))
    for load, c in zip(loads, copies):
        load.wait()
        c.start()
    for c in copies:
        c.wait()


def close(*arrays):
    vmem = pl.BlockSpec(memory_space=pltpu.VMEM)
    hbm = pl.BlockSpec(memory_space=pl.ANY)
    small = [(2, 32)] + [(1, 32)] * 6 + [(1, 128), (1, 5)]
    return pl.pallas_call(
        close_kernel,
        out_shape=tuple(jax.ShapeDtypeStruct(a.shape, a.dtype) for a in arrays[:6])
        + tuple(jax.ShapeDtypeStruct(n, F32) for n in small),
        in_specs=[hbm] * 6 + [vmem],
        out_specs=(hbm,) * 6 + (vmem,) * 9,
        scratch_shapes=[pltpu.VMEM(a.shape, a.dtype) for a in arrays[:6]] + [pltpu.SemaphoreType.DMA((2, 6))],
    )(*arrays)


def local_fast(
    stream, counts, cotangent, w_qkv, b_qv, w_out, b_out, w_fc1, b_fc1, w_fc2, b_fc2,
    gain_one, shift_one, gain_two, shift_two,
):
    acts, grad_in, p_qkv, p_out, p_up, p_down, bqv, *rest = close(
        *block(
            counts, stream, cotangent, w_qkv, w_out.T, w_fc1, w_fc2.T, b_qv, b_out, b_fc1, b_fc2,
            gain_one, shift_one, gain_two, shift_two,
        )
    )
    bout, bdown, gain1, shift1, gain2, shift2, bup, rms = (v.reshape(-1) for v in rest[:8])
    return (
        acts, grad_in, p_qkv, bqv, p_out.T, bout, p_up, bup, p_down.T, bdown,
        gain1, shift1, gain2, shift2, rms,
    )

def layer_norm(values, gain, shift):
    centre = jnp.mean(values, axis=-1, keepdims=True)
    offset = values - centre
    spread = jnp.mean(offset * offset, axis=-1, keepdims=True)
    return offset * lax.rsqrt(spread + eps_norm) * gain + shift


def gelu_exact(values):
    return jax.nn.gelu(values, approximate=False)


def masked_scores(queries, key_rows, validity):
    scores = jnp.einsum(
        "bqhd,bkhd->bhqk", queries, key_rows, preferred_element_type=jnp.float32
    ) * HD ** (-0.5)
    return jnp.where(validity[:, None, None, :] > 0, scores, -1e30)


def attend_block(members):
    queries, key_rows, values, validity = members
    scores = masked_scores(queries, key_rows, validity)
    highest = jnp.max(scores, axis=-1, keepdims=True)
    expo_terms = jnp.exp(scores - highest)
    totals = jnp.sum(expo_terms, axis=-1, keepdims=True)
    weights = (expo_terms / totals).astype(jnp.bfloat16)
    mixture = jnp.einsum("bhqk,bkhd->bqhd", weights, values, preferred_element_type=jnp.float32)
    return (mixture.astype(jnp.bfloat16), (highest + jnp.log(totals))[..., 0])


def attend_back(members):
    queries, key_rows, values, validity, log_total, d_mixture = members
    scores = masked_scores(queries, key_rows, validity)
    probs = jnp.exp(scores - log_total[..., None])
    d_values = jnp.einsum(
        "bhqk,bqhd->bkhd", probs.astype(jnp.bfloat16), d_mixture, preferred_element_type=jnp.float32
    )
    d_probs = jnp.einsum("bqhd,bkhd->bhqk", d_mixture, values, preferred_element_type=jnp.float32)
    d_scores = (probs * (d_probs - jnp.sum(probs * d_probs, axis=-1, keepdims=True))).astype(
        jnp.bfloat16
    )
    d_queries = jnp.einsum(
        "bhqk,bkhd->bqhd", d_scores, key_rows, preferred_element_type=jnp.float32
    ) * HD ** (-0.5)
    d_keys = jnp.einsum(
        "bhqk,bqhd->bkhd", d_scores, queries, preferred_element_type=jnp.float32
    ) * HD ** (-0.5)
    return (
        d_queries.astype(jnp.bfloat16),
        d_keys.astype(jnp.bfloat16),
        d_values.astype(jnp.bfloat16),
    )


def local(
    stream,
    counts,
    cotangent,
    w_qkv,
    b_qv,
    w_out,
    b_out,
    w_fc1,
    b_fc1,
    w_fc2,
    b_fc2,
    gain_one,
    shift_one,
    gain_two,
    shift_two,
):
    tensor_pos = lax.axis_index("tensor")
    own_rows = stream.shape[0]
    width = stream.shape[1]
    own_images = own_rows // SLOTS
    slot_index = jnp.arange(SLOTS, dtype=jnp.int32)
    validity_all = (slot_index[None, :] < (BUFFER + counts)[:, None]).astype(jnp.float32)
    own_validity = lax.dynamic_slice_in_dim(validity_all, tensor_pos * own_images, own_images, 0)
    own_valid = own_validity.reshape(own_rows, 1)
    qkv_full, out_full, up_full, down_full = (
        lax.all_gather(w_qkv, "dp", axis=1, tiled=True),
        lax.all_gather(w_out, "dp", axis=1, tiled=True),
        lax.all_gather(w_fc1[None], "dp", axis=1, tiled=True),
        lax.all_gather(w_fc2, "dp", axis=1, tiled=True),
    )
    head_width = w_qkv.shape[2]
    unit_width = w_fc1.shape[1]
    bias_query = lax.dynamic_slice_in_dim(b_qv[0], tensor_pos * head_width, head_width, 0)
    bias_value = lax.dynamic_slice_in_dim(b_qv[1], tensor_pos * head_width, head_width, 0)
    bias_up = lax.dynamic_slice_in_dim(b_fc1, tensor_pos * unit_width, unit_width, 0)
    up_full = up_full[0]
    group_images = validity_all.shape[0]
    group_rows = group_images * SLOTS
    local_heads = head_width // HD
    pairing = 2
    block_count = group_images // pairing
    blocked_valid = validity_all.reshape(block_count, pairing, SLOTS)
    stream_f = stream.astype(jnp.float32)
    normed_one = layer_norm(stream_f, gain_one, shift_one).astype(jnp.bfloat16)
    first_rows = lax.all_gather(normed_one, "tensor", axis=0, tiled=True)
    projected = jnp.einsum("rd,cde->rce", first_rows, qkv_full, preferred_element_type=jnp.float32)
    shape_heads = (block_count, pairing, SLOTS, local_heads, HD)
    queries = (projected[:, 0] + bias_query).astype(jnp.bfloat16).reshape(shape_heads)
    key_rows = projected[:, 1].astype(jnp.bfloat16).reshape(shape_heads)
    values = (projected[:, 2] + bias_value).astype(jnp.bfloat16).reshape(shape_heads)
    mixture, log_total = lax.map(attend_block, (queries, key_rows, values, blocked_valid))
    attn_heads = mixture.reshape(group_rows, head_width)
    taken = attn_heads
    attn_total = lax.psum_scatter(
        jnp.dot(taken, out_full, preferred_element_type=jnp.float32).astype(jnp.bfloat16),
        "tensor",
        scatter_dimension=0,
        tiled=True,
    ).astype(jnp.float32)
    branch = attn_total + b_out
    middle = stream_f + branch
    normed_two = layer_norm(middle, gain_two, shift_two).astype(jnp.bfloat16)
    second_rows = lax.all_gather(normed_two, "tensor", axis=0, tiled=True)
    hidden_pre = jnp.dot(second_rows, up_full, preferred_element_type=jnp.float32) + bias_up
    hidden_act = gelu_exact(hidden_pre).astype(jnp.bfloat16)
    taken = hidden_act
    mlp_total = lax.psum_scatter(
        jnp.dot(taken, down_full, preferred_element_type=jnp.float32).astype(jnp.bfloat16),
        "tensor",
        scatter_dimension=0,
        tiled=True,
    ).astype(jnp.float32)
    feed = mlp_total + b_fc2
    result = middle + feed
    activations = (result * own_valid).astype(jnp.bfloat16)
    squares = jnp.stack(
        [
            jnp.sum(own_valid * member * member)
            for member in (stream_f, middle, result, branch, feed)
        ]
    )
    square_sums, valid_count = lax.psum((squares, jnp.sum(own_valid)), ("dp", "tensor"))
    rms_stats = jnp.sqrt(square_sums / (valid_count * width))
    d_result = cotangent.astype(jnp.float32) * own_valid
    d_feed_low = d_result.astype(jnp.bfloat16)
    d_feed_rows = lax.all_gather(d_feed_low, "tensor", axis=0, tiled=True)
    d_act = jnp.einsum("rd,ud->ru", d_feed_rows, down_full, preferred_element_type=jnp.float32)
    unused_act, gelu_pullback = jax.vjp(gelu_exact, hidden_pre)
    d_pre = gelu_pullback(d_act)[0].astype(jnp.bfloat16)
    grad_down = jnp.einsum("ru,rd->ud", hidden_act, d_feed_rows, preferred_element_type=jnp.float32)
    grad_up = jnp.einsum("rd,ru->du", second_rows, d_pre, preferred_element_type=jnp.float32)
    grad_bias_up = jnp.sum(d_pre, axis=0, dtype=jnp.float32)
    grad_bias_down = jnp.sum(d_feed_low, axis=0, dtype=jnp.float32)
    taken = d_pre
    d_normed_two = lax.psum_scatter(
        jnp.einsum("ru,du->rd", taken, up_full, preferred_element_type=jnp.float32).astype(
            jnp.bfloat16
        ),
        "tensor",
        scatter_dimension=0,
        tiled=True,
    ).astype(jnp.float32)
    unused_two, norm_two_pullback = jax.vjp(layer_norm, middle, gain_two, shift_two)
    d_middle_norm, grad_gain_two, grad_shift_two = norm_two_pullback(d_normed_two)
    d_middle = d_result + d_middle_norm
    d_branch_low = d_middle.astype(jnp.bfloat16)
    grad_bias_out = jnp.sum(d_branch_low, axis=0, dtype=jnp.float32)
    d_branch_rows = lax.all_gather(d_branch_low, "tensor", axis=0, tiled=True)
    d_attn = jnp.einsum(
        "rd,hd->rh", d_branch_rows, out_full, preferred_element_type=jnp.float32
    ).astype(jnp.bfloat16)
    grad_out = jnp.einsum(
        "rh,rd->hd", attn_heads, d_branch_rows, preferred_element_type=jnp.float32
    )
    d_queries, d_keys, d_values = lax.map(
        attend_back,
        (queries, key_rows, values, blocked_valid, log_total, d_attn.reshape(shape_heads)),
    )
    d_projected = jnp.stack(
        [
            d_queries.reshape(group_rows, head_width),
            d_keys.reshape(group_rows, head_width),
            d_values.reshape(group_rows, head_width),
        ],
        axis=1,
    )
    grad_qkv = jnp.einsum(
        "rd,rce->cde", first_rows, d_projected, preferred_element_type=jnp.float32
    )
    bias_terms = jnp.sum(d_projected, axis=0, dtype=jnp.float32)
    taken = d_projected
    d_normed_one = lax.psum_scatter(
        jnp.einsum("rce,cde->rd", taken, qkv_full, preferred_element_type=jnp.float32).astype(
            jnp.bfloat16
        ),
        "tensor",
        scatter_dimension=0,
        tiled=True,
    ).astype(jnp.float32)
    unused_one, norm_one_pullback = jax.vjp(layer_norm, stream_f, gain_one, shift_one)
    d_stream_norm, grad_gain_one, grad_shift_one = norm_one_pullback(d_normed_one)
    grad_input = d_middle + d_stream_norm
    grad_up = grad_up[None]
    bias_qv_full = lax.dynamic_update_slice(
        jnp.zeros((2, width), jnp.float32),
        jnp.stack([bias_terms[0], bias_terms[2]]),
        (jnp.int32(0), tensor_pos * head_width),
    )
    bias_up_full = lax.dynamic_update_slice(
        jnp.zeros((b_fc1.shape[0],), jnp.float32), grad_bias_up, (tensor_pos * unit_width,)
    )
    qkv_part, out_part, up_part, down_part = (
        lax.psum_scatter(
            grad_qkv.astype(jnp.bfloat16), "dp", scatter_dimension=1, tiled=True
        ).astype(jnp.float32),
        lax.psum_scatter(
            grad_out.astype(jnp.bfloat16), "dp", scatter_dimension=1, tiled=True
        ).astype(jnp.float32),
        lax.psum_scatter(
            grad_up.astype(jnp.bfloat16), "dp", scatter_dimension=1, tiled=True
        ).astype(jnp.float32),
        lax.psum_scatter(
            grad_down.astype(jnp.bfloat16), "dp", scatter_dimension=1, tiled=True
        ).astype(jnp.float32),
    )
    small_parts = (
        lax.psum_scatter(bias_qv_full, ("dp", "tensor"), scatter_dimension=1, tiled=True),
        lax.psum_scatter(grad_bias_out, ("dp", "tensor"), scatter_dimension=0, tiled=True),
        lax.psum_scatter(bias_up_full, ("dp", "tensor"), scatter_dimension=0, tiled=True),
        lax.psum_scatter(grad_bias_down, ("dp", "tensor"), scatter_dimension=0, tiled=True),
        lax.psum_scatter(grad_gain_one, ("dp", "tensor"), scatter_dimension=0, tiled=True),
        lax.psum_scatter(grad_shift_one, ("dp", "tensor"), scatter_dimension=0, tiled=True),
        lax.psum_scatter(grad_gain_two, ("dp", "tensor"), scatter_dimension=0, tiled=True),
        lax.psum_scatter(grad_shift_two, ("dp", "tensor"), scatter_dimension=0, tiled=True),
    )
    return (
        activations,
        grad_input,
        qkv_part,
        small_parts[0],
        out_part,
        small_parts[1],
        up_part[0],
        small_parts[2],
        down_part,
        small_parts[3],
        small_parts[4],
        small_parts[5],
        small_parts[6],
        small_parts[7],
        rms_stats,
    )


def solution(mesh):
    fast = mesh.shape["dp"] == 16 and mesh.shape["tensor"] == 2
    return jax.shard_map(
        local_fast if fast else local,
        mesh=mesh,
        in_specs=(
            P(("dp", "tensor"), None),
            P("dp"),
            P(("dp", "tensor"), None),
            P(None, "dp", "tensor"),
            P(),
            P("tensor", "dp"),
            P(),
            P("dp", "tensor"),
            P(),
            P("tensor", "dp"),
            P(),
            P(),
            P(),
            P(),
            P(),
        ),
        out_specs=(
            P(("dp", "tensor"), None),
            P(("dp", "tensor"), None),
            P(None, "dp", "tensor"),
            P(None, ("dp", "tensor")),
            P("tensor", "dp"),
            P(("dp", "tensor")),
            P("dp", "tensor"),
            P(("dp", "tensor")),
            P("tensor", "dp"),
            P(("dp", "tensor")),
            P(("dp", "tensor")),
            P(("dp", "tensor")),
            P(("dp", "tensor")),
            P(("dp", "tensor")),
            P(),
        ),
        check_vma=False,
    )
```

```python
import jax
import jax.numpy as jnp
from jax import lax
from jax.experimental import pallas as pl
from jax.experimental.pallas import tpu as pltpu
from jax.sharding import PartitionSpec as P

HD = 64
BUFFER = 64
SLOTS = 320


eps_norm = 1e-06


MESH = pl.DeviceIdType.MESH


class Place:
    def __init__(self):
        dp = lax.axis_index("dp")
        self.t = lax.axis_index("tensor")
        self.z, self.y, self.x = dp // 4, (dp // 2) % 2, dp % 2
        self.side = self.z // 2
        self.w = self.z + self.side * (3 - 2 * self.z)
        self.step = 1 - 2 * self.side
        self.dp = dp

    def order(self, k):
        o = (self.w, 1 - self.w, 2, 3)[k]
        return 3 * self.side + self.step * o

    def chip(self, z, y, x):
        return z * 4 + y * 2 + x

    def inward(self):
        return (self.chip(self.z + self.step, self.y, self.x), self.t)

    def outward(self):
        return (self.chip(self.z - self.step, self.y, self.x), self.t)

    def across_x(self):
        return (self.chip(self.z, self.y, 1 - self.x), self.t)

    def across_y(self):
        return (self.chip(self.z, 1 - self.y, self.x), self.t)

    def near(self):
        return (self.chip(self.z + 1 - 2 * (self.z % 2), self.y, self.x), self.t)

    def far(self):
        return (self.chip((self.z + 2) % 4, self.y, self.x), self.t)

    def twin(self):
        return (self.dp, 1 - self.t)


def greet(at):
    barrier = pltpu.get_barrier_semaphore()
    for other in (at.across_x(), at.across_y(), at.inward(), at.twin(), at.far()):
        pl.semaphore_signal(barrier, inc=1, device_id=other, device_id_type=MESH)

    @pl.when(at.w == 1)
    def _():
        pl.semaphore_signal(barrier, inc=1, device_id=at.outward(), device_id_type=MESH)


def enter(at):
    pl.semaphore_wait(pltpu.get_barrier_semaphore(), 5 + at.w)


def settle(ref, sem, at, sent):
    copy = pltpu.make_async_remote_copy(
        src_ref=ref, dst_ref=ref, send_sem=sem, recv_sem=sem, device_id=at.twin(), device_id_type=MESH
    )
    if sent:
        copy.wait_send()
    else:
        copy.wait_recv()


class Gather:
    def __init__(self, at, full, shard, pieces, send, recv):
        self.at, self.full, self.shard, self.pieces, self.send, self.recv = at, full, shard, pieces, send, recv

    def rows(self, p, z, y, x, part=None):
        c0, c1 = self.pieces[p]
        start, size = self.at.chip(z, y, x) * self.shard, self.shard
        if part is not None:
            size = self.shard // 2
            start = start + part * size
        return self.full.at[pl.ds(pl.multiple_of(start, size), size), pl.ds(c0, c1 - c0)]

    def copy(self, p, ref, s, r, other):
        return pltpu.make_async_remote_copy(
            src_ref=ref,
            dst_ref=ref,
            send_sem=self.send.at[s],
            recv_sem=self.recv.at[p, r],
            device_id=other,
            device_id_type=MESH,
        )

    def z_in(self, p, z):
        return self.copy(p, self.rows(p, z, self.at.y, self.at.x), 1, z, self.at.inward())

    def z_out(self, p, z):
        return self.copy(p, self.rows(p, z, self.at.y, self.at.x), 1, z, self.at.outward())

    def x_full(self, p, z):
        return self.copy(p, self.rows(p, z, self.at.y, self.at.x), 0, 4 + z, self.at.across_x())

    def y_full(self, p, z):
        return self.copy(p, self.rows(p, z, self.at.y, self.at.x), 0, 8 + z, self.at.across_y())

    def x_half(self, p, z):
        return self.copy(p, self.rows(p, z, 1 - self.at.y, self.at.x, 1), 0, 12, self.at.across_x())

    def y_half(self, p, z):
        return self.copy(p, self.rows(p, z, self.at.y, 1 - self.at.x, 0), 0, 12, self.at.across_y())

    def arrived(self, p, kind, z):
        at = self.at
        ref = (
            lambda: self.rows(p, z, at.y, at.x),
            lambda: self.rows(p, z, at.y, 1 - at.x),
            lambda: self.rows(p, z, 1 - at.y, at.x),
        )[kind]()
        settle(ref, self.recv.at[p, 4 * kind + z], at, False)

    def line(self, p, k, w):
        at = self.at

        @pl.when(at.w == w)
        def _():
            z = at.order(k)
            if k > 0:
                self.arrived(p, 0, z)
            if k == 0 or (k == 1 and w == 1):
                self.z_in(p, z).start()
            if w == 1 and k != 1:
                self.z_out(p, z).start()
            self.x_full(p, z).start()
            self.y_full(p, z).start()

    def plane(self, p, k):
        z = self.at.order(k)
        self.arrived(p, 1, z)
        self.y_half(p, z).start()
        self.arrived(p, 2, z)
        self.x_half(p, z).start()

    def finish(self, p):
        c0, c1 = self.pieces[p]
        settle(self.full.at[0 : 4 * self.shard, c0:c1], self.recv.at[p, 12], self.at, False)

    def drain(self):
        n = sum(c1 - c0 for c0, c1 in self.pieces)
        settle(self.full.at[0 : 12 * self.shard, 0:n], self.send.at[0], self.at, True)
        for w, blocks in ((0, 1), (1, 5)):

            @pl.when(self.at.w == w)
            def _(blocks=blocks):
                settle(self.full.at[0 : blocks * self.shard, 0:n], self.send.at[1], self.at, True)


class Scatter:
    def __init__(self, at, full, shard, pieces, xh, yh, xf, yf, zl, send, recv):
        self.at, self.full, self.shard, self.pieces = at, full, shard, pieces
        self.xh, self.yh, self.xf, self.yf, self.zl = xh, yh, xf, yf, zl
        self.send, self.recv = send, recv

    def cols(self, p):
        c0, c1 = self.pieces[p]
        return pl.ds(c0, c1 - c0)

    def rows(self, p, z, y, x, part=None):
        start, size = self.at.chip(z, y, x) * self.shard, self.shard
        if part is not None:
            size = self.shard // 2
            start = start + part * size
        ref, c0, c1 = self.full(p)
        return ref.at[pl.ds(pl.multiple_of(start, size), size), pl.ds(c0, c1 - c0)]

    def copy(self, p, src, dst, r, other):
        return pltpu.make_async_remote_copy(
            src_ref=src,
            dst_ref=dst,
            send_sem=self.send.at[0],
            recv_sem=self.recv.at[p, r],
            device_id=other,
            device_id_type=MESH,
        )

    def x_half(self, p, z):
        at = self.at
        return self.copy(
            p, self.rows(p, z, 1 - at.y, 1 - at.x, 0), self.xh.at[z, :, self.cols(p)], z, at.across_x()
        )

    def y_half(self, p, z):
        at = self.at
        return self.copy(
            p, self.rows(p, z, 1 - at.y, 1 - at.x, 1), self.yh.at[z, :, self.cols(p)], z, at.across_y()
        )

    def x_full(self, p, z):
        at = self.at
        return self.copy(
            p, self.rows(p, z, at.y, 1 - at.x), self.xf.at[z, :, self.cols(p)], 4 + z, at.across_x()
        )

    def y_full(self, p, z):
        at = self.at
        return self.copy(
            p, self.rows(p, z, 1 - at.y, at.x), self.yf.at[z, :, self.cols(p)], 4 + z, at.across_y()
        )

    def z_in(self, p, z, slot):
        at = self.at
        return self.copy(
            p, self.rows(p, z, at.y, at.x), self.zl.at[slot, :, self.cols(p)], 8 + slot, at.inward()
        )

    def z_out(self, p, z, slot):
        at = self.at
        return self.copy(
            p, self.rows(p, z, at.y, at.x), self.zl.at[slot, :, self.cols(p)], 8 + slot, at.outward()
        )

    def begin(self, p, k):
        z = self.at.order(k)
        self.x_half(p, z).start()
        self.y_half(p, z).start()

    def plane(self, p, k):
        at = self.at
        z = at.order(k)
        settle(self.xf.at[z, :, self.cols(p)], self.recv.at[p, z], at, False)
        ref = self.rows(p, z, 1 - at.y, at.x, 0)
        ref[...] = ref[...] + self.xh[z, :, self.cols(p)]
        self.y_full(p, z).start()
        ref = self.rows(p, z, at.y, 1 - at.x, 1)
        ref[...] = ref[...] + self.yh[z, :, self.cols(p)]
        self.x_full(p, z).start()

    def wait_line(self, p, z, slot):
        self.z_in(p, z, slot).wait_recv()

    def line(self, p, k, w, out):
        at = self.at

        @pl.when(at.w == w)
        def _():
            z = at.order(k)
            full, c0, c1 = self.full(p)
            settle(full.at[0 : 2 * self.shard, c0:c1], self.recv.at[p, 4 + z], at, False)
            ref = self.rows(p, z, at.y, at.x)
            parts = [self.xf.at[z, :, self.cols(p)], self.yf.at[z, :, self.cols(p)]]
            if w == 1:
                self.wait_line(p, z, z)
                parts.append(self.zl.at[z, :, self.cols(p)])
            if k == 0:
                self.wait_line(p, z, 4)
                parts.append(self.zl.at[4, :, self.cols(p)])
            total = ref[...].astype(jnp.float32)
            for part in parts:
                total = total + part[...].astype(jnp.float32)
            if k == 0:
                out(total)
            else:
                ref[...] = total.astype(jnp.bfloat16)
                if w == 0 or k == 3:
                    self.z_in(p, z, z).start()
                elif k == 2:
                    self.z_in(p, z, 4).start()
                else:
                    self.z_out(p, z, 4).start()

    def drain(self, ref):
        settle(ref, self.send.at[0], self.at, True)


class PairGather:
    def __init__(self, at, full, shard, columns, sources, send, recv):
        self.at, self.full, self.shard, self.columns, self.sources = at, full, shard, columns, sources
        self.send, self.recv = send, recv

    def far_x(self, h):
        return self.at.x if h == 0 else 1 - self.at.x

    def rows(self, m, z, y, x):
        c0, n = self.columns[m]
        start = self.at.chip(z, y, x) * self.shard
        return self.full.at[pl.ds(pl.multiple_of(start, self.shard), self.shard), pl.ds(c0, n)]

    def copy(self, m, src, dst, s, r, other):
        return pltpu.make_async_remote_copy(
            src_ref=src,
            dst_ref=dst,
            send_sem=self.send.at[s],
            recv_sem=self.recv.at[m, r],
            device_id=other,
            device_id_type=MESH,
        )

    def x_copy(self, m):
        at = self.at
        c0, n = self.columns[m]
        src = self.sources[m].at[:, pl.ds(pl.multiple_of((1 - at.x) * n, n), n)]
        return self.copy(m, src, self.rows(m, at.z, at.y, at.x), 0, 8, at.across_x())

    def z_in(self, m, h, z):
        ref = self.rows(m, z, self.at.y, self.far_x(h))
        return self.copy(m, ref, ref, 1, 4 * h + z, self.at.inward())

    def z_out(self, m, h, z):
        ref = self.rows(m, z, self.at.y, self.far_x(h))
        return self.copy(m, ref, ref, 1, 4 * h + z, self.at.outward())

    def y_copy(self, m, h, z):
        ref = self.rows(m, z, self.at.y, self.far_x(h))
        return self.copy(m, ref, ref, 0, 9, self.at.across_y())

    def line(self, m, h, k, w):
        at = self.at

        @pl.when(at.w == w)
        def _():
            z = at.order(k)
            ref = self.rows(m, z, at.y, self.far_x(h))
            if k > 0:
                settle(ref, self.recv.at[m, 4 * h + z], at, False)
            elif h == 1:
                settle(ref, self.recv.at[m, 8], at, False)
            if k == 0 or (k == 1 and w == 1):
                self.z_in(m, h, z).start()
            if w == 1 and k != 1:
                self.z_out(m, h, z).start()

    def cross(self, m, h, k, w):
        @pl.when(self.at.w == w)
        def _():
            self.y_copy(m, h, self.at.order(k)).start()

    def finish(self, m):
        c0, n = self.columns[m]
        settle(self.full.at[0 : 8 * self.shard, pl.ds(c0, n)], self.recv.at[m, 9], self.at, False)

    def drain(self, ref):
        settle(ref.at[0 : 18 * self.shard, :], self.send.at[0], self.at, True)
        for w, blocks in ((0, 4), (1, 20)):

            @pl.when(self.at.w == w)
            def _(blocks=blocks):
                settle(ref.at[0 : blocks * self.shard, :], self.send.at[1], self.at, True)


class PairScatter:
    def __init__(self, at, full, shard, first, units, xs, xr, send, recv):
        self.at, self.full, self.shard, self.first = at, full, shard, first
        self.units, self.xs, self.xr, self.send, self.recv = units, xs, xr, send, recv
        self.base = {1: 0, 0: 11 if 1 in first else 9}

    def unit(self, m, z, y):
        ref, c0, n = self.full(m)
        size = 2 * self.shard
        return ref.at[pl.ds(pl.multiple_of((z * 2 + y) * size, size), size), pl.ds(c0, n)]

    def copy(self, m, src, dst, r, other):
        return pltpu.make_async_remote_copy(
            src_ref=src,
            dst_ref=dst,
            send_sem=self.send.at[0],
            recv_sem=self.recv.at[m, r],
            device_id=other,
            device_id_type=MESH,
        )

    def from_y(self, m, z):
        return self.units.at[self.base[m] + (10 if m in self.first else z)]

    def from_z(self, m, col, slot):
        return self.units.at[self.base[m] + (5 * col if m in self.first else 4) + slot]

    def column(self, col):
        return self.at.y if col == 0 else 1 - self.at.y

    def y_copy(self, m, z):
        return self.copy(m, self.unit(m, z, 1 - self.at.y), self.from_y(m, z), 10 if m in self.first else z, self.at.across_y())

    def z_copy(self, m, col, z, slot, other):
        return self.copy(
            m, self.unit(m, z, self.column(col)), self.from_z(m, col, slot), (5 * col if m in self.first else 4) + slot, other
        )

    def x_copy(self, m):
        return self.copy(m, self.xs.at[m], self.xr.at[m], 11, self.at.across_x())

    def begin(self, m, k):
        self.y_copy(m, self.at.order(k)).start()

    def pass_on(self, m, col, k, w):
        at = self.at
        z = at.order(k)
        if w == 0:
            self.z_copy(m, col, z, z, at.inward()).start()
        elif k == 1:
            self.z_copy(m, col, z, 4, at.outward()).start()
        else:
            self.z_copy(m, col, z, z if k == 3 else 4, at.inward()).start()

    def add_line(self, m, col, k, w, extra):
        at = self.at
        z = at.order(k)
        ref = self.unit(m, z, self.column(col))
        parts = list(extra)
        if k == 0:
            self.z_copy(m, col, z, 4, at.inward()).wait_recv()
            parts.append(self.from_z(m, col, 4))
        if w == 1:
            self.z_copy(m, col, z, z, at.inward()).wait_recv()
            parts.append(self.from_z(m, col, z))
        if parts:
            v = ref[...].astype(jnp.float32)
            for part in parts:
                v = v + part[...].astype(jnp.float32)
            ref[...] = v.astype(jnp.bfloat16)

    def finish(self, m, out, second):
        at = self.at
        size = self.shard
        full, c0, n = self.full(m)

        def total(x):
            rows = pl.ds(pl.multiple_of(at.chip(at.z, at.y, x) * size, size), size)
            v = full[rows, pl.ds(c0, n)].astype(jnp.float32)
            if second:
                v = v + self.from_y(m, at.z)[pl.ds(pl.multiple_of(x * size, size), size), :].astype(jnp.float32)
            return v

        self.xs[m] = total(1 - at.x).astype(jnp.bfloat16)
        self.x_copy(m).start()
        out(at.x, total(at.x))

    def line(self, m, k, w, out):
        at = self.at

        @pl.when(at.w == w)
        def _():
            z = at.order(k)
            self.y_copy(m, z).wait_recv()
            self.add_line(m, 0, k, w, [self.from_y(m, z)])
            if k > 0:
                self.pass_on(m, 0, k, w)
            else:
                self.finish(m, out, False)

    def line_first(self, m, col, k, w):
        @pl.when(self.at.w == w)
        def _():
            self.add_line(m, col, k, w, [])
            if k > 0:
                self.pass_on(m, col, k, w)
            elif col == 1:
                self.y_copy(m, self.at.z).start()

    def meet(self, m, out):
        self.y_copy(m, self.at.z).wait_recv()
        self.finish(m, out, True)

    def last(self, m, out):
        self.x_copy(m).wait_recv()
        out(1 - self.at.x, self.xr[m].astype(jnp.float32))

    def drain(self, ref):
        settle(ref, self.send.at[0], self.at, True)


QKV, OUT, UP, DOWN, COLS = 0, 1536, 2048, 3072, 4096
PIECES = ((0, 384), (384, 768), (768, 1152), (1152, 1536), (1536, 2048))
LINE_FIRST = ()
PLAN = (
    ((0, 3, 0, 1), (0, 0, 0, 1), (0, 2, 0, 1), (0, 3, 0, 0), (3, 1, 0, 0, 0), (0, 0, 0, 0), (0, 1, 0, 0), (0, 3, 1, 1), (3, 0, 0, 0, 1), (0, 3, 1, 0), (4, 1, 0, 0, 0), (0, 4, 0, 1), (0, 1, 0, 1), (0, 2, 0, 0), (0, 2, 1, 0), (3, 1, 0, 0, 1), (0, 0, 1, 1), (3, 0, 0, 0, 0), (4, 0, 0, 0, 1), (2, 0), (0, 0, 1, 0), (0, 0, 2, 1), (3, 0, 0, 1, 0), (4, 0, 0, 0, 0), (0, 1, 1, 1), (1, 2, 0), (0, 3, 2, 1), (0, 1, 2, 1), (3, 0, 1, 0, 0), (3, 0, 0, 1, 1), (1, 1, 0), (0, 4, 0, 0), (0, 4, 1, 0), (1, 0, 0), (0, 0, 2, 0), (0, 2, 1, 1), (0, 2, 2, 1), (0, 1, 1, 0), (0, 1, 2, 0), (0, 3, 2, 0), (0, 0, 3, 1), (0, 4, 1, 1), (2, 1), (3, 1, 0, 1, 1), (0, 0, 3, 0), (0, 2, 2, 0), (0, 1, 3, 1), (1, 0, 1), (3, 1, 0, 2, 1), (1, 3, 0), (1, 0, 2), (0, 3, 3, 1), (0, 1, 3, 0), (1, 0, 3), (0, 2, 3, 1), (3, 0, 0, 2, 1), (3, 1, 0, 3, 1), (1, 2, 1), (0, 2, 3, 0), (1, 3, 1),),
    ((1, 1, 1), (0, 4, 2, 1), (1, 1, 2),),
    ((1, 1, 3), (0, 4, 3, 1), (1, 2, 2), (3, 0, 1, 0, 1), (3, 1, 1, 0, 0), (3, 0, 0, 2, 0), (0, 3, 3, 0),),
    ((3, 1, 1, 0, 1), (1, 3, 2), (1, 2, 3), (3, 0, 1, 1, 1), (0, 4, 2, 0), (0, 4, 3, 0), (4, 0, 0, 1, 0), (4, 1, 0, 0, 1), (1, 3, 3),),
    (),
    ((4, 0, 1, 0, 1), (1, 4, 0), (1, 4, 1), (4, 0, 1, 0, 0), (1, 4, 2), (3, 0, 0, 3, 1),),
    ((4, 1, 1, 0, 1), (1, 4, 3),),
    ((3, 0, 1, 1, 0), (3, 1, 1, 1, 1), (5,), (4, 0, 1, 1, 1),),
    (),
    ((3, 0, 1, 2, 1), (4, 0, 0, 1, 1),),
    ((4, 0, 0, 2, 0),),
    (),
    ((3, 1, 0, 1, 0),),
    ((3, 0, 0, 3, 0), (3, 1, 1, 1, 0), (3, 0, 1, 3, 1),),
    (),
    (),
    ((3, 1, 1, 2, 1), (3, 0, 1, 2, 0), (4, 1, 0, 1, 0), (4, 0, 0, 2, 1), (4, 0, 1, 2, 1),),
    (),
    (),
    ((3, 1, 1, 3, 1), (4, 0, 0, 3, 1),),
    ((4, 0, 1, 3, 1), (4, 1, 0, 1, 1), (4, 1, 1, 1, 1), (4, 0, 1, 1, 0), (4, 0, 1, 2, 0), (3, 0, 1, 3, 0), (4, 0, 1, 3, 0), (3, 1, 0, 2, 0),),
    ((4, 1, 0, 2, 1),),
    ((4, 0, 0, 3, 0), (3, 1, 0, 3, 0), (3, 1, 1, 2, 0), (3, 1, 1, 3, 0),),
    (),
    (),
    ((4, 1, 0, 3, 1), (4, 1, 1, 0, 0), (4, 1, 1, 1, 0),),
    (),
    (),
    ((4, 1, 1, 2, 1), (4, 1, 0, 2, 0), (4, 1, 0, 3, 0), (4, 1, 1, 2, 0), (4, 1, 1, 3, 0), (4, 1, 1, 3, 1),),
    (),
    (),
    (),
    (),
    (),
    (),
    (),
    (),
    ((13, 1, 3), (13, 1, 2), (13, 1, 1), (13, 1, 0),),
    (),
    (),
    (),
    (),
    (),
    ((14, 1, 3, 0),),
    (),
    (),
    ((14, 1, 2, 0),),
    (),
    (),
    ((13, 0, 3),),
    ((14, 1, 3, 1),),
    ((13, 0, 2), (13, 0, 1),),
    (),
    (),
    (),
    (),
    (),
    (),
    (),
    (),
    (),
    (),
    (),
    ((14, 0, 3, 0),),
    (),
    (),
    ((10, 4, 3),),
    ((14, 1, 1, 0), (10, 0, 3),),
    (),
    ((14, 1, 2, 1), (14, 1, 1, 1), (14, 0, 2, 0), (10, 4, 2),),
    ((14, 0, 3, 1), (10, 4, 1), (10, 1, 3),),
    ((10, 4, 0),),
    ((11, 4, 3),),
    ((10, 2, 3), (10, 2, 2), (11, 4, 2), (10, 1, 2), (10, 1, 1), (14, 0, 1, 0),),
    ((10, 2, 1), (11, 1, 3), (12, 4, 3, 0), (10, 1, 0),),
    ((14, 1, 0, 0), (10, 0, 2), (11, 4, 1),),
    ((13, 0, 0), (11, 4, 0),),
    (),
    (),
    ((10, 2, 0), (11, 2, 3), (14, 1, 0, 1),),
    ((11, 0, 3),),
    ((14, 0, 2, 1), (11, 1, 2), (11, 2, 2),),
    ((10, 3, 3), (10, 3, 2), (10, 3, 1),),
    (),
    (),
    ((11, 1, 1), (12, 1, 3, 0), (10, 0, 1), (12, 4, 3, 1), (14, 0, 1, 1), (12, 4, 2, 0), (11, 0, 2), (12, 1, 2, 0), (11, 3, 3),),
    (),
    ((11, 2, 1), (12, 1, 3, 1), (12, 2, 3, 0), (11, 3, 2), (12, 2, 2, 0), (11, 3, 1), (12, 0, 3, 0), (12, 4, 2, 1), (12, 4, 1, 1),),
    (),
    ((10, 3, 0), (12, 1, 2, 1), (12, 3, 3, 0), (12, 2, 3, 1), (11, 2, 0), (12, 1, 1, 1), (12, 0, 2, 0), (10, 0, 0), (11, 1, 0), (12, 3, 2, 0),),
    (),
    ((12, 0, 3, 1), (11, 0, 1), (12, 4, 1, 0), (12, 3, 3, 1), (14, 0, 0, 0), (14, 0, 0, 1), (12, 2, 2, 1), (12, 2, 1, 0), (12, 2, 1, 1),),
    (),
    ((12, 3, 1, 0), (12, 1, 1, 0), (12, 3, 2, 1), (12, 3, 1, 1), (11, 3, 0), (11, 0, 0), (12, 0, 1, 0), (12, 0, 2, 1), (12, 0, 1, 1), (12, 1, 0, 0),),
    (),
    ((12, 4, 0, 1), (12, 2, 0, 0), (15, 0), (15, 1), (12, 1, 0, 1), (12, 4, 0, 0), (12, 3, 0, 0), (12, 2, 0, 1), (12, 3, 0, 1), (12, 0, 0, 1), (12, 0, 0, 0),),
)
BF, F32 = jnp.bfloat16, jnp.float32
SUMS = ("bq", "bv", "bout", "bdown", "g1", "s1", "g2", "s2", "x", "mid", "res", "branch", "feed")
BLOCK = 32


def nn(a, b):
    return lax.dot_general(a, b, (((1,), (0,)), ((), ())), preferred_element_type=F32)


def nt(a, b):
    return lax.dot_general(a, b, (((1,), (1,)), ((), ())), preferred_element_type=F32)


def tn(a, b):
    return lax.dot_general(a, b, (((0,), (0,)), ((), ())), preferred_element_type=F32)


def at_rows(start, size):
    return pl.ds(pl.multiple_of(start, size), size)


def fold(v):
    return jnp.sum(v.reshape(v.shape[0] // 8, 8, v.shape[1]), axis=0)


def normed(v):
    centre = jnp.mean(v, axis=1, keepdims=True)
    offset = v - centre
    r = lax.rsqrt(jnp.mean(offset * offset, axis=1, keepdims=True) + eps_norm)
    return offset * r, r


def norm_back(dy, n, r, gain):
    dn = dy * gain
    first = jnp.mean(dn, axis=1, keepdims=True)
    second = jnp.mean(dn * n, axis=1, keepdims=True)
    return r * (dn - first - n * second)


def block_kernel(
    counts, x_hbm, cot_hbm, wqkv, wout, wup, wdown, bqv, bout, bup, bdown, g1, s1, g2, s2,
    act_hbm, gin_hbm, qkv_hbm, out_hbm, up_hbm, down_hbm, o_sums,
    x_ref, cot_ref, act_out, gin_out, o_qkv, o_out, o_up, o_down,
    W, G2, G3, xh, yh, xf, yf, zl, units, xs2, xr2,
    rows1, dfeed, qkv, probs, heads, mid, rows2, act, gp, datt,
    own_a, own_c, send_t, send_x, got, got_t, acc, acc_up, sums, sums_got,
    sem_in, ag_send, ag_recv, pg_send, pg_recv, rs_send, rs_recv, ps_send, ps_recv,
    pair_send, pair_recv, sums_send, sums_recv,
):
    at = Place()
    greet(at)
    rows_in = [pltpu.make_async_copy(a, b, sem_in.at[1 + i]) for i, (a, b) in enumerate(((x_hbm, x_ref), (cot_hbm, cot_ref)))]
    for c in rows_in:
        c.start()
    t, x = at.t, at.x
    shard = wup.shape[0]
    own = x_ref.shape[0]
    width = x_ref.shape[1]
    dbr = dfeed.at[0 : 2 * own, :]
    dproj = qkv

    def spot(far_x, far_t):
        return at_rows((far_x * 2 + far_t) * own, own)

    mine, theirs = at_rows(t * own, own), at_rows((1 - t) * own, own)

    here = at_rows(at.dp * shard, shard)
    quarter = pl.ds(pl.multiple_of(x * 1024, 1024), 1024)
    loads = [
        pltpu.make_async_copy(src, W.at[here, pl.ds(c0, n)], sem_in.at[0])
        for src, c0, n in (
            [(wqkv.at[j, :, pl.ds(128 * h, 128)], QKV + 384 * h + 128 * j, 128) for h in range(4) for j in range(3)]
            + [(wout, OUT, 512), (wup.at[:, quarter], UP, 1024), (wdown.at[:, quarter], DOWN, 1024)]
        )
    ]
    for c in loads:
        c.start()
    enter(at)
    g = Gather(at, W, shard, PIECES, ag_send, ag_recv)
    pg = PairGather(at, W, shard, ((UP, 1024), (DOWN, 1024)), (wup, wdown), pg_send, pg_recv)
    pltpu.make_async_copy(W.at[here, :], W.at[here, :], sem_in.at[0]).wait()

    home = {0: (W, DOWN, DOWN + 384), 1: (W, DOWN + 384, DOWN + 768), 2: (G3, 512, 896), 3: (W, OUT, OUT + 384), 4: (G3, 0, 512)}
    sc = Scatter(at, lambda p: home[p], shard, PIECES, xh, yh, xf, yf, zl, rs_send, rs_recv)
    home_pair = {0: (W, UP, 1024), 1: (G2, 0, 1024)}
    ps = PairScatter(at, lambda m: home_pair[m], shard, LINE_FIRST, units, xs2, xr2, ps_send, ps_recv)

    def write(p):
        def store(total):
            if p < 4:
                for j in range(3):
                    o_qkv[j, :, 128 * p : 128 * (p + 1)] = total[:, 128 * j : 128 * (j + 1)]
            else:
                o_out[...] = total
        return store

    def write_pair(m):
        ref = o_up if m == 0 else o_down

        def store(far_x, total):
            ref[:, pl.ds(pl.multiple_of(far_x * 1024, 1024), 1024)] = total
        return store

    def share_feed():
        shares.append(share(2, dfeed, spot(x, t), at.across_x()))

    actions = {
        0: g.line, 1: g.plane, 2: lambda m: pg.x_copy(m).start(), 3: pg.line, 4: pg.cross, 5: share_feed,
        10: sc.begin, 11: sc.plane, 12: lambda p, k, w: sc.line(p, k, w, write(p)),
        13: ps.begin, 14: lambda m, k, w: ps.line(m, k, w, write_pair(m)), 15: lambda m: ps.last(m, write_pair(m)),
        16: ps.line_first, 17: lambda m: ps.meet(m, write_pair(m)),
    }
    done = [0]

    def run(part):
        while done[0] <= min(part, len(PLAN) - 1):
            for kind, *a in PLAN[done[0]]:
                actions[kind](*a)
            done[0] += 1

    def quiet(part):
        return part >= len(PLAN) or not PLAN[part]

    def send(i, src, dst, other):
        return pltpu.make_async_remote_copy(
            src_ref=src, dst_ref=dst, send_sem=pair_send.at[i], recv_sem=pair_recv.at[i],
            device_id=other, device_id_type=MESH,
        )

    def share(i, ref, r, other):
        c = send(i, ref.at[r, :], ref.at[r, :], other)
        c.start()
        return c

    def take(i, ref, r):
        send(i, ref.at[r, :], ref.at[r, :], at.twin()).wait_recv()

    for ref in (acc, acc_up):
        ref[...] = jnp.zeros_like(ref)
    total_of = {name: acc.at[i] for i, name in enumerate(SUMS)}

    def add(name, v):
        ref = total_of[name]
        ref[...] += fold(v)

    def valid_of(image, start, size):
        slot = lax.broadcasted_iota(jnp.int32, (size, 1), 0) + start
        return slot < counts[image] + BUFFER

    def each_block(body):
        def go(b, _):
            body(b * BLOCK, pl.ds(pl.multiple_of(b * BLOCK, BLOCK), BLOCK))
            return 0
        lax.fori_loop(0, own // BLOCK, go, 0)

    def tiles(first, last, body, size=256):
        def go(i, _):
            body(pl.multiple_of(i * size, size))
            return 0
        lax.fori_loop(first // size, last // size, go, 0)

    def first_norm(b, r):
        xv = x_ref[r, :].astype(F32)
        keep = valid_of(t, b, BLOCK).astype(F32)
        n, _ = normed(xv)
        mine_b = pl.ds(pl.multiple_of(t * own + b, BLOCK), BLOCK)
        rows1[mine_b, :] = (n * g1[...] + s1[...]).astype(BF)
        add("x", keep * xv * xv)
        low = (cot_ref[r, :].astype(F32) * keep).astype(BF)
        dfeed[pl.ds(pl.multiple_of((x * 2 + t) * own + b, BLOCK), BLOCK), :] = low
        add("bdown", low.astype(F32))

    for c in rows_in:
        c.wait()
    run(0)
    each_block(first_norm)
    shares = [share(0, rows1, mine, at.twin()), share(1, dfeed, spot(x, t), at.twin())]

    def project(j):
        heads_of = pl.ds(pl.multiple_of(t * 512 + 128 * j, 128), 128)
        cols = pl.ds(QKV + 384 * j, 384)
        bias = jnp.concatenate([bqv[0:1, heads_of], jnp.zeros((1, 128), F32), bqv[1:2, heads_of]], axis=1)
        scale = jnp.where(lax.broadcasted_iota(jnp.int32, (1, 384), 1) < 128, HD**-0.5, 1.0)

        def body(i, _):
            r = at_rows(i * own, own)
            qkv[r, pl.ds(384 * j, 384)] = ((nn(rows1[r, :], W[:, cols]) + bias) * scale).astype(BF)
            return 0
        lax.fori_loop(0, 2, body, 0)

    first_lanes = lax.broadcasted_iota(jnp.int32, (own, 128), 1) < HD

    def attend(image, j):
        r = pl.ds(pl.multiple_of(image * own, own), own)
        c = 384 * j
        q2 = qkv[r, c : c + 128]
        k2 = qkv[r, c + 128 : c + 256]
        v_t = qkv[r, c + 256 : c + 384].T
        hide = jnp.where(valid_of(image, 0, own), 0.0, -1e30)
        outs = []
        for a in range(2):
            qm = jnp.where(first_lanes if a == 0 else ~first_lanes, q2, jnp.zeros_like(q2))
            s = nt(k2, qm) + hide
            e = jnp.exp(s - jnp.max(s, axis=0, keepdims=True))
            low = (e * (1.0 / jnp.sum(e, axis=0, keepdims=True))).astype(BF)
            probs[(j * 2 + image) * 2 + a] = low
            outs.append(nn(v_t[a * HD : (a + 1) * HD], low))
        heads[r, 128 * j : 128 * (j + 1)] = jnp.concatenate(outs, axis=0).T.astype(BF)

    def images(part, body, j):
        run(part)
        if quiet(part + 1):
            def go(i, _):
                body(i, j)
                return 0
            lax.fori_loop(0, 2, go, 0)
        else:
            body(0, j)
            run(part + 1)
            body(1, j)

    for j in range(4):
        run(1 + 4 * j)
        g.finish(j)
        if j == 0:
            take(0, rows1, theirs)
        run(2 + 4 * j)
        project(j)
        images(3 + 4 * j, attend, j)
    run(17)
    g.finish(4)
    run(18)

    def others(i, src, cols, k):
        def body(c):
            send_t[0, :, pl.ds(c, 512)] = nt(src[theirs, :], W[pl.ds(c, 512), cols]).astype(BF)
        tiles(0, width, body, 512)
        copy = send(i, send_t.at[0], got.at[k], at.twin())
        copy.start()
        return copy

    def owns(src, cols, keep):
        def body(c):
            keep[:, pl.ds(c, 512)] = nt(src[mine, :], W[pl.ds(c, 512), cols])
        tiles(0, width, body, 512)

    branch_copy = others(3, heads, pl.ds(OUT, 512), 0)
    run(19)
    owns(heads, pl.ds(OUT, 512), own_a)
    run(20)
    branch_copy.wait()

    def second_norm(b, r):
        keep = valid_of(t, b, BLOCK).astype(F32)
        branch = own_a[r, :] + got[0, r, :].astype(F32) + bout[...]
        m = x_ref[r, :].astype(F32) + branch
        mid[r, :] = m
        add("branch", keep * branch * branch)
        add("mid", keep * m * m)
        n, _ = normed(m)
        rows2[pl.ds(pl.multiple_of((x * 2 + t) * own + b, BLOCK), BLOCK), :] = (n * g2[...] + s2[...]).astype(BF)

    run(21)
    each_block(second_norm)
    run(22)
    shares.append(share(4, rows2, spot(x, t), at.across_x()))
    shares.append(share(5, rows2, spot(x, t), at.twin()))
    run(23)

    take(2, dfeed, spot(1 - x, t))
    shares.append(share(6, dfeed, spot(1 - x, t), at.twin()))
    take(1, dfeed, spot(x, 1 - t))
    run(24)
    take(5, rows2, spot(x, 1 - t))

    chip_rows = lambda far_x: at_rows(far_x * 2 * own, 2 * own)

    def halves(part, body):
        run(part)
        if quiet(part + 1):
            tiles(0, 1024, body, 512)
        else:
            body(0)
            run(part + 1)
            body(512)

    def hidden(far_x, part):
        r = chip_rows(far_x)

        def body(c):
            def part_of(d):
                cols = pl.multiple_of(c + d, 256)
                lanes = pl.ds(pl.multiple_of(t * 2048 + x * 1024 + cols, 256), 256)
                u = nn(rows2[r, :], W[:, pl.ds(UP + cols, 256)]) + bup[:, lanes]
                below = 0.5 * (1.0 + lax.erf(u * (0.5**0.5)))
                dense = jnp.exp(-0.5 * u * u) * 0.3989422804014327
                act[r, pl.ds(cols, 256)] = (u * below).astype(BF)
                gp[r, pl.ds(cols, 256)] = (below + u * dense).astype(BF)
            tiles(0, 512, part_of)
        halves(part, body)

    def grad_down(c):
        def part(d):
            cols = pl.ds(pl.multiple_of(c + d, 256), 256)
            G2[:, cols] = tn(dfeed[...], act[:, cols]).astype(BF)
        tiles(0, 512, part)

    run(25)
    pg.finish(0)
    hidden(x, 26)
    run(28)
    take(4, rows2, spot(1 - x, t))
    shares.append(share(7, rows2, spot(1 - x, t), at.twin()))
    run(29)
    take(7, rows2, spot(1 - x, 1 - t))
    hidden(1 - x, 30)
    take(6, dfeed, spot(1 - x, 1 - t))
    halves(33, grad_down)
    run(37)

    def back_act(far_x):
        r = chip_rows(far_x)

        def body(c):
            cols = pl.ds(c, 256)
            d = nn(dfeed[r, :], W[:, pl.ds(DOWN + c, 256)])
            low = (d * gp[r, cols].astype(F32)).astype(BF)
            gp[r, cols] = low
            acc_up[t * 2 + x, :, cols] += fold(low.astype(F32))
        tiles(0, 1024, body)

    class Sum4:
        def __init__(self, i, n, src, cols, keep, parts):
            self.i, self.n, self.src, self.cols, self.keep, self.parts = i, n, src, cols, keep, parts

        def away(self, far_x, slot):
            r = spot(far_x, 1 - t)

            def body(c):
                send_t[slot, :, pl.ds(c, 512)] = nt(self.src[r, :], W[pl.ds(c, 512), self.cols]).astype(BF)
            tiles(0, width, body, 512)
            copy = send(self.i + slot, send_t.at[slot], got_t.at[self.n, slot], at.twin())
            copy.start()
            return copy

        def far(self):
            first = self.away(1 - x, 0)

            r = spot(1 - x, t)

            def product(c):
                send_x[self.n, :, pl.ds(c, 512)] = nt(self.src[r, :], W[pl.ds(c, 512), self.cols]).astype(BF)
            tiles(0, width, product, 512)
            run(self.parts[0])
            first.wait()

            def body(b, r):
                send_x[self.n, r, :] = send_x[self.n, r, :] + got_t[self.n, 0, r, :]
            each_block(body)
            self.cross = send(self.i + 2, send_x.at[self.n], got.at[2 + self.n], at.across_x())
            run(self.parts[1])
            self.cross.start()

        def near(self):
            self.second = self.away(x, 1)
            r = spot(x, t)

            def body(c):
                self.keep[:, pl.ds(c, 512)] = nt(self.src[r, :], W[pl.ds(c, 512), self.cols])
            tiles(0, width, body, 512)

        def value(self, r):
            return self.keep[r, :] + got_t[self.n, 1, r, :].astype(F32) + got[2 + self.n, r, :].astype(F32)

    pg.finish(1)
    run(39)
    back_act(1 - x)
    run(40)
    two = Sum4(8, 0, gp, pl.ds(UP, 1024), own_a, (41, 42))
    two.far()
    run(43)
    back_act(x)
    run(44)
    two.near()
    g.drain()
    pg.drain(dfeed)

    def grad_up(c):
        def part(d):
            cols = pl.multiple_of(c + d, 256)
            W[:, pl.ds(UP + cols, 256)] = tn(rows2[...], gp[:, pl.ds(cols, 256)]).astype(BF)
        tiles(0, 512, part)

    halves(45, grad_up)
    run(48)
    four = Sum4(11, 1, act, pl.ds(DOWN, 1024), own_c, (49, 50))
    four.far()
    run(51)
    two.second.wait()
    four.near()
    run(52)
    two.cross.wait()
    for i in (1, 2, 5):
        shares[i].wait_send()

    def second_back(b, r):
        dy = two.value(r)
        n, scale = normed(mid[r, :])
        keep = valid_of(t, b, BLOCK).astype(F32)
        add("g2", dy * n)
        add("s2", dy)
        d = cot_ref[r, :].astype(F32) * keep + norm_back(dy, n, scale, g2[...])
        gin_out[r, :] = d
        low = d.astype(BF)
        dbr[pl.ds(pl.multiple_of(t * own + b, BLOCK), BLOCK), :] = low
        add("bout", low.astype(F32))

    run(54)
    each_block(second_back)
    shares.append(share(14, dbr, mine, at.twin()))
    run(55)
    take(14, dbr, theirs)
    run(56)

    def back_heads(c):
        datt[:, pl.ds(c, 512)] = nn(dbr[...], W[:, pl.ds(OUT + c, 512)]).astype(BF)

    back_heads(0)
    run(59)

    def grad_out(c):
        G3[:, pl.ds(c, 512)] = tn(dbr[...], heads[:, pl.ds(c, 512)]).astype(BF)

    grad_out(0)
    run(60)

    def grad_heads(p):
        ref, c0, c1 = home[p]

        def body(c):
            ref[pl.ds(c, 512), c0:c1] = tn(rows1[:, pl.ds(c, 512)], dproj[:, 384 * p : 384 * (p + 1)]).astype(BF)
        tiles(0, width, body, 512)

    def attend_back(image, j):
        r = pl.ds(pl.multiple_of(image * own, own), own)
        c = 384 * j
        q2 = qkv[r, c : c + 128]
        k_t = qkv[r, c + 128 : c + 256].T
        v2 = qkv[r, c + 256 : c + 384]
        da = datt[r, 128 * j : 128 * (j + 1)]
        dq, dk, dv = [], [], []
        for a in range(2):
            dam = jnp.where(first_lanes if a == 0 else ~first_lanes, da, jnp.zeros_like(da))
            low = probs[(j * 2 + image) * 2 + a]
            p = low.astype(F32)
            dp = nt(v2, dam)
            ds = (p * (dp - jnp.sum(p * dp, axis=0, keepdims=True))).astype(BF)
            dq.append(nn(k_t[a * HD : (a + 1) * HD], ds))
            dk.append(nn(ds, q2))
            dv.append(nn(low, da))
        for base, v in (
            (0, jnp.concatenate(dq, axis=0).T * HD**-0.5),
            (128, jnp.where(first_lanes, dk[0], dk[1])),
            (256, jnp.where(first_lanes, dv[0], dv[1])),
        ):
            v = v.astype(BF)
            dproj[r, c + base : c + base + 128] = v
            if base != 128:
                lanes = pl.ds(pl.multiple_of(t * 512 + 128 * j, 128), 128)
                ref = total_of["bq" if base == 0 else "bv"]
                ref[:, lanes] += fold(v.astype(F32))

    def finish_feed(b, r):
        keep = valid_of(t, b, BLOCK).astype(F32)
        feed = four.value(r) + bdown[...]
        res = mid[r, :] + feed
        add("feed", keep * feed * feed)
        add("res", keep * res * res)
        act_out[r, :] = (keep * res).astype(BF)

    for j in range(3):
        images(61 + 4 * j, attend_back, j)
        run(63 + 4 * j)
        grad_heads(j)
    run(73)
    four.second.wait()
    four.cross.wait()
    run(74)
    each_block(finish_feed)
    outs = [pltpu.make_async_copy(act_out, act_hbm, sem_in.at[3])]
    outs[0].start()
    images(75, attend_back, 3)
    run(77)
    one_copy = others(15, dproj, pl.ds(QKV, 1536), 1)
    run(78)
    grad_heads(3)
    run(80)
    owns(dproj, pl.ds(QKV, 1536), own_a)
    run(81)
    one_copy.wait()
    run(82)

    def first_back(b, r):
        dy = own_a[r, :] + got[1, r, :].astype(F32)
        n, scale = normed(x_ref[r, :].astype(F32))
        add("g1", dy * n)
        add("s1", dy)
        gin_out[r, :] += norm_back(dy, n, scale, g1[...])

    each_block(first_back)
    outs.append(pltpu.make_async_copy(gin_out, gin_hbm, sem_in.at[4]))
    outs[1].start()
    run(83)

    for i in range(8):
        sums[i : i + 1, :] = jnp.sum(acc[i], axis=0, keepdims=True)
    for i in range(4):
        sums[8 + i : 9 + i, :] = jnp.sum(acc_up[i], axis=0, keepdims=True)
    lane = lax.broadcasted_iota(jnp.int32, (1, width), 1)
    row = jnp.where(lane == 5, (counts[t] + BUFFER).astype(F32), 0.0)
    for i, name in enumerate(("x", "mid", "res", "branch", "feed")):
        row = jnp.where(lane == i, jnp.sum(jnp.sum(total_of[name][...], axis=0, keepdims=True), axis=1, keepdims=True), row)
    sums[12:13, :] = row
    sums[13:16, :] = jnp.zeros((3, width), F32)
    for i, other in enumerate((at.twin(), at.across_x(), at.across_y(), at.near(), at.far())):
        c = pltpu.make_async_remote_copy(
            src_ref=sums, dst_ref=sums_got.at[i], send_sem=sums_send.at[i], recv_sem=sums_recv.at[i],
            device_id=other, device_id_type=MESH,
        )
        run(84 + 2 * i)
        c.start()
        run(85 + 2 * i)
        c.wait()
        sums[...] += sums_got[i]
    o_sums[...] = sums[...]
    run(1000)
    for i, (a, b) in enumerate(((o_qkv, qkv_hbm), (o_out, out_hbm), (o_up, up_hbm), (o_down, down_hbm))):
        outs.append(pltpu.make_async_copy(a, b, sem_in.at[5 + i]))
        outs[-1].start()
    sent = W.at[0 : 15 * shard, 0:2048]
    sc.drain(sent)
    ps.drain(sent)
    for c in outs:
        c.wait()
    for i in (0, 3, 4, 6, 7):
        shares[i].wait_send()


def block(counts, stream, cotangent, w_qkv, w_out_t, w_up, w_down_t, b_qv, b_out, b_up, b_down, g1, s1, g2, s2):
    own, width = stream.shape
    shard = w_up.shape[0]
    rows = 16 * shard
    group = 2 * own
    vmem = pl.BlockSpec(memory_space=pltpu.VMEM)
    hbm = pl.BlockSpec(memory_space=pl.ANY)
    dma = pltpu.SemaphoreType.DMA
    row = lambda v: v.reshape(1, -1)
    return pl.pallas_call(
        block_kernel,
        out_shape=(
            jax.ShapeDtypeStruct((own, width), BF),
            jax.ShapeDtypeStruct((own, width), F32),
            jax.ShapeDtypeStruct((3, shard, 512), F32),
            jax.ShapeDtypeStruct((shard, 512), F32),
            jax.ShapeDtypeStruct((shard, 2048), F32),
            jax.ShapeDtypeStruct((shard, 2048), F32),
            jax.ShapeDtypeStruct((16, width), F32),
        ),
        in_specs=[pl.BlockSpec(memory_space=pltpu.SMEM)] + [hbm] * 6 + [vmem] * 8,
        out_specs=(hbm,) * 6 + (vmem,),
        scratch_shapes=[
            pltpu.VMEM((own, width), BF),
            pltpu.VMEM((own, width), BF),
            pltpu.VMEM((own, width), BF),
            pltpu.VMEM((own, width), F32),
            pltpu.VMEM((3, shard, 512), F32),
            pltpu.VMEM((shard, 512), F32),
            pltpu.VMEM((shard, 2048), F32),
            pltpu.VMEM((shard, 2048), F32),
            pltpu.VMEM((rows, COLS), BF),
            pltpu.VMEM((rows, 1024), BF),
            pltpu.VMEM((rows, 1024), BF),
            pltpu.VMEM((4, shard // 2, 2048), BF),
            pltpu.VMEM((4, shard // 2, 2048), BF),
            pltpu.VMEM((4, shard, 2048), BF),
            pltpu.VMEM((4, shard, 2048), BF),
            pltpu.VMEM((5, shard, 2048), BF),
            pltpu.VMEM((18 + 2 * len(LINE_FIRST), 2 * shard, 1024), BF),
            pltpu.VMEM((2, shard, 1024), BF),
            pltpu.VMEM((2, shard, 1024), BF),
            pltpu.VMEM((group, width), BF),
            pltpu.VMEM((2 * group, width), BF),
            pltpu.VMEM((group, 1536), BF),
            pltpu.VMEM((16, own, own), BF),
            pltpu.VMEM((group, 512), BF),
            pltpu.VMEM((own, width), F32),
            pltpu.VMEM((2 * group, width), BF),
            pltpu.VMEM((2 * group, 1024), BF),
            pltpu.VMEM((2 * group, 1024), BF),
            pltpu.VMEM((group, 512), BF),
            pltpu.VMEM((own, width), F32),
            pltpu.VMEM((own, width), F32),
            pltpu.VMEM((2, own, width), BF),
            pltpu.VMEM((2, own, width), BF),
            pltpu.VMEM((4, own, width), BF),
            pltpu.VMEM((2, 2, own, width), BF),
            pltpu.VMEM((len(SUMS), 8, width), F32),
            pltpu.VMEM((4, 8, 1024), F32),
            pltpu.VMEM((16, width), F32),
            pltpu.VMEM((5, 16, width), F32),
            dma((9,)),
            dma((2,)),
            dma((5, 13)),
            dma((2,)),
            dma((2, 10)),
            dma((1,)),
            dma((5, 13)),
            dma((1,)),
            dma((2, 12)),
            dma((16,)),
            dma((16,)),
            dma((5,)),
            dma((5,)),
        ],
        compiler_params=pltpu.CompilerParams(
            collective_id=1, has_side_effects=True, vmem_limit_bytes=63 << 20
        ),
    )(
        counts, stream, cotangent, w_qkv, w_out_t, w_up, w_down_t,
        b_qv, row(b_out), row(b_up), row(b_down), row(g1), row(s1), row(g2), row(s2),
    )


def close_kernel(*refs):
    big, sums, out, small, held, sem = refs[:6], refs[6], refs[7:13], refs[13:22], refs[22:28], refs[28]
    loads = [pltpu.make_async_copy(a, h, sem.at[0, i]) for i, (a, h) in enumerate(zip(big, held))]
    copies = [pltpu.make_async_copy(h, b, sem.at[1, i]) for i, (h, b) in enumerate(zip(held, out))]
    for c in loads:
        c.start()
    place = lax.axis_index("dp") * 2 + lax.axis_index("tensor")
    width = sums.shape[1]
    turned = pltpu.roll(sums[0:8, :], width - place * 32, 1)
    small[0][...] = turned[0:2, :32]
    for i in range(1, 7):
        small[i][...] = turned[i + 1 : i + 2, :32]
    up = pl.ds(pl.multiple_of((place % 8) * 128, 128), 128)
    which = lax.broadcasted_iota(jnp.int32, (8, 128), 0) == place // 8
    small[7][...] = jnp.sum(jnp.where(which, sums[8:16, up], 0.0), axis=0, keepdims=True)
    row = sums[12:13, :]
    small[8][...] = jnp.sqrt(row[:, 0:5] / (row[:, 5:6] * width))
    for load, c in zip(loads, copies):
        load.wait()
        c.start()
    for c in copies:
        c.wait()


def close(*arrays):
    vmem = pl.BlockSpec(memory_space=pltpu.VMEM)
    hbm = pl.BlockSpec(memory_space=pl.ANY)
    small = [(2, 32)] + [(1, 32)] * 6 + [(1, 128), (1, 5)]
    return pl.pallas_call(
        close_kernel,
        out_shape=tuple(jax.ShapeDtypeStruct(a.shape, a.dtype) for a in arrays[:6])
        + tuple(jax.ShapeDtypeStruct(n, F32) for n in small),
        in_specs=[hbm] * 6 + [vmem],
        out_specs=(hbm,) * 6 + (vmem,) * 9,
        scratch_shapes=[pltpu.VMEM(a.shape, a.dtype) for a in arrays[:6]] + [pltpu.SemaphoreType.DMA((2, 6))],
    )(*arrays)


def local_fast(
    stream, counts, cotangent, w_qkv, b_qv, w_out, b_out, w_fc1, b_fc1, w_fc2, b_fc2,
    gain_one, shift_one, gain_two, shift_two,
):
    acts, grad_in, p_qkv, p_out, p_up, p_down, bqv, *rest = close(
        *block(
            counts, stream, cotangent, w_qkv, w_out.T, w_fc1, w_fc2.T, b_qv, b_out, b_fc1, b_fc2,
            gain_one, shift_one, gain_two, shift_two,
        )
    )
    bout, bdown, gain1, shift1, gain2, shift2, bup, rms = (v.reshape(-1) for v in rest[:8])
    return (
        acts, grad_in, p_qkv, bqv, p_out.T, bout, p_up, bup, p_down.T, bdown,
        gain1, shift1, gain2, shift2, rms,
    )

def layer_norm(values, gain, shift):
    centre = jnp.mean(values, axis=-1, keepdims=True)
    offset = values - centre
    spread = jnp.mean(offset * offset, axis=-1, keepdims=True)
    return offset * lax.rsqrt(spread + eps_norm) * gain + shift


def gelu_exact(values):
    return jax.nn.gelu(values, approximate=False)


def masked_scores(queries, key_rows, validity):
    scores = jnp.einsum(
        "bqhd,bkhd->bhqk", queries, key_rows, preferred_element_type=jnp.float32
    ) * HD ** (-0.5)
    return jnp.where(validity[:, None, None, :] > 0, scores, -1e30)


def attend_block(members):
    queries, key_rows, values, validity = members
    scores = masked_scores(queries, key_rows, validity)
    highest = jnp.max(scores, axis=-1, keepdims=True)
    expo_terms = jnp.exp(scores - highest)
    totals = jnp.sum(expo_terms, axis=-1, keepdims=True)
    weights = (expo_terms / totals).astype(jnp.bfloat16)
    mixture = jnp.einsum("bhqk,bkhd->bqhd", weights, values, preferred_element_type=jnp.float32)
    return (mixture.astype(jnp.bfloat16), (highest + jnp.log(totals))[..., 0])


def attend_back(members):
    queries, key_rows, values, validity, log_total, d_mixture = members
    scores = masked_scores(queries, key_rows, validity)
    probs = jnp.exp(scores - log_total[..., None])
    d_values = jnp.einsum(
        "bhqk,bqhd->bkhd", probs.astype(jnp.bfloat16), d_mixture, preferred_element_type=jnp.float32
    )
    d_probs = jnp.einsum("bqhd,bkhd->bhqk", d_mixture, values, preferred_element_type=jnp.float32)
    d_scores = (probs * (d_probs - jnp.sum(probs * d_probs, axis=-1, keepdims=True))).astype(
        jnp.bfloat16
    )
    d_queries = jnp.einsum(
        "bhqk,bkhd->bqhd", d_scores, key_rows, preferred_element_type=jnp.float32
    ) * HD ** (-0.5)
    d_keys = jnp.einsum(
        "bhqk,bqhd->bkhd", d_scores, queries, preferred_element_type=jnp.float32
    ) * HD ** (-0.5)
    return (
        d_queries.astype(jnp.bfloat16),
        d_keys.astype(jnp.bfloat16),
        d_values.astype(jnp.bfloat16),
    )


def local(
    stream,
    counts,
    cotangent,
    w_qkv,
    b_qv,
    w_out,
    b_out,
    w_fc1,
    b_fc1,
    w_fc2,
    b_fc2,
    gain_one,
    shift_one,
    gain_two,
    shift_two,
):
    tensor_pos = lax.axis_index("tensor")
    own_rows = stream.shape[0]
    width = stream.shape[1]
    own_images = own_rows // SLOTS
    slot_index = jnp.arange(SLOTS, dtype=jnp.int32)
    validity_all = (slot_index[None, :] < (BUFFER + counts)[:, None]).astype(jnp.float32)
    own_validity = lax.dynamic_slice_in_dim(validity_all, tensor_pos * own_images, own_images, 0)
    own_valid = own_validity.reshape(own_rows, 1)
    qkv_full, out_full, up_full, down_full = (
        lax.all_gather(w_qkv, "dp", axis=1, tiled=True),
        lax.all_gather(w_out, "dp", axis=1, tiled=True),
        lax.all_gather(w_fc1[None], "dp", axis=1, tiled=True),
        lax.all_gather(w_fc2, "dp", axis=1, tiled=True),
    )
    head_width = w_qkv.shape[2]
    unit_width = w_fc1.shape[1]
    bias_query = lax.dynamic_slice_in_dim(b_qv[0], tensor_pos * head_width, head_width, 0)
    bias_value = lax.dynamic_slice_in_dim(b_qv[1], tensor_pos * head_width, head_width, 0)
    bias_up = lax.dynamic_slice_in_dim(b_fc1, tensor_pos * unit_width, unit_width, 0)
    up_full = up_full[0]
    group_images = validity_all.shape[0]
    group_rows = group_images * SLOTS
    local_heads = head_width // HD
    pairing = 2
    block_count = group_images // pairing
    blocked_valid = validity_all.reshape(block_count, pairing, SLOTS)
    stream_f = stream.astype(jnp.float32)
    normed_one = layer_norm(stream_f, gain_one, shift_one).astype(jnp.bfloat16)
    first_rows = lax.all_gather(normed_one, "tensor", axis=0, tiled=True)
    projected = jnp.einsum("rd,cde->rce", first_rows, qkv_full, preferred_element_type=jnp.float32)
    shape_heads = (block_count, pairing, SLOTS, local_heads, HD)
    queries = (projected[:, 0] + bias_query).astype(jnp.bfloat16).reshape(shape_heads)
    key_rows = projected[:, 1].astype(jnp.bfloat16).reshape(shape_heads)
    values = (projected[:, 2] + bias_value).astype(jnp.bfloat16).reshape(shape_heads)
    mixture, log_total = lax.map(attend_block, (queries, key_rows, values, blocked_valid))
    attn_heads = mixture.reshape(group_rows, head_width)
    taken = attn_heads
    attn_total = lax.psum_scatter(
        jnp.dot(taken, out_full, preferred_element_type=jnp.float32).astype(jnp.bfloat16),
        "tensor",
        scatter_dimension=0,
        tiled=True,
    ).astype(jnp.float32)
    branch = attn_total + b_out
    middle = stream_f + branch
    normed_two = layer_norm(middle, gain_two, shift_two).astype(jnp.bfloat16)
    second_rows = lax.all_gather(normed_two, "tensor", axis=0, tiled=True)
    hidden_pre = jnp.dot(second_rows, up_full, preferred_element_type=jnp.float32) + bias_up
    hidden_act = gelu_exact(hidden_pre).astype(jnp.bfloat16)
    taken = hidden_act
    mlp_total = lax.psum_scatter(
        jnp.dot(taken, down_full, preferred_element_type=jnp.float32).astype(jnp.bfloat16),
        "tensor",
        scatter_dimension=0,
        tiled=True,
    ).astype(jnp.float32)
    feed = mlp_total + b_fc2
    result = middle + feed
    activations = (result * own_valid).astype(jnp.bfloat16)
    squares = jnp.stack(
        [
            jnp.sum(own_valid * member * member)
            for member in (stream_f, middle, result, branch, feed)
        ]
    )
    square_sums, valid_count = lax.psum((squares, jnp.sum(own_valid)), ("dp", "tensor"))
    rms_stats = jnp.sqrt(square_sums / (valid_count * width))
    d_result = cotangent.astype(jnp.float32) * own_valid
    d_feed_low = d_result.astype(jnp.bfloat16)
    d_feed_rows = lax.all_gather(d_feed_low, "tensor", axis=0, tiled=True)
    d_act = jnp.einsum("rd,ud->ru", d_feed_rows, down_full, preferred_element_type=jnp.float32)
    unused_act, gelu_pullback = jax.vjp(gelu_exact, hidden_pre)
    d_pre = gelu_pullback(d_act)[0].astype(jnp.bfloat16)
    grad_down = jnp.einsum("ru,rd->ud", hidden_act, d_feed_rows, preferred_element_type=jnp.float32)
    grad_up = jnp.einsum("rd,ru->du", second_rows, d_pre, preferred_element_type=jnp.float32)
    grad_bias_up = jnp.sum(d_pre, axis=0, dtype=jnp.float32)
    grad_bias_down = jnp.sum(d_feed_low, axis=0, dtype=jnp.float32)
    taken = d_pre
    d_normed_two = lax.psum_scatter(
        jnp.einsum("ru,du->rd", taken, up_full, preferred_element_type=jnp.float32).astype(
            jnp.bfloat16
        ),
        "tensor",
        scatter_dimension=0,
        tiled=True,
    ).astype(jnp.float32)
    unused_two, norm_two_pullback = jax.vjp(layer_norm, middle, gain_two, shift_two)
    d_middle_norm, grad_gain_two, grad_shift_two = norm_two_pullback(d_normed_two)
    d_middle = d_result + d_middle_norm
    d_branch_low = d_middle.astype(jnp.bfloat16)
    grad_bias_out = jnp.sum(d_branch_low, axis=0, dtype=jnp.float32)
    d_branch_rows = lax.all_gather(d_branch_low, "tensor", axis=0, tiled=True)
    d_attn = jnp.einsum(
        "rd,hd->rh", d_branch_rows, out_full, preferred_element_type=jnp.float32
    ).astype(jnp.bfloat16)
    grad_out = jnp.einsum(
        "rh,rd->hd", attn_heads, d_branch_rows, preferred_element_type=jnp.float32
    )
    d_queries, d_keys, d_values = lax.map(
        attend_back,
        (queries, key_rows, values, blocked_valid, log_total, d_attn.reshape(shape_heads)),
    )
    d_projected = jnp.stack(
        [
            d_queries.reshape(group_rows, head_width),
            d_keys.reshape(group_rows, head_width),
            d_values.reshape(group_rows, head_width),
        ],
        axis=1,
    )
    grad_qkv = jnp.einsum(
        "rd,rce->cde", first_rows, d_projected, preferred_element_type=jnp.float32
    )
    bias_terms = jnp.sum(d_projected, axis=0, dtype=jnp.float32)
    taken = d_projected
    d_normed_one = lax.psum_scatter(
        jnp.einsum("rce,cde->rd", taken, qkv_full, preferred_element_type=jnp.float32).astype(
            jnp.bfloat16
        ),
        "tensor",
        scatter_dimension=0,
        tiled=True,
    ).astype(jnp.float32)
    unused_one, norm_one_pullback = jax.vjp(layer_norm, stream_f, gain_one, shift_one)
    d_stream_norm, grad_gain_one, grad_shift_one = norm_one_pullback(d_normed_one)
    grad_input = d_middle + d_stream_norm
    grad_up = grad_up[None]
    bias_qv_full = lax.dynamic_update_slice(
        jnp.zeros((2, width), jnp.float32),
        jnp.stack([bias_terms[0], bias_terms[2]]),
        (jnp.int32(0), tensor_pos * head_width),
    )
    bias_up_full = lax.dynamic_update_slice(
        jnp.zeros((b_fc1.shape[0],), jnp.float32), grad_bias_up, (tensor_pos * unit_width,)
    )
    qkv_part, out_part, up_part, down_part = (
        lax.psum_scatter(
            grad_qkv.astype(jnp.bfloat16), "dp", scatter_dimension=1, tiled=True
        ).astype(jnp.float32),
        lax.psum_scatter(
            grad_out.astype(jnp.bfloat16), "dp", scatter_dimension=1, tiled=True
        ).astype(jnp.float32),
        lax.psum_scatter(
            grad_up.astype(jnp.bfloat16), "dp", scatter_dimension=1, tiled=True
        ).astype(jnp.float32),
        lax.psum_scatter(
            grad_down.astype(jnp.bfloat16), "dp", scatter_dimension=1, tiled=True
        ).astype(jnp.float32),
    )
    small_parts = (
        lax.psum_scatter(bias_qv_full, ("dp", "tensor"), scatter_dimension=1, tiled=True),
        lax.psum_scatter(grad_bias_out, ("dp", "tensor"), scatter_dimension=0, tiled=True),
        lax.psum_scatter(bias_up_full, ("dp", "tensor"), scatter_dimension=0, tiled=True),
        lax.psum_scatter(grad_bias_down, ("dp", "tensor"), scatter_dimension=0, tiled=True),
        lax.psum_scatter(grad_gain_one, ("dp", "tensor"), scatter_dimension=0, tiled=True),
        lax.psum_scatter(grad_shift_one, ("dp", "tensor"), scatter_dimension=0, tiled=True),
        lax.psum_scatter(grad_gain_two, ("dp", "tensor"), scatter_dimension=0, tiled=True),
        lax.psum_scatter(grad_shift_two, ("dp", "tensor"), scatter_dimension=0, tiled=True),
    )
    return (
        activations,
        grad_input,
        qkv_part,
        small_parts[0],
        out_part,
        small_parts[1],
        up_part[0],
        small_parts[2],
        down_part,
        small_parts[3],
        small_parts[4],
        small_parts[5],
        small_parts[6],
        small_parts[7],
        rms_stats,
    )


def solution(mesh):
    fast = mesh.shape["dp"] == 16 and mesh.shape["tensor"] == 2
    return jax.shard_map(
        local_fast if fast else local,
        mesh=mesh,
        in_specs=(
            P(("dp", "tensor"), None),
            P("dp"),
            P(("dp", "tensor"), None),
            P(None, "dp", "tensor"),
            P(),
            P("tensor", "dp"),
            P(),
            P("dp", "tensor"),
            P(),
            P("tensor", "dp"),
            P(),
            P(),
            P(),
            P(),
            P(),
        ),
        out_specs=(
            P(("dp", "tensor"), None),
            P(("dp", "tensor"), None),
            P(None, "dp", "tensor"),
            P(None, ("dp", "tensor")),
            P("tensor", "dp"),
            P(("dp", "tensor")),
            P("dp", "tensor"),
            P(("dp", "tensor")),
            P("tensor", "dp"),
            P(("dp", "tensor")),
            P(("dp", "tensor")),
            P(("dp", "tensor")),
            P(("dp", "tensor")),
            P(("dp", "tensor")),
            P(),
        ),
        check_vma=False,
    )
```

```python
import jax
import jax.numpy as jnp
from jax import lax
from jax.experimental import pallas as pl
from jax.experimental.pallas import tpu as pltpu
from jax.sharding import PartitionSpec as P

HD = 64
BUFFER = 64
SLOTS = 320


eps_norm = 1e-06


MESH = pl.DeviceIdType.MESH


class Place:
    def __init__(self):
        dp = lax.axis_index("dp")
        self.t = lax.axis_index("tensor")
        self.z, self.y, self.x = dp // 4, (dp // 2) % 2, dp % 2
        self.side = self.z // 2
        self.w = self.z + self.side * (3 - 2 * self.z)
        self.step = 1 - 2 * self.side
        self.dp = dp

    def order(self, k):
        o = (self.w, 1 - self.w, 2, 3)[k]
        return 3 * self.side + self.step * o

    def chip(self, z, y, x):
        return z * 4 + y * 2 + x

    def inward(self):
        return (self.chip(self.z + self.step, self.y, self.x), self.t)

    def outward(self):
        return (self.chip(self.z - self.step, self.y, self.x), self.t)

    def across_x(self):
        return (self.chip(self.z, self.y, 1 - self.x), self.t)

    def across_y(self):
        return (self.chip(self.z, 1 - self.y, self.x), self.t)

    def near(self):
        return (self.chip(self.z + 1 - 2 * (self.z % 2), self.y, self.x), self.t)

    def far(self):
        return (self.chip((self.z + 2) % 4, self.y, self.x), self.t)

    def twin(self):
        return (self.dp, 1 - self.t)


def greet(at):
    barrier = pltpu.get_barrier_semaphore()
    for other in (at.across_x(), at.across_y(), at.inward(), at.twin(), at.far()):
        pl.semaphore_signal(barrier, inc=1, device_id=other, device_id_type=MESH)

    @pl.when(at.w == 1)
    def _():
        pl.semaphore_signal(barrier, inc=1, device_id=at.outward(), device_id_type=MESH)


def enter(at):
    pl.semaphore_wait(pltpu.get_barrier_semaphore(), 5 + at.w)


def settle(ref, sem, at, sent):
    copy = pltpu.make_async_remote_copy(
        src_ref=ref, dst_ref=ref, send_sem=sem, recv_sem=sem, device_id=at.twin(), device_id_type=MESH
    )
    if sent:
        copy.wait_send()
    else:
        copy.wait_recv()


class Gather:
    def __init__(self, at, full, shard, pieces, send, recv):
        self.at, self.full, self.shard, self.pieces, self.send, self.recv = at, full, shard, pieces, send, recv

    def rows(self, p, z, y, x, part=None):
        c0, c1 = self.pieces[p]
        start, size = self.at.chip(z, y, x) * self.shard, self.shard
        if part is not None:
            size = self.shard // 2
            start = start + part * size
        return self.full.at[pl.ds(pl.multiple_of(start, size), size), pl.ds(c0, c1 - c0)]

    def copy(self, p, ref, s, r, other):
        return pltpu.make_async_remote_copy(
            src_ref=ref,
            dst_ref=ref,
            send_sem=self.send.at[s],
            recv_sem=self.recv.at[p, r],
            device_id=other,
            device_id_type=MESH,
        )

    def z_in(self, p, z):
        return self.copy(p, self.rows(p, z, self.at.y, self.at.x), 1, z, self.at.inward())

    def z_out(self, p, z):
        return self.copy(p, self.rows(p, z, self.at.y, self.at.x), 1, z, self.at.outward())

    def x_full(self, p, z):
        return self.copy(p, self.rows(p, z, self.at.y, self.at.x), 0, 4 + z, self.at.across_x())

    def y_full(self, p, z):
        return self.copy(p, self.rows(p, z, self.at.y, self.at.x), 0, 8 + z, self.at.across_y())

    def x_half(self, p, z):
        return self.copy(p, self.rows(p, z, 1 - self.at.y, self.at.x, 1), 0, 12, self.at.across_x())

    def y_half(self, p, z):
        return self.copy(p, self.rows(p, z, self.at.y, 1 - self.at.x, 0), 0, 12, self.at.across_y())

    def arrived(self, p, kind, z):
        at = self.at
        ref = (
            lambda: self.rows(p, z, at.y, at.x),
            lambda: self.rows(p, z, at.y, 1 - at.x),
            lambda: self.rows(p, z, 1 - at.y, at.x),
        )[kind]()
        settle(ref, self.recv.at[p, 4 * kind + z], at, False)

    def line(self, p, k, w):
        at = self.at

        @pl.when(at.w == w)
        def _():
            z = at.order(k)
            if k > 0:
                self.arrived(p, 0, z)
            if k == 0 or (k == 1 and w == 1):
                self.z_in(p, z).start()
            if w == 1 and k != 1:
                self.z_out(p, z).start()
            self.x_full(p, z).start()
            self.y_full(p, z).start()

    def plane(self, p, k):
        z = self.at.order(k)
        self.arrived(p, 1, z)
        self.y_half(p, z).start()
        self.arrived(p, 2, z)
        self.x_half(p, z).start()

    def finish(self, p):
        c0, c1 = self.pieces[p]
        settle(self.full.at[0 : 4 * self.shard, c0:c1], self.recv.at[p, 12], self.at, False)

    def drain(self):
        n = sum(c1 - c0 for c0, c1 in self.pieces)
        settle(self.full.at[0 : 12 * self.shard, 0:n], self.send.at[0], self.at, True)
        for w, blocks in ((0, 1), (1, 5)):

            @pl.when(self.at.w == w)
            def _(blocks=blocks):
                settle(self.full.at[0 : blocks * self.shard, 0:n], self.send.at[1], self.at, True)


class Scatter:
    def __init__(self, at, full, shard, pieces, xh, yh, xf, yf, zl, send, recv):
        self.at, self.full, self.shard, self.pieces = at, full, shard, pieces
        self.xh, self.yh, self.xf, self.yf, self.zl = xh, yh, xf, yf, zl
        self.send, self.recv = send, recv

    def cols(self, p):
        c0, c1 = self.pieces[p]
        return pl.ds(c0, c1 - c0)

    def rows(self, p, z, y, x, part=None):
        start, size = self.at.chip(z, y, x) * self.shard, self.shard
        if part is not None:
            size = self.shard // 2
            start = start + part * size
        ref, c0, c1 = self.full(p)
        return ref.at[pl.ds(pl.multiple_of(start, size), size), pl.ds(c0, c1 - c0)]

    def copy(self, p, src, dst, r, other):
        return pltpu.make_async_remote_copy(
            src_ref=src,
            dst_ref=dst,
            send_sem=self.send.at[0],
            recv_sem=self.recv.at[p, r],
            device_id=other,
            device_id_type=MESH,
        )

    def x_half(self, p, z):
        at = self.at
        return self.copy(
            p, self.rows(p, z, 1 - at.y, 1 - at.x, 0), self.xh.at[z, :, self.cols(p)], z, at.across_x()
        )

    def y_half(self, p, z):
        at = self.at
        return self.copy(
            p, self.rows(p, z, 1 - at.y, 1 - at.x, 1), self.yh.at[z, :, self.cols(p)], z, at.across_y()
        )

    def x_full(self, p, z):
        at = self.at
        return self.copy(
            p, self.rows(p, z, at.y, 1 - at.x), self.xf.at[z, :, self.cols(p)], 4 + z, at.across_x()
        )

    def y_full(self, p, z):
        at = self.at
        return self.copy(
            p, self.rows(p, z, 1 - at.y, at.x), self.yf.at[z, :, self.cols(p)], 4 + z, at.across_y()
        )

    def z_in(self, p, z, slot):
        at = self.at
        return self.copy(
            p, self.rows(p, z, at.y, at.x), self.zl.at[slot, :, self.cols(p)], 8 + slot, at.inward()
        )

    def z_out(self, p, z, slot):
        at = self.at
        return self.copy(
            p, self.rows(p, z, at.y, at.x), self.zl.at[slot, :, self.cols(p)], 8 + slot, at.outward()
        )

    def begin(self, p, k):
        z = self.at.order(k)
        self.x_half(p, z).start()
        self.y_half(p, z).start()

    def plane(self, p, k):
        at = self.at
        z = at.order(k)
        settle(self.xf.at[z, :, self.cols(p)], self.recv.at[p, z], at, False)
        ref = self.rows(p, z, 1 - at.y, at.x, 0)
        ref[...] = ref[...] + self.xh[z, :, self.cols(p)]
        self.y_full(p, z).start()
        ref = self.rows(p, z, at.y, 1 - at.x, 1)
        ref[...] = ref[...] + self.yh[z, :, self.cols(p)]
        self.x_full(p, z).start()

    def wait_line(self, p, z, slot):
        self.z_in(p, z, slot).wait_recv()

    def line(self, p, k, w, out):
        at = self.at

        @pl.when(at.w == w)
        def _():
            z = at.order(k)
            full, c0, c1 = self.full(p)
            settle(full.at[0 : 2 * self.shard, c0:c1], self.recv.at[p, 4 + z], at, False)
            ref = self.rows(p, z, at.y, at.x)
            parts = [self.xf.at[z, :, self.cols(p)], self.yf.at[z, :, self.cols(p)]]
            if w == 1:
                self.wait_line(p, z, z)
                parts.append(self.zl.at[z, :, self.cols(p)])
            if k == 0:
                self.wait_line(p, z, 4)
                parts.append(self.zl.at[4, :, self.cols(p)])
            total = ref[...].astype(jnp.float32)
            for part in parts:
                total = total + part[...].astype(jnp.float32)
            if k == 0:
                out(total)
            else:
                ref[...] = total.astype(jnp.bfloat16)
                if w == 0 or k == 3:
                    self.z_in(p, z, z).start()
                elif k == 2:
                    self.z_in(p, z, 4).start()
                else:
                    self.z_out(p, z, 4).start()

    def drain(self, ref):
        settle(ref, self.send.at[0], self.at, True)


class PairGather:
    def __init__(self, at, full, shard, first, columns, sources, send, recv):
        self.first = first
        self.at, self.full, self.shard, self.columns, self.sources = at, full, shard, columns, sources
        self.send, self.recv = send, recv

    def far_x(self, h):
        return self.at.x if h == 0 else 1 - self.at.x

    def rows(self, m, z, y, x):
        c0, n = self.columns[m]
        start = self.at.chip(z, y, x) * self.shard
        return self.full.at[pl.ds(pl.multiple_of(start, self.shard), self.shard), pl.ds(c0, n)]

    def copy(self, m, src, dst, s, r, other):
        return pltpu.make_async_remote_copy(
            src_ref=src,
            dst_ref=dst,
            send_sem=self.send.at[s],
            recv_sem=self.recv.at[m, r],
            device_id=other,
            device_id_type=MESH,
        )

    def x_copy(self, m):
        at = self.at
        c0, n = self.columns[m]
        src = self.sources[m].at[:, pl.ds(pl.multiple_of((1 - at.x) * n, n), n)]
        return self.copy(m, src, self.rows(m, at.z, at.y, at.x), 0, 16, at.across_x())

    def z_in(self, m, h, z):
        ref = self.rows(m, z, self.at.y, self.far_x(h))
        return self.copy(m, ref, ref, 1, 4 * h + z, self.at.inward())

    def z_out(self, m, h, z):
        ref = self.rows(m, z, self.at.y, self.far_x(h))
        return self.copy(m, ref, ref, 1, 4 * h + z, self.at.outward())

    def y_copy(self, m, h, z):
        ref = self.rows(m, z, self.at.y, self.far_x(h))
        return self.copy(m, ref, ref, 0, 17, self.at.across_y())

    def line(self, m, h, k, w):
        at = self.at

        @pl.when(at.w == w)
        def _():
            z = at.order(k)
            ref = self.rows(m, z, at.y, self.far_x(h))
            if k > 0:
                settle(ref, self.recv.at[m, 4 * h + z], at, False)
            elif h == 1:
                settle(ref, self.recv.at[m, 16], at, False)
            if k == 0 or (k == 1 and w == 1):
                self.z_in(m, h, z).start()
            if w == 1 and k != 1:
                self.z_out(m, h, z).start()

    def cross(self, m, h, k, w):
        @pl.when(self.at.w == w)
        def _():
            self.y_copy(m, h, self.at.order(k)).start()

    def over_copy(self, m, h):
        at = self.at
        ref = self.rows(m, at.z, at.y, self.far_x(h))
        return self.copy(m, ref, ref, 0, 17 + h, at.across_y())

    def over(self, m, h):
        at = self.at
        if h == 1:
            settle(self.rows(m, at.z, at.y, 1 - at.x), self.recv.at[m, 16], at, False)
        self.over_copy(m, h).start()

    def column_line(self, m, h, col, k, w):
        at = self.at

        @pl.when(at.w == w)
        def _():
            z = at.order(k)
            ref = self.rows(m, z, at.y if col == 0 else 1 - at.y, self.far_x(h))
            slot = 4 * (2 * h + col) + z
            if k > 0:
                settle(ref, self.recv.at[m, slot], at, False)
            elif col == 1:
                settle(ref, self.recv.at[m, 17 + h], at, False)
            if k == 0 or (k == 1 and w == 1):
                self.copy(m, ref, ref, 1, slot, at.inward()).start()
            if w == 1 and k != 1:
                self.copy(m, ref, ref, 1, slot, at.outward()).start()

    def finish(self, m):
        if m not in self.first:
            c0, n = self.columns[m]
            settle(self.full.at[0 : 8 * self.shard, pl.ds(c0, n)], self.recv.at[m, 17], self.at, False)

    def drain(self, ref):
        later = len(self.first)
        settle(ref.at[0 : (18 - 6 * later) * self.shard // 2, :], self.send.at[0], self.at, True)
        for w, blocks in ((0, 2), (1, 10)):

            @pl.when(self.at.w == w)
            def _(blocks=blocks * (2 + later)):
                settle(ref.at[0 : blocks * self.shard // 2, :], self.send.at[1], self.at, True)


class PairScatter:
    def __init__(self, at, full, shard, first, units, xs, xr, send, recv):
        self.at, self.full, self.shard, self.first = at, full, shard, first
        self.units, self.xs, self.xr, self.send, self.recv = units, xs, xr, send, recv
        self.base = {1: 0, 0: 11 if 1 in first else 9}

    def unit(self, m, z, y):
        ref, c0, n = self.full(m)
        size = 2 * self.shard
        return ref.at[pl.ds(pl.multiple_of((z * 2 + y) * size, size), size), pl.ds(c0, n)]

    def copy(self, m, src, dst, r, other):
        return pltpu.make_async_remote_copy(
            src_ref=src,
            dst_ref=dst,
            send_sem=self.send.at[0],
            recv_sem=self.recv.at[m, r],
            device_id=other,
            device_id_type=MESH,
        )

    def from_y(self, m, z):
        return self.units.at[self.base[m] + (10 if m in self.first else z)]

    def from_z(self, m, col, slot):
        return self.units.at[self.base[m] + (5 * col if m in self.first else 4) + slot]

    def column(self, col):
        return self.at.y if col == 0 else 1 - self.at.y

    def y_copy(self, m, z):
        return self.copy(m, self.unit(m, z, 1 - self.at.y), self.from_y(m, z), 10 if m in self.first else z, self.at.across_y())

    def z_copy(self, m, col, z, slot, other):
        return self.copy(
            m, self.unit(m, z, self.column(col)), self.from_z(m, col, slot), (5 * col if m in self.first else 4) + slot, other
        )

    def x_copy(self, m):
        return self.copy(m, self.xs.at[m], self.xr.at[m], 11, self.at.across_x())

    def begin(self, m, k):
        self.y_copy(m, self.at.order(k)).start()

    def pass_on(self, m, col, k, w):
        at = self.at
        z = at.order(k)
        if w == 0:
            self.z_copy(m, col, z, z, at.inward()).start()
        elif k == 1:
            self.z_copy(m, col, z, 4, at.outward()).start()
        else:
            self.z_copy(m, col, z, z if k == 3 else 4, at.inward()).start()

    def add_line(self, m, col, k, w, extra):
        at = self.at
        z = at.order(k)
        ref = self.unit(m, z, self.column(col))
        parts = list(extra)
        if k == 0:
            self.z_copy(m, col, z, 4, at.inward()).wait_recv()
            parts.append(self.from_z(m, col, 4))
        if w == 1:
            self.z_copy(m, col, z, z, at.inward()).wait_recv()
            parts.append(self.from_z(m, col, z))
        if parts:
            v = ref[...].astype(jnp.float32)
            for part in parts:
                v = v + part[...].astype(jnp.float32)
            ref[...] = v.astype(jnp.bfloat16)

    def finish(self, m, out, second):
        at = self.at
        size = self.shard
        full, c0, n = self.full(m)

        def total(x):
            rows = pl.ds(pl.multiple_of(at.chip(at.z, at.y, x) * size, size), size)
            v = full[rows, pl.ds(c0, n)].astype(jnp.float32)
            if second:
                v = v + self.from_y(m, at.z)[pl.ds(pl.multiple_of(x * size, size), size), :].astype(jnp.float32)
            return v

        self.xs[m] = total(1 - at.x).astype(jnp.bfloat16)
        self.x_copy(m).start()
        out(at.x, total(at.x))

    def line(self, m, k, w, out):
        at = self.at

        @pl.when(at.w == w)
        def _():
            z = at.order(k)
            self.y_copy(m, z).wait_recv()
            self.add_line(m, 0, k, w, [self.from_y(m, z)])
            if k > 0:
                self.pass_on(m, 0, k, w)
            else:
                self.finish(m, out, False)

    def line_first(self, m, col, k, w):
        @pl.when(self.at.w == w)
        def _():
            self.add_line(m, col, k, w, [])
            if k > 0:
                self.pass_on(m, col, k, w)
            elif col == 1:
                self.y_copy(m, self.at.z).start()

    def meet(self, m, out):
        self.y_copy(m, self.at.z).wait_recv()
        self.finish(m, out, True)

    def last(self, m, out):
        self.x_copy(m).wait_recv()
        out(1 - self.at.x, self.xr[m].astype(jnp.float32))

    def drain(self, ref):
        settle(ref, self.send.at[0], self.at, True)


QKV, OUT, UP, DOWN, COLS = 0, 1536, 2048, 3072, 4096
PIECES = ((0, 384), (384, 768), (768, 1152), (1152, 1536), (1536, 2048))
LINE_FIRST = ()
OVER_FIRST = (1,)
PLAN = (
    ((2, 1), (0, 0, 0, 1), (0, 0, 0, 0), (0, 3, 0, 1), (0, 2, 0, 0), (3, 0, 0, 0, 0), (0, 0, 1, 0), (0, 2, 0, 1), (6, 1, 0), (2, 0), (0, 1, 0, 1), (0, 1, 0, 0), (0, 3, 0, 0), (3, 0, 0, 0, 1), (0, 2, 1, 1), (0, 2, 1, 0), (0, 0, 1, 1), (0, 2, 2, 1), (0, 0, 2, 1), (0, 4, 0, 1), (0, 4, 0, 0), (6, 1, 1), (0, 0, 3, 1), (0, 3, 1, 1), (1, 0, 0), (0, 4, 1, 0), (3, 0, 1, 0, 0), (0, 3, 1, 0), (7, 1, 1, 1, 0, 0), (0, 0, 2, 0), (0, 1, 1, 1), (3, 0, 1, 0, 1), (0, 2, 3, 1), (0, 4, 1, 1), (1, 0, 1), (0, 1, 2, 1), (0, 0, 3, 0), (0, 1, 1, 0), (1, 2, 0), (0, 1, 2, 0), (1, 0, 2), (3, 0, 0, 1, 1), (0, 2, 2, 0), (0, 3, 2, 1), (0, 3, 3, 1), (0, 1, 3, 0), (1, 4, 0), (0, 1, 3, 1), (1, 0, 3), (3, 0, 1, 1, 0), (7, 1, 1, 1, 0, 1), (0, 4, 2, 1), (3, 0, 1, 1, 1), (7, 1, 1, 0, 0, 0), (1, 1, 0), (1, 3, 0), (7, 1, 1, 1, 1, 1),),
    ((0, 3, 2, 0), (1, 2, 1), (7, 1, 0, 0, 0, 0), (0, 4, 3, 1), (7, 1, 1, 0, 0, 1), (0, 2, 3, 0), (0, 3, 3, 0), (3, 0, 0, 2, 1), (3, 0, 0, 3, 1), (1, 1, 1), (0, 4, 2, 0), (3, 0, 0, 1, 0), (0, 4, 3, 0), (3, 0, 1, 2, 1),),
    ((1, 1, 2), (1, 1, 3), (7, 1, 0, 1, 0, 1), (3, 0, 0, 2, 0), (7, 1, 1, 0, 1, 1), (1, 2, 2), (1, 2, 3), (7, 1, 0, 0, 0, 1), (7, 1, 1, 0, 2, 1), (1, 4, 1),),
    ((1, 3, 1), (1, 3, 2),),
    (),
    ((1, 4, 2), (4, 0, 1, 0, 0), (4, 0, 0, 0, 1), (1, 4, 3), (1, 3, 3), (7, 1, 0, 1, 0, 0),),
    ((5,),),
    ((7, 1, 1, 0, 1, 0), (4, 0, 0, 0, 0), (7, 1, 1, 1, 1, 0), (3, 0, 1, 2, 0), (4, 0, 0, 1, 0), (3, 0, 1, 3, 1), (4, 0, 1, 0, 1), (7, 1, 0, 0, 1, 1),),
    (),
    (),
    ((4, 0, 0, 2, 0),),
    ((7, 1, 0, 1, 1, 0),),
    (),
    ((7, 1, 0, 1, 1, 1),),
    (),
    (),
    ((4, 0, 0, 1, 1), (4, 0, 0, 2, 1),),
    ((4, 0, 1, 1, 0), (4, 0, 1, 2, 0),),
    ((7, 1, 0, 1, 2, 1),),
    (),
    ((7, 1, 1, 0, 2, 0), (4, 0, 0, 3, 1),),
    ((4, 0, 1, 1, 1),),
    (),
    ((7, 1, 1, 0, 3, 1), (7, 1, 0, 0, 1, 0), (4, 0, 1, 2, 1), (4, 0, 1, 3, 1),),
    ((7, 1, 0, 0, 2, 1), (7, 1, 0, 1, 3, 1), (3, 0, 0, 3, 0), (7, 1, 0, 0, 3, 1), (7, 1, 0, 1, 2, 0), (7, 1, 1, 0, 3, 0), (3, 0, 1, 3, 0),),
    ((4, 0, 1, 3, 0), (4, 0, 0, 3, 0),),
    ((7, 1, 1, 1, 2, 1), (7, 1, 1, 1, 3, 1),),
    (),
    (),
    ((7, 1, 0, 1, 3, 0), (7, 1, 0, 0, 2, 0),),
    ((7, 1, 1, 1, 2, 0), (7, 1, 0, 0, 3, 0),),
    (),
    (),
    (),
    (),
    (),
    (),
    ((13, 1, 3), (7, 1, 1, 1, 3, 0),),
    (),
    (),
    (),
    (),
    (),
    ((13, 1, 2),),
    ((14, 1, 3, 0), (13, 1, 1),),
    (),
    ((13, 1, 0),),
    (),
    (),
    ((13, 0, 3), (14, 1, 3, 1),),
    ((13, 0, 2),),
    ((14, 1, 2, 0),),
    ((13, 0, 1),),
    (),
    (),
    (),
    (),
    (),
    (),
    (),
    (),
    ((10, 4, 3),),
    (),
    (),
    ((10, 4, 2),),
    ((10, 4, 1),),
    (),
    ((14, 1, 2, 1),),
    (),
    ((14, 0, 3, 0), (10, 0, 3),),
    (),
    ((14, 1, 1, 1), (14, 0, 2, 0),),
    (),
    ((10, 1, 3), (10, 1, 2), (10, 2, 3), (10, 2, 2), (10, 0, 2), (10, 4, 0), (10, 0, 1),),
    ((14, 1, 1, 0), (11, 4, 3),),
    ((11, 2, 3), (11, 2, 2), (11, 0, 3), (11, 4, 2), (11, 4, 1), (10, 2, 1),),
    (),
    ((11, 1, 3),),
    (),
    ((10, 1, 1), (11, 4, 0), (12, 4, 3, 0), (12, 4, 2, 0), (11, 0, 2),),
    ((10, 2, 0), (10, 3, 3), (10, 3, 2), (14, 0, 3, 1), (14, 1, 0, 0), (13, 0, 0), (14, 0, 2, 1), (14, 1, 0, 1), (14, 0, 1, 0), (10, 3, 1),),
    ((11, 1, 2), (10, 1, 0),),
    (),
    (),
    (),
    ((14, 0, 1, 1), (11, 1, 1), (12, 0, 3, 0), (11, 3, 3), (12, 1, 3, 0), (11, 2, 1), (12, 4, 3, 1), (12, 2, 3, 0),),
    (),
    ((11, 0, 1), (12, 0, 2, 0), (11, 3, 2), (12, 2, 2, 0), (12, 4, 2, 1), (12, 0, 3, 1), (11, 3, 1), (12, 1, 2, 0), (12, 1, 3, 1), (10, 0, 0),),
    (),
    ((12, 3, 3, 0), (14, 0, 0, 1), (10, 3, 0), (11, 2, 0), (12, 4, 1, 1), (12, 2, 3, 1), (12, 4, 1, 0), (14, 0, 0, 0), (12, 0, 2, 1), (12, 0, 1, 1), (12, 3, 2, 0),),
    (),
    ((12, 1, 2, 1), (12, 2, 1, 0), (12, 0, 1, 0), (12, 1, 1, 0), (12, 1, 1, 1), (12, 3, 3, 1), (11, 1, 0), (12, 2, 2, 1), (12, 2, 1, 1), (12, 3, 1, 0), (11, 0, 0),),
    (),
    ((11, 3, 0), (12, 3, 2, 1), (12, 3, 1, 1), (12, 1, 0, 0), (12, 4, 0, 0), (15, 1), (12, 2, 0, 0), (12, 4, 0, 1), (15, 0), (12, 0, 0, 0), (12, 0, 0, 1), (12, 1, 0, 1),),
    (),
    ((12, 3, 0, 0), (12, 2, 0, 1), (12, 3, 0, 1),),
)
BF, F32 = jnp.bfloat16, jnp.float32
SUMS = ("bq", "bv", "bout", "bdown", "g1", "s1", "g2", "s2", "x", "mid", "res", "branch", "feed")
BLOCK = 32


def nn(a, b):
    return lax.dot_general(a, b, (((1,), (0,)), ((), ())), preferred_element_type=F32)


def nt(a, b):
    return lax.dot_general(a, b, (((1,), (1,)), ((), ())), preferred_element_type=F32)


def tn(a, b):
    return lax.dot_general(a, b, (((0,), (0,)), ((), ())), preferred_element_type=F32)


def at_rows(start, size):
    return pl.ds(pl.multiple_of(start, size), size)


def fold(v):
    return jnp.sum(v.reshape(v.shape[0] // 8, 8, v.shape[1]), axis=0)


def normed(v):
    centre = jnp.mean(v, axis=1, keepdims=True)
    offset = v - centre
    r = lax.rsqrt(jnp.mean(offset * offset, axis=1, keepdims=True) + eps_norm)
    return offset * r, r


def norm_back(dy, n, r, gain):
    dn = dy * gain
    first = jnp.mean(dn, axis=1, keepdims=True)
    second = jnp.mean(dn * n, axis=1, keepdims=True)
    return r * (dn - first - n * second)


def block_kernel(
    counts, x_hbm, cot_hbm, wqkv, wout, wup, wdown, bqv, bout, bup, bdown, g1, s1, g2, s2,
    act_hbm, gin_hbm, qkv_hbm, out_hbm, up_hbm, down_hbm, o_sums,
    x_ref, cot_ref, act_out, gin_out, o_qkv, o_out, o_up, o_down,
    W, G2, G3, xh, yh, xf, yf, zl, units, xs2, xr2,
    rows1, dfeed, qkv, probs, heads, mid, rows2, act, gp, datt,
    own_a, own_c, send_t, send_x, got, got_t, acc, acc_up, sums, sums_got,
    sem_in, ag_send, ag_recv, pg_send, pg_recv, rs_send, rs_recv, ps_send, ps_recv,
    pair_send, pair_recv, sums_send, sums_recv,
):
    at = Place()
    greet(at)
    rows_in = [pltpu.make_async_copy(a, b, sem_in.at[1 + i]) for i, (a, b) in enumerate(((x_hbm, x_ref), (cot_hbm, cot_ref)))]
    for c in rows_in:
        c.start()
    t, x = at.t, at.x
    shard = wup.shape[0]
    own = x_ref.shape[0]
    width = x_ref.shape[1]
    dbr = dfeed.at[0 : 2 * own, :]
    dproj = qkv

    def spot(far_x, far_t):
        return at_rows((far_x * 2 + far_t) * own, own)

    mine, theirs = at_rows(t * own, own), at_rows((1 - t) * own, own)

    here = at_rows(at.dp * shard, shard)
    quarter = pl.ds(pl.multiple_of(x * 1024, 1024), 1024)
    loads = [
        pltpu.make_async_copy(src, W.at[here, pl.ds(c0, n)], sem_in.at[0])
        for src, c0, n in (
            [(wqkv.at[j, :, pl.ds(128 * h, 128)], QKV + 384 * h + 128 * j, 128) for h in range(4) for j in range(3)]
            + [(wout, OUT, 512), (wup.at[:, quarter], UP, 1024), (wdown.at[:, quarter], DOWN, 1024)]
        )
    ]
    for c in loads:
        c.start()
    enter(at)
    g = Gather(at, W, shard, PIECES, ag_send, ag_recv)
    pg = PairGather(at, W, shard, OVER_FIRST, ((UP, 1024), (DOWN, 1024)), (wup, wdown), pg_send, pg_recv)
    pltpu.make_async_copy(W.at[here, :], W.at[here, :], sem_in.at[0]).wait()

    home = {0: (W, DOWN, DOWN + 384), 1: (W, DOWN + 384, DOWN + 768), 2: (G3, 512, 896), 3: (W, OUT, OUT + 384), 4: (G3, 0, 512)}
    sc = Scatter(at, lambda p: home[p], shard, PIECES, xh, yh, xf, yf, zl, rs_send, rs_recv)
    home_pair = {0: (W, UP, 1024), 1: (G2, 0, 1024)}
    ps = PairScatter(at, lambda m: home_pair[m], shard, LINE_FIRST, units, xs2, xr2, ps_send, ps_recv)

    def write(p):
        def store(total):
            if p < 4:
                for j in range(3):
                    o_qkv[j, :, 128 * p : 128 * (p + 1)] = total[:, 128 * j : 128 * (j + 1)]
            else:
                o_out[...] = total
        return store

    def write_pair(m):
        ref = o_up if m == 0 else o_down

        def store(far_x, total):
            ref[:, pl.ds(pl.multiple_of(far_x * 1024, 1024), 1024)] = total
        return store

    def share_feed():
        shares.append(share(2, dfeed, spot(x, t), at.across_x()))

    actions = {
        0: g.line, 1: g.plane, 2: lambda m: pg.x_copy(m).start(), 3: pg.line, 4: pg.cross, 5: share_feed, 6: pg.over, 7: pg.column_line,
        10: sc.begin, 11: sc.plane, 12: lambda p, k, w: sc.line(p, k, w, write(p)),
        13: ps.begin, 14: lambda m, k, w: ps.line(m, k, w, write_pair(m)), 15: lambda m: ps.last(m, write_pair(m)),
        16: ps.line_first, 17: lambda m: ps.meet(m, write_pair(m)),
    }
    done = [0]

    def run(part):
        while done[0] <= min(part, len(PLAN) - 1):
            for kind, *a in PLAN[done[0]]:
                actions[kind](*a)
            done[0] += 1

    def quiet(part):
        return part >= len(PLAN) or not PLAN[part]

    def send(i, src, dst, other):
        return pltpu.make_async_remote_copy(
            src_ref=src, dst_ref=dst, send_sem=pair_send.at[i], recv_sem=pair_recv.at[i],
            device_id=other, device_id_type=MESH,
        )

    def share(i, ref, r, other):
        c = send(i, ref.at[r, :], ref.at[r, :], other)
        c.start()
        return c

    def take(i, ref, r):
        send(i, ref.at[r, :], ref.at[r, :], at.twin()).wait_recv()

    for ref in (acc, acc_up):
        ref[...] = jnp.zeros_like(ref)
    total_of = {name: acc.at[i] for i, name in enumerate(SUMS)}

    def add(name, v):
        ref = total_of[name]
        ref[...] += fold(v)

    def valid_of(image, start, size):
        slot = lax.broadcasted_iota(jnp.int32, (size, 1), 0) + start
        return slot < counts[image] + BUFFER

    def each_block(body):
        def go(b, _):
            body(b * BLOCK, pl.ds(pl.multiple_of(b * BLOCK, BLOCK), BLOCK))
            return 0
        lax.fori_loop(0, own // BLOCK, go, 0)

    def tiles(first, last, body, size=256):
        def go(i, _):
            body(pl.multiple_of(i * size, size))
            return 0
        lax.fori_loop(first // size, last // size, go, 0)

    def first_norm(b, r):
        xv = x_ref[r, :].astype(F32)
        keep = valid_of(t, b, BLOCK).astype(F32)
        n, _ = normed(xv)
        mine_b = pl.ds(pl.multiple_of(t * own + b, BLOCK), BLOCK)
        rows1[mine_b, :] = (n * g1[...] + s1[...]).astype(BF)
        add("x", keep * xv * xv)
        low = (cot_ref[r, :].astype(F32) * keep).astype(BF)
        dfeed[pl.ds(pl.multiple_of((x * 2 + t) * own + b, BLOCK), BLOCK), :] = low
        add("bdown", low.astype(F32))

    for c in rows_in:
        c.wait()
    run(0)
    each_block(first_norm)
    shares = [share(0, rows1, mine, at.twin()), share(1, dfeed, spot(x, t), at.twin())]

    def project(j):
        heads_of = pl.ds(pl.multiple_of(t * 512 + 128 * j, 128), 128)
        cols = pl.ds(QKV + 384 * j, 384)
        bias = jnp.concatenate([bqv[0:1, heads_of], jnp.zeros((1, 128), F32), bqv[1:2, heads_of]], axis=1)
        scale = jnp.where(lax.broadcasted_iota(jnp.int32, (1, 384), 1) < 128, HD**-0.5, 1.0)

        def body(i, _):
            r = at_rows(i * own, own)
            qkv[r, pl.ds(384 * j, 384)] = ((nn(rows1[r, :], W[:, cols]) + bias) * scale).astype(BF)
            return 0
        lax.fori_loop(0, 2, body, 0)

    first_lanes = lax.broadcasted_iota(jnp.int32, (own, 128), 1) < HD

    def attend(image, j):
        r = pl.ds(pl.multiple_of(image * own, own), own)
        c = 384 * j
        q2 = qkv[r, c : c + 128]
        k2 = qkv[r, c + 128 : c + 256]
        v_t = qkv[r, c + 256 : c + 384].T
        hide = jnp.where(valid_of(image, 0, own), 0.0, -1e30)
        outs = []
        for a in range(2):
            qm = jnp.where(first_lanes if a == 0 else ~first_lanes, q2, jnp.zeros_like(q2))
            s = nt(k2, qm) + hide
            e = jnp.exp(s - jnp.max(s, axis=0, keepdims=True))
            low = (e * (1.0 / jnp.sum(e, axis=0, keepdims=True))).astype(BF)
            probs[(j * 2 + image) * 2 + a] = low
            outs.append(nn(v_t[a * HD : (a + 1) * HD], low))
        heads[r, 128 * j : 128 * (j + 1)] = jnp.concatenate(outs, axis=0).T.astype(BF)

    def images(part, body, j):
        run(part)
        if quiet(part + 1):
            def go(i, _):
                body(i, j)
                return 0
            lax.fori_loop(0, 2, go, 0)
        else:
            body(0, j)
            run(part + 1)
            body(1, j)

    for j in range(4):
        run(1 + 4 * j)
        g.finish(j)
        if j == 0:
            take(0, rows1, theirs)
        run(2 + 4 * j)
        project(j)
        images(3 + 4 * j, attend, j)
    run(17)
    g.finish(4)
    run(18)

    def others(i, src, cols, k):
        def body(c):
            send_t[0, :, pl.ds(c, 512)] = nt(src[theirs, :], W[pl.ds(c, 512), cols]).astype(BF)
        tiles(0, width, body, 512)
        copy = send(i, send_t.at[0], got.at[k], at.twin())
        copy.start()
        return copy

    def owns(src, cols, keep):
        def body(c):
            keep[:, pl.ds(c, 512)] = nt(src[mine, :], W[pl.ds(c, 512), cols])
        tiles(0, width, body, 512)

    branch_copy = others(3, heads, pl.ds(OUT, 512), 0)
    run(19)
    owns(heads, pl.ds(OUT, 512), own_a)
    run(20)
    branch_copy.wait()

    def second_norm(b, r):
        keep = valid_of(t, b, BLOCK).astype(F32)
        branch = own_a[r, :] + got[0, r, :].astype(F32) + bout[...]
        m = x_ref[r, :].astype(F32) + branch
        mid[r, :] = m
        add("branch", keep * branch * branch)
        add("mid", keep * m * m)
        n, _ = normed(m)
        rows2[pl.ds(pl.multiple_of((x * 2 + t) * own + b, BLOCK), BLOCK), :] = (n * g2[...] + s2[...]).astype(BF)

    run(21)
    each_block(second_norm)
    run(22)
    shares.append(share(4, rows2, spot(x, t), at.across_x()))
    shares.append(share(5, rows2, spot(x, t), at.twin()))
    run(23)

    take(2, dfeed, spot(1 - x, t))
    shares.append(share(6, dfeed, spot(1 - x, t), at.twin()))
    take(1, dfeed, spot(x, 1 - t))
    run(24)
    take(5, rows2, spot(x, 1 - t))

    chip_rows = lambda far_x: at_rows(far_x * 2 * own, 2 * own)

    def halves(part, body):
        run(part)
        if quiet(part + 1):
            tiles(0, 1024, body, 512)
        else:
            body(0)
            run(part + 1)
            body(512)

    def hidden(far_x, part):
        r = chip_rows(far_x)

        def body(c):
            def part_of(d):
                cols = pl.multiple_of(c + d, 256)
                lanes = pl.ds(pl.multiple_of(t * 2048 + x * 1024 + cols, 256), 256)
                u = nn(rows2[r, :], W[:, pl.ds(UP + cols, 256)]) + bup[:, lanes]
                below = 0.5 * (1.0 + lax.erf(u * (0.5**0.5)))
                dense = jnp.exp(-0.5 * u * u) * 0.3989422804014327
                act[r, pl.ds(cols, 256)] = (u * below).astype(BF)
                gp[r, pl.ds(cols, 256)] = (below + u * dense).astype(BF)
            tiles(0, 512, part_of)
        halves(part, body)

    def grad_down(c):
        def part(d):
            cols = pl.ds(pl.multiple_of(c + d, 256), 256)
            G2[:, cols] = tn(dfeed[...], act[:, cols]).astype(BF)
        tiles(0, 512, part)

    run(25)
    pg.finish(0)
    hidden(x, 26)
    run(28)
    take(4, rows2, spot(1 - x, t))
    shares.append(share(7, rows2, spot(1 - x, t), at.twin()))
    run(29)
    take(7, rows2, spot(1 - x, 1 - t))
    hidden(1 - x, 30)
    take(6, dfeed, spot(1 - x, 1 - t))
    halves(33, grad_down)
    run(37)

    def back_act(far_x):
        r = chip_rows(far_x)

        def body(c):
            cols = pl.ds(c, 256)
            d = nn(dfeed[r, :], W[:, pl.ds(DOWN + c, 256)])
            low = (d * gp[r, cols].astype(F32)).astype(BF)
            gp[r, cols] = low
            acc_up[t * 2 + x, :, cols] += fold(low.astype(F32))
        tiles(0, 1024, body)

    class Sum4:
        def __init__(self, i, n, src, cols, keep, parts):
            self.i, self.n, self.src, self.cols, self.keep, self.parts = i, n, src, cols, keep, parts

        def away(self, far_x, slot):
            r = spot(far_x, 1 - t)

            def body(c):
                send_t[slot, :, pl.ds(c, 512)] = nt(self.src[r, :], W[pl.ds(c, 512), self.cols]).astype(BF)
            tiles(0, width, body, 512)
            copy = send(self.i + slot, send_t.at[slot], got_t.at[self.n, slot], at.twin())
            copy.start()
            return copy

        def far(self):
            first = self.away(1 - x, 0)

            r = spot(1 - x, t)

            def product(c):
                send_x[self.n, :, pl.ds(c, 512)] = nt(self.src[r, :], W[pl.ds(c, 512), self.cols]).astype(BF)
            tiles(0, width, product, 512)
            run(self.parts[0])
            first.wait()

            def body(b, r):
                send_x[self.n, r, :] = send_x[self.n, r, :] + got_t[self.n, 0, r, :]
            each_block(body)
            self.cross = send(self.i + 2, send_x.at[self.n], got.at[2 + self.n], at.across_x())
            run(self.parts[1])
            self.cross.start()

        def near(self):
            self.second = self.away(x, 1)
            r = spot(x, t)

            def body(c):
                self.keep[:, pl.ds(c, 512)] = nt(self.src[r, :], W[pl.ds(c, 512), self.cols])
            tiles(0, width, body, 512)

        def value(self, r):
            return self.keep[r, :] + got_t[self.n, 1, r, :].astype(F32) + got[2 + self.n, r, :].astype(F32)

    pg.finish(1)
    run(39)
    back_act(1 - x)
    run(40)
    two = Sum4(8, 0, gp, pl.ds(UP, 1024), own_a, (41, 42))
    two.far()
    run(43)
    back_act(x)
    run(44)
    two.near()
    g.drain()
    pg.drain(W.at[:, 0:2048])

    def grad_up(c):
        def part(d):
            cols = pl.multiple_of(c + d, 256)
            W[:, pl.ds(UP + cols, 256)] = tn(rows2[...], gp[:, pl.ds(cols, 256)]).astype(BF)
        tiles(0, 512, part)

    halves(45, grad_up)
    run(48)
    four = Sum4(11, 1, act, pl.ds(DOWN, 1024), own_c, (49, 50))
    four.far()
    run(51)
    two.second.wait()
    four.near()
    run(52)
    two.cross.wait()
    for i in (1, 2, 5):
        shares[i].wait_send()

    def second_back(b, r):
        dy = two.value(r)
        n, scale = normed(mid[r, :])
        keep = valid_of(t, b, BLOCK).astype(F32)
        add("g2", dy * n)
        add("s2", dy)
        d = cot_ref[r, :].astype(F32) * keep + norm_back(dy, n, scale, g2[...])
        gin_out[r, :] = d
        low = d.astype(BF)
        dbr[pl.ds(pl.multiple_of(t * own + b, BLOCK), BLOCK), :] = low
        add("bout", low.astype(F32))

    run(54)
    each_block(second_back)
    shares.append(share(14, dbr, mine, at.twin()))
    run(55)
    take(14, dbr, theirs)
    run(56)

    def back_heads(c):
        datt[:, pl.ds(c, 512)] = nn(dbr[...], W[:, pl.ds(OUT + c, 512)]).astype(BF)

    back_heads(0)
    run(59)

    def grad_out(c):
        G3[:, pl.ds(c, 512)] = tn(dbr[...], heads[:, pl.ds(c, 512)]).astype(BF)

    grad_out(0)
    run(60)

    def grad_heads(p):
        ref, c0, c1 = home[p]

        def body(c):
            ref[pl.ds(c, 512), c0:c1] = tn(rows1[:, pl.ds(c, 512)], dproj[:, 384 * p : 384 * (p + 1)]).astype(BF)
        tiles(0, width, body, 512)

    def attend_back(image, j):
        r = pl.ds(pl.multiple_of(image * own, own), own)
        c = 384 * j
        q2 = qkv[r, c : c + 128]
        k_t = qkv[r, c + 128 : c + 256].T
        v2 = qkv[r, c + 256 : c + 384]
        da = datt[r, 128 * j : 128 * (j + 1)]
        dq, dk, dv = [], [], []
        for a in range(2):
            dam = jnp.where(first_lanes if a == 0 else ~first_lanes, da, jnp.zeros_like(da))
            low = probs[(j * 2 + image) * 2 + a]
            p = low.astype(F32)
            dp = nt(v2, dam)
            ds = (p * (dp - jnp.sum(p * dp, axis=0, keepdims=True))).astype(BF)
            dq.append(nn(k_t[a * HD : (a + 1) * HD], ds))
            dk.append(nn(ds, q2))
            dv.append(nn(low, da))
        for base, v in (
            (0, jnp.concatenate(dq, axis=0).T * HD**-0.5),
            (128, jnp.where(first_lanes, dk[0], dk[1])),
            (256, jnp.where(first_lanes, dv[0], dv[1])),
        ):
            v = v.astype(BF)
            dproj[r, c + base : c + base + 128] = v
            if base != 128:
                lanes = pl.ds(pl.multiple_of(t * 512 + 128 * j, 128), 128)
                ref = total_of["bq" if base == 0 else "bv"]
                ref[:, lanes] += fold(v.astype(F32))

    def finish_feed(b, r):
        keep = valid_of(t, b, BLOCK).astype(F32)
        feed = four.value(r) + bdown[...]
        res = mid[r, :] + feed
        add("feed", keep * feed * feed)
        add("res", keep * res * res)
        act_out[r, :] = (keep * res).astype(BF)

    for j in range(3):
        images(61 + 4 * j, attend_back, j)
        run(63 + 4 * j)
        grad_heads(j)
    run(73)
    four.second.wait()
    four.cross.wait()
    run(74)
    each_block(finish_feed)
    outs = [pltpu.make_async_copy(act_out, act_hbm, sem_in.at[3])]
    outs[0].start()
    images(75, attend_back, 3)
    run(77)
    one_copy = others(15, dproj, pl.ds(QKV, 1536), 1)
    run(78)
    grad_heads(3)
    run(80)
    owns(dproj, pl.ds(QKV, 1536), own_a)
    run(81)
    one_copy.wait()
    run(82)

    def first_back(b, r):
        dy = own_a[r, :] + got[1, r, :].astype(F32)
        n, scale = normed(x_ref[r, :].astype(F32))
        add("g1", dy * n)
        add("s1", dy)
        gin_out[r, :] += norm_back(dy, n, scale, g1[...])

    each_block(first_back)
    outs.append(pltpu.make_async_copy(gin_out, gin_hbm, sem_in.at[4]))
    outs[1].start()
    run(83)

    for i in range(8):
        sums[i : i + 1, :] = jnp.sum(acc[i], axis=0, keepdims=True)
    for i in range(4):
        sums[8 + i : 9 + i, :] = jnp.sum(acc_up[i], axis=0, keepdims=True)
    lane = lax.broadcasted_iota(jnp.int32, (1, width), 1)
    row = jnp.where(lane == 5, (counts[t] + BUFFER).astype(F32), 0.0)
    for i, name in enumerate(("x", "mid", "res", "branch", "feed")):
        row = jnp.where(lane == i, jnp.sum(jnp.sum(total_of[name][...], axis=0, keepdims=True), axis=1, keepdims=True), row)
    sums[12:13, :] = row
    sums[13:16, :] = jnp.zeros((3, width), F32)
    for i, other in enumerate((at.twin(), at.across_x(), at.across_y(), at.near(), at.far())):
        c = pltpu.make_async_remote_copy(
            src_ref=sums, dst_ref=sums_got.at[i], send_sem=sums_send.at[i], recv_sem=sums_recv.at[i],
            device_id=other, device_id_type=MESH,
        )
        run(84 + 2 * i)
        c.start()
        run(85 + 2 * i)
        c.wait()
        sums[...] += sums_got[i]
    o_sums[...] = sums[...]
    run(1000)
    for i, (a, b) in enumerate(((o_qkv, qkv_hbm), (o_out, out_hbm), (o_up, up_hbm), (o_down, down_hbm))):
        outs.append(pltpu.make_async_copy(a, b, sem_in.at[5 + i]))
        outs[-1].start()
    sent = W.at[0 : 15 * shard, 0:2048]
    sc.drain(sent)
    ps.drain(sent)
    for c in outs:
        c.wait()
    for i in (0, 3, 4, 6, 7):
        shares[i].wait_send()


def block(counts, stream, cotangent, w_qkv, w_out_t, w_up, w_down_t, b_qv, b_out, b_up, b_down, g1, s1, g2, s2):
    own, width = stream.shape
    shard = w_up.shape[0]
    rows = 16 * shard
    group = 2 * own
    vmem = pl.BlockSpec(memory_space=pltpu.VMEM)
    hbm = pl.BlockSpec(memory_space=pl.ANY)
    dma = pltpu.SemaphoreType.DMA
    row = lambda v: v.reshape(1, -1)
    return pl.pallas_call(
        block_kernel,
        out_shape=(
            jax.ShapeDtypeStruct((own, width), BF),
            jax.ShapeDtypeStruct((own, width), F32),
            jax.ShapeDtypeStruct((3, shard, 512), F32),
            jax.ShapeDtypeStruct((shard, 512), F32),
            jax.ShapeDtypeStruct((shard, 2048), F32),
            jax.ShapeDtypeStruct((shard, 2048), F32),
            jax.ShapeDtypeStruct((16, width), F32),
        ),
        in_specs=[pl.BlockSpec(memory_space=pltpu.SMEM)] + [hbm] * 6 + [vmem] * 8,
        out_specs=(hbm,) * 6 + (vmem,),
        scratch_shapes=[
            pltpu.VMEM((own, width), BF),
            pltpu.VMEM((own, width), BF),
            pltpu.VMEM((own, width), BF),
            pltpu.VMEM((own, width), F32),
            pltpu.VMEM((3, shard, 512), F32),
            pltpu.VMEM((shard, 512), F32),
            pltpu.VMEM((shard, 2048), F32),
            pltpu.VMEM((shard, 2048), F32),
            pltpu.VMEM((rows, COLS), BF),
            pltpu.VMEM((rows, 1024), BF),
            pltpu.VMEM((rows, 1024), BF),
            pltpu.VMEM((4, shard // 2, 2048), BF),
            pltpu.VMEM((4, shard // 2, 2048), BF),
            pltpu.VMEM((4, shard, 2048), BF),
            pltpu.VMEM((4, shard, 2048), BF),
            pltpu.VMEM((5, shard, 2048), BF),
            pltpu.VMEM((18 + 2 * len(LINE_FIRST), 2 * shard, 1024), BF),
            pltpu.VMEM((2, shard, 1024), BF),
            pltpu.VMEM((2, shard, 1024), BF),
            pltpu.VMEM((group, width), BF),
            pltpu.VMEM((2 * group, width), BF),
            pltpu.VMEM((group, 1536), BF),
            pltpu.VMEM((16, own, own), BF),
            pltpu.VMEM((group, 512), BF),
            pltpu.VMEM((own, width), F32),
            pltpu.VMEM((2 * group, width), BF),
            pltpu.VMEM((2 * group, 1024), BF),
            pltpu.VMEM((2 * group, 1024), BF),
            pltpu.VMEM((group, 512), BF),
            pltpu.VMEM((own, width), F32),
            pltpu.VMEM((own, width), F32),
            pltpu.VMEM((2, own, width), BF),
            pltpu.VMEM((2, own, width), BF),
            pltpu.VMEM((4, own, width), BF),
            pltpu.VMEM((2, 2, own, width), BF),
            pltpu.VMEM((len(SUMS), 8, width), F32),
            pltpu.VMEM((4, 8, 1024), F32),
            pltpu.VMEM((16, width), F32),
            pltpu.VMEM((5, 16, width), F32),
            dma((9,)),
            dma((2,)),
            dma((5, 13)),
            dma((2,)),
            dma((2, 19)),
            dma((1,)),
            dma((5, 13)),
            dma((1,)),
            dma((2, 12)),
            dma((16,)),
            dma((16,)),
            dma((5,)),
            dma((5,)),
        ],
        compiler_params=pltpu.CompilerParams(
            collective_id=1, has_side_effects=True, vmem_limit_bytes=63 << 20
        ),
    )(
        counts, stream, cotangent, w_qkv, w_out_t, w_up, w_down_t,
        b_qv, row(b_out), row(b_up), row(b_down), row(g1), row(s1), row(g2), row(s2),
    )


def close_kernel(*refs):
    big, sums, out, small, held, sem = refs[:6], refs[6], refs[7:13], refs[13:22], refs[22:28], refs[28]
    loads = [pltpu.make_async_copy(a, h, sem.at[0, i]) for i, (a, h) in enumerate(zip(big, held))]
    copies = [pltpu.make_async_copy(h, b, sem.at[1, i]) for i, (h, b) in enumerate(zip(held, out))]
    for c in loads:
        c.start()
    place = lax.axis_index("dp") * 2 + lax.axis_index("tensor")
    width = sums.shape[1]
    turned = pltpu.roll(sums[0:8, :], width - place * 32, 1)
    small[0][...] = turned[0:2, :32]
    for i in range(1, 7):
        small[i][...] = turned[i + 1 : i + 2, :32]
    up = pl.ds(pl.multiple_of((place % 8) * 128, 128), 128)
    which = lax.broadcasted_iota(jnp.int32, (8, 128), 0) == place // 8
    small[7][...] = jnp.sum(jnp.where(which, sums[8:16, up], 0.0), axis=0, keepdims=True)
    row = sums[12:13, :]
    small[8][...] = jnp.sqrt(row[:, 0:5] / (row[:, 5:6] * width))
    for load, c in zip(loads, copies):
        load.wait()
        c.start()
    for c in copies:
        c.wait()


def close(*arrays):
    vmem = pl.BlockSpec(memory_space=pltpu.VMEM)
    hbm = pl.BlockSpec(memory_space=pl.ANY)
    small = [(2, 32)] + [(1, 32)] * 6 + [(1, 128), (1, 5)]
    return pl.pallas_call(
        close_kernel,
        out_shape=tuple(jax.ShapeDtypeStruct(a.shape, a.dtype) for a in arrays[:6])
        + tuple(jax.ShapeDtypeStruct(n, F32) for n in small),
        in_specs=[hbm] * 6 + [vmem],
        out_specs=(hbm,) * 6 + (vmem,) * 9,
        scratch_shapes=[pltpu.VMEM(a.shape, a.dtype) for a in arrays[:6]] + [pltpu.SemaphoreType.DMA((2, 6))],
    )(*arrays)


def local_fast(
    stream, counts, cotangent, w_qkv, b_qv, w_out, b_out, w_fc1, b_fc1, w_fc2, b_fc2,
    gain_one, shift_one, gain_two, shift_two,
):
    acts, grad_in, p_qkv, p_out, p_up, p_down, bqv, *rest = close(
        *block(
            counts, stream, cotangent, w_qkv, w_out.T, w_fc1, w_fc2.T, b_qv, b_out, b_fc1, b_fc2,
            gain_one, shift_one, gain_two, shift_two,
        )
    )
    bout, bdown, gain1, shift1, gain2, shift2, bup, rms = (v.reshape(-1) for v in rest[:8])
    return (
        acts, grad_in, p_qkv, bqv, p_out.T, bout, p_up, bup, p_down.T, bdown,
        gain1, shift1, gain2, shift2, rms,
    )

def layer_norm(values, gain, shift):
    centre = jnp.mean(values, axis=-1, keepdims=True)
    offset = values - centre
    spread = jnp.mean(offset * offset, axis=-1, keepdims=True)
    return offset * lax.rsqrt(spread + eps_norm) * gain + shift


def gelu_exact(values):
    return jax.nn.gelu(values, approximate=False)


def masked_scores(queries, key_rows, validity):
    scores = jnp.einsum(
        "bqhd,bkhd->bhqk", queries, key_rows, preferred_element_type=jnp.float32
    ) * HD ** (-0.5)
    return jnp.where(validity[:, None, None, :] > 0, scores, -1e30)


def attend_block(members):
    queries, key_rows, values, validity = members
    scores = masked_scores(queries, key_rows, validity)
    highest = jnp.max(scores, axis=-1, keepdims=True)
    expo_terms = jnp.exp(scores - highest)
    totals = jnp.sum(expo_terms, axis=-1, keepdims=True)
    weights = (expo_terms / totals).astype(jnp.bfloat16)
    mixture = jnp.einsum("bhqk,bkhd->bqhd", weights, values, preferred_element_type=jnp.float32)
    return (mixture.astype(jnp.bfloat16), (highest + jnp.log(totals))[..., 0])


def attend_back(members):
    queries, key_rows, values, validity, log_total, d_mixture = members
    scores = masked_scores(queries, key_rows, validity)
    probs = jnp.exp(scores - log_total[..., None])
    d_values = jnp.einsum(
        "bhqk,bqhd->bkhd", probs.astype(jnp.bfloat16), d_mixture, preferred_element_type=jnp.float32
    )
    d_probs = jnp.einsum("bqhd,bkhd->bhqk", d_mixture, values, preferred_element_type=jnp.float32)
    d_scores = (probs * (d_probs - jnp.sum(probs * d_probs, axis=-1, keepdims=True))).astype(
        jnp.bfloat16
    )
    d_queries = jnp.einsum(
        "bhqk,bkhd->bqhd", d_scores, key_rows, preferred_element_type=jnp.float32
    ) * HD ** (-0.5)
    d_keys = jnp.einsum(
        "bhqk,bqhd->bkhd", d_scores, queries, preferred_element_type=jnp.float32
    ) * HD ** (-0.5)
    return (
        d_queries.astype(jnp.bfloat16),
        d_keys.astype(jnp.bfloat16),
        d_values.astype(jnp.bfloat16),
    )


def local(
    stream,
    counts,
    cotangent,
    w_qkv,
    b_qv,
    w_out,
    b_out,
    w_fc1,
    b_fc1,
    w_fc2,
    b_fc2,
    gain_one,
    shift_one,
    gain_two,
    shift_two,
):
    tensor_pos = lax.axis_index("tensor")
    own_rows = stream.shape[0]
    width = stream.shape[1]
    own_images = own_rows // SLOTS
    slot_index = jnp.arange(SLOTS, dtype=jnp.int32)
    validity_all = (slot_index[None, :] < (BUFFER + counts)[:, None]).astype(jnp.float32)
    own_validity = lax.dynamic_slice_in_dim(validity_all, tensor_pos * own_images, own_images, 0)
    own_valid = own_validity.reshape(own_rows, 1)
    qkv_full, out_full, up_full, down_full = (
        lax.all_gather(w_qkv, "dp", axis=1, tiled=True),
        lax.all_gather(w_out, "dp", axis=1, tiled=True),
        lax.all_gather(w_fc1[None], "dp", axis=1, tiled=True),
        lax.all_gather(w_fc2, "dp", axis=1, tiled=True),
    )
    head_width = w_qkv.shape[2]
    unit_width = w_fc1.shape[1]
    bias_query = lax.dynamic_slice_in_dim(b_qv[0], tensor_pos * head_width, head_width, 0)
    bias_value = lax.dynamic_slice_in_dim(b_qv[1], tensor_pos * head_width, head_width, 0)
    bias_up = lax.dynamic_slice_in_dim(b_fc1, tensor_pos * unit_width, unit_width, 0)
    up_full = up_full[0]
    group_images = validity_all.shape[0]
    group_rows = group_images * SLOTS
    local_heads = head_width // HD
    pairing = 2
    block_count = group_images // pairing
    blocked_valid = validity_all.reshape(block_count, pairing, SLOTS)
    stream_f = stream.astype(jnp.float32)
    normed_one = layer_norm(stream_f, gain_one, shift_one).astype(jnp.bfloat16)
    first_rows = lax.all_gather(normed_one, "tensor", axis=0, tiled=True)
    projected = jnp.einsum("rd,cde->rce", first_rows, qkv_full, preferred_element_type=jnp.float32)
    shape_heads = (block_count, pairing, SLOTS, local_heads, HD)
    queries = (projected[:, 0] + bias_query).astype(jnp.bfloat16).reshape(shape_heads)
    key_rows = projected[:, 1].astype(jnp.bfloat16).reshape(shape_heads)
    values = (projected[:, 2] + bias_value).astype(jnp.bfloat16).reshape(shape_heads)
    mixture, log_total = lax.map(attend_block, (queries, key_rows, values, blocked_valid))
    attn_heads = mixture.reshape(group_rows, head_width)
    taken = attn_heads
    attn_total = lax.psum_scatter(
        jnp.dot(taken, out_full, preferred_element_type=jnp.float32).astype(jnp.bfloat16),
        "tensor",
        scatter_dimension=0,
        tiled=True,
    ).astype(jnp.float32)
    branch = attn_total + b_out
    middle = stream_f + branch
    normed_two = layer_norm(middle, gain_two, shift_two).astype(jnp.bfloat16)
    second_rows = lax.all_gather(normed_two, "tensor", axis=0, tiled=True)
    hidden_pre = jnp.dot(second_rows, up_full, preferred_element_type=jnp.float32) + bias_up
    hidden_act = gelu_exact(hidden_pre).astype(jnp.bfloat16)
    taken = hidden_act
    mlp_total = lax.psum_scatter(
        jnp.dot(taken, down_full, preferred_element_type=jnp.float32).astype(jnp.bfloat16),
        "tensor",
        scatter_dimension=0,
        tiled=True,
    ).astype(jnp.float32)
    feed = mlp_total + b_fc2
    result = middle + feed
    activations = (result * own_valid).astype(jnp.bfloat16)
    squares = jnp.stack(
        [
            jnp.sum(own_valid * member * member)
            for member in (stream_f, middle, result, branch, feed)
        ]
    )
    square_sums, valid_count = lax.psum((squares, jnp.sum(own_valid)), ("dp", "tensor"))
    rms_stats = jnp.sqrt(square_sums / (valid_count * width))
    d_result = cotangent.astype(jnp.float32) * own_valid
    d_feed_low = d_result.astype(jnp.bfloat16)
    d_feed_rows = lax.all_gather(d_feed_low, "tensor", axis=0, tiled=True)
    d_act = jnp.einsum("rd,ud->ru", d_feed_rows, down_full, preferred_element_type=jnp.float32)
    unused_act, gelu_pullback = jax.vjp(gelu_exact, hidden_pre)
    d_pre = gelu_pullback(d_act)[0].astype(jnp.bfloat16)
    grad_down = jnp.einsum("ru,rd->ud", hidden_act, d_feed_rows, preferred_element_type=jnp.float32)
    grad_up = jnp.einsum("rd,ru->du", second_rows, d_pre, preferred_element_type=jnp.float32)
    grad_bias_up = jnp.sum(d_pre, axis=0, dtype=jnp.float32)
    grad_bias_down = jnp.sum(d_feed_low, axis=0, dtype=jnp.float32)
    taken = d_pre
    d_normed_two = lax.psum_scatter(
        jnp.einsum("ru,du->rd", taken, up_full, preferred_element_type=jnp.float32).astype(
            jnp.bfloat16
        ),
        "tensor",
        scatter_dimension=0,
        tiled=True,
    ).astype(jnp.float32)
    unused_two, norm_two_pullback = jax.vjp(layer_norm, middle, gain_two, shift_two)
    d_middle_norm, grad_gain_two, grad_shift_two = norm_two_pullback(d_normed_two)
    d_middle = d_result + d_middle_norm
    d_branch_low = d_middle.astype(jnp.bfloat16)
    grad_bias_out = jnp.sum(d_branch_low, axis=0, dtype=jnp.float32)
    d_branch_rows = lax.all_gather(d_branch_low, "tensor", axis=0, tiled=True)
    d_attn = jnp.einsum(
        "rd,hd->rh", d_branch_rows, out_full, preferred_element_type=jnp.float32
    ).astype(jnp.bfloat16)
    grad_out = jnp.einsum(
        "rh,rd->hd", attn_heads, d_branch_rows, preferred_element_type=jnp.float32
    )
    d_queries, d_keys, d_values = lax.map(
        attend_back,
        (queries, key_rows, values, blocked_valid, log_total, d_attn.reshape(shape_heads)),
    )
    d_projected = jnp.stack(
        [
            d_queries.reshape(group_rows, head_width),
            d_keys.reshape(group_rows, head_width),
            d_values.reshape(group_rows, head_width),
        ],
        axis=1,
    )
    grad_qkv = jnp.einsum(
        "rd,rce->cde", first_rows, d_projected, preferred_element_type=jnp.float32
    )
    bias_terms = jnp.sum(d_projected, axis=0, dtype=jnp.float32)
    taken = d_projected
    d_normed_one = lax.psum_scatter(
        jnp.einsum("rce,cde->rd", taken, qkv_full, preferred_element_type=jnp.float32).astype(
            jnp.bfloat16
        ),
        "tensor",
        scatter_dimension=0,
        tiled=True,
    ).astype(jnp.float32)
    unused_one, norm_one_pullback = jax.vjp(layer_norm, stream_f, gain_one, shift_one)
    d_stream_norm, grad_gain_one, grad_shift_one = norm_one_pullback(d_normed_one)
    grad_input = d_middle + d_stream_norm
    grad_up = grad_up[None]
    bias_qv_full = lax.dynamic_update_slice(
        jnp.zeros((2, width), jnp.float32),
        jnp.stack([bias_terms[0], bias_terms[2]]),
        (jnp.int32(0), tensor_pos * head_width),
    )
    bias_up_full = lax.dynamic_update_slice(
        jnp.zeros((b_fc1.shape[0],), jnp.float32), grad_bias_up, (tensor_pos * unit_width,)
    )
    qkv_part, out_part, up_part, down_part = (
        lax.psum_scatter(
            grad_qkv.astype(jnp.bfloat16), "dp", scatter_dimension=1, tiled=True
        ).astype(jnp.float32),
        lax.psum_scatter(
            grad_out.astype(jnp.bfloat16), "dp", scatter_dimension=1, tiled=True
        ).astype(jnp.float32),
        lax.psum_scatter(
            grad_up.astype(jnp.bfloat16), "dp", scatter_dimension=1, tiled=True
        ).astype(jnp.float32),
        lax.psum_scatter(
            grad_down.astype(jnp.bfloat16), "dp", scatter_dimension=1, tiled=True
        ).astype(jnp.float32),
    )
    small_parts = (
        lax.psum_scatter(bias_qv_full, ("dp", "tensor"), scatter_dimension=1, tiled=True),
        lax.psum_scatter(grad_bias_out, ("dp", "tensor"), scatter_dimension=0, tiled=True),
        lax.psum_scatter(bias_up_full, ("dp", "tensor"), scatter_dimension=0, tiled=True),
        lax.psum_scatter(grad_bias_down, ("dp", "tensor"), scatter_dimension=0, tiled=True),
        lax.psum_scatter(grad_gain_one, ("dp", "tensor"), scatter_dimension=0, tiled=True),
        lax.psum_scatter(grad_shift_one, ("dp", "tensor"), scatter_dimension=0, tiled=True),
        lax.psum_scatter(grad_gain_two, ("dp", "tensor"), scatter_dimension=0, tiled=True),
        lax.psum_scatter(grad_shift_two, ("dp", "tensor"), scatter_dimension=0, tiled=True),
    )
    return (
        activations,
        grad_input,
        qkv_part,
        small_parts[0],
        out_part,
        small_parts[1],
        up_part[0],
        small_parts[2],
        down_part,
        small_parts[3],
        small_parts[4],
        small_parts[5],
        small_parts[6],
        small_parts[7],
        rms_stats,
    )


def solution(mesh):
    fast = mesh.shape["dp"] == 16 and mesh.shape["tensor"] == 2
    return jax.shard_map(
        local_fast if fast else local,
        mesh=mesh,
        in_specs=(
            P(("dp", "tensor"), None),
            P("dp"),
            P(("dp", "tensor"), None),
            P(None, "dp", "tensor"),
            P(),
            P("tensor", "dp"),
            P(),
            P("dp", "tensor"),
            P(),
            P("tensor", "dp"),
            P(),
            P(),
            P(),
            P(),
            P(),
        ),
        out_specs=(
            P(("dp", "tensor"), None),
            P(("dp", "tensor"), None),
            P(None, "dp", "tensor"),
            P(None, ("dp", "tensor")),
            P("tensor", "dp"),
            P(("dp", "tensor")),
            P("dp", "tensor"),
            P(("dp", "tensor")),
            P("tensor", "dp"),
            P(("dp", "tensor")),
            P(("dp", "tensor")),
            P(("dp", "tensor")),
            P(("dp", "tensor")),
            P(("dp", "tensor")),
            P(),
        ),
        check_vma=False,
    )
```

```python
import jax
import jax.numpy as jnp
from jax import lax
from jax.experimental import pallas as pl
from jax.experimental.pallas import tpu as pltpu
from jax.sharding import PartitionSpec as P

HD = 64
BUFFER = 64
SLOTS = 320


eps_norm = 1e-06


MESH = pl.DeviceIdType.MESH


class Place:
    def __init__(self):
        dp = lax.axis_index("dp")
        self.t = lax.axis_index("tensor")
        self.z, self.y, self.x = dp // 4, (dp // 2) % 2, dp % 2
        self.side = self.z // 2
        self.w = self.z + self.side * (3 - 2 * self.z)
        self.step = 1 - 2 * self.side
        self.dp = dp

    def order(self, k):
        o = (self.w, 1 - self.w, 2, 3)[k]
        return 3 * self.side + self.step * o

    def chip(self, z, y, x):
        return z * 4 + y * 2 + x

    def inward(self):
        return (self.chip(self.z + self.step, self.y, self.x), self.t)

    def outward(self):
        return (self.chip(self.z - self.step, self.y, self.x), self.t)

    def across_x(self):
        return (self.chip(self.z, self.y, 1 - self.x), self.t)

    def across_y(self):
        return (self.chip(self.z, 1 - self.y, self.x), self.t)

    def near(self):
        return (self.chip(self.z + 1 - 2 * (self.z % 2), self.y, self.x), self.t)

    def far(self):
        return (self.chip((self.z + 2) % 4, self.y, self.x), self.t)

    def twin(self):
        return (self.dp, 1 - self.t)


def greet(at):
    barrier = pltpu.get_barrier_semaphore()
    for other in (at.across_x(), at.across_y(), at.inward(), at.twin(), at.far()):
        pl.semaphore_signal(barrier, inc=1, device_id=other, device_id_type=MESH)

    @pl.when(at.w == 1)
    def _():
        pl.semaphore_signal(barrier, inc=1, device_id=at.outward(), device_id_type=MESH)


def enter(at):
    pl.semaphore_wait(pltpu.get_barrier_semaphore(), 5 + at.w)


def settle(ref, sem, at, sent):
    copy = pltpu.make_async_remote_copy(
        src_ref=ref, dst_ref=ref, send_sem=sem, recv_sem=sem, device_id=at.twin(), device_id_type=MESH
    )
    if sent:
        copy.wait_send()
    else:
        copy.wait_recv()


class Gather:
    def __init__(self, at, full, shard, pieces, send, recv):
        self.at, self.full, self.shard, self.pieces, self.send, self.recv = at, full, shard, pieces, send, recv

    def rows(self, p, z, y, x, part=None):
        c0, c1 = self.pieces[p]
        start, size = self.at.chip(z, y, x) * self.shard, self.shard
        if part is not None:
            size = self.shard // 2
            start = start + part * size
        return self.full.at[pl.ds(pl.multiple_of(start, size), size), pl.ds(c0, c1 - c0)]

    def copy(self, p, ref, s, r, other):
        return pltpu.make_async_remote_copy(
            src_ref=ref,
            dst_ref=ref,
            send_sem=self.send.at[s],
            recv_sem=self.recv.at[p, r],
            device_id=other,
            device_id_type=MESH,
        )

    def z_in(self, p, z):
        return self.copy(p, self.rows(p, z, self.at.y, self.at.x), 1, z, self.at.inward())

    def z_out(self, p, z):
        return self.copy(p, self.rows(p, z, self.at.y, self.at.x), 1, z, self.at.outward())

    def x_full(self, p, z):
        return self.copy(p, self.rows(p, z, self.at.y, self.at.x), 0, 4 + z, self.at.across_x())

    def y_full(self, p, z):
        return self.copy(p, self.rows(p, z, self.at.y, self.at.x), 0, 8 + z, self.at.across_y())

    def x_half(self, p, z):
        return self.copy(p, self.rows(p, z, 1 - self.at.y, self.at.x, 1), 0, 12, self.at.across_x())

    def y_half(self, p, z):
        return self.copy(p, self.rows(p, z, self.at.y, 1 - self.at.x, 0), 0, 12, self.at.across_y())

    def arrived(self, p, kind, z):
        at = self.at
        ref = (
            lambda: self.rows(p, z, at.y, at.x),
            lambda: self.rows(p, z, at.y, 1 - at.x),
            lambda: self.rows(p, z, 1 - at.y, at.x),
        )[kind]()
        settle(ref, self.recv.at[p, 4 * kind + z], at, False)

    def line(self, p, k, w):
        at = self.at

        @pl.when(at.w == w)
        def _():
            z = at.order(k)
            if k > 0:
                self.arrived(p, 0, z)
            if k == 0 or (k == 1 and w == 1):
                self.z_in(p, z).start()
            if w == 1 and k != 1:
                self.z_out(p, z).start()
            self.x_full(p, z).start()
            self.y_full(p, z).start()

    def plane(self, p, k):
        z = self.at.order(k)
        self.arrived(p, 1, z)
        self.y_half(p, z).start()
        self.arrived(p, 2, z)
        self.x_half(p, z).start()

    def finish(self, p):
        c0, c1 = self.pieces[p]
        settle(self.full.at[0 : 4 * self.shard, c0:c1], self.recv.at[p, 12], self.at, False)

    def drain(self):
        n = sum(c1 - c0 for c0, c1 in self.pieces)
        settle(self.full.at[0 : 12 * self.shard, 0:n], self.send.at[0], self.at, True)
        for w, blocks in ((0, 1), (1, 5)):

            @pl.when(self.at.w == w)
            def _(blocks=blocks):
                settle(self.full.at[0 : blocks * self.shard, 0:n], self.send.at[1], self.at, True)


class Scatter:
    def __init__(self, at, full, shard, pieces, xh, yh, xf, yf, zl, send, recv):
        self.at, self.full, self.shard, self.pieces = at, full, shard, pieces
        self.xh, self.yh, self.xf, self.yf, self.zl = xh, yh, xf, yf, zl
        self.send, self.recv = send, recv

    def cols(self, p):
        c0, c1 = self.pieces[p]
        return pl.ds(c0, c1 - c0)

    def rows(self, p, z, y, x, part=None):
        start, size = self.at.chip(z, y, x) * self.shard, self.shard
        if part is not None:
            size = self.shard // 2
            start = start + part * size
        ref, c0, c1 = self.full(p)
        return ref.at[pl.ds(pl.multiple_of(start, size), size), pl.ds(c0, c1 - c0)]

    def copy(self, p, src, dst, r, other):
        return pltpu.make_async_remote_copy(
            src_ref=src,
            dst_ref=dst,
            send_sem=self.send.at[0],
            recv_sem=self.recv.at[p, r],
            device_id=other,
            device_id_type=MESH,
        )

    def x_half(self, p, z):
        at = self.at
        return self.copy(
            p, self.rows(p, z, 1 - at.y, 1 - at.x, 0), self.xh.at[z, :, self.cols(p)], z, at.across_x()
        )

    def y_half(self, p, z):
        at = self.at
        return self.copy(
            p, self.rows(p, z, 1 - at.y, 1 - at.x, 1), self.yh.at[z, :, self.cols(p)], z, at.across_y()
        )

    def x_full(self, p, z):
        at = self.at
        return self.copy(
            p, self.rows(p, z, at.y, 1 - at.x), self.xf.at[z, :, self.cols(p)], 4 + z, at.across_x()
        )

    def y_full(self, p, z):
        at = self.at
        return self.copy(
            p, self.rows(p, z, 1 - at.y, at.x), self.yf.at[z, :, self.cols(p)], 4 + z, at.across_y()
        )

    def z_in(self, p, z, slot):
        at = self.at
        return self.copy(
            p, self.rows(p, z, at.y, at.x), self.zl.at[slot, :, self.cols(p)], 8 + slot, at.inward()
        )

    def z_out(self, p, z, slot):
        at = self.at
        return self.copy(
            p, self.rows(p, z, at.y, at.x), self.zl.at[slot, :, self.cols(p)], 8 + slot, at.outward()
        )

    def begin(self, p, k):
        z = self.at.order(k)
        self.x_half(p, z).start()
        self.y_half(p, z).start()

    def plane(self, p, k):
        at = self.at
        z = at.order(k)
        settle(self.xf.at[z, :, self.cols(p)], self.recv.at[p, z], at, False)
        ref = self.rows(p, z, 1 - at.y, at.x, 0)
        ref[...] = ref[...] + self.xh[z, :, self.cols(p)]
        self.y_full(p, z).start()
        ref = self.rows(p, z, at.y, 1 - at.x, 1)
        ref[...] = ref[...] + self.yh[z, :, self.cols(p)]
        self.x_full(p, z).start()

    def wait_line(self, p, z, slot):
        self.z_in(p, z, slot).wait_recv()

    def line(self, p, k, w, out):
        at = self.at

        @pl.when(at.w == w)
        def _():
            z = at.order(k)
            full, c0, c1 = self.full(p)
            settle(full.at[0 : 2 * self.shard, c0:c1], self.recv.at[p, 4 + z], at, False)
            ref = self.rows(p, z, at.y, at.x)
            parts = [self.xf.at[z, :, self.cols(p)], self.yf.at[z, :, self.cols(p)]]
            if w == 1:
                self.wait_line(p, z, z)
                parts.append(self.zl.at[z, :, self.cols(p)])
            if k == 0:
                self.wait_line(p, z, 4)
                parts.append(self.zl.at[4, :, self.cols(p)])
            total = ref[...].astype(jnp.float32)
            for part in parts:
                total = total + part[...].astype(jnp.float32)
            if k == 0:
                out(total)
            else:
                ref[...] = total.astype(jnp.bfloat16)
                if w == 0 or k == 3:
                    self.z_in(p, z, z).start()
                elif k == 2:
                    self.z_in(p, z, 4).start()
                else:
                    self.z_out(p, z, 4).start()

    def drain(self, ref):
        settle(ref, self.send.at[0], self.at, True)


class PairGather:
    def __init__(self, at, full, shard, first, columns, sources, send, recv):
        self.first = first
        self.at, self.full, self.shard, self.columns, self.sources = at, full, shard, columns, sources
        self.send, self.recv = send, recv

    def far_x(self, h):
        return self.at.x if h == 0 else 1 - self.at.x

    def rows(self, m, z, y, x):
        c0, n = self.columns[m]
        start = self.at.chip(z, y, x) * self.shard
        return self.full.at[pl.ds(pl.multiple_of(start, self.shard), self.shard), pl.ds(c0, n)]

    def copy(self, m, src, dst, s, r, other):
        return pltpu.make_async_remote_copy(
            src_ref=src,
            dst_ref=dst,
            send_sem=self.send.at[s],
            recv_sem=self.recv.at[m, r],
            device_id=other,
            device_id_type=MESH,
        )

    def x_copy(self, m):
        at = self.at
        c0, n = self.columns[m]
        src = self.sources[m].at[:, pl.ds(pl.multiple_of((1 - at.x) * n, n), n)]
        return self.copy(m, src, self.rows(m, at.z, at.y, at.x), 0, 16, at.across_x())

    def z_in(self, m, h, z):
        ref = self.rows(m, z, self.at.y, self.far_x(h))
        return self.copy(m, ref, ref, 1, 4 * h + z, self.at.inward())

    def z_out(self, m, h, z):
        ref = self.rows(m, z, self.at.y, self.far_x(h))
        return self.copy(m, ref, ref, 1, 4 * h + z, self.at.outward())

    def y_copy(self, m, h, z):
        ref = self.rows(m, z, self.at.y, self.far_x(h))
        return self.copy(m, ref, ref, 0, 17, self.at.across_y())

    def line(self, m, h, k, w):
        at = self.at

        @pl.when(at.w == w)
        def _():
            z = at.order(k)
            ref = self.rows(m, z, at.y, self.far_x(h))
            if k > 0:
                settle(ref, self.recv.at[m, 4 * h + z], at, False)
            elif h == 1:
                settle(ref, self.recv.at[m, 16], at, False)
            if k == 0 or (k == 1 and w == 1):
                self.z_in(m, h, z).start()
            if w == 1 and k != 1:
                self.z_out(m, h, z).start()

    def cross(self, m, h, k, w):
        @pl.when(self.at.w == w)
        def _():
            self.y_copy(m, h, self.at.order(k)).start()

    def over_copy(self, m, h):
        at = self.at
        ref = self.rows(m, at.z, at.y, self.far_x(h))
        return self.copy(m, ref, ref, 0, 17 + h, at.across_y())

    def over(self, m, h):
        at = self.at
        if h == 1:
            settle(self.rows(m, at.z, at.y, 1 - at.x), self.recv.at[m, 16], at, False)
        self.over_copy(m, h).start()

    def column_line(self, m, h, col, k, w):
        at = self.at

        @pl.when(at.w == w)
        def _():
            z = at.order(k)
            ref = self.rows(m, z, at.y if col == 0 else 1 - at.y, self.far_x(h))
            slot = 4 * (2 * h + col) + z
            if k > 0:
                settle(ref, self.recv.at[m, slot], at, False)
            elif col == 1:
                settle(ref, self.recv.at[m, 17 + h], at, False)
            if k == 0 or (k == 1 and w == 1):
                self.copy(m, ref, ref, 1, slot, at.inward()).start()
            if w == 1 and k != 1:
                self.copy(m, ref, ref, 1, slot, at.outward()).start()

    def finish(self, m):
        if m not in self.first:
            c0, n = self.columns[m]
            settle(self.full.at[0 : 8 * self.shard, pl.ds(c0, n)], self.recv.at[m, 17], self.at, False)

    def drain(self, ref):
        later = len(self.first)
        settle(ref.at[0 : (18 - 6 * later) * self.shard // 2, :], self.send.at[0], self.at, True)
        for w, blocks in ((0, 2), (1, 10)):

            @pl.when(self.at.w == w)
            def _(blocks=blocks * (2 + later)):
                settle(ref.at[0 : blocks * self.shard // 2, :], self.send.at[1], self.at, True)


class PairScatter:
    def __init__(self, at, full, shard, first, units, xs, xr, send, recv):
        self.at, self.full, self.shard, self.first = at, full, shard, first
        self.units, self.xs, self.xr, self.send, self.recv = units, xs, xr, send, recv
        self.base = {1: 0, 0: 11 if 1 in first else 9}

    def unit(self, m, z, y):
        ref, c0, n = self.full(m)
        size = 2 * self.shard
        return ref.at[pl.ds(pl.multiple_of((z * 2 + y) * size, size), size), pl.ds(c0, n)]

    def copy(self, m, src, dst, r, other):
        return pltpu.make_async_remote_copy(
            src_ref=src,
            dst_ref=dst,
            send_sem=self.send.at[0],
            recv_sem=self.recv.at[m, r],
            device_id=other,
            device_id_type=MESH,
        )

    def from_y(self, m, z):
        return self.units.at[self.base[m] + (10 if m in self.first else z)]

    def from_z(self, m, col, slot):
        return self.units.at[self.base[m] + (5 * col if m in self.first else 4) + slot]

    def column(self, col):
        return self.at.y if col == 0 else 1 - self.at.y

    def y_copy(self, m, z):
        return self.copy(m, self.unit(m, z, 1 - self.at.y), self.from_y(m, z), 10 if m in self.first else z, self.at.across_y())

    def z_copy(self, m, col, z, slot, other):
        return self.copy(
            m, self.unit(m, z, self.column(col)), self.from_z(m, col, slot), (5 * col if m in self.first else 4) + slot, other
        )

    def x_copy(self, m):
        return self.copy(m, self.xs.at[m], self.xr.at[m], 11, self.at.across_x())

    def begin(self, m, k):
        self.y_copy(m, self.at.order(k)).start()

    def pass_on(self, m, col, k, w):
        at = self.at
        z = at.order(k)
        if w == 0:
            self.z_copy(m, col, z, z, at.inward()).start()
        elif k == 1:
            self.z_copy(m, col, z, 4, at.outward()).start()
        else:
            self.z_copy(m, col, z, z if k == 3 else 4, at.inward()).start()

    def add_line(self, m, col, k, w, extra):
        at = self.at
        z = at.order(k)
        ref = self.unit(m, z, self.column(col))
        parts = list(extra)
        if k == 0:
            self.z_copy(m, col, z, 4, at.inward()).wait_recv()
            parts.append(self.from_z(m, col, 4))
        if w == 1:
            self.z_copy(m, col, z, z, at.inward()).wait_recv()
            parts.append(self.from_z(m, col, z))
        if parts:
            v = ref[...].astype(jnp.float32)
            for part in parts:
                v = v + part[...].astype(jnp.float32)
            ref[...] = v.astype(jnp.bfloat16)

    def finish(self, m, out, second):
        at = self.at
        size = self.shard
        full, c0, n = self.full(m)

        def total(x):
            rows = pl.ds(pl.multiple_of(at.chip(at.z, at.y, x) * size, size), size)
            v = full[rows, pl.ds(c0, n)].astype(jnp.float32)
            if second:
                v = v + self.from_y(m, at.z)[pl.ds(pl.multiple_of(x * size, size), size), :].astype(jnp.float32)
            return v

        self.xs[m] = total(1 - at.x).astype(jnp.bfloat16)
        self.x_copy(m).start()
        out(at.x, total(at.x))

    def line(self, m, k, w, out):
        at = self.at

        @pl.when(at.w == w)
        def _():
            z = at.order(k)
            self.y_copy(m, z).wait_recv()
            self.add_line(m, 0, k, w, [self.from_y(m, z)])
            if k > 0:
                self.pass_on(m, 0, k, w)
            else:
                self.finish(m, out, False)

    def line_first(self, m, col, k, w):
        @pl.when(self.at.w == w)
        def _():
            self.add_line(m, col, k, w, [])
            if k > 0:
                self.pass_on(m, col, k, w)
            elif col == 1:
                self.y_copy(m, self.at.z).start()

    def meet(self, m, out):
        self.y_copy(m, self.at.z).wait_recv()
        self.finish(m, out, True)

    def last(self, m, out):
        self.x_copy(m).wait_recv()
        out(1 - self.at.x, self.xr[m].astype(jnp.float32))

    def drain(self, ref):
        settle(ref, self.send.at[0], self.at, True)


QKV, OUT, UP, DOWN, COLS = 0, 1536, 2048, 3072, 4096
PIECES = ((0, 384), (384, 768), (768, 1152), (1152, 1536), (1536, 2048))
LINE_FIRST = ()
OVER_FIRST = (1,)
PLAN = (
    ((2, 1), (0, 0, 0, 1), (0, 0, 0, 0), (0, 3, 0, 1), (0, 2, 0, 0), (3, 0, 0, 0, 0), (0, 0, 1, 0), (0, 2, 0, 1), (6, 1, 0), (2, 0), (0, 1, 0, 1), (0, 1, 0, 0), (0, 3, 0, 0), (3, 0, 0, 0, 1), (0, 2, 1, 1), (0, 2, 1, 0), (0, 0, 1, 1), (0, 2, 2, 1), (0, 0, 2, 1), (0, 4, 0, 1), (0, 4, 0, 0), (6, 1, 1), (0, 0, 3, 1), (0, 3, 1, 1), (1, 0, 0), (0, 4, 1, 0), (3, 0, 1, 0, 0), (0, 3, 1, 0), (7, 1, 1, 1, 0, 0), (0, 0, 2, 0), (0, 1, 1, 1), (3, 0, 1, 0, 1), (0, 2, 3, 1), (0, 4, 1, 1), (1, 0, 1), (0, 1, 2, 1), (0, 0, 3, 0), (0, 1, 1, 0), (1, 2, 0), (0, 1, 2, 0), (1, 0, 2), (3, 0, 0, 1, 1), (0, 2, 2, 0), (0, 3, 2, 1), (0, 3, 3, 1), (0, 1, 3, 0), (1, 4, 0), (0, 1, 3, 1), (1, 0, 3), (3, 0, 1, 1, 0), (7, 1, 1, 1, 0, 1), (0, 4, 2, 1), (3, 0, 1, 1, 1), (7, 1, 1, 0, 0, 0), (1, 1, 0), (1, 3, 0), (7, 1, 1, 1, 1, 1),),
    ((0, 3, 2, 0), (1, 2, 1), (7, 1, 0, 0, 0, 0), (0, 4, 3, 1), (7, 1, 1, 0, 0, 1), (0, 2, 3, 0), (0, 3, 3, 0), (3, 0, 0, 2, 1), (3, 0, 0, 3, 1), (1, 1, 1), (0, 4, 2, 0), (3, 0, 0, 1, 0), (0, 4, 3, 0), (3, 0, 1, 2, 1),),
    ((1, 1, 2), (1, 1, 3), (7, 1, 0, 1, 0, 1), (3, 0, 0, 2, 0), (7, 1, 1, 0, 1, 1), (1, 2, 2), (1, 2, 3), (7, 1, 0, 0, 0, 1), (7, 1, 1, 0, 2, 1), (1, 4, 1),),
    ((1, 3, 1), (1, 3, 2),),
    (),
    ((1, 4, 2), (4, 0, 1, 0, 0), (4, 0, 0, 0, 1), (1, 4, 3), (1, 3, 3), (7, 1, 0, 1, 0, 0),),
    ((5,),),
    ((7, 1, 1, 0, 1, 0), (4, 0, 0, 0, 0), (7, 1, 1, 1, 1, 0), (3, 0, 1, 2, 0), (4, 0, 0, 1, 0), (3, 0, 1, 3, 1), (4, 0, 1, 0, 1), (7, 1, 0, 0, 1, 1),),
    (),
    (),
    ((4, 0, 0, 2, 0),),
    ((7, 1, 0, 1, 1, 0),),
    (),
    ((7, 1, 0, 1, 1, 1),),
    (),
    (),
    ((4, 0, 0, 1, 1), (4, 0, 0, 2, 1),),
    ((4, 0, 1, 1, 0), (4, 0, 1, 2, 0),),
    ((7, 1, 0, 1, 2, 1),),
    (),
    ((7, 1, 1, 0, 2, 0), (4, 0, 0, 3, 1),),
    ((4, 0, 1, 1, 1),),
    (),
    ((7, 1, 1, 0, 3, 1), (7, 1, 0, 0, 1, 0), (4, 0, 1, 2, 1), (4, 0, 1, 3, 1),),
    ((7, 1, 0, 0, 2, 1), (7, 1, 0, 1, 3, 1), (3, 0, 0, 3, 0), (7, 1, 0, 0, 3, 1), (7, 1, 0, 1, 2, 0), (7, 1, 1, 0, 3, 0), (3, 0, 1, 3, 0),),
    ((4, 0, 1, 3, 0), (4, 0, 0, 3, 0),),
    ((7, 1, 1, 1, 2, 1), (7, 1, 1, 1, 3, 1),),
    (),
    (),
    ((7, 1, 0, 1, 3, 0), (7, 1, 0, 0, 2, 0),),
    ((7, 1, 1, 1, 2, 0), (7, 1, 0, 0, 3, 0),),
    (),
    (),
    (),
    (),
    (),
    (),
    ((13, 1, 3), (7, 1, 1, 1, 3, 0),),
    (),
    (),
    (),
    (),
    (),
    ((13, 1, 2),),
    ((14, 1, 3, 0), (13, 1, 1),),
    (),
    ((13, 1, 0),),
    (),
    (),
    ((13, 0, 3), (14, 1, 3, 1),),
    ((13, 0, 2),),
    ((14, 1, 2, 0),),
    ((13, 0, 1),),
    (),
    (),
    (),
    (),
    (),
    (),
    (),
    (),
    ((10, 4, 3),),
    (),
    (),
    ((10, 4, 2),),
    ((10, 4, 1),),
    (),
    ((14, 1, 2, 1),),
    (),
    ((14, 0, 3, 0), (10, 0, 3),),
    (),
    ((14, 1, 1, 1), (14, 0, 2, 0),),
    (),
    ((10, 1, 3), (10, 1, 2), (10, 2, 3), (10, 2, 2), (10, 0, 2), (10, 4, 0), (10, 0, 1),),
    ((14, 1, 1, 0), (11, 4, 3),),
    ((11, 2, 3), (11, 2, 2), (11, 0, 3), (11, 4, 2), (11, 4, 1), (10, 2, 1),),
    (),
    ((11, 1, 3),),
    (),
    ((10, 1, 1), (11, 4, 0), (12, 4, 3, 0), (12, 4, 2, 0), (11, 0, 2),),
    ((10, 2, 0), (10, 3, 3), (10, 3, 2), (14, 0, 3, 1), (14, 1, 0, 0), (13, 0, 0), (14, 0, 2, 1), (14, 1, 0, 1), (14, 0, 1, 0), (10, 3, 1),),
    ((11, 1, 2), (10, 1, 0),),
    (),
    (),
    (),
    ((14, 0, 1, 1), (11, 1, 1), (12, 0, 3, 0), (11, 3, 3), (12, 1, 3, 0), (11, 2, 1), (12, 4, 3, 1), (12, 2, 3, 0),),
    (),
    ((11, 0, 1), (12, 0, 2, 0), (11, 3, 2), (12, 2, 2, 0), (12, 4, 2, 1), (12, 0, 3, 1), (11, 3, 1), (12, 1, 2, 0), (12, 1, 3, 1), (10, 0, 0),),
    (),
    ((12, 3, 3, 0), (14, 0, 0, 1), (10, 3, 0), (11, 2, 0), (12, 4, 1, 1), (12, 2, 3, 1), (12, 4, 1, 0), (14, 0, 0, 0), (12, 0, 2, 1), (12, 0, 1, 1), (12, 3, 2, 0),),
    (),
    ((12, 1, 2, 1), (12, 2, 1, 0), (12, 0, 1, 0), (12, 1, 1, 0), (12, 1, 1, 1), (12, 3, 3, 1), (11, 1, 0), (12, 2, 2, 1), (12, 2, 1, 1), (12, 3, 1, 0), (11, 0, 0),),
    (),
    ((11, 3, 0), (12, 3, 2, 1), (12, 3, 1, 1), (12, 1, 0, 0), (12, 4, 0, 0), (15, 1), (12, 2, 0, 0), (12, 4, 0, 1), (15, 0), (12, 0, 0, 0), (12, 0, 0, 1), (12, 1, 0, 1),),
    (),
    ((12, 3, 0, 0), (12, 2, 0, 1), (12, 3, 0, 1),),
)
BF, F32 = jnp.bfloat16, jnp.float32
SUMS = ("bq", "bv", "bout", "bdown", "g1", "s1", "g2", "s2", "x", "mid", "res", "branch", "feed")
BLOCK = 32


def nn(a, b):
    return lax.dot_general(a, b, (((1,), (0,)), ((), ())), preferred_element_type=F32)


def nt(a, b):
    return lax.dot_general(a, b, (((1,), (1,)), ((), ())), preferred_element_type=F32)


def tn(a, b):
    return lax.dot_general(a, b, (((0,), (0,)), ((), ())), preferred_element_type=F32)


def at_rows(start, size):
    return pl.ds(pl.multiple_of(start, size), size)


def fold(v):
    return jnp.sum(v.reshape(v.shape[0] // 8, 8, v.shape[1]), axis=0)


def normed(v):
    centre = jnp.mean(v, axis=1, keepdims=True)
    offset = v - centre
    r = lax.rsqrt(jnp.mean(offset * offset, axis=1, keepdims=True) + eps_norm)
    return offset * r, r


def norm_back(dy, n, r, gain):
    dn = dy * gain
    first = jnp.mean(dn, axis=1, keepdims=True)
    second = jnp.mean(dn * n, axis=1, keepdims=True)
    return r * (dn - first - n * second)


def block_kernel(
    counts, x_hbm, cot_hbm, wqkv, wout, wup, wdown, bqv, bout, bup, bdown, g1, s1, g2, s2,
    act_hbm, gin_hbm, qkv_hbm, out_hbm, up_hbm, down_hbm, o_sums,
    x_ref, cot_ref, act_out, gin_out, o_qkv, o_out, o_up, o_down,
    W, G2, G3, xh, yh, xf, yf, zl, units, xs2, xr2,
    rows1, dfeed, qkv, probs, heads, mid, rows2, act, gp, datt,
    own_a, own_c, send_t, send_x, got, got_t, acc, acc_up, sums, sums_got,
    sem_in, ag_send, ag_recv, pg_send, pg_recv, rs_send, rs_recv, ps_send, ps_recv,
    pair_send, pair_recv, sums_send, sums_recv,
):
    at = Place()
    greet(at)
    rows_in = [pltpu.make_async_copy(a, b, sem_in.at[1 + i]) for i, (a, b) in enumerate(((x_hbm, x_ref), (cot_hbm, cot_ref)))]
    for c in rows_in:
        c.start()
    t, x = at.t, at.x
    shard = wup.shape[0]
    own = x_ref.shape[0]
    width = x_ref.shape[1]
    dbr = dfeed.at[0 : 2 * own, :]
    dproj = qkv

    def spot(far_x, far_t):
        return at_rows((far_x * 2 + far_t) * own, own)

    mine, theirs = at_rows(t * own, own), at_rows((1 - t) * own, own)

    here = at_rows(at.dp * shard, shard)
    quarter = pl.ds(pl.multiple_of(x * 1024, 1024), 1024)
    loads = [
        pltpu.make_async_copy(src, W.at[here, pl.ds(c0, n)], sem_in.at[0])
        for src, c0, n in (
            [(wqkv.at[j, :, pl.ds(128 * h, 128)], QKV + 384 * h + 128 * j, 128) for h in range(4) for j in range(3)]
            + [(wout, OUT, 512), (wup.at[:, quarter], UP, 1024), (wdown.at[:, quarter], DOWN, 1024)]
        )
    ]
    for c in loads:
        c.start()
    enter(at)
    g = Gather(at, W, shard, PIECES, ag_send, ag_recv)
    pg = PairGather(at, W, shard, OVER_FIRST, ((UP, 1024), (DOWN, 1024)), (wup, wdown), pg_send, pg_recv)
    pltpu.make_async_copy(W.at[here, :], W.at[here, :], sem_in.at[0]).wait()

    home = {0: (W, DOWN, DOWN + 384), 1: (W, DOWN + 384, DOWN + 768), 2: (G3, 512, 896), 3: (W, OUT, OUT + 384), 4: (G3, 0, 512)}
    sc = Scatter(at, lambda p: home[p], shard, PIECES, xh, yh, xf, yf, zl, rs_send, rs_recv)
    home_pair = {0: (W, UP, 1024), 1: (G2, 0, 1024)}
    ps = PairScatter(at, lambda m: home_pair[m], shard, LINE_FIRST, units, xs2, xr2, ps_send, ps_recv)

    def write(p):
        def store(total):
            if p < 4:
                for j in range(3):
                    o_qkv[j, :, 128 * p : 128 * (p + 1)] = total[:, 128 * j : 128 * (j + 1)]
            else:
                o_out[...] = total
        return store

    def write_pair(m):
        ref = o_up if m == 0 else o_down

        def store(far_x, total):
            ref[:, pl.ds(pl.multiple_of(far_x * 1024, 1024), 1024)] = total
        return store

    def share_feed():
        shares.append(share(2, dfeed, spot(x, t), at.across_x()))

    actions = {
        0: g.line, 1: g.plane, 2: lambda m: pg.x_copy(m).start(), 3: pg.line, 4: pg.cross, 5: share_feed, 6: pg.over, 7: pg.column_line,
        10: sc.begin, 11: sc.plane, 12: lambda p, k, w: sc.line(p, k, w, write(p)),
        13: ps.begin, 14: lambda m, k, w: ps.line(m, k, w, write_pair(m)), 15: lambda m: ps.last(m, write_pair(m)),
        16: ps.line_first, 17: lambda m: ps.meet(m, write_pair(m)),
    }
    done = [0]

    def run(part):
        while done[0] <= min(part, len(PLAN) - 1):
            for kind, *a in PLAN[done[0]]:
                actions[kind](*a)
            done[0] += 1

    def quiet(part):
        return part >= len(PLAN) or not PLAN[part]

    def send(i, src, dst, other):
        return pltpu.make_async_remote_copy(
            src_ref=src, dst_ref=dst, send_sem=pair_send.at[i], recv_sem=pair_recv.at[i],
            device_id=other, device_id_type=MESH,
        )

    def share(i, ref, r, other):
        c = send(i, ref.at[r, :], ref.at[r, :], other)
        c.start()
        return c

    def take(i, ref, r):
        send(i, ref.at[r, :], ref.at[r, :], at.twin()).wait_recv()

    for ref in (acc, acc_up):
        ref[...] = jnp.zeros_like(ref)
    total_of = {name: acc.at[i] for i, name in enumerate(SUMS)}

    def add(name, v):
        ref = total_of[name]
        ref[...] += fold(v)

    def valid_of(image, start, size):
        slot = lax.broadcasted_iota(jnp.int32, (size, 1), 0) + start
        return slot < counts[image] + BUFFER

    def each_block(body):
        def go(b, _):
            body(b * BLOCK, pl.ds(pl.multiple_of(b * BLOCK, BLOCK), BLOCK))
            return 0
        lax.fori_loop(0, own // BLOCK, go, 0)

    def tiles(first, last, body, size=256):
        def go(i, _):
            body(pl.multiple_of(i * size, size))
            return 0
        lax.fori_loop(first // size, last // size, go, 0)

    def first_norm(b, r):
        xv = x_ref[r, :].astype(F32)
        keep = valid_of(t, b, BLOCK).astype(F32)
        n, _ = normed(xv)
        mine_b = pl.ds(pl.multiple_of(t * own + b, BLOCK), BLOCK)
        rows1[mine_b, :] = (n * g1[...] + s1[...]).astype(BF)
        add("x", keep * xv * xv)
        low = (cot_ref[r, :].astype(F32) * keep).astype(BF)
        dfeed[pl.ds(pl.multiple_of((x * 2 + t) * own + b, BLOCK), BLOCK), :] = low
        add("bdown", low.astype(F32))

    for c in rows_in:
        c.wait()
    run(0)
    each_block(first_norm)
    shares = [share(0, rows1, mine, at.twin()), share(1, dfeed, spot(x, t), at.twin())]

    def project(j):
        heads_of = pl.ds(pl.multiple_of(t * 512 + 128 * j, 128), 128)
        cols = pl.ds(QKV + 384 * j, 384)
        bias = jnp.concatenate([bqv[0:1, heads_of], jnp.zeros((1, 128), F32), bqv[1:2, heads_of]], axis=1)
        scale = jnp.where(lax.broadcasted_iota(jnp.int32, (1, 384), 1) < 128, HD**-0.5, 1.0)

        def body(i, _):
            r = at_rows(i * own, own)
            qkv[r, pl.ds(384 * j, 384)] = ((nn(rows1[r, :], W[:, cols]) + bias) * scale).astype(BF)
            return 0
        lax.fori_loop(0, 2, body, 0)

    first_lanes = lax.broadcasted_iota(jnp.int32, (own, 128), 1) < HD

    def attend(image, j):
        r = pl.ds(pl.multiple_of(image * own, own), own)
        c = 384 * j
        q2 = qkv[r, c : c + 128]
        k2 = qkv[r, c + 128 : c + 256]
        v_t = qkv[r, c + 256 : c + 384].T
        hide = jnp.where(valid_of(image, 0, own), 0.0, -1e30)
        outs = []
        for a in range(2):
            qm = jnp.where(first_lanes if a == 0 else ~first_lanes, q2, jnp.zeros_like(q2))
            s = nt(k2, qm) + hide
            e = jnp.exp(s - jnp.max(s, axis=0, keepdims=True))
            low = (e * (1.0 / jnp.sum(e, axis=0, keepdims=True))).astype(BF)
            probs[(j * 2 + image) * 2 + a] = low
            outs.append(nn(v_t[a * HD : (a + 1) * HD], low))
        heads[r, 128 * j : 128 * (j + 1)] = jnp.concatenate(outs, axis=0).T.astype(BF)

    def images(part, body, j):
        run(part)
        if quiet(part + 1):
            def go(i, _):
                body(i, j)
                return 0
            lax.fori_loop(0, 2, go, 0)
        else:
            body(0, j)
            run(part + 1)
            body(1, j)

    for j in range(4):
        run(1 + 4 * j)
        g.finish(j)
        if j == 0:
            take(0, rows1, theirs)
        run(2 + 4 * j)
        project(j)
        images(3 + 4 * j, attend, j)
    run(17)
    g.finish(4)
    run(18)

    def others(i, src, cols, k):
        send_t[0] = nt(src[theirs, :], W[:, cols]).astype(BF)
        copy = send(i, send_t.at[0], got.at[k], at.twin())
        copy.start()
        return copy

    def owns(src, cols, keep):
        keep[...] = nt(src[mine, :], W[:, cols])

    branch_copy = others(3, heads, pl.ds(OUT, 512), 0)
    run(19)
    owns(heads, pl.ds(OUT, 512), own_a)
    run(20)
    branch_copy.wait()

    def second_norm(b, r):
        keep = valid_of(t, b, BLOCK).astype(F32)
        branch = own_a[r, :] + got[0, r, :].astype(F32) + bout[...]
        m = x_ref[r, :].astype(F32) + branch
        mid[r, :] = m
        add("branch", keep * branch * branch)
        add("mid", keep * m * m)
        n, _ = normed(m)
        rows2[pl.ds(pl.multiple_of((x * 2 + t) * own + b, BLOCK), BLOCK), :] = (n * g2[...] + s2[...]).astype(BF)

    run(21)
    each_block(second_norm)
    run(22)
    shares.append(share(4, rows2, spot(x, t), at.across_x()))
    shares.append(share(5, rows2, spot(x, t), at.twin()))
    run(23)

    take(2, dfeed, spot(1 - x, t))
    shares.append(share(6, dfeed, spot(1 - x, t), at.twin()))
    take(1, dfeed, spot(x, 1 - t))
    run(24)
    take(5, rows2, spot(x, 1 - t))

    chip_rows = lambda far_x: at_rows(far_x * 2 * own, 2 * own)

    def halves(part, body):
        run(part)
        if quiet(part + 1):
            tiles(0, 1024, body, 512)
        else:
            body(0)
            run(part + 1)
            body(512)

    def hidden(far_x, part):
        r = chip_rows(far_x)

        def body(c):
            def part_of(d):
                cols = pl.multiple_of(c + d, 256)
                lanes = pl.ds(pl.multiple_of(t * 2048 + x * 1024 + cols, 256), 256)
                u = nn(rows2[r, :], W[:, pl.ds(UP + cols, 256)]) + bup[:, lanes]
                below = 0.5 * (1.0 + lax.erf(u * (0.5**0.5)))
                dense = jnp.exp(-0.5 * u * u) * 0.3989422804014327
                act[r, pl.ds(cols, 256)] = (u * below).astype(BF)
                gp[r, pl.ds(cols, 256)] = (below + u * dense).astype(BF)
            tiles(0, 512, part_of)
        halves(part, body)

    def grad_down(c):
        def part(d):
            cols = pl.ds(pl.multiple_of(c + d, 256), 256)
            G2[:, cols] = tn(dfeed[...], act[:, cols]).astype(BF)
        tiles(0, 512, part)

    run(25)
    pg.finish(0)
    hidden(x, 26)
    run(28)
    take(4, rows2, spot(1 - x, t))
    shares.append(share(7, rows2, spot(1 - x, t), at.twin()))
    run(29)
    take(7, rows2, spot(1 - x, 1 - t))
    hidden(1 - x, 30)
    take(6, dfeed, spot(1 - x, 1 - t))
    halves(33, grad_down)
    run(37)

    def back_act(far_x):
        r = chip_rows(far_x)

        def body(c):
            cols = pl.ds(c, 256)
            d = nn(dfeed[r, :], W[:, pl.ds(DOWN + c, 256)])
            low = (d * gp[r, cols].astype(F32)).astype(BF)
            gp[r, cols] = low
            acc_up[t * 2 + x, :, cols] += fold(low.astype(F32))
        tiles(0, 1024, body)

    class Sum4:
        def __init__(self, i, n, src, cols, keep, parts):
            self.i, self.n, self.src, self.cols, self.keep, self.parts = i, n, src, cols, keep, parts

        def away(self, far_x, slot):
            r = spot(far_x, 1 - t)

            def body(c):
                send_t[slot, :, pl.ds(c, 512)] = nt(self.src[r, :], W[pl.ds(c, 512), self.cols]).astype(BF)
            tiles(0, width, body, 512)
            copy = send(self.i + slot, send_t.at[slot], got_t.at[self.n, slot], at.twin())
            copy.start()
            return copy

        def far(self):
            first = self.away(1 - x, 0)

            r = spot(1 - x, t)

            def product(c):
                send_x[self.n, :, pl.ds(c, 512)] = nt(self.src[r, :], W[pl.ds(c, 512), self.cols]).astype(BF)
            tiles(0, width, product, 512)
            run(self.parts[0])
            first.wait()

            def body(b, r):
                send_x[self.n, r, :] = send_x[self.n, r, :] + got_t[self.n, 0, r, :]
            each_block(body)
            self.cross = send(self.i + 2, send_x.at[self.n], got.at[2 + self.n], at.across_x())
            run(self.parts[1])
            self.cross.start()

        def near(self):
            self.second = self.away(x, 1)
            r = spot(x, t)

            def body(c):
                self.keep[:, pl.ds(c, 512)] = nt(self.src[r, :], W[pl.ds(c, 512), self.cols])
            tiles(0, width, body, 512)

        def value(self, r):
            return self.keep[r, :] + got_t[self.n, 1, r, :].astype(F32) + got[2 + self.n, r, :].astype(F32)

    pg.finish(1)
    run(39)
    back_act(1 - x)
    run(40)
    two = Sum4(8, 0, gp, pl.ds(UP, 1024), own_a, (41, 42))
    two.far()
    run(43)
    back_act(x)
    run(44)
    two.near()
    g.drain()
    pg.drain(W.at[:, 0:2048])

    def grad_up(c):
        def part(d):
            cols = pl.multiple_of(c + d, 256)
            W[:, pl.ds(UP + cols, 256)] = tn(rows2[...], gp[:, pl.ds(cols, 256)]).astype(BF)
        tiles(0, 512, part)

    halves(45, grad_up)
    run(48)
    four = Sum4(11, 1, act, pl.ds(DOWN, 1024), own_c, (49, 50))
    four.far()
    run(51)
    two.second.wait()
    four.near()
    run(52)
    two.cross.wait()
    for i in (1, 2, 5):
        shares[i].wait_send()

    def second_back(b, r):
        dy = two.value(r)
        n, scale = normed(mid[r, :])
        keep = valid_of(t, b, BLOCK).astype(F32)
        add("g2", dy * n)
        add("s2", dy)
        d = cot_ref[r, :].astype(F32) * keep + norm_back(dy, n, scale, g2[...])
        gin_out[r, :] = d
        low = d.astype(BF)
        dbr[pl.ds(pl.multiple_of(t * own + b, BLOCK), BLOCK), :] = low
        add("bout", low.astype(F32))

    run(54)
    each_block(second_back)
    shares.append(share(14, dbr, mine, at.twin()))
    run(55)
    take(14, dbr, theirs)
    run(56)

    def back_heads(c):
        datt[:, pl.ds(c, 512)] = nn(dbr[...], W[:, pl.ds(OUT + c, 512)]).astype(BF)

    back_heads(0)
    run(59)

    def grad_out(c):
        G3[:, pl.ds(c, 512)] = tn(dbr[...], heads[:, pl.ds(c, 512)]).astype(BF)

    grad_out(0)
    run(60)

    def grad_heads(p):
        ref, c0, c1 = home[p]

        ref[:, c0:c1] = tn(rows1[...], dproj[:, 384 * p : 384 * (p + 1)]).astype(BF)

    def attend_back(image, j):
        r = pl.ds(pl.multiple_of(image * own, own), own)
        c = 384 * j
        q2 = qkv[r, c : c + 128]
        k_t = qkv[r, c + 128 : c + 256].T
        v2 = qkv[r, c + 256 : c + 384]
        da = datt[r, 128 * j : 128 * (j + 1)]
        dq, dk, dv = [], [], []
        for a in range(2):
            dam = jnp.where(first_lanes if a == 0 else ~first_lanes, da, jnp.zeros_like(da))
            low = probs[(j * 2 + image) * 2 + a]
            p = low.astype(F32)
            dp = nt(v2, dam)
            ds = (p * (dp - jnp.sum(p * dp, axis=0, keepdims=True))).astype(BF)
            dq.append(nn(k_t[a * HD : (a + 1) * HD], ds))
            dk.append(nn(ds, q2))
            dv.append(nn(low, da))
        for base, v in (
            (0, jnp.concatenate(dq, axis=0).T * HD**-0.5),
            (128, jnp.where(first_lanes, dk[0], dk[1])),
            (256, jnp.where(first_lanes, dv[0], dv[1])),
        ):
            v = v.astype(BF)
            dproj[r, c + base : c + base + 128] = v
            if base != 128:
                lanes = pl.ds(pl.multiple_of(t * 512 + 128 * j, 128), 128)
                ref = total_of["bq" if base == 0 else "bv"]
                ref[:, lanes] += fold(v.astype(F32))

    def finish_feed(b, r):
        keep = valid_of(t, b, BLOCK).astype(F32)
        feed = four.value(r) + bdown[...]
        res = mid[r, :] + feed
        add("feed", keep * feed * feed)
        add("res", keep * res * res)
        act_out[r, :] = (keep * res).astype(BF)

    for j in range(3):
        images(61 + 4 * j, attend_back, j)
        run(63 + 4 * j)
        grad_heads(j)
    run(73)
    four.second.wait()
    four.cross.wait()
    run(74)
    each_block(finish_feed)
    outs = [pltpu.make_async_copy(act_out, act_hbm, sem_in.at[3])]
    outs[0].start()
    images(75, attend_back, 3)
    run(77)
    one_copy = others(15, dproj, pl.ds(QKV, 1536), 1)
    run(78)
    grad_heads(3)
    run(80)
    owns(dproj, pl.ds(QKV, 1536), own_a)
    run(81)
    one_copy.wait()
    run(82)

    def first_back(b, r):
        dy = own_a[r, :] + got[1, r, :].astype(F32)
        n, scale = normed(x_ref[r, :].astype(F32))
        add("g1", dy * n)
        add("s1", dy)
        gin_out[r, :] += norm_back(dy, n, scale, g1[...])

    each_block(first_back)
    outs.append(pltpu.make_async_copy(gin_out, gin_hbm, sem_in.at[4]))
    outs[1].start()
    run(83)

    for i in range(8):
        sums[i : i + 1, :] = jnp.sum(acc[i], axis=0, keepdims=True)
    for i in range(4):
        sums[8 + i : 9 + i, :] = jnp.sum(acc_up[i], axis=0, keepdims=True)
    lane = lax.broadcasted_iota(jnp.int32, (1, width), 1)
    row = jnp.where(lane == 5, (counts[t] + BUFFER).astype(F32), 0.0)
    for i, name in enumerate(("x", "mid", "res", "branch", "feed")):
        row = jnp.where(lane == i, jnp.sum(jnp.sum(total_of[name][...], axis=0, keepdims=True), axis=1, keepdims=True), row)
    sums[12:13, :] = row
    sums[13:16, :] = jnp.zeros((3, width), F32)
    for i, other in enumerate((at.twin(), at.across_x(), at.across_y(), at.near(), at.far())):
        c = pltpu.make_async_remote_copy(
            src_ref=sums, dst_ref=sums_got.at[i], send_sem=sums_send.at[i], recv_sem=sums_recv.at[i],
            device_id=other, device_id_type=MESH,
        )
        run(84 + 2 * i)
        c.start()
        run(85 + 2 * i)
        c.wait()
        sums[...] += sums_got[i]
    o_sums[...] = sums[...]
    run(1000)
    for i, (a, b) in enumerate(((o_qkv, qkv_hbm), (o_out, out_hbm), (o_up, up_hbm), (o_down, down_hbm))):
        outs.append(pltpu.make_async_copy(a, b, sem_in.at[5 + i]))
        outs[-1].start()
    sent = W.at[0 : 15 * shard, 0:2048]
    sc.drain(sent)
    ps.drain(sent)
    for c in outs:
        c.wait()
    for i in (0, 3, 4, 6, 7):
        shares[i].wait_send()


def block(counts, stream, cotangent, w_qkv, w_out_t, w_up, w_down_t, b_qv, b_out, b_up, b_down, g1, s1, g2, s2):
    own, width = stream.shape
    shard = w_up.shape[0]
    rows = 16 * shard
    group = 2 * own
    vmem = pl.BlockSpec(memory_space=pltpu.VMEM)
    hbm = pl.BlockSpec(memory_space=pl.ANY)
    dma = pltpu.SemaphoreType.DMA
    row = lambda v: v.reshape(1, -1)
    return pl.pallas_call(
        block_kernel,
        out_shape=(
            jax.ShapeDtypeStruct((own, width), BF),
            jax.ShapeDtypeStruct((own, width), F32),
            jax.ShapeDtypeStruct((3, shard, 512), F32),
            jax.ShapeDtypeStruct((shard, 512), F32),
            jax.ShapeDtypeStruct((shard, 2048), F32),
            jax.ShapeDtypeStruct((shard, 2048), F32),
            jax.ShapeDtypeStruct((16, width), F32),
        ),
        in_specs=[pl.BlockSpec(memory_space=pltpu.SMEM)] + [hbm] * 6 + [vmem] * 8,
        out_specs=(hbm,) * 6 + (vmem,),
        scratch_shapes=[
            pltpu.VMEM((own, width), BF),
            pltpu.VMEM((own, width), BF),
            pltpu.VMEM((own, width), BF),
            pltpu.VMEM((own, width), F32),
            pltpu.VMEM((3, shard, 512), F32),
            pltpu.VMEM((shard, 512), F32),
            pltpu.VMEM((shard, 2048), F32),
            pltpu.VMEM((shard, 2048), F32),
            pltpu.VMEM((rows, COLS), BF),
            pltpu.VMEM((rows, 1024), BF),
            pltpu.VMEM((rows, 1024), BF),
            pltpu.VMEM((4, shard // 2, 2048), BF),
            pltpu.VMEM((4, shard // 2, 2048), BF),
            pltpu.VMEM((4, shard, 2048), BF),
            pltpu.VMEM((4, shard, 2048), BF),
            pltpu.VMEM((5, shard, 2048), BF),
            pltpu.VMEM((18 + 2 * len(LINE_FIRST), 2 * shard, 1024), BF),
            pltpu.VMEM((2, shard, 1024), BF),
            pltpu.VMEM((2, shard, 1024), BF),
            pltpu.VMEM((group, width), BF),
            pltpu.VMEM((2 * group, width), BF),
            pltpu.VMEM((group, 1536), BF),
            pltpu.VMEM((16, own, own), BF),
            pltpu.VMEM((group, 512), BF),
            pltpu.VMEM((own, width), F32),
            pltpu.VMEM((2 * group, width), BF),
            pltpu.VMEM((2 * group, 1024), BF),
            pltpu.VMEM((2 * group, 1024), BF),
            pltpu.VMEM((group, 512), BF),
            pltpu.VMEM((own, width), F32),
            pltpu.VMEM((own, width), F32),
            pltpu.VMEM((2, own, width), BF),
            pltpu.VMEM((2, own, width), BF),
            pltpu.VMEM((4, own, width), BF),
            pltpu.VMEM((2, 2, own, width), BF),
            pltpu.VMEM((len(SUMS), 8, width), F32),
            pltpu.VMEM((4, 8, 1024), F32),
            pltpu.VMEM((16, width), F32),
            pltpu.VMEM((5, 16, width), F32),
            dma((9,)),
            dma((2,)),
            dma((5, 13)),
            dma((2,)),
            dma((2, 19)),
            dma((1,)),
            dma((5, 13)),
            dma((1,)),
            dma((2, 12)),
            dma((16,)),
            dma((16,)),
            dma((5,)),
            dma((5,)),
        ],
        compiler_params=pltpu.CompilerParams(
            collective_id=1, has_side_effects=True, vmem_limit_bytes=63 << 20
        ),
    )(
        counts, stream, cotangent, w_qkv, w_out_t, w_up, w_down_t,
        b_qv, row(b_out), row(b_up), row(b_down), row(g1), row(s1), row(g2), row(s2),
    )


def close_kernel(*refs):
    big, sums, out, small, held, sem = refs[:6], refs[6], refs[7:13], refs[13:22], refs[22:28], refs[28]
    loads = [pltpu.make_async_copy(a, h, sem.at[0, i]) for i, (a, h) in enumerate(zip(big, held))]
    copies = [pltpu.make_async_copy(h, b, sem.at[1, i]) for i, (h, b) in enumerate(zip(held, out))]
    for c in loads:
        c.start()
    place = lax.axis_index("dp") * 2 + lax.axis_index("tensor")
    width = sums.shape[1]
    turned = pltpu.roll(sums[0:8, :], width - place * 32, 1)
    small[0][...] = turned[0:2, :32]
    for i in range(1, 7):
        small[i][...] = turned[i + 1 : i + 2, :32]
    up = pl.ds(pl.multiple_of((place % 8) * 128, 128), 128)
    which = lax.broadcasted_iota(jnp.int32, (8, 128), 0) == place // 8
    small[7][...] = jnp.sum(jnp.where(which, sums[8:16, up], 0.0), axis=0, keepdims=True)
    row = sums[12:13, :]
    small[8][...] = jnp.sqrt(row[:, 0:5] / (row[:, 5:6] * width))
    for load, c in zip(loads, copies):
        load.wait()
        c.start()
    for c in copies:
        c.wait()


def close(*arrays):
    vmem = pl.BlockSpec(memory_space=pltpu.VMEM)
    hbm = pl.BlockSpec(memory_space=pl.ANY)
    small = [(2, 32)] + [(1, 32)] * 6 + [(1, 128), (1, 5)]
    return pl.pallas_call(
        close_kernel,
        out_shape=tuple(jax.ShapeDtypeStruct(a.shape, a.dtype) for a in arrays[:6])
        + tuple(jax.ShapeDtypeStruct(n, F32) for n in small),
        in_specs=[hbm] * 6 + [vmem],
        out_specs=(hbm,) * 6 + (vmem,) * 9,
        scratch_shapes=[pltpu.VMEM(a.shape, a.dtype) for a in arrays[:6]] + [pltpu.SemaphoreType.DMA((2, 6))],
    )(*arrays)


def local_fast(
    stream, counts, cotangent, w_qkv, b_qv, w_out, b_out, w_fc1, b_fc1, w_fc2, b_fc2,
    gain_one, shift_one, gain_two, shift_two,
):
    acts, grad_in, p_qkv, p_out, p_up, p_down, bqv, *rest = close(
        *block(
            counts, stream, cotangent, w_qkv, w_out.T, w_fc1, w_fc2.T, b_qv, b_out, b_fc1, b_fc2,
            gain_one, shift_one, gain_two, shift_two,
        )
    )
    bout, bdown, gain1, shift1, gain2, shift2, bup, rms = (v.reshape(-1) for v in rest[:8])
    return (
        acts, grad_in, p_qkv, bqv, p_out.T, bout, p_up, bup, p_down.T, bdown,
        gain1, shift1, gain2, shift2, rms,
    )

def layer_norm(values, gain, shift):
    centre = jnp.mean(values, axis=-1, keepdims=True)
    offset = values - centre
    spread = jnp.mean(offset * offset, axis=-1, keepdims=True)
    return offset * lax.rsqrt(spread + eps_norm) * gain + shift


def gelu_exact(values):
    return jax.nn.gelu(values, approximate=False)


def masked_scores(queries, key_rows, validity):
    scores = jnp.einsum(
        "bqhd,bkhd->bhqk", queries, key_rows, preferred_element_type=jnp.float32
    ) * HD ** (-0.5)
    return jnp.where(validity[:, None, None, :] > 0, scores, -1e30)


def attend_block(members):
    queries, key_rows, values, validity = members
    scores = masked_scores(queries, key_rows, validity)
    highest = jnp.max(scores, axis=-1, keepdims=True)
    expo_terms = jnp.exp(scores - highest)
    totals = jnp.sum(expo_terms, axis=-1, keepdims=True)
    weights = (expo_terms / totals).astype(jnp.bfloat16)
    mixture = jnp.einsum("bhqk,bkhd->bqhd", weights, values, preferred_element_type=jnp.float32)
    return (mixture.astype(jnp.bfloat16), (highest + jnp.log(totals))[..., 0])


def attend_back(members):
    queries, key_rows, values, validity, log_total, d_mixture = members
    scores = masked_scores(queries, key_rows, validity)
    probs = jnp.exp(scores - log_total[..., None])
    d_values = jnp.einsum(
        "bhqk,bqhd->bkhd", probs.astype(jnp.bfloat16), d_mixture, preferred_element_type=jnp.float32
    )
    d_probs = jnp.einsum("bqhd,bkhd->bhqk", d_mixture, values, preferred_element_type=jnp.float32)
    d_scores = (probs * (d_probs - jnp.sum(probs * d_probs, axis=-1, keepdims=True))).astype(
        jnp.bfloat16
    )
    d_queries = jnp.einsum(
        "bhqk,bkhd->bqhd", d_scores, key_rows, preferred_element_type=jnp.float32
    ) * HD ** (-0.5)
    d_keys = jnp.einsum(
        "bhqk,bqhd->bkhd", d_scores, queries, preferred_element_type=jnp.float32
    ) * HD ** (-0.5)
    return (
        d_queries.astype(jnp.bfloat16),
        d_keys.astype(jnp.bfloat16),
        d_values.astype(jnp.bfloat16),
    )


def local(
    stream,
    counts,
    cotangent,
    w_qkv,
    b_qv,
    w_out,
    b_out,
    w_fc1,
    b_fc1,
    w_fc2,
    b_fc2,
    gain_one,
    shift_one,
    gain_two,
    shift_two,
):
    tensor_pos = lax.axis_index("tensor")
    own_rows = stream.shape[0]
    width = stream.shape[1]
    own_images = own_rows // SLOTS
    slot_index = jnp.arange(SLOTS, dtype=jnp.int32)
    validity_all = (slot_index[None, :] < (BUFFER + counts)[:, None]).astype(jnp.float32)
    own_validity = lax.dynamic_slice_in_dim(validity_all, tensor_pos * own_images, own_images, 0)
    own_valid = own_validity.reshape(own_rows, 1)
    qkv_full, out_full, up_full, down_full = (
        lax.all_gather(w_qkv, "dp", axis=1, tiled=True),
        lax.all_gather(w_out, "dp", axis=1, tiled=True),
        lax.all_gather(w_fc1[None], "dp", axis=1, tiled=True),
        lax.all_gather(w_fc2, "dp", axis=1, tiled=True),
    )
    head_width = w_qkv.shape[2]
    unit_width = w_fc1.shape[1]
    bias_query = lax.dynamic_slice_in_dim(b_qv[0], tensor_pos * head_width, head_width, 0)
    bias_value = lax.dynamic_slice_in_dim(b_qv[1], tensor_pos * head_width, head_width, 0)
    bias_up = lax.dynamic_slice_in_dim(b_fc1, tensor_pos * unit_width, unit_width, 0)
    up_full = up_full[0]
    group_images = validity_all.shape[0]
    group_rows = group_images * SLOTS
    local_heads = head_width // HD
    pairing = 2
    block_count = group_images // pairing
    blocked_valid = validity_all.reshape(block_count, pairing, SLOTS)
    stream_f = stream.astype(jnp.float32)
    normed_one = layer_norm(stream_f, gain_one, shift_one).astype(jnp.bfloat16)
    first_rows = lax.all_gather(normed_one, "tensor", axis=0, tiled=True)
    projected = jnp.einsum("rd,cde->rce", first_rows, qkv_full, preferred_element_type=jnp.float32)
    shape_heads = (block_count, pairing, SLOTS, local_heads, HD)
    queries = (projected[:, 0] + bias_query).astype(jnp.bfloat16).reshape(shape_heads)
    key_rows = projected[:, 1].astype(jnp.bfloat16).reshape(shape_heads)
    values = (projected[:, 2] + bias_value).astype(jnp.bfloat16).reshape(shape_heads)
    mixture, log_total = lax.map(attend_block, (queries, key_rows, values, blocked_valid))
    attn_heads = mixture.reshape(group_rows, head_width)
    taken = attn_heads
    attn_total = lax.psum_scatter(
        jnp.dot(taken, out_full, preferred_element_type=jnp.float32).astype(jnp.bfloat16),
        "tensor",
        scatter_dimension=0,
        tiled=True,
    ).astype(jnp.float32)
    branch = attn_total + b_out
    middle = stream_f + branch
    normed_two = layer_norm(middle, gain_two, shift_two).astype(jnp.bfloat16)
    second_rows = lax.all_gather(normed_two, "tensor", axis=0, tiled=True)
    hidden_pre = jnp.dot(second_rows, up_full, preferred_element_type=jnp.float32) + bias_up
    hidden_act = gelu_exact(hidden_pre).astype(jnp.bfloat16)
    taken = hidden_act
    mlp_total = lax.psum_scatter(
        jnp.dot(taken, down_full, preferred_element_type=jnp.float32).astype(jnp.bfloat16),
        "tensor",
        scatter_dimension=0,
        tiled=True,
    ).astype(jnp.float32)
    feed = mlp_total + b_fc2
    result = middle + feed
    activations = (result * own_valid).astype(jnp.bfloat16)
    squares = jnp.stack(
        [
            jnp.sum(own_valid * member * member)
            for member in (stream_f, middle, result, branch, feed)
        ]
    )
    square_sums, valid_count = lax.psum((squares, jnp.sum(own_valid)), ("dp", "tensor"))
    rms_stats = jnp.sqrt(square_sums / (valid_count * width))
    d_result = cotangent.astype(jnp.float32) * own_valid
    d_feed_low = d_result.astype(jnp.bfloat16)
    d_feed_rows = lax.all_gather(d_feed_low, "tensor", axis=0, tiled=True)
    d_act = jnp.einsum("rd,ud->ru", d_feed_rows, down_full, preferred_element_type=jnp.float32)
    unused_act, gelu_pullback = jax.vjp(gelu_exact, hidden_pre)
    d_pre = gelu_pullback(d_act)[0].astype(jnp.bfloat16)
    grad_down = jnp.einsum("ru,rd->ud", hidden_act, d_feed_rows, preferred_element_type=jnp.float32)
    grad_up = jnp.einsum("rd,ru->du", second_rows, d_pre, preferred_element_type=jnp.float32)
    grad_bias_up = jnp.sum(d_pre, axis=0, dtype=jnp.float32)
    grad_bias_down = jnp.sum(d_feed_low, axis=0, dtype=jnp.float32)
    taken = d_pre
    d_normed_two = lax.psum_scatter(
        jnp.einsum("ru,du->rd", taken, up_full, preferred_element_type=jnp.float32).astype(
            jnp.bfloat16
        ),
        "tensor",
        scatter_dimension=0,
        tiled=True,
    ).astype(jnp.float32)
    unused_two, norm_two_pullback = jax.vjp(layer_norm, middle, gain_two, shift_two)
    d_middle_norm, grad_gain_two, grad_shift_two = norm_two_pullback(d_normed_two)
    d_middle = d_result + d_middle_norm
    d_branch_low = d_middle.astype(jnp.bfloat16)
    grad_bias_out = jnp.sum(d_branch_low, axis=0, dtype=jnp.float32)
    d_branch_rows = lax.all_gather(d_branch_low, "tensor", axis=0, tiled=True)
    d_attn = jnp.einsum(
        "rd,hd->rh", d_branch_rows, out_full, preferred_element_type=jnp.float32
    ).astype(jnp.bfloat16)
    grad_out = jnp.einsum(
        "rh,rd->hd", attn_heads, d_branch_rows, preferred_element_type=jnp.float32
    )
    d_queries, d_keys, d_values = lax.map(
        attend_back,
        (queries, key_rows, values, blocked_valid, log_total, d_attn.reshape(shape_heads)),
    )
    d_projected = jnp.stack(
        [
            d_queries.reshape(group_rows, head_width),
            d_keys.reshape(group_rows, head_width),
            d_values.reshape(group_rows, head_width),
        ],
        axis=1,
    )
    grad_qkv = jnp.einsum(
        "rd,rce->cde", first_rows, d_projected, preferred_element_type=jnp.float32
    )
    bias_terms = jnp.sum(d_projected, axis=0, dtype=jnp.float32)
    taken = d_projected
    d_normed_one = lax.psum_scatter(
        jnp.einsum("rce,cde->rd", taken, qkv_full, preferred_element_type=jnp.float32).astype(
            jnp.bfloat16
        ),
        "tensor",
        scatter_dimension=0,
        tiled=True,
    ).astype(jnp.float32)
    unused_one, norm_one_pullback = jax.vjp(layer_norm, stream_f, gain_one, shift_one)
    d_stream_norm, grad_gain_one, grad_shift_one = norm_one_pullback(d_normed_one)
    grad_input = d_middle + d_stream_norm
    grad_up = grad_up[None]
    bias_qv_full = lax.dynamic_update_slice(
        jnp.zeros((2, width), jnp.float32),
        jnp.stack([bias_terms[0], bias_terms[2]]),
        (jnp.int32(0), tensor_pos * head_width),
    )
    bias_up_full = lax.dynamic_update_slice(
        jnp.zeros((b_fc1.shape[0],), jnp.float32), grad_bias_up, (tensor_pos * unit_width,)
    )
    qkv_part, out_part, up_part, down_part = (
        lax.psum_scatter(
            grad_qkv.astype(jnp.bfloat16), "dp", scatter_dimension=1, tiled=True
        ).astype(jnp.float32),
        lax.psum_scatter(
            grad_out.astype(jnp.bfloat16), "dp", scatter_dimension=1, tiled=True
        ).astype(jnp.float32),
        lax.psum_scatter(
            grad_up.astype(jnp.bfloat16), "dp", scatter_dimension=1, tiled=True
        ).astype(jnp.float32),
        lax.psum_scatter(
            grad_down.astype(jnp.bfloat16), "dp", scatter_dimension=1, tiled=True
        ).astype(jnp.float32),
    )
    small_parts = (
        lax.psum_scatter(bias_qv_full, ("dp", "tensor"), scatter_dimension=1, tiled=True),
        lax.psum_scatter(grad_bias_out, ("dp", "tensor"), scatter_dimension=0, tiled=True),
        lax.psum_scatter(bias_up_full, ("dp", "tensor"), scatter_dimension=0, tiled=True),
        lax.psum_scatter(grad_bias_down, ("dp", "tensor"), scatter_dimension=0, tiled=True),
        lax.psum_scatter(grad_gain_one, ("dp", "tensor"), scatter_dimension=0, tiled=True),
        lax.psum_scatter(grad_shift_one, ("dp", "tensor"), scatter_dimension=0, tiled=True),
        lax.psum_scatter(grad_gain_two, ("dp", "tensor"), scatter_dimension=0, tiled=True),
        lax.psum_scatter(grad_shift_two, ("dp", "tensor"), scatter_dimension=0, tiled=True),
    )
    return (
        activations,
        grad_input,
        qkv_part,
        small_parts[0],
        out_part,
        small_parts[1],
        up_part[0],
        small_parts[2],
        down_part,
        small_parts[3],
        small_parts[4],
        small_parts[5],
        small_parts[6],
        small_parts[7],
        rms_stats,
    )


def solution(mesh):
    fast = mesh.shape["dp"] == 16 and mesh.shape["tensor"] == 2
    return jax.shard_map(
        local_fast if fast else local,
        mesh=mesh,
        in_specs=(
            P(("dp", "tensor"), None),
            P("dp"),
            P(("dp", "tensor"), None),
            P(None, "dp", "tensor"),
            P(),
            P("tensor", "dp"),
            P(),
            P("dp", "tensor"),
            P(),
            P("tensor", "dp"),
            P(),
            P(),
            P(),
            P(),
            P(),
        ),
        out_specs=(
            P(("dp", "tensor"), None),
            P(("dp", "tensor"), None),
            P(None, "dp", "tensor"),
            P(None, ("dp", "tensor")),
            P("tensor", "dp"),
            P(("dp", "tensor")),
            P("dp", "tensor"),
            P(("dp", "tensor")),
            P("tensor", "dp"),
            P(("dp", "tensor")),
            P(("dp", "tensor")),
            P(("dp", "tensor")),
            P(("dp", "tensor")),
            P(("dp", "tensor")),
            P(),
        ),
        check_vma=False,
    )
```
